32 devices in a mesh: rows: 8 (over y, x, core), heads: 4 (over z).
Axes of the slice: x: 2, y: 2, z: 4, core: 2. Of those that a mesh axis runs over, the one named last changes fastest.
Arguments:
- layer_in: bfloat16 [32768, 768], P(('rows', 'heads')), may hold values from -6 to 6
- segment_ids: int32 [64, 512], P('rows'), may hold values from 0 to 3, never falling along the last dimension, each value on 1 to 256 neighbouring positions
- w_query: bfloat16 [768, 768], P(None, 'heads'), may hold values from -0.21875 to 0.21875
- w_key: bfloat16 [768, 768], P(None, 'heads'), may hold values from -0.21875 to 0.21875
- w_value: bfloat16 [768, 768], P(None, 'heads'), may hold values from -0.21875 to 0.21875
- b_query: bfloat16 [768], P('heads'), may hold values from -3 to 3
- b_value: bfloat16 [768], P('heads'), may hold values from -3 to 3
- w_output: bfloat16 [768, 768], replicated, may hold values from -0.875 to 0.875
- b_output: float32 [768], replicated, may hold values from -3 to 3
- gain_attn: float32 [768], replicated, may hold values from 0.5 to 1.5
- shift_attn: float32 [768], replicated, may hold values from -3 to 3
- w_inner: bfloat16 [768, 3072], replicated, may hold values from -0.21875 to 0.21875
- b_inner: float32 [3072], replicated, may hold values from -3 to 3
- w_outer: bfloat16 [3072, 768], replicated, may hold values from -0.109375 to 0.109375
- b_outer: float32 [768], replicated, may hold values from -3 to 3
- gain_ffn: float32 [768], replicated, may hold values from 0.5 to 1.5
- shift_ffn: float32 [768], replicated, may hold values from -3 to 3
- cotangent: bfloat16 [32768, 768], P(('rows', 'heads')), may hold values from -6 to 6
Outputs:
- layer_out: bfloat16 [32768, 768], P(('rows', 'heads'))
- input_grad: float32 [32768, 768], P(('rows', 'heads'))
- w_query_grad: float32 [768, 768], P(None, 'heads')
- w_key_grad: float32 [768, 768], P(None, 'heads')
- w_value_grad: float32 [768, 768], P(None, 'heads')
- b_query_grad: float32 [768], P('heads')
- b_value_grad: float32 [768], P('heads')
- w_output_grad: float32 [768, 768], replicated
- b_output_grad: float32 [768], replicated
- gain_attn_grad: float32 [768], replicated
- shift_attn_grad: float32 [768], replicated
- w_inner_grad: float32 [768, 3072], P(None, ('rows', 'heads'))
- b_inner_grad: float32 [3072], P(('rows', 'heads'))
- w_outer_grad: float32 [3072, 768], P(('rows', 'heads'))
- b_outer_grad: float32 [768], replicated
- gain_ffn_grad: float32 [768], replicated
- shift_ffn_grad: float32 [768], replicated
The draws below stay inside these ranges and needn't reach their ends.
Inputs may be any that keep to these rules, and one draw needn't show every extreme that they name: `segment_ids`: within each packed row the ids number its documents in order, never falling; every row holds 256 positions of one document at most, and some document reaches that.
All inputs are finite; a program needn't handle non-finite values.
Results may differ from the reference program's by a relative error of at most 0.015.
Values may be sent and summed in bfloat16 or wider, within the bound.
No kernel may reach another device: no remote copies, remote signals or barrier semaphores. Data moves between devices by JAX's collectives and lax.ppermute only.
A program may use at most 192 MiB of HBM per device.

```python
import math
import jax
import jax.numpy as jnp
import numpy as np
from jax import lax

D = 768
H = 12
HD = 64
FF = 3072
L = 512
SEQS = 64
TOKENS = 32768


def block_levels(stream_key, dims, cuts, smallest, largest):
    def one(dim, shards_of):
        draws = jax.random.uniform(jax.random.fold_in(jax.random.fold_in(stream_key, 6), dim), (shards_of,), jnp.float32, smallest / len(cuts), largest / len(cuts))
        return jnp.repeat(jnp.exp(draws), dims[dim] // shards_of).reshape((-1,) + (1,) * (len(dims) - dim - 1))

    loudness = one(*cuts[0])
    for cut in cuts[1:]:
        loudness = loudness * one(*cut)
    return loudness


def profile(number_of, total, most, lean):
    loads = [(1 << 20) // math.isqrt(rank ** lean) + 1 for rank in range(2, number_of + 1)]
    spare, given = total - most - (number_of - 1), [1] * (number_of - 1)
    while spare > 0:
        free = [i for i in range(number_of - 1) if given[i] < most]
        mass, left = sum([loads[i] for i in free]), spare
        for i in free:
            more = min(most - given[i], max(1, left * loads[i] // mass), spare)
            given[i] = given[i] + more
            spare = spare - more
    return np.array([most] + given)


def ragged_sizes(rng, amount, total, bound, lean):
    if amount == 2:
        one = jax.random.randint(rng, (), max(1, total - bound), min(bound, total - 1) + 1)
        return jnp.stack([one, total - one])
    lengths = jnp.asarray(profile(amount, total, bound, lean), jnp.int32)
    couples = (amount - 1) // 2
    source_of, receiver = lengths[1:1 + 2 * couples:2], lengths[2:2 + 2 * couples:2]
    slack = jnp.minimum(source_of - 1, bound - receiver)
    passed = jax.random.randint(jax.random.fold_in(rng, 1), (couples,), 0, 1 << 20) % (slack + 1)
    lengths = lengths.at[1:1 + 2 * couples:2].set(source_of - passed).at[2:2 + 2 * couples:2].set(receiver + passed)
    return lengths[jax.random.permutation(jax.random.fold_in(rng, 2), amount)]


def normal_values(own_key, extent, deviation, limit, shards=(), held_as=jnp.bfloat16):
    values = deviation * jax.random.normal(own_key, extent, jnp.float32)
    if shards:
        values = values * block_levels(own_key, extent, shards, -0.22, 0.18)
    return jnp.clip(values, -limit, limit).astype(held_as)


def setup_inputs(seed: int = 0) -> dict:
    key_list = jax.random.split(jax.random.key(seed), 19)
    layer_in = normal_values(key_list[0], (TOKENS, D), 1.0, 6.0, ((0, 32),))
    segment_ids = jax.vmap(lambda own: jnp.searchsorted(jnp.cumsum(ragged_sizes(own, 4, L, L // 2, 0)), jnp.arange(L), side="right"))(jax.random.split(key_list[1], SEQS)).reshape((SEQS, L)).astype(jnp.int32)
    w_query = normal_values(key_list[2], (D, D), D ** -0.5, 0.21875, ((1, 4),))
    w_key = normal_values(key_list[3], (D, D), D ** -0.5, 0.21875, ((1, 4),))
    w_value = normal_values(key_list[4], (D, D), D ** -0.5, 0.21875, ((1, 4),))
    b_query = normal_values(key_list[5], (D,), 0.5, 3.0, ((0, 4),))
    b_value = normal_values(key_list[6], (D,), 0.5, 3.0, ((0, 4),))
    w_output = normal_values(key_list[7], (D, D), (D // 16) ** -0.5, 0.875)
    b_output = normal_values(key_list[8], (D,), 0.5, 3.0, (), jnp.float32)
    gain_attn = jnp.clip(1.0 + 0.1 * jax.random.normal(key_list[9], (D,), jnp.float32), 0.5, 1.5)
    shift_attn = normal_values(key_list[10], (D,), 0.5, 3.0, (), jnp.float32)
    w_inner = normal_values(key_list[11], (D, FF), D ** -0.5, 0.21875)
    b_inner = normal_values(key_list[12], (FF,), 0.5, 3.0, (), jnp.float32)
    w_outer = normal_values(key_list[13], (FF, D), FF ** -0.5, 0.109375)
    b_outer = normal_values(key_list[14], (D,), 0.5, 3.0, (), jnp.float32)
    gain_ffn = jnp.clip(1.0 + 0.1 * jax.random.normal(key_list[15], (D,), jnp.float32), 0.5, 1.5)
    shift_ffn = normal_values(key_list[16], (D,), 0.5, 3.0, (), jnp.float32)
    cotangent = normal_values(key_list[17], (TOKENS, D), 1.0, 6.0, ((0, 32),))
    return dict(layer_in=layer_in, segment_ids=segment_ids, w_query=w_query, w_key=w_key, w_value=w_value, b_query=b_query, b_value=b_value, w_output=w_output, b_output=b_output, gain_attn=gain_attn, shift_attn=shift_attn, w_inner=w_inner, b_inner=b_inner, w_outer=w_outer, b_outer=b_outer, gain_ffn=gain_ffn, shift_ffn=shift_ffn, cotangent=cotangent)


@jax.custom_vjp
def low(v):
    return lax.optimization_barrier(v.astype(jnp.bfloat16)).astype(jnp.float32)

@jax.custom_vjp
def low_back(v):
    return v

def low_keep(v):
    return (low(v), None)

def low_pass(kept, grad):
    return (grad,)

def back_keep(v):
    return (v, None)

def back_low(kept, grad):
    return (low(grad),)
low.defvjp(low_keep, low_pass)
low_back.defvjp(back_keep, back_low)
epsilon = 1e-06
masked_score = -1000000000.0

def matmul(left_side, right_side):
    return jnp.dot(left_side, right_side, precision=lax.Precision.HIGHEST, preferred_element_type=jnp.float32)

def gelu_value(values):
    return 0.5 * values * (1.0 + lax.erf(values * 0.7071067811865476))

def layer_norm(values, gain_row, shift_row):
    mean_value = lax.optimization_barrier(jnp.mean(values, -1, keepdims=True))
    centred = values - mean_value
    variance = lax.optimization_barrier(jnp.mean(centred * centred, -1, keepdims=True))
    return centred * lax.rsqrt(variance + epsilon) * gain_row + shift_row

def forward(params, inputs, segments):
    w_query, w_key, w_value, b_query, b_value, w_output, b_output, gain_attn, shift_attn, w_inner, b_inner, w_outer, b_outer, gain_ffn, shift_ffn = params
    count_seq = segments.shape[0]
    length = segments.shape[1]
    split_shape = (count_seq, length, H, HD)
    query = low_back(low(matmul(inputs, w_query) + b_query)).reshape(split_shape)
    keys_all = low_back(low(matmul(inputs, w_key))).reshape(split_shape)
    values_all = low_back(low(matmul(inputs, w_value) + b_value)).reshape(split_shape)
    scores = jnp.einsum('sqhc,skhc->shqk', query, keys_all, precision=lax.Precision.HIGHEST) * HD ** (-0.5)
    same_doc = segments[:, :, None] == segments[:, None, :]
    scores = low_back(jnp.where(same_doc[:, None], scores, masked_score))
    weights = low(jax.nn.softmax(scores, axis=-1))
    context = jnp.einsum('shqk,skhc->sqhc', weights, values_all, precision=lax.Precision.HIGHEST)
    context = low_back(low(context.reshape(count_seq * length, H * HD)))
    branch = low_back(matmul(context, w_output) + b_output)
    normed = layer_norm(inputs + branch, gain_attn, shift_attn)
    inner_pre = low_back(matmul(low(normed), w_inner) + b_inner)
    outer_out = low_back(matmul(low(gelu_value(inner_pre)), w_outer) + b_outer)
    return layer_norm(normed + outer_out, gain_ffn, shift_ffn)

def reference(layer_in, segment_ids, w_query, w_key, w_value, b_query, b_value, w_output, b_output, gain_attn, shift_attn, w_inner, b_inner, w_outer, b_outer, gain_ffn, shift_ffn, cotangent):
    params = tuple((value.astype(jnp.float32) for value in (w_query, w_key, w_value, b_query, b_value, w_output, b_output, gain_attn, shift_attn, w_inner, b_inner, w_outer, b_outer, gain_ffn, shift_ffn)))
    block_seqs = math.gcd(SEQS, max(1, 4096 // L))
    block_count = SEQS // block_seqs
    inputs = layer_in.astype(jnp.float32).reshape(block_count, block_seqs * L, D)
    segments = segment_ids.reshape(block_count, block_seqs, L)
    cotangents = cotangent.astype(jnp.float32).reshape(block_count, block_seqs * L, D)

    def one_block(totals, block_parts):
        block_in, block_seg, block_cot = block_parts
        result, pullback = jax.vjp(lambda weights_now, inputs_now: forward(weights_now, inputs_now, block_seg), params, block_in)
        grad_params, grad_inputs = pullback(block_cot)
        totals = jax.tree.map(lambda first_term, second_term: first_term + second_term, totals, grad_params)
        return (totals, (result.astype(jnp.bfloat16), grad_inputs))
    zero_grads = tuple((jnp.zeros_like(value) for value in params))
    totals, (outputs, grad_in) = lax.scan(one_block, zero_grads, (inputs, segments, cotangents))
    return (outputs.reshape(TOKENS, D), grad_in.reshape(TOKENS, D), totals[0], totals[1], totals[2], totals[3], totals[4], totals[5], totals[6], totals[7], totals[8], totals[9], totals[10], totals[11], totals[12], totals[13], totals[14])
```

```python
import jax
import jax.numpy as jnp
from jax import lax
from jax.sharding import PartitionSpec as P

HD = 64


epsilon = 1e-06
masked_score = -1000000000.0


def gelu_value(values):
    return 0.5 * values * (1.0 + lax.erf(values * 0.7071067811865476))


def gelu_slope(values):
    cumulative = 0.5 * (1.0 + lax.erf(values * 0.7071067811865476))
    density = jnp.exp(-0.5 * values * values) * 0.3989422804014327
    return cumulative + values * density


def norm_forward(values, gain_row, shift_row):
    mean_value = jnp.mean(values, -1, keepdims=True)
    centred = values - mean_value
    variance = jnp.mean(centred * centred, -1, keepdims=True)
    rstd_rows = lax.rsqrt(variance + epsilon)
    normal = centred * rstd_rows
    return (normal * gain_row + shift_row, normal, rstd_rows)


def norm_backward(grad_rows, normal, rstd_rows, gain_row):
    scaled = grad_rows * gain_row
    return rstd_rows * (
        scaled
        - jnp.mean(scaled, -1, keepdims=True)
        - normal * jnp.mean(scaled * normal, -1, keepdims=True)
    )


def masked_scores(query_seq, keys_seq, seg_seq, scaling):
    scores = (
        jnp.einsum("qhc,khc->hqk", query_seq, keys_seq, preferred_element_type=jnp.float32)
        * scaling
    )
    same_doc = seg_seq[:, None] == seg_seq[None, :]
    return jnp.where(same_doc[None], scores, masked_score)


def attend_forward(query, keys_all, values_all, segments, scaling):
    count_seq, length = segments.shape
    heads_here = query.shape[1] // HD

    def one_sequence(sequence_parts):
        query_seq, keys_seq, values_seq, seg_seq = sequence_parts
        query_seq = query_seq.reshape(length, heads_here, HD)
        keys_seq = keys_seq.reshape(length, heads_here, HD)
        values_seq = values_seq.reshape(length, heads_here, HD)
        scores = masked_scores(query_seq, keys_seq, seg_seq, scaling)
        highest = jnp.max(scores, -1, keepdims=True)
        exponent = jnp.exp(scores - highest)
        totals = jnp.sum(exponent, -1, keepdims=True)
        weights_low = (exponent / totals).astype(jnp.bfloat16)
        context = jnp.einsum(
            "hqk,khc->qhc", weights_low, values_seq, preferred_element_type=jnp.float32
        )
        return (
            context.reshape(length, heads_here * HD).astype(jnp.bfloat16),
            highest + jnp.log(totals),
        )

    context, log_sums = lax.map(
        one_sequence,
        (
            query.reshape(count_seq, length, -1),
            keys_all.reshape(count_seq, length, -1),
            values_all.reshape(count_seq, length, -1),
            segments,
        ),
    )
    return (context.reshape(count_seq * length, -1), log_sums)


def attend_backward(query, keys_all, values_all, segments, log_sums, grad_context, scaling):
    count_seq, length = segments.shape
    heads_here = query.shape[1] // HD

    def one_sequence(sequence_parts):
        query_seq, keys_seq, values_seq, seg_seq, log_seq, grad_seq = sequence_parts
        query_seq = query_seq.reshape(length, heads_here, HD)
        keys_seq = keys_seq.reshape(length, heads_here, HD)
        values_seq = values_seq.reshape(length, heads_here, HD)
        grad_seq = grad_seq.reshape(length, heads_here, HD)
        scores = masked_scores(query_seq, keys_seq, seg_seq, scaling)
        probs_full = jnp.exp(scores - log_seq)
        grad_probs = jnp.einsum(
            "qhc,khc->hqk", grad_seq, values_seq, preferred_element_type=jnp.float32
        )
        grad_values = jnp.einsum(
            "hqk,qhc->khc",
            probs_full.astype(jnp.bfloat16),
            grad_seq,
            preferred_element_type=jnp.float32,
        )
        inner_sum = jnp.sum(probs_full * grad_probs, -1, keepdims=True)
        grad_scores = (probs_full * (grad_probs - inner_sum)).astype(jnp.bfloat16)
        grad_query = (
            jnp.einsum("hqk,khc->qhc", grad_scores, keys_seq, preferred_element_type=jnp.float32)
            * scaling
        )
        grad_keys = (
            jnp.einsum("hqk,qhc->khc", grad_scores, query_seq, preferred_element_type=jnp.float32)
            * scaling
        )
        flat_shape = (length, heads_here * HD)
        return (
            grad_query.reshape(flat_shape).astype(jnp.bfloat16),
            grad_keys.reshape(flat_shape).astype(jnp.bfloat16),
            grad_values.reshape(flat_shape).astype(jnp.bfloat16),
        )

    grad_query, grad_keys, grad_values = lax.map(
        one_sequence,
        (
            query.reshape(count_seq, length, -1),
            keys_all.reshape(count_seq, length, -1),
            values_all.reshape(count_seq, length, -1),
            segments,
            log_sums,
            grad_context.reshape(count_seq, length, -1),
        ),
    )
    rows_all = count_seq * length
    return (
        grad_query.reshape(rows_all, -1),
        grad_keys.reshape(rows_all, -1),
        grad_values.reshape(rows_all, -1),
    )


def bits_of(count):
    return count.bit_length() - 1


class Grid:
    def __init__(self, mesh):
        self.rows = mesh.shape["rows"]
        self.heads = mesh.shape["heads"]
        count = bits_of(self.rows) - 1
        up = list(range(1, count + 1))
        self.orders = (up, up[::-1])
        self.steps = count

    def permute(self, values, partner):
        pairs = []
        for row in range(self.rows):
            for head in range(self.heads):
                row_to, head_to = partner(row, head)
                pairs.append((row * self.heads + head, row_to * self.heads + head_to))
        return lax.ppermute(values, ("rows", "heads"), pairs)

    def across_core(self, values):
        return self.permute(values, lambda row, head: (row ^ 1, head))

    def across_chip(self, values, step):
        return self.permute(
            values, lambda row, head: (row ^ (1 << self.orders[row & 1][step]), head)
        )

    def across_heads(self, values, offset):
        return self.permute(values, lambda row, head: (row, head ^ offset))

    def slot_masks(self, core):
        last = self.steps - 1
        masks = []
        for slot in range(1 << self.steps):
            mask = 0
            for step in range(self.steps):
                mask |= ((slot >> (last - step)) & 1) << self.orders[core][step]
            masks.append(mask)
        return masks

    def row_slots(self):
        row = lax.axis_index("rows")
        masks = jnp.array([self.slot_masks(0), self.slot_masks(1)], jnp.int32)
        core = row & 1
        return jnp.stack([row ^ masks[core], (row ^ 1) ^ masks[1 - core]]).reshape(-1)

    def head_slots(self):
        return lax.axis_index("heads") ^ jnp.arange(self.heads, dtype=jnp.int32)

    def block_slots(self):
        return (self.row_slots()[:, None] * self.heads + self.head_slots()[None, :]).reshape(-1)

    def reduce_scatter(self, parts):
        held = parts.reshape((2, self.rows // 2) + parts.shape[1:])
        held = add_low(held[0], self.across_core(held[1]))
        for step in range(self.steps):
            half = held.shape[0] // 2
            held = add_low(held[:half], self.across_chip(held[half:], step))
        held = held[0]
        total = held[0].astype(jnp.float32)
        for offset in range(1, self.heads):
            total = total + self.across_heads(held[offset], offset).astype(jnp.float32)
        return total

    def gather_rows(self, block):
        held = block[None]
        for step in reversed(range(self.steps)):
            held = jnp.concatenate([held, self.across_chip(held, step)], 0)
        held = jnp.concatenate([held, self.across_core(held)], 0)
        order = self.row_slots()
        places = jnp.argsort(order)
        return jnp.take(held, places, axis=0)

    def gather_heads(self, block):
        return jnp.stack(
            [block] + [self.across_heads(block, offset) for offset in range(1, self.heads)]
        )

    def sum_all(self, values):
        values = values + self.across_core(values)
        for step in range(self.steps):
            values = values + self.across_chip(values, step)
        offset = 1
        while offset < self.heads:
            values = values + self.across_heads(values, offset)
            offset *= 2
        return values


def add_low(first, second):
    return (first.astype(jnp.float32) + second.astype(jnp.float32)).astype(jnp.bfloat16)


def dot32(spec, left, right):
    return jnp.einsum(spec, left, right, preferred_element_type=jnp.float32)


def gather_projections(grid, shard):
    helpers = 8
    row = lax.axis_index("rows")
    size = shard.shape[0] // helpers
    part = lax.dynamic_slice_in_dim(shard, (row % helpers) * size, size, 0)
    held = grid.gather_heads(part)[None]
    for core_bit, other_bit in ((1, 2), (2, 1)):
        got = grid.permute(
            held, lambda r, h, b=core_bit, o=other_bit: (r ^ (1 << (o if r & 1 else b)), h)
        )
        held = jnp.concatenate([held, got], 0)
    held = jnp.concatenate([held, grid.across_core(held)], 0)
    core = row & 1
    masks = jnp.array([[0, 2, 4, 6], [0, 4, 2, 6]], jnp.int32)
    order = (
        jnp.concatenate([row ^ masks[core], (row ^ 1) ^ masks[1 - core]]) % helpers
    )
    held = jnp.take(held, jnp.argsort(order), axis=0)
    return held.transpose(1, 0, 2, 3).reshape(grid.heads, shard.shape[0], shard.shape[1])


def local(
    grid,
    layer_in,
    segment_ids,
    w_query,
    w_key,
    w_value,
    b_query,
    b_value,
    w_output,
    b_output,
    gain_attn,
    shift_attn,
    w_inner,
    b_inner,
    w_outer,
    b_outer,
    gain_ffn,
    shift_ffn,
    cotangent,
):
    scaling = HD ** (-0.5)
    tokens, width = layer_in.shape
    length = segment_ids.shape[1]
    seqs = tokens // length
    group = w_query.shape[1]
    hidden = w_inner.shape[1]
    devices = grid.rows * grid.heads
    head = lax.axis_index("heads")
    segments = lax.dynamic_slice_in_dim(segment_ids, head * seqs, seqs, 0)
    slots = grid.block_slots()
    head_slots = grid.head_slots()

    shard = jnp.concatenate([w_query, w_key, w_value], 1).T
    shard = jnp.concatenate([shard, jnp.zeros((0, width), shard.dtype)], 0)
    projections = gather_projections(grid, shard).reshape(grid.heads, 3, group, width)
    biases = jnp.stack([b_query, b_value])
    biases = grid.gather_heads(biases)
    w_query_all = projections[:, 0].reshape(-1, width)
    w_key_all = projections[:, 1].reshape(-1, width)
    w_value_all = projections[:, 2].reshape(-1, width)
    b_query_all = biases[:, 0].reshape(-1)
    b_value_all = biases[:, 1].reshape(-1)

    def by_slot(values, block):
        return jnp.take(values.reshape((devices, block) + values.shape[1:]), slots, axis=0).reshape(values.shape)

    w_inner_t = by_slot(w_inner.T, hidden // devices)
    w_outer_s = by_slot(w_outer, hidden // devices)
    b_inner_s = by_slot(b_inner, hidden // devices)
    w_output_s = jnp.take(w_output.reshape(grid.heads, group, width), head_slots, axis=0).reshape(width, width)

    query = (dot32("td,cd->tc", layer_in, w_query_all) + b_query_all).astype(jnp.bfloat16)
    keys_all = dot32("td,cd->tc", layer_in, w_key_all).astype(jnp.bfloat16)
    values_all = (dot32("td,cd->tc", layer_in, w_value_all) + b_value_all).astype(jnp.bfloat16)
    context, log_sums = attend_forward(query, keys_all, values_all, segments, scaling)
    inputs_wide = layer_in.astype(jnp.float32)
    branch = dot32("tc,cd->td", context, w_output_s) + b_output
    normed, normal_one, rstd_one = norm_forward(inputs_wide + branch, gain_attn, shift_attn)
    normed_low = normed.astype(jnp.bfloat16)
    inner_pre = dot32("td,id->ti", normed_low, w_inner_t) + b_inner_s
    active = gelu_value(inner_pre).astype(jnp.bfloat16)
    outer_out = dot32("ti,id->td", active, w_outer_s) + b_outer
    result, normal_two, rstd_two = norm_forward(normed + outer_out, gain_ffn, shift_ffn)
    layer_out = result.astype(jnp.bfloat16)
    grad_result = cotangent.astype(jnp.float32)
    grad_gain_ffn = jnp.sum(grad_result * normal_two, 0)
    grad_shift_ffn = jnp.sum(grad_result, 0)
    grad_sum_two = norm_backward(grad_result, normal_two, rstd_two, gain_ffn)
    grad_outer = grad_sum_two.astype(jnp.bfloat16)
    grad_b_outer = jnp.sum(grad_outer.astype(jnp.float32), 0)
    block_shape = (grid.rows, grid.heads, hidden // devices, width)
    grad_w_outer = dot32("ti,td->id", active, grad_outer).astype(jnp.bfloat16)
    out_w_outer = grid.reduce_scatter(grad_w_outer.reshape(block_shape))
    grad_active = dot32("td,id->ti", grad_outer, w_outer_s)
    grad_inner = (grad_active * gelu_slope(inner_pre)).astype(jnp.bfloat16)
    grad_w_inner = dot32("ti,td->id", grad_inner, normed_low).astype(jnp.bfloat16)
    out_w_inner = grid.reduce_scatter(grad_w_inner.reshape(block_shape)).T
    grad_b_inner = jnp.sum(grad_inner.astype(jnp.float32), 0)
    grad_normed = grad_sum_two + dot32("ti,id->td", grad_inner, w_inner_t)
    grad_gain_attn = jnp.sum(grad_normed * normal_one, 0)
    grad_shift_attn = jnp.sum(grad_normed, 0)
    grad_sum_one = norm_backward(grad_normed, normal_one, rstd_one, gain_attn)
    grad_branch = grad_sum_one.astype(jnp.bfloat16)
    grad_b_output = jnp.sum(grad_branch.astype(jnp.float32), 0)
    grad_w_output = dot32("tc,td->cd", context, grad_branch)
    grad_context = dot32("td,cd->tc", grad_branch, w_output_s).astype(jnp.bfloat16)
    grad_query, grad_keys, grad_values = attend_backward(
        query, keys_all, values_all, segments, log_sums, grad_context, scaling
    )
    input_grad = grad_sum_one + (
        dot32("tc,cd->td", grad_query, w_query_all)
        + dot32("tc,cd->td", grad_keys, w_key_all)
        + dot32("tc,cd->td", grad_values, w_value_all)
    )
    four = jnp.stack(
        [
            dot32("tc,td->cd", grad_query, layer_in).reshape(grid.heads, group, width),
            dot32("tc,td->cd", grad_keys, layer_in).reshape(grid.heads, group, width),
            dot32("tc,td->cd", grad_values, layer_in).reshape(grid.heads, group, width),
            grad_w_output.reshape(grid.heads, group, width),
        ],
        1,
    ).astype(jnp.bfloat16)
    per_row = group // grid.rows
    four = four.reshape(grid.heads, 4, grid.rows, per_row, width).transpose(2, 0, 1, 3, 4)
    four = jnp.take(four, grid.row_slots(), axis=0)
    four = grid.reduce_scatter(four.reshape(grid.rows, grid.heads, 4 * per_row, width)).astype(jnp.bfloat16)
    four = grid.gather_rows(four).reshape(grid.rows, 4, per_row, width)
    four = four.transpose(1, 0, 2, 3).reshape(4, group, width)
    own_output = four[3]
    grad_w_output = jnp.take(grid.gather_heads(own_output), head_slots, axis=0).reshape(width, width)
    grad_w_output = grad_w_output.astype(jnp.float32)
    wide = four[:3].astype(jnp.float32).transpose(0, 2, 1)

    def back(values):
        return jnp.take(values.reshape(grid.heads, group), head_slots, axis=0).reshape(1, width)

    b_inner_back = jnp.take(
        grad_b_inner.reshape(devices, hidden // devices), jnp.argsort(slots), axis=0
    ).reshape(-1, width)
    small = jnp.concatenate(
        [
            back(jnp.sum(grad_query.astype(jnp.float32), 0)),
            back(jnp.sum(grad_values.astype(jnp.float32), 0)),
            grad_b_output[None],
            grad_gain_attn[None],
            grad_shift_attn[None],
            grad_b_outer[None],
            grad_gain_ffn[None],
            grad_shift_ffn[None],
            b_inner_back,
        ],
        0,
    )
    small = grid.sum_all(small)
    own_device = lax.axis_index("rows") * grid.heads + head
    return (
        layer_out,
        input_grad,
        wide[0],
        wide[1],
        wide[2],
        lax.dynamic_slice_in_dim(small[0], head * group, group, 0),
        lax.dynamic_slice_in_dim(small[1], head * group, group, 0),
        grad_w_output,
        small[2],
        small[3],
        small[4],
        out_w_inner,
        lax.dynamic_slice_in_dim(
            small[8:].reshape(-1), own_device * (hidden // devices), hidden // devices, 0
        ),
        out_w_outer,
        small[5],
        small[6],
        small[7],
    )


def solution(mesh):
    grid = Grid(mesh)
    return jax.shard_map(
        lambda *values: local(grid, *values),
        mesh=mesh,
        in_specs=(
            P(("rows", "heads"), None),
            P("rows", None),
            P(None, "heads"),
            P(None, "heads"),
            P(None, "heads"),
            P("heads"),
            P("heads"),
            P(),
            P(),
            P(),
            P(),
            P(),
            P(),
            P(),
            P(),
            P(),
            P(),
            P(("rows", "heads"), None),
        ),
        out_specs=(
            P(("rows", "heads"), None),
            P(("rows", "heads"), None),
            P(None, "heads"),
            P(None, "heads"),
            P(None, "heads"),
            P("heads"),
            P("heads"),
            P(),
            P(),
            P(),
            P(),
            P(None, ("rows", "heads")),
            P(("rows", "heads")),
            P(("rows", "heads"), None),
            P(),
            P(),
            P(),
        ),
        check_vma=False,
    )
```

```python
import functools

import jax
import jax.numpy as jnp
from jax import lax
from jax.experimental import pallas as pl
from jax.experimental.pallas import tpu as pltpu
from jax.sharding import PartitionSpec as P

HD = 64
PARTS = 8
epsilon = 1e-06
masked_score = -1000000000.0
low_type = jnp.bfloat16
wide_type = jnp.float32
room = pltpu.CompilerParams(vmem_limit_bytes=60 * 1024 * 1024)


def contract(left, right, left_dim, right_dim):
    return lax.dot_general(
        left, right, (((left_dim,), (right_dim,)), ((), ())), preferred_element_type=wide_type
    )


def dot_nn(left, right):
    return contract(left, right, 1, 0)


def dot_nt(left, right):
    return contract(left, right, 1, 1)


def dot_tn(left, right):
    return contract(left, right, 0, 0)


def add_like(first, second):
    if first.dtype == wide_type:
        return first + second
    return (first.astype(wide_type) + second.astype(wide_type)).astype(first.dtype)


def tree_add(first, second):
    return jax.tree.map(add_like, first, second)


class Grid:
    def __init__(self, mesh):
        self.rows = mesh.shape["rows"]
        self.heads = mesh.shape["heads"]
        self.steps = self.rows.bit_length() - 2
        up = list(range(1, self.steps + 1))
        self.orders = (up, up[::-1])
        self.native = self.rows == PARTS

    def permute(self, values, partner):
        pairs = []
        for row in range(self.rows):
            for head in range(self.heads):
                row_to, head_to = partner(row, head)
                pairs.append((row * self.heads + head, row_to * self.heads + head_to))
        return jax.tree.map(lambda leaf: lax.ppermute(leaf, ("rows", "heads"), pairs), values)

    def across_core(self, values):
        return self.permute(values, lambda row, head: (row ^ 1, head))

    def across_bits(self, values, bits):
        return self.permute(values, lambda row, head: (row ^ (1 << bits[row & 1]), head))

    def across_chip(self, values, step):
        return self.across_bits(values, [order[step] for order in self.orders])

    def across_heads(self, values, offset):
        return self.permute(values, lambda row, head: (row, head ^ offset))

    def slot_masks(self, core):
        last = self.steps - 1
        masks = []
        for slot in range(1 << self.steps):
            mask = 0
            for step in range(self.steps):
                mask |= ((slot >> (last - step)) & 1) << self.orders[core][step]
            masks.append(mask)
        return masks

    def row_slots(self):
        row = lax.axis_index("rows")
        masks = jnp.array([self.slot_masks(0), self.slot_masks(1)], jnp.int32)
        core = row & 1
        return jnp.concatenate([row ^ masks[core], (row ^ 1) ^ masks[1 - core]])

    def row_places(self):
        row = lax.axis_index("rows")
        half = self.rows // 2
        inverse = []
        for core in (0, 1):
            table = [0] * half
            for slot, mask in enumerate(self.slot_masks(core)):
                table[mask >> 1] = slot
            inverse.append(table)
        inverse = jnp.array(inverse, jnp.int32)
        apart = jnp.arange(self.rows, dtype=jnp.int32) ^ row
        other = apart & 1
        return other * half + inverse[(row & 1) ^ other, apart >> 1]

    def helper_slots(self):
        row = lax.axis_index("rows")
        masks = jnp.array([[0, 2, 4, 6], [0, 4, 2, 6]], jnp.int32)
        core = row & 1
        return jnp.concatenate([row ^ masks[core], (row ^ 1) ^ masks[1 - core]]) % PARTS

    def block_slots(self):
        heads = lax.axis_index("heads") ^ jnp.arange(self.heads, dtype=jnp.int32)
        return (self.row_slots()[:, None] * self.heads + heads[None, :]).reshape(-1)

    def scatter_core(self, parts):
        half = self.rows // 2
        got = self.across_core(jax.tree.map(lambda leaf: leaf[half:], parts))
        return tree_add(jax.tree.map(lambda leaf: leaf[:half], parts), got)

    def scatter_chip(self, held, step):
        half = self.rows // 2 >> (step + 1)
        got = self.across_chip(jax.tree.map(lambda leaf: leaf[half:], held), step)
        return tree_add(jax.tree.map(lambda leaf: leaf[:half], held), got)

    def scatter_heads(self, held):
        total = held[0].astype(wide_type)
        for offset in range(1, self.heads):
            total = total + self.across_heads(held[offset], offset).astype(wide_type)
        return total

    def gather_chips(self, block):
        held = jax.tree.map(lambda leaf: leaf[None], block)
        for step in reversed(range(self.steps)):
            got = self.across_chip(held, step)
            held = jax.tree.map(lambda a, b: jnp.concatenate([a, b], 0), held, got)
        return held

    def gather_heads(self, block):
        return [block] + [self.across_heads(block, offset) for offset in range(1, self.heads)]

    def spread_parts(self, parts):
        if self.native:
            return parts
        count, rows, cols = parts.shape[1:]
        finer = self.rows // PARTS
        parts = parts.reshape(PARTS, count, finer, rows // finer, cols).transpose(0, 2, 1, 3, 4)
        parts = parts.reshape(self.rows, count, rows // finer, cols)
        return jnp.take(parts, self.row_slots(), axis=0)

    def join_parts(self, halves):
        if self.native:
            return halves, self.row_slots()
        whole = jnp.take(jnp.concatenate(halves, 0), self.row_places(), axis=0)
        count, rows, cols = whole.shape[1:]
        finer = self.rows // PARTS
        whole = whole.reshape(PARTS, finer, count, rows, cols).transpose(0, 2, 1, 3, 4)
        whole = whole.reshape(PARTS, count, finer * rows, cols)
        return (whole[: PARTS // 2], whole[PARTS // 2 :]), jnp.arange(PARTS, dtype=jnp.int32)


def estimate(flops, moved, exps=0):
    return pl.CostEstimate(flops=flops, bytes_accessed=moved, transcendentals=exps)


def like(shape, dtype=low_type):
    return jax.ShapeDtypeStruct(shape, dtype)


def whole_spec(shape, **options):
    return pl.BlockSpec(shape, lambda *ids: (0,) * len(shape), **options)


anywhere = pl.BlockSpec(memory_space=pl.ANY)


def three_parts(values):
    first = values.astype(low_type).astype(wide_type)
    rest = values - first
    second = rest.astype(low_type).astype(wide_type)
    return first, second, (rest - second).astype(low_type).astype(wide_type)


def pair_up(low_lanes, first, second):
    return jnp.where(low_lanes, first, pltpu.roll(second, HD, 1))


def attend_body(x_ref, weights, bias_row, seg_ref, q_ref, k_ref, v_ref, ctx_ref):
    seqs, _, length = seg_ref.shape
    lane = lax.broadcasted_iota(jnp.int32, (1, 128), 1)
    low = lane < HD
    row8 = lax.broadcasted_iota(jnp.int32, (8, length), 0)
    for seq in range(seqs):
        at = slice(seq * length, (seq + 1) * length)
        qkv = (dot_nt(x_ref[at, :], weights) + bias_row).astype(low_type).astype(wide_type)
        q01 = qkv[:, 0:128] * 0.125
        k01 = qkv[:, 128:256]
        v01 = qkv[:, 256:384]
        qk2 = qkv[:, 384:512]
        v2 = jnp.concatenate([qkv[:, 512:576], jnp.zeros((length, HD), wide_type)], 1)
        queries = [q01, pltpu.roll(q01, HD, 1), qk2 * 0.125]
        keys = [k01, pltpu.roll(k01, HD, 1), pltpu.roll(qk2, HD, 1)]
        values = [v01, pltpu.roll(v01, HD, 1), v2]
        seg_rows = jnp.broadcast_to(seg_ref[seq], (8, length)).astype(wide_type)
        seg_col = seg_rows.T[:, 0:1].astype(jnp.int32) + HD
        same = lane == seg_col
        in_seg = (lane >= HD) & (lane < HD + 4)
        extra_q = jnp.where(same, 1.0, 0.0)
        extra_k = jnp.where(
            in_seg & ~same,
            masked_score,
            jnp.where((lane >= HD + 4) & (lane < HD + 7), 1.0, 0.0),
        )
        extra_v = jnp.where((lane >= HD) & (lane < HD + 3), 1.0, 0.0)
        contexts = []
        for head in range(3):
            query = jnp.where(low, queries[head], extra_q)
            key = jnp.where(low, keys[head], extra_k).astype(low_type)
            value = jnp.where(low, values[head], extra_v).astype(low_type)
            k_ref[0, head, at, :] = key
            v_ref[0, head, at, :] = value
            scores = dot_nt(key, query.astype(low_type))
            highest = jnp.max(scores, 0, keepdims=True)
            weights_low = jnp.exp(scores - highest).astype(low_type)
            summed = dot_tn(value, weights_low)
            total = summed[HD : HD + 1, :]
            first, second, third = three_parts(-(highest + jnp.log(total)))
            extra = jnp.where(
                row8 == 4, first, jnp.where(row8 == 5, second, jnp.where(row8 == 6, third, 0.0))
            )
            full = jnp.concatenate(
                [summed[:HD] * (1.0 / total), extra, jnp.zeros((56, length), wide_type)], 0
            ).T
            q_ref[0, head, at, :] = jnp.where(low, query, full + extra_q).astype(low_type)
            contexts.append(full)
        ctx_ref[0, at, 0:128] = pair_up(low, contexts[0], contexts[1]).astype(low_type)
        ctx_ref[0, at, 128:192] = contexts[2][:, :HD].astype(low_type)


def attend_own_kernel(x_ref, w_ref, b_ref, seg_ref, q_ref, k_ref, v_ref, ctx_ref):
    attend_body(x_ref, w_ref[0], b_ref[0], seg_ref, q_ref, k_ref, v_ref, ctx_ref)


def attend_rest_kernel(
    parts_ref, x_ref, near_ref, far_ref, b_ref, seg_ref, q_ref, k_ref, v_ref, ctx_ref, w_ref, held
):
    rows, cols = near_ref.shape[2:]
    for slot in range(PARTS):
        piece = near_ref[slot, 0] if slot < PARTS // 2 else far_ref[slot - PARTS // 2, 0]
        held[parts_ref[slot]] = piece
    for part in range(PARTS):
        across, down = divmod(part, 4)
        w_ref[0, down * rows : (down + 1) * rows, across * cols : (across + 1) * cols] = held[part]
    attend_body(x_ref, w_ref[0], b_ref[0], seg_ref, q_ref, k_ref, v_ref, ctx_ref)


def attend_cost(count, tokens, length, width):
    return estimate(
        count * (2 * tokens * width * 576 + 3 * 4 * tokens * length * 128),
        2 * tokens * width + count * 2 * (576 * width + 10 * tokens * 128),
        count * 3 * tokens * length,
    )


def attend_outputs(count, tokens):
    heads = pl.BlockSpec((1, 3, tokens, 128), lambda g, *_: (g, 0, 0, 0))
    specs = [heads, heads, heads, pl.BlockSpec((1, tokens, 192), lambda g, *_: (g, 0, 0))]
    shapes = [like((count, 3, tokens, 128))] * 3 + [like((count, tokens, 192))]
    return specs, shapes


def attend_own(layer_in, shard, bias, segments):
    tokens, width = layer_in.shape
    specs, shapes = attend_outputs(1, tokens)
    return pl.pallas_call(
        attend_own_kernel,
        grid=(1,),
        in_specs=[
            whole_spec((tokens, width)),
            whole_spec(shard.shape),
            whole_spec(bias.shape),
            whole_spec(segments.shape),
        ],
        out_specs=specs,
        out_shape=shapes,
        compiler_params=room,
        cost_estimate=attend_cost(1, tokens, segments.shape[2], width),
    )(layer_in, shard, bias, segments)


def attend_rest(parts, layer_in, near, far, bias, segments):
    tokens, width = layer_in.shape
    count, rows, cols = near.shape[1:]
    specs, shapes = attend_outputs(count, tokens)
    piece = pl.BlockSpec((PARTS // 2, 1, rows, cols), lambda g, *_: (0, g, 0, 0))
    return pl.pallas_call(
        attend_rest_kernel,
        grid_spec=pltpu.PrefetchScalarGridSpec(
            num_scalar_prefetch=1,
            grid=(count,),
            in_specs=[
                whole_spec((tokens, width)),
                piece,
                piece,
                pl.BlockSpec((1, 1, 576), lambda g, *_: (g, 0, 0)),
                whole_spec(segments.shape),
            ],
            out_specs=specs + [pl.BlockSpec((1, 576, width), lambda g, *_: (g, 0, 0))],
            scratch_shapes=[pltpu.VMEM((PARTS, rows, cols), low_type)],
        ),
        out_shape=shapes + [like((count, 576, width))],
        compiler_params=room,
        cost_estimate=attend_cost(count, tokens, segments.shape[2], width),
    )(parts, layer_in, near, far, bias, segments)


def attend_back_kernel(
    length, slots_ref, x_ref, q_ref, k_ref, v_ref, ctx_ref, dctx_ref, dep_ref, dqkv_ref, dw_ref, held
):
    del dep_ref
    tokens = x_ref.shape[0]
    rows = 576 // 4
    cols = x_ref.shape[1] // 2
    lane = lax.broadcasted_iota(jnp.int32, (1, 128), 1)
    low = lane < HD
    for seq in range(tokens // length):
        at = slice(seq * length, (seq + 1) * length)
        grad01 = dctx_ref[0, at, 0:128].astype(wide_type)
        grad2 = dctx_ref[0, at, 128:192].astype(wide_type)
        both = grad01 * ctx_ref[0, at, 0:128].astype(wide_type)
        inner = [
            jnp.sum(jnp.where(low, both, 0.0), -1, keepdims=True),
            jnp.sum(jnp.where(low, 0.0, both), -1, keepdims=True),
            jnp.sum(grad2 * ctx_ref[0, at, 128:192].astype(wide_type), -1, keepdims=True),
        ]
        grads = [
            grad01,
            pltpu.roll(grad01, HD, 1),
            jnp.concatenate([grad2, jnp.zeros((length, HD), wide_type)], 1),
        ]
        grad_q, grad_k, grad_v = [], [], []
        for head in range(3):
            first, second, third = three_parts(-inner[head])
            extra = jnp.where(
                lane == HD,
                first,
                jnp.where(lane == HD + 1, second, jnp.where(lane == HD + 2, third, 0.0)),
            )
            grad = jnp.where(low, grads[head], extra).astype(low_type)
            query = q_ref[0, head, at, :]
            key = k_ref[0, head, at, :]
            probs = jnp.exp(dot_nt(key, query))
            grad_scores = (probs * dot_nt(v_ref[0, head, at, :], grad)).astype(low_type)
            grad_v.append(dot_nn(probs.astype(low_type), grad))
            grad_k.append(dot_nn(grad_scores, query))
            grad_q.append(dot_tn(key, grad_scores).T * 0.125)
        dqkv_ref[0, at, 0:128] = pair_up(low, grad_q[0], grad_q[1]).astype(low_type)
        dqkv_ref[0, at, 128:256] = pair_up(low, grad_k[0], grad_k[1]).astype(low_type)
        dqkv_ref[0, at, 256:384] = pair_up(low, grad_v[0], grad_v[1]).astype(low_type)
        dqkv_ref[0, at, 384:512] = pair_up(low, grad_q[2], grad_k[2]).astype(low_type)
        dqkv_ref[0, at, 512:576] = grad_v[2][:, :HD].astype(low_type)
    grad_all = dqkv_ref[0]
    total = dot_tn(grad_all, x_ref[...])
    sums = jnp.sum(grad_all.astype(wide_type), 0, keepdims=True)
    for part in range(PARTS):
        across, down = divmod(part, 4)
        held[part, 0:rows] = total[
            down * rows : (down + 1) * rows, across * cols : (across + 1) * cols
        ].astype(low_type)
        tail = jnp.zeros((16, cols), wide_type)
        if across == 0:
            piece = sums[:, down * rows : (down + 1) * rows]
            tail = jnp.concatenate([piece, jnp.zeros((1, cols - rows), wide_type)], 1)
            tail = jnp.broadcast_to(tail, (16, cols))
        held[part, rows : rows + 16] = tail.astype(low_type)
    for slot in range(PARTS):
        dw_ref[slot, 0] = held[slots_ref[slot]]


def attend_back(slots, layer_in, queries, keys, values, context, grad_context, dep, length, start, count):
    tokens, width = layer_in.shape
    rows, cols = 576 // 4 + 16, width // 2
    heads = pl.BlockSpec((1, 3, tokens, 128), lambda g, *_: (g + start, 0, 0, 0))
    group = pl.BlockSpec((1, tokens, 192), lambda g, *_: (g + start, 0, 0))
    return pl.pallas_call(
        functools.partial(attend_back_kernel, length),
        grid_spec=pltpu.PrefetchScalarGridSpec(
            num_scalar_prefetch=1,
            grid=(count,),
            in_specs=[whole_spec((tokens, width)), heads, heads, heads, group, group, anywhere],
            out_specs=[
                pl.BlockSpec((1, tokens, 576), lambda g, *_: (g, 0, 0)),
                pl.BlockSpec((PARTS, 1, rows, cols), lambda g, *_: (0, g, 0, 0)),
            ],
            scratch_shapes=[pltpu.VMEM((PARTS, rows, cols), low_type)],
        ),
        out_shape=[like((count, tokens, 576)), like((PARTS, count, rows, cols))],
        compiler_params=room,
        cost_estimate=estimate(
            count * (2 * tokens * width * 576 + 3 * 10 * tokens * length * 128),
            2 * tokens * width + count * 2 * (576 * width + 16 * tokens * 128),
            count * 3 * tokens * length,
        ),
    )(slots, layer_in, queries, keys, values, context, grad_context, dep)


def mean_last(values):
    return jnp.mean(values, -1, keepdims=True)


def tiles(tokens, size, body):
    def step(index, carry):
        body(pl.ds(pl.multiple_of(index * size, size), size))
        return carry

    lax.fori_loop(0, tokens // size, step, 0)


def gelu_pair(values):
    cumulative = 0.5 * (1.0 + lax.erf(values * 0.7071067811865476))
    density = jnp.exp(-0.5 * values * values) * 0.3989422804014327
    return values * cumulative, cumulative + values * density


def forward_kernel(
    chunks,
    head_ref,
    x_ref,
    own_ref,
    rest_ref,
    wo_ref,
    cot_ref,
    vec_ref,
    w_in_ref,
    w_out_ref,
    b_in_ref,
    low_ref,
    normal_ref,
    rstd_ref,
    slope_ref,
    out_ref,
    grad_ref,
    gw_ref,
    sums_ref,
    normed,
    outer,
    active,
):
    step = pl.program_id(0)
    tokens = x_ref.shape[0]
    head = head_ref[0]
    b_output, gain_attn, shift_attn = vec_ref[0:1, :], vec_ref[1:2, :], vec_ref[2:3, :]
    b_outer, gain_ffn, shift_ffn = vec_ref[3:4, :], vec_ref[4:5, :], vec_ref[5:6, :]

    @pl.when(step == 0)
    def _():
        outer[...] = jnp.zeros_like(outer)
        branch = dot_nn(own_ref[0], wo_ref[head])
        for offset in range(1, wo_ref.shape[0]):
            branch += dot_nn(rest_ref[offset - 1], wo_ref[head ^ offset])
        normed[...] = branch

        def one(at):
            total = x_ref[at, :].astype(wide_type) + (normed[at, :] + b_output)
            centred = total - mean_last(total)
            rstd = lax.rsqrt(mean_last(centred * centred) + epsilon)
            normal = centred * rstd
            result = normal * gain_attn + shift_attn
            normed[at, :] = result
            low_ref[at, :] = result.astype(low_type)
            normal_ref[at, :] = normal.astype(low_type)
            rstd_ref[at, :] = jnp.broadcast_to(rstd, (rstd.shape[0], 128))

        tiles(tokens, 128, one)

    @pl.when(step < chunks)
    def _():
        inner = dot_nt(low_ref[...], w_in_ref[...]) + b_in_ref[...]
        values, slope = gelu_pair(inner)
        values = values.astype(low_type)
        active[step] = values
        slope_ref[...] = slope.astype(low_type)
        outer[...] += dot_nn(values, w_out_ref[...])

    @pl.when(step == chunks - 1)
    def _():
        sums_ref[...] = jnp.zeros_like(sums_ref)

        def one(at):
            total = normed[at, :] + (outer[at, :] + b_outer)
            centred = total - mean_last(total)
            rstd = lax.rsqrt(mean_last(centred * centred) + epsilon)
            normal = centred * rstd
            out_ref[at, :] = (normal * gain_ffn + shift_ffn).astype(low_type)
            grad = cot_ref[at, :].astype(wide_type)
            scaled = grad * gain_ffn
            grad_sum = rstd * (scaled - mean_last(scaled) - normal * mean_last(scaled * normal))
            grad_low = grad_sum.astype(low_type)
            grad_ref[at, :] = grad_low
            sums_ref[0:1, :] += jnp.sum(grad * normal, 0, keepdims=True)
            sums_ref[1:2, :] += jnp.sum(grad, 0, keepdims=True)
            sums_ref[2:3, :] += jnp.sum(grad_low.astype(wide_type), 0, keepdims=True)

        tiles(tokens, 128, one)

    @pl.when(step >= chunks)
    def _():
        gw_ref[...] = dot_tn(active[step - chunks], grad_ref[...]).astype(low_type)


def forward_ffn(head, layer_in, ctx_own, ctx_rest, w_output, cotangent, vectors, w_in, w_out, b_in):
    tokens, width = layer_in.shape
    hidden = w_in.shape[0]
    chunks = 3
    size = hidden // chunks
    early = lambda i, *_: (jnp.minimum(i, chunks - 1), 0)
    late = lambda i, *_: (jnp.maximum(i - chunks, 0), 0)
    wide_chunk = lambda i, *_: (0, jnp.minimum(i, chunks - 1))
    once = dict(pipeline_mode=pl.Buffered(1))
    full = whole_spec((tokens, width))
    return pl.pallas_call(
        functools.partial(forward_kernel, chunks),
        grid_spec=pltpu.PrefetchScalarGridSpec(
            num_scalar_prefetch=1,
            grid=(2 * chunks,),
            in_specs=[
                whole_spec((tokens, width), **once),
                whole_spec(ctx_own.shape, **once),
                whole_spec(ctx_rest.shape, **once),
                whole_spec(w_output.shape, **once),
                whole_spec((tokens, width), **once),
                whole_spec(vectors.shape, **once),
                pl.BlockSpec((size, width), early),
                pl.BlockSpec((size, width), early),
                pl.BlockSpec((1, size), wide_chunk),
            ],
            out_specs=[
                full,
                full,
                whole_spec((tokens, 128)),
                pl.BlockSpec((tokens, size), wide_chunk),
                full,
                full,
                pl.BlockSpec((size, width), late),
                whole_spec((8, width)),
            ],
            scratch_shapes=[
                pltpu.VMEM((tokens, width), wide_type),
                pltpu.VMEM((tokens, width), wide_type),
                pltpu.VMEM((chunks, tokens, size), low_type),
            ],
        ),
        out_shape=[
            like((tokens, width)),
            like((tokens, width)),
            like((tokens, 128), wide_type),
            like((tokens, hidden)),
            like((tokens, width)),
            like((tokens, width)),
            like((hidden, width)),
            like((8, width), wide_type),
        ],
        compiler_params=room,
        cost_estimate=estimate(
            2 * tokens * width * (3 * hidden + width),
            2 * (tokens * (7 * width + hidden) + 3 * hidden * width),
            tokens * hidden,
        ),
    )(head, layer_in, ctx_own, ctx_rest, w_output, cotangent, vectors, w_in, w_out, b_in)


def inner_back_kernel(
    grad_ref, low_ref, slope_ref, w_out_ref, w_in_ref, gw_ref, sums_ref, total_ref
):
    step = pl.program_id(0)
    grad_inner = (
        dot_nt(grad_ref[...], w_out_ref[...]) * slope_ref[...].astype(wide_type)
    ).astype(low_type)
    sums_ref[...] = jnp.sum(grad_inner.astype(wide_type), 0, keepdims=True)
    gw_ref[...] = dot_tn(grad_inner, low_ref[...]).astype(low_type)
    part = dot_nn(grad_inner, w_in_ref[...])

    @pl.when(step == 0)
    def _():
        total_ref[...] = part

    @pl.when(step > 0)
    def _():
        total_ref[...] += part


def inner_back(grad_outer, normed_low, slope, w_out, w_in):
    tokens, width = grad_outer.shape
    hidden = w_in.shape[0]
    chunks = 3
    size = hidden // chunks
    down = pl.BlockSpec((size, width), lambda i: (i, 0))
    return pl.pallas_call(
        inner_back_kernel,
        grid=(chunks,),
        in_specs=[
            whole_spec((tokens, width)),
            whole_spec((tokens, width)),
            pl.BlockSpec((tokens, size), lambda i: (0, i)),
            down,
            down,
        ],
        out_specs=[down, pl.BlockSpec((1, size), lambda i: (0, i)), whole_spec((tokens, width))],
        out_shape=[
            like((hidden, width)),
            like((1, hidden), wide_type),
            like((tokens, width), wide_type),
        ],
        compiler_params=room,
        cost_estimate=estimate(
            6 * tokens * width * hidden,
            2 * (tokens * (4 * width + hidden) + 3 * hidden * width),
        ),
    )(grad_outer, normed_low, slope, w_out, w_in)


def norm_back_kernel(
    index_ref,
    total_ref,
    grad_ref,
    normal_ref,
    rstd_ref,
    own_ref,
    rest_ref,
    wo_ref,
    vec_ref,
    sums_in_ref,
    dep_ref,
    branch_ref,
    down_ref,
    drest_ref,
    gw_ref,
    sums,
    acc,
    held,
):
    del dep_ref
    step = pl.program_id(0)
    size = branch_ref.shape[0]
    head = index_ref[PARTS]
    gain_attn = vec_ref[1:2, :]
    heads = wo_ref.shape[0]
    rows = wo_ref.shape[1] // 4
    cols = wo_ref.shape[2] // 2

    @pl.when(step == 0)
    def _():
        sums[...] = jnp.zeros_like(sums)
        sums[0:8, :] = sums_in_ref[...]

    def one(at):
        grad = grad_ref[at, :].astype(wide_type) + total_ref[at, :]
        normal = normal_ref[at, :].astype(wide_type)
        scaled = grad * gain_attn
        rstd = rstd_ref[at, 0:1]
        grad_sum = rstd * (scaled - mean_last(scaled) - normal * mean_last(scaled * normal))
        grad_low = grad_sum.astype(low_type)
        branch_ref[at, :] = grad_low
        sums[3:4, :] += jnp.sum(grad * normal, 0, keepdims=True)
        sums[4:5, :] += jnp.sum(grad, 0, keepdims=True)
        sums[5:6, :] += jnp.sum(grad_low.astype(wide_type), 0, keepdims=True)

    tiles(size, 128, one)
    branch = branch_ref[...]
    for offset in range(heads):
        context = own_ref[0] if offset == 0 else rest_ref[offset - 1]
        weights = wo_ref[head ^ offset]
        grad_context = dot_nt(branch, weights).astype(low_type)
        if offset == 0:
            down_ref[0] = grad_context
        else:
            drest_ref[offset - 1] = grad_context
        part = dot_tn(context, branch)

        @pl.when(step == 0)
        def _():
            acc[offset] = part

        @pl.when(step > 0)
        def _():
            acc[offset] += part

    @pl.when(step == pl.num_programs(0) - 1)
    def _():
        for offset in range(heads):
            for part in range(PARTS):
                across, below = divmod(part, 4)
                lanes = slice(across * cols, (across + 1) * cols)
                held[part, offset, 0:rows] = acc[
                    offset, below * rows : (below + 1) * rows, lanes
                ].astype(low_type)
                row = sums[pl.ds(below * 4 + (head ^ offset), 1), lanes]
                held[part, offset, rows : rows + 16] = jnp.broadcast_to(row, (16, cols)).astype(
                    low_type
                )
        for slot in range(PARTS):
            gw_ref[slot] = held[index_ref[slot]]


def norm_back(index, total, grad_outer, normal, rstd, ctx_own, ctx_rest, w_output, vectors, sums, dep):
    tokens, width = grad_outer.shape
    heads, group = w_output.shape[:2]
    size = tokens // 2
    tile = pl.BlockSpec((size, width), lambda i, *_: (i, 0))
    own = pl.BlockSpec((1, size, group), lambda i, *_: (0, i, 0))
    rest = pl.BlockSpec((heads - 1, size, group), lambda i, *_: (0, i, 0))
    parts = (PARTS, heads, group // 4 + 16, width // 2)
    return pl.pallas_call(
        norm_back_kernel,
        grid_spec=pltpu.PrefetchScalarGridSpec(
            num_scalar_prefetch=1,
            grid=(2,),
            in_specs=[
                tile,
                tile,
                tile,
                pl.BlockSpec((size, 128), lambda i, *_: (i, 0)),
                own,
                rest,
                whole_spec(w_output.shape),
                whole_spec(vectors.shape),
                whole_spec(sums.shape),
                anywhere,
            ],
            out_specs=[tile, own, rest, whole_spec(parts)],
            scratch_shapes=[
                pltpu.VMEM((16, width), wide_type),
                pltpu.VMEM((heads, group, width), wide_type),
                pltpu.VMEM(parts, low_type),
            ],
        ),
        out_shape=[
            like((tokens, width)),
            like(ctx_own.shape),
            like(ctx_rest.shape),
            like(parts),
        ],
        compiler_params=room,
        cost_estimate=estimate(
            4 * tokens * width * width, 2 * tokens * width * 8 + 6 * width * width
        ),
    )(index, total, grad_outer, normal, rstd, ctx_own, ctx_rest, w_output, vectors, sums, dep)


def input_kernel(branch_ref, *refs):
    out_ref = refs[-1]
    total = branch_ref[...].astype(wide_type)
    for grads, weights in zip(refs[:-1:2], refs[1:-1:2]):
        for group in range(grads.shape[0]):
            total += dot_nn(grads[group], weights[group])
    out_ref[...] = total


def input_back(branch, pairs):
    tokens, width = branch.shape
    size = tokens // 2
    tile = pl.BlockSpec((size, width), lambda i: (i, 0))
    specs, values, flops = [tile], [branch], 0
    for grads, weights in pairs:
        specs.append(pl.BlockSpec((grads.shape[0], size, 576), lambda i: (0, i, 0)))
        specs.append(whole_spec(weights.shape))
        values += [grads, weights]
        flops += 2 * tokens * width * 576 * grads.shape[0]
    return pl.pallas_call(
        input_kernel,
        grid=(2,),
        in_specs=specs,
        out_specs=tile,
        out_shape=like((tokens, width), wide_type),
        compiler_params=room,
        cost_estimate=estimate(flops, sum(2 * value.size for value in values)),
    )(*values)


def finish_kernel(
    index_ref, near_ref, far_ref, near_wo_ref, far_wo_ref, q_ref, k_ref, v_ref, wo_ref, vec_ref, held, back
):
    rows = near_ref.shape[2] - 16
    cols = near_ref.shape[3]
    small = near_wo_ref.shape[2] - 16
    heads = near_wo_ref.shape[1]
    head = index_ref[PARTS]
    for slot in range(PARTS):
        here = slot < PARTS // 2
        near = slot % (PARTS // 2)
        held[index_ref[slot]] = (near_ref if here else far_ref)[near, 0]
        back[index_ref[slot]] = (near_wo_ref if here else far_wo_ref)[near]
    vec_ref[...] = jnp.zeros_like(vec_ref)
    for across in range(2):
        lanes = slice(across * cols, (across + 1) * cols)
        whole = jnp.concatenate([held[across * 4 + down, :rows] for down in range(4)], 0)
        whole = whole.astype(wide_type).T
        q_ref[lanes, 0:128] = whole[:, 0:128]
        q_ref[lanes, 128:192] = whole[:, 384:448]
        k_ref[lanes, 0:128] = whole[:, 128:256]
        k_ref[lanes, 128:192] = whole[:, 448:512]
        v_ref[lanes, 0:128] = whole[:, 256:384]
        v_ref[lanes, 128:192] = whole[:, 512:576]
        for down in range(4):
            sums = held[across * 4 + down, rows : rows + 16].astype(wide_type)
            if across == 0:
                vec_ref[16 + down : 17 + down, 0:rows] = sums[0:1, 0:rows]
            for offset in range(heads):
                other = head ^ offset
                block = back[across * 4 + down, offset].astype(wide_type)
                wo_ref[other, down * small : (down + 1) * small, lanes] = block[:small]
                vec_ref[pl.ds(down * 4 + other, 1), lanes] = block[small : small + 1]


def finish(index, near, far, near_wo, far_wo):
    rows, cols = near.shape[2] - 16, near.shape[3]
    heads, small = near_wo.shape[1], near_wo.shape[2] - 16
    width, group = 2 * cols, rows // 3 * 4
    shapes = [
        like((width, group), wide_type),
        like((width, group), wide_type),
        like((width, group), wide_type),
        like((heads, 4 * small, width), wide_type),
        like((24, width), wide_type),
    ]
    return pl.pallas_call(
        finish_kernel,
        grid_spec=pltpu.PrefetchScalarGridSpec(
            num_scalar_prefetch=1,
            grid=(1,),
            in_specs=[whole_spec(value.shape) for value in (near, far, near_wo, far_wo)],
            out_specs=[whole_spec(shape.shape) for shape in shapes],
            scratch_shapes=[
                pltpu.VMEM((PARTS,) + near.shape[2:], low_type),
                pltpu.VMEM((PARTS,) + near_wo.shape[1:], low_type),
            ],
        ),
        out_shape=shapes,
        compiler_params=room,
        cost_estimate=estimate(0, 16 * width * width),
    )(index, near, far, near_wo, far_wo)


def local(
    grid,
    layer_in,
    segment_ids,
    w_query,
    w_key,
    w_value,
    b_query,
    b_value,
    w_output,
    b_output,
    gain_attn,
    shift_attn,
    w_inner,
    b_inner,
    w_outer,
    b_outer,
    gain_ffn,
    shift_ffn,
    cotangent,
):
    tokens, width = layer_in.shape
    length = segment_ids.shape[1]
    seqs = tokens // length
    group = w_query.shape[1]
    hidden = w_inner.shape[1]
    heads = grid.heads
    devices = grid.rows * heads
    row = lax.axis_index("rows")
    head = lax.axis_index("heads")
    segments = lax.dynamic_slice_in_dim(segment_ids, head * seqs, seqs, 0)[:, None, :]

    def by_head(query, key, value):
        return jnp.concatenate(
            [query[:128], key[:128], value[:128], query[128:], key[128:], value[128:]], 0
        )

    shard = by_head(w_query.T, w_key.T, w_value.T)
    bias = by_head(b_query, jnp.zeros_like(b_query), b_value)
    part = row % PARTS
    piece = lax.dynamic_slice(
        shard, ((part % 4) * (3 * group // 4), (part // 4) * (width // 2)), (3 * group // 4, width // 2)
    )
    gathered = [grid.across_heads((piece, bias), offset) for offset in range(1, heads)]
    biases = jnp.stack([pair[1] for pair in gathered])[:, None, :].astype(wide_type)
    near = jnp.stack([pair[0] for pair in gathered])[None]
    for bits in ((1, 2), (2, 1)):
        near = jnp.concatenate([near, grid.across_bits(near, bits)], 0)
    far = grid.across_core(near)

    slots = grid.block_slots()

    def by_slot(values):
        return jnp.take(values.reshape((devices, -1) + values.shape[1:]), slots, axis=0).reshape(values.shape)

    w_in = by_slot(w_inner.T)
    w_out = by_slot(w_outer)
    b_in = by_slot(b_inner)[None]
    w_output_heads = w_output.reshape(heads, group, width)
    vectors = jnp.stack(
        [b_output, gain_attn, shift_attn, b_outer, gain_ffn, shift_ffn, b_output, b_output]
    )
    head_index = head.astype(jnp.int32)[None]
    natural = jnp.arange(PARTS, dtype=jnp.int32)
    out_slots = grid.row_slots() if grid.native else natural
    index = jnp.concatenate([out_slots, head_index])

    q_own, k_own, v_own, ctx_own = attend_own(
        layer_in, shard[None], bias.astype(wide_type)[None, None], segments
    )
    q_rest, k_rest, v_rest, ctx_rest, w_rest = attend_rest(
        grid.helper_slots(), layer_in, near, far, biases, segments
    )
    normed_low, normal, rstd, slope, layer_out, grad_outer, gw_outer, sums = forward_ffn(
        head_index, layer_in, ctx_own, ctx_rest, w_output_heads, cotangent, vectors, w_in, w_out, b_in
    )
    block_shape = (grid.rows, heads, hidden // devices, width)
    outer_held = grid.scatter_core(gw_outer.reshape(block_shape))
    gw_inner, gb_inner, total = inner_back(grad_outer, normed_low, slope, w_out, w_in)
    inner_parts = (gw_inner.reshape(block_shape), gb_inner.reshape(block_shape[:3]))
    branch, dctx_own, dctx_rest, gw_output = norm_back(
        index, total, grad_outer, normal, rstd, ctx_own, ctx_rest, w_output_heads, vectors, sums,
        outer_held,
    )
    inner_held = grid.scatter_core(inner_parts)
    outer_held = grid.scatter_chip(outer_held, 0)

    def back(start, count, dep):
        return attend_back(
            out_slots, layer_in, q_rest, k_rest, v_rest, ctx_rest, dctx_rest, dep, length, start, count
        )

    dqkv_late, dw_late = back(1, 2, inner_held[0])
    for step in range(1, grid.steps):
        outer_held = grid.scatter_chip(outer_held, step)
    inner_held = grid.scatter_chip(inner_held, 0)
    late = grid.scatter_core(grid.spread_parts(dw_late))
    dqkv_mid, dw_mid = back(0, 1, outer_held)
    mid = grid.scatter_core((grid.spread_parts(dw_mid), grid.spread_parts(gw_output)))
    for step in range(1, grid.steps):
        inner_held = grid.scatter_chip(inner_held, step)
    out_w_outer = grid.scatter_heads(outer_held[0])
    dqkv_own, dw_own = attend_back(
        out_slots, layer_in, q_own, k_own, v_own, ctx_own, dctx_own, inner_held[0], length, 0, 1
    )
    out_w_inner, out_b_inner = (grid.scatter_heads(leaf[0]) for leaf in inner_held)
    rest = (late, mid)
    own = grid.scatter_core(grid.spread_parts(dw_own))
    for step in range(grid.steps):
        rest, own = grid.scatter_chip((rest, own), step)
    (late, (mid, wo)), own = jax.tree.map(lambda leaf: leaf[0], (rest, own))
    input_grad = input_back(
        branch, [(dqkv_own, shard[None]), (dqkv_mid, w_rest[0:1]), (dqkv_late, w_rest[1:3])]
    )
    total = own[0].astype(wide_type)
    for offset, values in ((1, mid[0]), (2, late[0]), (3, late[1])):
        total = total + grid.across_heads(values, offset).astype(wide_type)
    wo = grid.scatter_heads(wo).astype(low_type)
    wo = jnp.stack(grid.gather_heads(wo))
    near, near_wo = grid.gather_chips((total.astype(low_type)[None], wo))
    far, far_wo = grid.across_core((near, near_wo))
    (near, far), places = grid.join_parts((near, far))
    (near_wo, far_wo), _ = grid.join_parts((near_wo, far_wo))
    gw_query, gw_key, gw_value, gw_output, small = finish(
        jnp.concatenate([places, head_index]), near, far, near_wo, far_wo
    )
    gb = small[16:20, : 3 * group // 4].reshape(-1)
    return (
        layer_out,
        input_grad,
        gw_query,
        gw_key,
        gw_value,
        jnp.concatenate([gb[0:128], gb[384:448]]),
        jnp.concatenate([gb[256:384], gb[512:576]]),
        gw_output.reshape(width, width),
        small[5],
        small[3],
        small[4],
        out_w_inner.T,
        out_b_inner,
        out_w_outer,
        small[2],
        small[0],
        small[1],
    )


def solution(mesh):
    grid = Grid(mesh)
    return jax.shard_map(
        lambda *values: local(grid, *values),
        mesh=mesh,
        in_specs=(
            P(("rows", "heads"), None),
            P("rows", None),
            P(None, "heads"),
            P(None, "heads"),
            P(None, "heads"),
            P("heads"),
            P("heads"),
            P(),
            P(),
            P(),
            P(),
            P(),
            P(),
            P(),
            P(),
            P(),
            P(),
            P(("rows", "heads"), None),
        ),
        out_specs=(
            P(("rows", "heads"), None),
            P(("rows", "heads"), None),
            P(None, "heads"),
            P(None, "heads"),
            P(None, "heads"),
            P("heads"),
            P("heads"),
            P(),
            P(),
            P(),
            P(),
            P(None, ("rows", "heads")),
            P(("rows", "heads")),
            P(("rows", "heads"), None),
            P(),
            P(),
            P(),
        ),
        check_vma=False,
    )
```

```python
import functools

import jax
import jax.numpy as jnp
from jax import lax
from jax.experimental import pallas as pl
from jax.experimental.pallas import tpu as pltpu
from jax.sharding import PartitionSpec as P

HD = 64
PARTS = 8
epsilon = 1e-06
masked_score = -1000000000.0
low_type = jnp.bfloat16
wide_type = jnp.float32
room = pltpu.CompilerParams(vmem_limit_bytes=60 * 1024 * 1024)


def contract(left, right, left_dim, right_dim):
    return lax.dot_general(
        left, right, (((left_dim,), (right_dim,)), ((), ())), preferred_element_type=wide_type
    )


def dot_nn(left, right):
    return contract(left, right, 1, 0)


def dot_nt(left, right):
    return contract(left, right, 1, 1)


def dot_tn(left, right):
    return contract(left, right, 0, 0)


class Grid:
    def __init__(self, mesh):
        self.rows = mesh.shape["rows"]
        self.heads = mesh.shape["heads"]
        self.steps = self.rows.bit_length() - 2
        up = list(range(1, self.steps + 1))
        self.orders = (up, up[::-1])
        self.native = self.rows == PARTS

    def permute(self, values, partner):
        pairs = []
        for row in range(self.rows):
            for head in range(self.heads):
                row_to, head_to = partner(row, head)
                pairs.append((row * self.heads + head, row_to * self.heads + head_to))
        return jax.tree.map(lambda leaf: lax.ppermute(leaf, ("rows", "heads"), pairs), values)

    def across_core(self, values):
        return self.permute(values, lambda row, head: (row ^ 1, head))

    def across_bits(self, values, bits):
        return self.permute(values, lambda row, head: (row ^ (1 << bits[row & 1]), head))

    def across_chip(self, values, step):
        return self.across_bits(values, [order[step] for order in self.orders])

    def across_heads(self, values, offset):
        return self.permute(values, lambda row, head: (row, head ^ offset))

    def slot_masks(self, core):
        last = self.steps - 1
        masks = []
        for slot in range(1 << self.steps):
            mask = 0
            for step in range(self.steps):
                mask |= ((slot >> (last - step)) & 1) << self.orders[core][step]
            masks.append(mask)
        return masks

    def row_slots(self):
        row = lax.axis_index("rows")
        masks = jnp.array([self.slot_masks(0), self.slot_masks(1)], jnp.int32)
        core = row & 1
        return jnp.concatenate([row ^ masks[core], (row ^ 1) ^ masks[1 - core]])

    def row_places(self):
        row = lax.axis_index("rows")
        half = self.rows // 2
        inverse = []
        for core in (0, 1):
            table = [0] * half
            for slot, mask in enumerate(self.slot_masks(core)):
                table[mask >> 1] = slot
            inverse.append(table)
        inverse = jnp.array(inverse, jnp.int32)
        apart = jnp.arange(self.rows, dtype=jnp.int32) ^ row
        other = apart & 1
        return other * half + inverse[(row & 1) ^ other, apart >> 1]

    def helper_slots(self):
        row = lax.axis_index("rows")
        masks = jnp.array([[0, 2, 4, 6], [0, 4, 2, 6]], jnp.int32)
        core = row & 1
        return jnp.concatenate([row ^ masks[core], (row ^ 1) ^ masks[1 - core]]) % PARTS

    def gather_chips(self, block):
        held = jax.tree.map(lambda leaf: leaf[None], block)
        for step in reversed(range(self.steps)):
            got = self.across_chip(held, step)
            held = jax.tree.map(lambda a, b: jnp.concatenate([a, b], 0), held, got)
        return held

    def gather_heads(self, block):
        return [block] + [self.across_heads(block, offset) for offset in range(1, self.heads)]

    def spread_parts(self, near, far):
        if self.native:
            return near, far
        parts = jnp.concatenate([near, far], 0)
        count, rows, cols = parts.shape[1:]
        finer = self.rows // PARTS
        parts = parts.reshape(PARTS, count, finer, rows // finer, cols).transpose(0, 2, 1, 3, 4)
        parts = parts.reshape(self.rows, count, rows // finer, cols)
        parts = jnp.take(parts, self.row_slots(), axis=0)
        return parts[: self.rows // 2], parts[self.rows // 2 :]

    def join_parts(self, near, far):
        if self.native:
            return near, far
        whole = jnp.take(jnp.concatenate([near, far], 0), self.row_places(), axis=0)
        count, rows, cols = whole.shape[1:]
        finer = self.rows // PARTS
        whole = whole.reshape(PARTS, finer, count, rows, cols).transpose(0, 2, 1, 3, 4)
        whole = whole.reshape(PARTS, count, finer * rows, cols)
        return whole[: PARTS // 2], whole[PARTS // 2 :]


def estimate(flops, moved, exps=0):
    return pl.CostEstimate(
        flops=flops, bytes_accessed=moved, transcendentals=exps
    )


def like(shape, dtype=low_type):
    return jax.ShapeDtypeStruct(shape, dtype)


def whole_spec(shape, **options):
    return pl.BlockSpec(shape, lambda *ids: (0,) * len(shape), **options)


anywhere = pl.BlockSpec(memory_space=pl.ANY)


def join_kernel(count, *refs):
    out_ref = refs[-1]
    place = 0
    for ref in refs[:count]:
        size = ref.shape[0]
        out_ref[place : place + size] = ref[...]
        place += size


def join(values, deps=()):
    shape = (sum(value.shape[0] for value in values),) + values[0].shape[1:]
    return pl.pallas_call(
        functools.partial(join_kernel, len(values)),
        grid=(1,),
        in_specs=[whole_spec(value.shape) for value in values] + [anywhere] * len(deps),
        out_specs=whole_spec(shape),
        out_shape=like(shape),
        compiler_params=room,
        cost_estimate=estimate(0, 4 * values[0].size),
    )(*values, *deps)


def fold_kernel(count, *refs):
    mine, theirs = refs[:count], refs[count : 2 * count]
    outs = refs[-sum(1 if ref.shape[0] == 1 else 2 for ref in mine) :]
    place = 0
    for own, got in zip(mine, theirs):
        size = own.shape[0]
        kept = max(size // 2, 1)
        for slot in range(size):
            out = outs[place] if slot < kept else outs[place + 1]
            out[slot % kept] = (own[slot].astype(wide_type) + got[slot].astype(wide_type)).astype(
                out.dtype
            )
        place += 1 if size == 1 else 2


def fold(mine, theirs, deps=()):
    shapes = []
    for value in mine:
        kept = max(value.shape[0] // 2, 1)
        shapes += [like((kept,) + value.shape[1:])] * (1 if value.shape[0] == 1 else 2)
    values = list(mine) + list(theirs)
    outs = pl.pallas_call(
        functools.partial(fold_kernel, len(mine)),
        grid=(1,),
        in_specs=[whole_spec(value.shape) for value in values] + [anywhere] * len(deps),
        out_specs=[whole_spec(shape.shape) for shape in shapes],
        out_shape=shapes,
        compiler_params=room,
        cost_estimate=estimate(0, sum(3 * value.size for value in values)),
    )(*values, *deps)
    states, place = [], 0
    for value in mine:
        if value.shape[0] == 1:
            states.append((outs[place], None))
            place += 1
        else:
            states.append((outs[place], outs[place + 1]))
            place += 2
    return states


def three_parts(values):
    first = values.astype(low_type).astype(wide_type)
    rest = values - first
    second = rest.astype(low_type).astype(wide_type)
    return first, second, (rest - second).astype(low_type).astype(wide_type)


def pair_up(low_lanes, first, second):
    return jnp.where(low_lanes, first, pltpu.roll(second, HD, 1))


def pack_kernel(index_ref, q_ref, k_ref, v_ref, bias_ref, w_ref, piece_ref):
    rows = piece_ref.shape[0]
    w_ref[0, 0:128, :] = q_ref[0:128, :]
    w_ref[0, 128:256, :] = k_ref[0:128, :]
    w_ref[0, 256:384, :] = v_ref[0:128, :]
    w_ref[0, 384:448, :] = q_ref[128:192, :]
    w_ref[0, 448:512, :] = k_ref[128:192, :]
    w_ref[0, 512:576, :] = v_ref[128:192, :]
    row = lax.broadcasted_iota(jnp.int32, (HD, w_ref.shape[2]), 0)
    w_ref[0, 576:640, :] = jnp.where(row == 0, bias_ref[...], 0.0).astype(low_type)
    mine = pl.multiple_of(index_ref[0] * rows, 16)
    piece_ref[...] = w_ref[0, pl.ds(mine, rows), :]


def pack(part, w_query, w_key, w_value, bias):
    width = w_query.shape[1]
    rows = 640 // PARTS
    return pl.pallas_call(
        pack_kernel,
        grid_spec=pltpu.PrefetchScalarGridSpec(
            num_scalar_prefetch=1,
            grid=(1,),
            in_specs=[whole_spec(w_query.shape)] * 3 + [whole_spec(bias.shape)],
            out_specs=[whole_spec((1, 640, width)), whole_spec((rows, width))],
        ),
        out_shape=[like((1, 640, width)), like((rows, width))],
        compiler_params=room,
        cost_estimate=estimate(0, 4 * width * 640),
    )(part, w_query, w_key, w_value, bias)


def attend_body(x_ref, w_ref, seg_ref, q_ref, k_ref, v_ref, ctx_ref):
    seqs, _, length = seg_ref.shape
    lane = lax.broadcasted_iota(jnp.int32, (1, 128), 1)
    low = lane < HD
    row8 = lax.broadcasted_iota(jnp.int32, (8, length), 0)
    bias_row = w_ref[0, 576:592, :][0:1, 0:640].astype(wide_type)
    for seq in range(seqs):
        at = slice(seq * length, (seq + 1) * length)
        qkv = (dot_nt(x_ref[at, :], w_ref[0]) + bias_row).astype(low_type).astype(wide_type)
        q01 = qkv[:, 0:128] * 0.125
        k01 = qkv[:, 128:256]
        v01 = qkv[:, 256:384]
        qk2 = qkv[:, 384:512]
        queries = [q01, pltpu.roll(q01, HD, 1), qk2 * 0.125]
        keys = [k01, pltpu.roll(k01, HD, 1), pltpu.roll(qk2, HD, 1)]
        values = [v01, pltpu.roll(v01, HD, 1), qkv[:, 512:640]]
        seg_rows = jnp.broadcast_to(seg_ref[seq], (8, length)).astype(wide_type)
        seg_col = seg_rows.T[:, 0:1].astype(jnp.int32) + HD
        same = lane == seg_col
        in_seg = (lane >= HD) & (lane < HD + 4)
        extra_q = jnp.where(same, 1.0, 0.0)
        extra_k = jnp.where(
            in_seg & ~same,
            masked_score,
            jnp.where((lane >= HD + 4) & (lane < HD + 7), 1.0, 0.0),
        )
        extra_v = jnp.where((lane >= HD) & (lane < HD + 3), 1.0, 0.0)
        contexts = []
        for head in range(3):
            query = jnp.where(low, queries[head], extra_q)
            key = jnp.where(low, keys[head], extra_k).astype(low_type)
            value = jnp.where(low, values[head], extra_v).astype(low_type)
            k_ref[0, head, at, :] = key
            v_ref[0, head, at, :] = value
            scores = dot_nt(key, query.astype(low_type))
            highest = jnp.max(scores, 0, keepdims=True)
            weights_low = jnp.exp(scores - highest).astype(low_type)
            summed = dot_tn(value, weights_low)
            total = summed[HD : HD + 1, :]
            first, second, third = three_parts(-(highest + jnp.log(total)))
            extra = jnp.where(
                row8 == 4, first, jnp.where(row8 == 5, second, jnp.where(row8 == 6, third, 0.0))
            )
            full = jnp.concatenate(
                [summed[:HD] * (1.0 / total), extra, jnp.zeros((56, length), wide_type)], 0
            ).T
            q_ref[0, head, at, :] = jnp.where(low, query, full + extra_q).astype(low_type)
            contexts.append(full)
        ctx_ref[0, at, 0:128] = pair_up(low, contexts[0], contexts[1]).astype(low_type)
        ctx_ref[0, at, 128:192] = contexts[2][:, :HD].astype(low_type)


def attend_own_kernel(x_ref, w_ref, seg_ref, q_ref, k_ref, v_ref, ctx_ref):
    attend_body(x_ref, w_ref, seg_ref, q_ref, k_ref, v_ref, ctx_ref)


def attend_rest_kernel(
    parts_ref, x_ref, near_ref, far_ref, seg_ref, q_ref, k_ref, v_ref, ctx_ref, w_ref
):
    rows = near_ref.shape[2]
    for slot in range(PARTS):
        piece = near_ref[slot, 0] if slot < PARTS // 2 else far_ref[slot - PARTS // 2, 0]
        w_ref[0, pl.ds(pl.multiple_of(parts_ref[slot] * rows, 16), rows), :] = piece
    attend_body(x_ref, w_ref, seg_ref, q_ref, k_ref, v_ref, ctx_ref)


def attend_cost(count, tokens, length, width):
    return estimate(
        count * (2 * tokens * width * 576 + 3 * 4 * tokens * length * 128),
        2 * tokens * width + count * 2 * (576 * width + 10 * tokens * 128),
        count * 3 * tokens * length,
    )


def attend_outputs(count, tokens):
    heads = pl.BlockSpec((1, 3, tokens, 128), lambda g, *_: (g, 0, 0, 0))
    specs = [heads, heads, heads, pl.BlockSpec((1, tokens, 192), lambda g, *_: (g, 0, 0))]
    shapes = [like((count, 3, tokens, 128))] * 3 + [like((count, tokens, 192))]
    return specs, shapes


def attend_own(layer_in, shard, segments):
    tokens, width = layer_in.shape
    specs, shapes = attend_outputs(1, tokens)
    return pl.pallas_call(
        attend_own_kernel,
        grid=(1,),
        in_specs=[
            whole_spec((tokens, width)),
            whole_spec(shard.shape),
            whole_spec(segments.shape),
        ],
        out_specs=specs,
        out_shape=shapes,
        compiler_params=room,
        cost_estimate=attend_cost(1, tokens, segments.shape[2], width),
    )(layer_in, shard, segments)


def attend_rest(parts, layer_in, near, far, segments):
    tokens, width = layer_in.shape
    count, rows, width = near.shape[1:]
    specs, shapes = attend_outputs(count, tokens)
    piece = pl.BlockSpec((PARTS // 2, 1, rows, width), lambda g, *_: (0, g, 0, 0))
    return pl.pallas_call(
        attend_rest_kernel,
        grid_spec=pltpu.PrefetchScalarGridSpec(
            num_scalar_prefetch=1,
            grid=(count,),
            in_specs=[
                whole_spec((tokens, width)),
                piece,
                piece,
                whole_spec(segments.shape),
            ],
            out_specs=specs + [pl.BlockSpec((1, 640, width), lambda g, *_: (g, 0, 0))],
        ),
        out_shape=shapes + [like((count, 640, width))],
        compiler_params=room,
        cost_estimate=attend_cost(count, tokens, segments.shape[2], width),
    )(parts, layer_in, near, far, segments)


def attend_back_kernel(
    length,
    slots_ref,
    x_ref,
    q_ref,
    k_ref,
    v_ref,
    ctx_ref,
    dctx_ref,
    spare_ref,
    *refs,
):
    dqkv_ref, near_ref, far_ref, held = refs[-4:]
    tokens, width = x_ref.shape
    rows = 640 // PARTS
    lane = lax.broadcasted_iota(jnp.int32, (1, 128), 1)
    low = lane < HD
    for seq in range(tokens // length):
        at = slice(seq * length, (seq + 1) * length)
        grad01 = dctx_ref[0, at, 0:128].astype(wide_type)
        grad2 = dctx_ref[0, at, 128:192].astype(wide_type)
        both = grad01 * ctx_ref[0, at, 0:128].astype(wide_type)
        inner = [
            jnp.sum(jnp.where(low, both, 0.0), -1, keepdims=True),
            jnp.sum(jnp.where(low, 0.0, both), -1, keepdims=True),
            jnp.sum(grad2 * ctx_ref[0, at, 128:192].astype(wide_type), -1, keepdims=True),
        ]
        grads = [
            grad01,
            pltpu.roll(grad01, HD, 1),
            jnp.concatenate([grad2, jnp.zeros((length, HD), wide_type)], 1),
        ]
        grad_q, grad_k, grad_v = [], [], []
        for head in range(3):
            first, second, third = three_parts(-inner[head])
            extra = jnp.where(
                lane == HD,
                first,
                jnp.where(lane == HD + 1, second, jnp.where(lane == HD + 2, third, 0.0)),
            )
            grad = jnp.where(low, grads[head], extra).astype(low_type)
            query = q_ref[0, head, at, :]
            key = k_ref[0, head, at, :]
            probs = jnp.exp(dot_nt(key, query))
            grad_scores = (probs * dot_nt(v_ref[0, head, at, :], grad)).astype(low_type)
            grad_v.append(dot_nn(probs.astype(low_type), grad))
            grad_k.append(dot_nn(grad_scores, query))
            grad_q.append(dot_tn(key, grad_scores).T * 0.125)
        dqkv_ref[0, at, 0:128] = pair_up(low, grad_q[0], grad_q[1]).astype(low_type)
        dqkv_ref[0, at, 128:256] = pair_up(low, grad_k[0], grad_k[1]).astype(low_type)
        dqkv_ref[0, at, 256:384] = pair_up(low, grad_v[0], grad_v[1]).astype(low_type)
        dqkv_ref[0, at, 384:512] = pair_up(low, grad_q[2], grad_k[2]).astype(low_type)
        dqkv_ref[0, at, 512:640] = jnp.where(low, grad_v[2], 0.0).astype(low_type)
    grad_all = dqkv_ref[0]
    total = dot_tn(grad_all, x_ref[...])
    sums = jnp.sum(grad_all.astype(wide_type), 0, keepdims=True)
    sums = jnp.concatenate([sums, jnp.zeros((1, width - 640), wide_type)], 1)
    for part in range(PARTS):
        held[part] = total[part * rows : (part + 1) * rows].astype(low_type)
    row = lax.broadcasted_iota(jnp.int32, (HD, width), 0)
    spare = jnp.where(row == 0, sums, spare_ref[...].astype(wide_type))
    held[PARTS - 1, rows - HD : rows] = spare.astype(low_type)
    for slot in range(PARTS // 2):
        near_ref[slot, 0] = held[slots_ref[slot]]
        far_ref[slot, 0] = held[slots_ref[slot + PARTS // 2]]


def attend_back(
    slots, layer_in, queries, keys, values, context, grad_context, spare, deps, length
):
    tokens, width = layer_in.shape
    count = context.shape[0]
    rows = 640 // PARTS
    heads = pl.BlockSpec((1, 3, tokens, 128), lambda g, *_: (g, 0, 0, 0))
    group = pl.BlockSpec((1, tokens, 192), lambda g, *_: (g, 0, 0))
    half = pl.BlockSpec((PARTS // 2, 1, rows, width), lambda g, *_: (0, g, 0, 0))
    return pl.pallas_call(
        functools.partial(attend_back_kernel, length),
        grid_spec=pltpu.PrefetchScalarGridSpec(
            num_scalar_prefetch=1,
            grid=(count,),
            in_specs=[whole_spec((tokens, width)), heads, heads, heads, group, group]
            + [whole_spec(spare.shape)]
            + [anywhere] * len(deps),
            out_specs=[pl.BlockSpec((1, tokens, 640), lambda g, *_: (g, 0, 0)), half, half],
            scratch_shapes=[pltpu.VMEM((PARTS, rows, width), low_type)],
        ),
        out_shape=[
            like((count, tokens, 640)),
            like((PARTS // 2, count, rows, width)),
            like((PARTS // 2, count, rows, width)),
        ],
        compiler_params=room,
        cost_estimate=estimate(
            count * (2 * tokens * width * 576 + 3 * 10 * tokens * length * 128),
            2 * tokens * width + count * 2 * (576 * width + 16 * tokens * 128),
            count * 3 * tokens * length,
        ),
    )(slots, layer_in, queries, keys, values, context, grad_context, spare, *deps)


def mean_last(values):
    return jnp.mean(values, -1, keepdims=True)


def tiles(tokens, size, body):
    def step(index, carry):
        body(pl.ds(pl.multiple_of(index * size, size), size))
        return carry

    lax.fori_loop(0, tokens // size, step, 0)


def gelu_pair(values):
    cumulative = 0.5 * (1.0 + lax.erf(values * 0.7071067811865476))
    density = jnp.exp(-0.5 * values * values) * 0.3989422804014327
    return values * cumulative, cumulative + values * density


class Loads:
    def __init__(self, slots_ref, w_in_hbm, w_out_hbm, w_in, w_out, sems):
        self.count = sems.shape[1]
        self.size = w_out.shape[0] // self.count
        self.copies = []
        for slot in range(self.count):
            source = pl.ds(pl.multiple_of(slots_ref[slot] * self.size, 128), self.size)
            target = pl.ds(slot * self.size, self.size)
            self.copies.append(
                (
                    pltpu.make_async_copy(w_in_hbm.at[:, source], w_in.at[:, target], sems.at[0, slot]),
                    pltpu.make_async_copy(w_out_hbm.at[source], w_out.at[target], sems.at[1, slot]),
                )
            )

    def start(self):
        for copies in self.copies:
            for copy in copies:
                copy.start()

    def wait(self, low, high):
        for slot in range(-(-low // self.size), -(-high // self.size)):
            for copy in self.copies[slot]:
                copy.wait()


def forward_kernel(
    chunks,
    slots_ref,
    x_ref,
    own_ref,
    rest_ref,
    wo_ref,
    cot_ref,
    vec_ref,
    b_in_ref,
    w_in_hbm,
    w_out_hbm,
    slope_ref,
    rstd_ref,
    sums_ref,
    low_hbm,
    normal_hbm,
    out_hbm,
    grad_hbm,
    gw_hbm,
    w_in,
    w_out,
    normed,
    outer,
    active,
    low,
    normal_low,
    result_low,
    grad_out,
    sems,
    out_sems,
):
    step = pl.program_id(0)
    tokens = x_ref.shape[0]
    hidden = w_out.shape[0]
    size = hidden // chunks
    loads = Loads(slots_ref, w_in_hbm, w_out_hbm, w_in, w_out, sems)
    head = slots_ref[loads.count]
    b_output, gain_attn, shift_attn = vec_ref[0:1, :], vec_ref[1:2, :], vec_ref[2:3, :]
    b_outer, gain_ffn, shift_ffn = vec_ref[3:4, :], vec_ref[4:5, :], vec_ref[5:6, :]
    small = [
        pltpu.make_async_copy(source, target, out_sems.at[place])
        for place, (source, target) in enumerate(
            ((low, low_hbm), (normal_low, normal_hbm), (result_low, out_hbm), (grad_out, grad_hbm))
        )
    ]
    grads = []
    for slot in range(loads.count):
        target = pl.ds(pl.multiple_of(slots_ref[slot] * loads.size, 128), loads.size)
        grads.append(
            pltpu.make_async_copy(
                w_out.at[pl.ds(slot * loads.size, loads.size)], gw_hbm.at[target], out_sems.at[4 + slot]
            )
        )

    @pl.when(step == 0)
    def _():
        loads.start()
        outer[...] = jnp.zeros_like(outer)
        branch = dot_nn(own_ref[0], wo_ref[head])
        for offset in range(1, wo_ref.shape[0]):
            branch += dot_nn(rest_ref[offset - 1], wo_ref[head ^ offset])
        normed[...] = branch

        def one(at):
            total = x_ref[at, :].astype(wide_type) + (normed[at, :] + b_output)
            centred = total - mean_last(total)
            rstd = lax.rsqrt(mean_last(centred * centred) + epsilon)
            normal = centred * rstd
            result = normal * gain_attn + shift_attn
            normed[at, :] = result
            low[at, :] = result.astype(low_type)
            normal_low[at, :] = normal.astype(low_type)
            rstd_ref[at, :] = jnp.broadcast_to(rstd, (rstd.shape[0], 128))

        tiles(tokens, 256, one)
        small[0].start()
        small[1].start()

    for chunk in range(chunks):

        @pl.when(step == chunk)
        def _():
            loads.wait(chunk * size, (chunk + 1) * size)

    @pl.when(step < chunks)
    def _():
        at = pl.ds(pl.multiple_of(step * size, 128), size)
        inner = dot_nn(low[...], w_in[:, at]) + b_in_ref[...]
        values, slope = gelu_pair(inner)
        values = values.astype(low_type)
        active[step] = values
        slope_ref[...] = slope.astype(low_type)
        outer[...] += dot_nn(values, w_out[at, :])

    @pl.when(step == chunks - 1)
    def _():
        sums_ref[...] = jnp.zeros_like(sums_ref)

        def one(at):
            total = normed[at, :] + (outer[at, :] + b_outer)
            centred = total - mean_last(total)
            rstd = lax.rsqrt(mean_last(centred * centred) + epsilon)
            normal = centred * rstd
            result_low[at, :] = (normal * gain_ffn + shift_ffn).astype(low_type)
            grad = cot_ref[at, :].astype(wide_type)
            scaled = grad * gain_ffn
            grad_sum = rstd * (scaled - mean_last(scaled) - normal * mean_last(scaled * normal))
            grad_low = grad_sum.astype(low_type)
            grad_out[at, :] = grad_low
            sums_ref[0:1, :] += jnp.sum(grad * normal, 0, keepdims=True)
            sums_ref[1:2, :] += jnp.sum(grad, 0, keepdims=True)
            sums_ref[2:3, :] += jnp.sum(grad_low.astype(wide_type), 0, keepdims=True)

        tiles(tokens, 256, one)
        small[2].start()
        small[3].start()

    @pl.when(step >= chunks)
    def _():
        which = step - chunks
        at = pl.ds(pl.multiple_of(which * size, 128), size)
        w_out[at, :] = dot_tn(active[which], grad_out[...]).astype(low_type)

    for chunk in range(chunks):

        @pl.when(step == chunks + chunk)
        def _():
            for slot in range(loads.count):
                if chunk * size < (slot + 1) * loads.size <= (chunk + 1) * size:
                    grads[slot].start()

    @pl.when(step == 2 * chunks - 1)
    def _():
        for copy in small:
            copy.wait()
        for copy in grads:
            copy.wait()


def forward_ffn(slots, layer_in, ctx_own, ctx_rest, w_output, cotangent, vectors, w_in, w_out, b_in):
    tokens, width = layer_in.shape
    hidden = w_out.shape[0]
    chunks = 3
    blocks = slots.shape[0] - 1
    size = hidden // chunks
    wide_chunk = lambda i, *_: (0, jnp.minimum(i, chunks - 1))
    once = dict(pipeline_mode=pl.Buffered(1))
    return pl.pallas_call(
        functools.partial(forward_kernel, chunks),
        grid_spec=pltpu.PrefetchScalarGridSpec(
            num_scalar_prefetch=1,
            grid=(2 * chunks,),
            in_specs=[
                whole_spec((tokens, width), **once),
                whole_spec(ctx_own.shape, **once),
                whole_spec(ctx_rest.shape, **once),
                whole_spec(w_output.shape, **once),
                whole_spec((tokens, width), **once),
                whole_spec(vectors.shape, **once),
                pl.BlockSpec((1, size), wide_chunk),
                anywhere,
                anywhere,
            ],
            out_specs=[
                pl.BlockSpec((tokens, size), wide_chunk),
                whole_spec((tokens, 128)),
                whole_spec((8, width)),
            ]
            + [anywhere] * 5,
            scratch_shapes=[
                pltpu.VMEM((width, hidden), low_type),
                pltpu.VMEM((hidden, width), low_type),
                pltpu.VMEM((tokens, width), wide_type),
                pltpu.VMEM((tokens, width), wide_type),
                pltpu.VMEM((chunks, tokens, size), low_type),
            ]
            + [pltpu.VMEM((tokens, width), low_type)] * 4
            + [pltpu.SemaphoreType.DMA((2, blocks)), pltpu.SemaphoreType.DMA((4 + blocks,))],
        ),
        out_shape=[
            like((tokens, hidden)),
            like((tokens, 128), wide_type),
            like((8, width), wide_type),
        ]
        + [like((tokens, width))] * 4
        + [like((hidden, width))],
        compiler_params=room,
        cost_estimate=estimate(
            2 * tokens * width * (3 * hidden + width),
            2 * (tokens * (7 * width + hidden) + 3 * hidden * width),
            tokens * hidden,
        ),
    )(slots, layer_in, ctx_own, ctx_rest, w_output, cotangent, vectors, b_in, w_in, w_out)


def inner_back_kernel(
    chunks,
    slots_ref,
    grad_ref,
    low_ref,
    slope_ref,
    w_in_hbm,
    w_out_hbm,
    sums_ref,
    total_ref,
    near_hbm,
    far_hbm,
    w_in,
    w_out,
    sems,
    out_sems,
):
    step = pl.program_id(0)
    hidden = w_out.shape[0]
    size = hidden // chunks
    half = hidden // 2
    loads = Loads(slots_ref, w_in_hbm, w_out_hbm, w_in, w_out, sems)
    pieces = []
    for chunk in range(chunks):
        begin, end = chunk * size, (chunk + 1) * size
        cuts = [begin, half, end] if begin < half < end else [begin, end]
        for low, high in zip(cuts, cuts[1:]):
            target, offset = (near_hbm, 0) if high <= half else (far_hbm, half)
            copy = pltpu.make_async_copy(
                w_out.at[pl.ds(low, high - low)],
                target.at[pl.ds(low - offset, high - low)],
                out_sems.at[len(pieces)],
            )
            pieces.append((chunk, copy))

    @pl.when(step == 0)
    def _():
        loads.start()

    for chunk in range(chunks):

        @pl.when(step == chunk)
        def _():
            loads.wait(chunk * size, (chunk + 1) * size)

    at = pl.ds(pl.multiple_of(step * size, 128), size)
    grad_inner = (
        dot_nt(grad_ref[...], w_out[at, :]) * slope_ref[...].astype(wide_type)
    ).astype(low_type)
    sums_ref[...] = jnp.sum(grad_inner.astype(wide_type), 0, keepdims=True)
    w_out[at, :] = dot_tn(grad_inner, low_ref[...]).astype(low_type)
    part = dot_nt(grad_inner, w_in[:, at])

    for chunk in range(chunks):

        @pl.when(step == chunk)
        def _():
            for owner, copy in pieces:
                if owner == chunk:
                    copy.start()

    @pl.when(step == 0)
    def _():
        total_ref[...] = part

    @pl.when(step > 0)
    def _():
        total_ref[...] += part

    @pl.when(step == chunks - 1)
    def _():
        for _, copy in pieces:
            copy.wait()


def inner_back(slots, grad_outer, normed_low, slope, w_in, w_out):
    tokens, width = grad_outer.shape
    hidden = w_out.shape[0]
    chunks = 3
    blocks = slots.shape[0] - 1
    size = hidden // chunks
    return pl.pallas_call(
        functools.partial(inner_back_kernel, chunks),
        grid_spec=pltpu.PrefetchScalarGridSpec(
            num_scalar_prefetch=1,
            grid=(chunks,),
            in_specs=[
                whole_spec((tokens, width)),
                whole_spec((tokens, width)),
                pl.BlockSpec((tokens, size), lambda i, *_: (0, i)),
                anywhere,
                anywhere,
            ],
            out_specs=[
                pl.BlockSpec((1, size), lambda i, *_: (0, i)),
                whole_spec((tokens, width)),
                anywhere,
                anywhere,
            ],
            scratch_shapes=[
                pltpu.VMEM((width, hidden), low_type),
                pltpu.VMEM((hidden, width), low_type),
                pltpu.SemaphoreType.DMA((2, blocks)),
                pltpu.SemaphoreType.DMA((2 * chunks,)),
            ],
        ),
        out_shape=[
            like((1, hidden), wide_type),
            like((tokens, width), wide_type),
            like((hidden // 2, width)),
            like((hidden // 2, width)),
        ],
        compiler_params=room,
        cost_estimate=estimate(
            6 * tokens * width * hidden, 2 * (tokens * (4 * width + hidden) + 3 * hidden * width)
        ),
    )(slots, grad_outer, normed_low, slope, w_in, w_out)


def norm_back_kernel(
    index_ref,
    total_ref,
    grad_ref,
    normal_ref,
    rstd_ref,
    own_ref,
    rest_ref,
    wo_ref,
    vec_ref,
    sums_in_ref,
    gb_ref,
    branch_ref,
    down_ref,
    drest_ref,
    near_ref,
    far_ref,
    spare_ref,
    sums,
    acc,
    held,
    inner_sums,
):
    step = pl.program_id(0)
    size = branch_ref.shape[0]
    head = index_ref[PARTS]
    gain_attn = vec_ref[1:2, :]
    heads = wo_ref.shape[0]
    rows = wo_ref.shape[1] // 4
    cols = wo_ref.shape[2] // 2

    @pl.when(step == 0)
    def _():
        sums[...] = sums_in_ref[...]

    def one(at):
        grad = grad_ref[at, :].astype(wide_type) + total_ref[at, :]
        normal = normal_ref[at, :].astype(wide_type)
        scaled = grad * gain_attn
        rstd = rstd_ref[at, 0:1]
        grad_sum = rstd * (scaled - mean_last(scaled) - normal * mean_last(scaled * normal))
        grad_low = grad_sum.astype(low_type)
        branch_ref[at, :] = grad_low
        sums[3:4, :] += jnp.sum(grad * normal, 0, keepdims=True)
        sums[4:5, :] += jnp.sum(grad, 0, keepdims=True)
        sums[5:6, :] += jnp.sum(grad_low.astype(wide_type), 0, keepdims=True)

    tiles(size, 256, one)
    branch = branch_ref[...]
    for offset in range(heads):
        context = own_ref[0] if offset == 0 else rest_ref[offset - 1]
        weights = wo_ref[head ^ offset]
        grad_context = dot_nt(branch, weights).astype(low_type)
        if offset == 0:
            down_ref[0] = grad_context
        else:
            drest_ref[offset - 1] = grad_context
        part = dot_tn(context, branch)

        @pl.when(step == 0)
        def _():
            acc[offset] = part

        @pl.when(step > 0)
        def _():
            acc[offset] += part

    @pl.when(step == pl.num_programs(0) - 1)
    def _():
        for offset in range(heads):
            for part in range(PARTS):
                across, below = divmod(part, 4)
                held[part, offset] = acc[
                    offset,
                    below * rows : (below + 1) * rows,
                    across * cols : (across + 1) * cols,
                ].astype(low_type)
        for slot in range(PARTS // 2):
            near_ref[slot] = held[index_ref[slot]]
            far_ref[slot] = held[index_ref[slot + PARTS // 2]]
        block = gb_ref.shape[1] // PARTS
        for slot in range(PARTS):
            inner_sums[pl.ds(index_ref[slot], 1), :] = gb_ref[:, slot * block : (slot + 1) * block]
        spare_ref[...] = jnp.zeros_like(spare_ref)
        rows_out = [jnp.zeros((1, 2 * block), wide_type), sums[0:6, :]]
        for pair in range(PARTS // 2):
            rows_out.append(
                jnp.concatenate(
                    [inner_sums[2 * pair : 2 * pair + 1], inner_sums[2 * pair + 1 : 2 * pair + 2]], 1
                )
            )
        rows_out.append(jnp.zeros((5, 2 * block), wide_type))
        spare_ref[0:16, :] = jnp.concatenate(rows_out, 0).astype(low_type)


def norm_back(
    index, total, grad_outer, normal, rstd, ctx_own, ctx_rest, w_output, vectors, sums, gb
):
    tokens, width = grad_outer.shape
    heads, group = w_output.shape[:2]
    size = tokens // 2
    tile = pl.BlockSpec((size, width), lambda i, *_: (i, 0))
    own = pl.BlockSpec((1, size, group), lambda i, *_: (0, i, 0))
    rest = pl.BlockSpec((heads - 1, size, group), lambda i, *_: (0, i, 0))
    half = (PARTS // 2, heads, group // 4, width // 2)
    return pl.pallas_call(
        norm_back_kernel,
        grid_spec=pltpu.PrefetchScalarGridSpec(
            num_scalar_prefetch=1,
            grid=(2,),
            in_specs=[
                tile,
                tile,
                tile,
                pl.BlockSpec((size, 128), lambda i, *_: (i, 0)),
                own,
                rest,
                whole_spec(w_output.shape),
                whole_spec(vectors.shape),
                whole_spec(sums.shape),
                whole_spec(gb.shape),
            ],
            out_specs=[
                tile,
                own,
                rest,
                whole_spec(half),
                whole_spec(half),
                whole_spec((HD, width)),
            ],
            scratch_shapes=[
                pltpu.VMEM((8, width), wide_type),
                pltpu.VMEM((heads, group, width), wide_type),
                pltpu.VMEM((PARTS,) + half[1:], low_type),
                pltpu.VMEM((PARTS, gb.shape[1] // PARTS), wide_type),
            ],
        ),
        out_shape=[
            like((tokens, width)),
            like(ctx_own.shape),
            like(ctx_rest.shape),
            like(half),
            like(half),
            like((HD, width)),
        ],
        compiler_params=room,
        cost_estimate=estimate(
            4 * tokens * width * width, 2 * tokens * width * 8 + 6 * width * width
        ),
    )(index, total, grad_outer, normal, rstd, ctx_own, ctx_rest, w_output, vectors, sums, gb)


def input_kernel(branch_ref, *refs):
    out_ref = refs[-1]
    total = branch_ref[...].astype(wide_type)
    for grads, weights in zip(refs[0:4:2], refs[1:4:2]):
        for group in range(grads.shape[0]):
            total += dot_nn(grads[group], weights[group])
    out_ref[...] = total


def input_back(branch, pairs, deps):
    tokens, width = branch.shape
    size = tokens // 2
    tile = pl.BlockSpec((size, width), lambda i: (i, 0))
    specs, values, flops = [tile], [branch], 0
    for grads, weights in pairs:
        specs.append(pl.BlockSpec((grads.shape[0], size, 640), lambda i: (0, i, 0)))
        specs.append(whole_spec(weights.shape))
        values += [grads, weights]
        flops += 2 * tokens * width * 576 * grads.shape[0]
    return pl.pallas_call(
        input_kernel,
        grid=(2,),
        in_specs=specs + [anywhere] * len(deps),
        out_specs=tile,
        out_shape=like((tokens, width), wide_type),
        compiler_params=room,
        cost_estimate=estimate(flops, sum(2 * value.size for value in values)),
    )(*values, *deps)


def finish_kernel(
    index_ref, near_ref, far_ref, near_wo_ref, far_wo_ref, q_ref, k_ref, v_ref, wo_ref, spare_ref, held, back
):
    cols = near_wo_ref.shape[3]
    small = near_wo_ref.shape[2]
    heads = near_wo_ref.shape[1]
    head = index_ref[PARTS]
    for slot in range(PARTS):
        here = slot < PARTS // 2
        near = slot % (PARTS // 2)
        held[index_ref[slot]] = (near_ref if here else far_ref)[near, 0]
        back[index_ref[slot]] = (near_wo_ref if here else far_wo_ref)[near]
    whole = held[...].reshape(640, held.shape[2])
    for ref, first, second in ((q_ref, 0, 384), (k_ref, 128, 448), (v_ref, 256, 512)):
        ref[0:128, :] = whole[first : first + 128].astype(wide_type)
        ref[128:192, :] = whole[second : second + HD].astype(wide_type)
    spare_ref[...] = whole[576:592].astype(wide_type)
    for part in range(PARTS):
        across, down = divmod(part, 4)
        for offset in range(heads):
            wo_ref[
                head ^ offset,
                down * small : (down + 1) * small,
                across * cols : (across + 1) * cols,
            ] = back[part, offset].astype(wide_type)


def finish(index, near, far, near_wo, far_wo):
    width = near.shape[3]
    heads, small, _ = near_wo.shape[1:]
    group = 4 * small
    shapes = [
        like((group, width), wide_type),
        like((group, width), wide_type),
        like((group, width), wide_type),
        like((heads, group, width), wide_type),
        like((16, width), wide_type),
    ]
    return pl.pallas_call(
        finish_kernel,
        grid_spec=pltpu.PrefetchScalarGridSpec(
            num_scalar_prefetch=1,
            grid=(1,),
            in_specs=[whole_spec(value.shape) for value in (near, far, near_wo, far_wo)],
            out_specs=[whole_spec(shape.shape) for shape in shapes],
            scratch_shapes=[
                pltpu.VMEM((PARTS,) + near.shape[2:], low_type),
                pltpu.VMEM((PARTS,) + near_wo.shape[1:], low_type),
            ],
        ),
        out_shape=shapes,
        compiler_params=room,
        cost_estimate=estimate(0, 16 * width * width),
    )(index, near, far, near_wo, far_wo)


def local(
    grid,
    layer_in,
    segment_ids,
    w_query,
    w_key,
    w_value,
    b_query,
    b_value,
    w_output,
    b_output,
    gain_attn,
    shift_attn,
    w_inner,
    b_inner,
    w_outer,
    b_outer,
    gain_ffn,
    shift_ffn,
    cotangent,
):
    tokens, width = layer_in.shape
    length = segment_ids.shape[1]
    seqs = tokens // length
    group = w_query.shape[1]
    hidden = w_inner.shape[1]
    heads = grid.heads
    row = lax.axis_index("rows")
    head = lax.axis_index("heads")
    segments = lax.dynamic_slice_in_dim(segment_ids, head * seqs, seqs, 0)[:, None, :]

    gap = jnp.zeros((128,), b_query.dtype)
    bias = jnp.concatenate(
        [b_query[:128], gap, b_value[:128], b_query[128:], gap[:HD], b_value[128:], gap, gap[:HD]]
    ).astype(wide_type)[None]
    part = (row % PARTS).astype(jnp.int32)[None]
    shard, piece = pack(part, w_query.T, w_key.T, w_value.T, bias)
    pieces = [grid.across_heads(piece, offset)[None] for offset in range(1, heads)]
    q_own, k_own, v_own, ctx_own = attend_own(layer_in, shard, segments)
    near = join(pieces, (ctx_own,))[None]
    for bits in ((1, 2), (2, 1)):
        near = join([near, grid.across_bits(near, bits)])
    far = grid.across_core(near)

    row_slots = grid.row_slots()
    b_in = jnp.take(b_inner.reshape(grid.rows, -1), row_slots, axis=0, mode="clip").reshape(1, hidden)
    natural = jnp.arange(PARTS, dtype=jnp.int32)
    w_in, w_out = w_inner, w_outer
    if not grid.native:
        w_in = jnp.take(w_in.reshape(width, grid.rows, -1), row_slots, axis=1).reshape(width, hidden)
        w_out = jnp.take(w_out.reshape(grid.rows, -1, width), row_slots, axis=0).reshape(hidden, width)
    head_index = head.astype(jnp.int32)[None]
    index = jnp.concatenate([row_slots if grid.native else natural, head_index])
    w_output_heads = w_output.reshape(heads, group, width)
    vectors = jnp.stack(
        [b_output, gain_attn, shift_attn, b_outer, gain_ffn, shift_ffn, b_output, b_output]
    )

    q_rest, k_rest, v_rest, ctx_rest, w_rest = attend_rest(
        grid.helper_slots(), layer_in, near, far, segments
    )
    slope, rstd, sums, normed_low, normal, layer_out, grad_outer, gw_outer = forward_ffn(
        index, layer_in, ctx_own, ctx_rest, w_output_heads, cotangent, vectors, w_in, w_out, b_in
    )
    if not grid.native:
        gw_outer = jnp.take(
            gw_outer.reshape(grid.rows, -1, width), grid.row_places(), axis=0
        ).reshape(hidden, width)
    outer_rows = lax.psum_scatter(gw_outer, "rows", scatter_dimension=0, tiled=True)
    gb_inner, total, inner_near, inner_far = inner_back(
        index, grad_outer, normed_low, slope, w_in, w_out
    )
    slot_shape = (grid.rows // 2, hidden // grid.rows, width)
    inner_near, inner_far = inner_near.reshape(slot_shape), inner_far.reshape(slot_shape)
    inner_got = grid.across_core(inner_far)
    if not grid.native:
        gb_inner = jnp.take(gb_inner.reshape(grid.rows, -1), grid.row_places(), axis=0).reshape(1, hidden)
    branch, dctx_own, dctx_rest, wo_near, wo_far, spare = norm_back(
        index,
        total,
        grad_outer,
        normal,
        rstd,
        ctx_own,
        ctx_rest,
        w_output_heads,
        vectors,
        sums,
        gb_inner,
    )
    wo_near, wo_far = grid.spread_parts(wo_near, wo_far)

    def later_steps(state, first):
        for step in range(first, grid.steps):
            (state,) = fold([state[0]], [grid.across_chip(state[1], step)])
        return state

    (inner,) = fold([inner_near], [inner_got], (branch,))
    inner_got = grid.across_chip(inner[1], 0)
    wo_got = grid.across_core(wo_far)
    dqkv_rest, rest_near, rest_far = attend_back(
        index, layer_in, q_rest, k_rest, v_rest, ctx_rest, dctx_rest, spare, (inner[1],), length
    )
    rest_near, rest_far = grid.spread_parts(rest_near, rest_far)
    inner, wo = fold([inner[0], wo_near], [inner_got, wo_got], (dqkv_rest,))
    inner_got = grid.across_chip(inner[1], 1)
    wo_got = grid.across_chip(wo[1], 0)
    rest_got = grid.across_core(rest_far)
    dqkv_own, own_near, own_far = attend_back(
        index, layer_in, q_own, k_own, v_own, ctx_own, dctx_own, spare, (inner[1], wo[1]), length
    )
    own_near, own_far = grid.spread_parts(own_near, own_far)
    inner, wo, rest = fold(
        [inner[0], wo[0], rest_near], [inner_got, wo_got, rest_got], (dqkv_own, outer_rows)
    )
    inner = later_steps(inner, 2)
    out_w_inner = lax.psum_scatter(inner[0][0], "heads", scatter_dimension=0, tiled=True)
    out_w_outer = lax.psum_scatter(outer_rows, "heads", scatter_dimension=0, tiled=True)
    wo_got = grid.across_chip(wo[1], 1)
    rest_got = grid.across_chip(rest[1], 0)
    own_got = grid.across_core(own_far)
    input_grad = input_back(branch, [(dqkv_own, shard), (dqkv_rest, w_rest)], (rest[1], wo[1]))
    wo, rest, own = fold([wo[0], rest[0], own_near], [wo_got, rest_got, own_got], (input_grad,))
    wo = later_steps(wo, 2)[0][0]
    wo_total = wo[0].astype(wide_type)
    for offset in range(1, heads):
        wo_total = wo_total + grid.across_heads(wo[offset], offset).astype(wide_type)
    wo = wo_total.astype(low_type)
    rest, own = fold(
        [rest[0], own[0]], [grid.across_chip(rest[1], 1), grid.across_chip(own[1], 0)]
    )
    rest = later_steps(rest, 2)[0][0]
    own = later_steps(own, 1)[0][0]
    total = own[0].astype(wide_type)
    backs = [wo]
    for offset in range(1, heads):
        got, back = grid.across_heads((rest[offset - 1], wo), offset)
        total = total + got.astype(wide_type)
        backs.append(back)
    near, near_wo = grid.gather_chips((total.astype(low_type)[None], jnp.stack(backs)))
    far, far_wo = grid.across_core((near, near_wo))
    near, far = grid.join_parts(near, far)
    near_wo, far_wo = grid.join_parts(near_wo, far_wo)
    gw_query, gw_key, gw_value, gw_output, small = finish(index, near, far, near_wo, far_wo)
    block = hidden // (grid.rows * heads)
    own_block = (row * heads + head) * block
    return (
        layer_out,
        input_grad,
        gw_query.T,
        gw_key.T,
        gw_value.T,
        jnp.concatenate([small[0, 0:128], small[0, 384:448]]),
        jnp.concatenate([small[0, 256:384], small[0, 512:576]]),
        gw_output.reshape(width, width),
        small[6],
        small[4],
        small[5],
        out_w_inner.astype(wide_type).T,
        lax.dynamic_slice_in_dim(small[7:11].reshape(-1), own_block, block, 0),
        out_w_outer.astype(wide_type),
        small[3],
        small[1],
        small[2],
    )


def solution(mesh):
    grid = Grid(mesh)
    return jax.shard_map(
        lambda *values: local(grid, *values),
        mesh=mesh,
        in_specs=(
            P(("rows", "heads"), None),
            P("rows", None),
            P(None, "heads"),
            P(None, "heads"),
            P(None, "heads"),
            P("heads"),
            P("heads"),
            P(),
            P(),
            P(),
            P(),
            P(),
            P(),
            P(),
            P(),
            P(),
            P(),
            P(("rows", "heads"), None),
        ),
        out_specs=(
            P(("rows", "heads"), None),
            P(("rows", "heads"), None),
            P(None, "heads"),
            P(None, "heads"),
            P(None, "heads"),
            P("heads"),
            P("heads"),
            P(),
            P(),
            P(),
            P(),
            P(None, ("rows", "heads")),
            P(("rows", "heads")),
            P(("rows", "heads"), None),
            P(),
            P(),
            P(),
        ),
        check_vma=False,
    )
```

```python
import functools

import jax
import jax.numpy as jnp
from jax import lax
from jax.experimental import pallas as pl
from jax.experimental.pallas import tpu as pltpu
from jax.sharding import PartitionSpec as P

HD = 64
PARTS = 8
epsilon = 1e-06
masked_score = -1000000000.0
low_type = jnp.bfloat16
wide_type = jnp.float32
room = pltpu.CompilerParams(vmem_limit_bytes=32 * 1024 * 1024)
large_room = pltpu.CompilerParams(vmem_limit_bytes=60 * 1024 * 1024)


def contract(left, right, left_dim, right_dim):
    return lax.dot_general(
        left, right, (((left_dim,), (right_dim,)), ((), ())), preferred_element_type=wide_type
    )


def dot_nn(left, right):
    return contract(left, right, 1, 0)


def dot_nt(left, right):
    return contract(left, right, 1, 1)


def dot_tn(left, right):
    return contract(left, right, 0, 0)


class Grid:
    def __init__(self, mesh):
        self.rows = mesh.shape["rows"]
        self.heads = mesh.shape["heads"]
        self.native = self.rows == PARTS
        self.steps = self.rows.bit_length() - 2
        up = list(range(1, self.steps + 1))
        self.orders = (up, up[::-1])

    def permute(self, value, row_masks, head_mask=0):
        pairs = [
            (row * self.heads + head, (row ^ row_masks[row & 1]) * self.heads + (head ^ head_mask))
            for row in range(self.rows)
            for head in range(self.heads)
        ]
        return lax.ppermute(value, ("rows", "heads"), pairs)

    def across_core(self, value):
        return self.permute(value, (1, 1))

    def across_heads(self, value, offset):
        return self.permute(value, (0, 0), offset)

    def across_chip(self, value, step):
        return self.permute(value, [1 << order[step] for order in self.orders])

    def across_chips(self, values):
        masks = [self.slot_masks(core) for core in (0, 1)]
        return [
            self.permute(value, (masks[0][slot], masks[1][slot]))
            for slot, value in enumerate(values)
            if slot
        ]

    def slot_masks(self, core):
        last = self.steps - 1
        masks = []
        for slot in range(1 << self.steps):
            mask = 0
            for step in range(self.steps):
                mask |= ((slot >> (last - step)) & 1) << self.orders[core][step]
            masks.append(mask)
        return masks

    def row_slots(self):
        row = lax.axis_index("rows").astype(jnp.int32)
        masks = jnp.array([self.slot_masks(0), self.slot_masks(1)], jnp.int32)
        core = row & 1
        return jnp.concatenate([row ^ masks[core], (row ^ 1) ^ masks[1 - core]])

    def row_places(self):
        row = lax.axis_index("rows").astype(jnp.int32)
        half = self.rows // 2
        inverse = []
        for core in (0, 1):
            table = [0] * half
            for slot, mask in enumerate(self.slot_masks(core)):
                table[mask >> 1] = slot
            inverse.append(table)
        inverse = jnp.array(inverse, jnp.int32)
        apart = jnp.arange(self.rows, dtype=jnp.int32) ^ row
        other = apart & 1
        return other * half + inverse[(row & 1) ^ other, apart >> 1]

    def helper_parts(self):
        row = lax.axis_index("rows").astype(jnp.int32)
        masks = jnp.array([self.slot_masks(0)[:4], self.slot_masks(1)[:4]], jnp.int32)
        core = row & 1
        return jnp.concatenate([row ^ masks[core], (row ^ 1) ^ masks[1 - core]])

    def part_of(self, row):
        if self.native:
            return row
        low, high = sorted(self.orders[0][-2:])
        return (row & 1) + 2 * ((row >> low) & 1) + 4 * ((row >> high) & 1)

    def scatter_wide(self, mine, got):
        held = add_like(mine, got)
        for step in range(self.steps - 2):
            half = held.shape[0] // 2
            held = add_like(held[:half], self.across_chip(held[half:], step))
        return held

    def gather(self, value):
        held = [value] + self.across_chips([value] * 4)
        if self.native:
            return held + [self.across_core(block) for block in held]
        held = jnp.stack(held)
        for step in reversed(range(self.steps - 2)):
            held = jnp.concatenate([held, self.across_chip(held, step)], 0)
        held = jnp.concatenate([held, self.across_core(held)], 0)
        return jnp.take(held, self.row_places(), axis=0)

    def coarse(self, blocks, rows, heads):
        finer = self.rows // PARTS
        blocks = blocks.reshape((PARTS, finer) + blocks.shape[1:])
        cols = blocks.shape[3]
        own = blocks[:, :, :rows].reshape(PARTS, finer, 2, rows // 2, cols).transpose(0, 2, 1, 3, 4)
        wo = blocks[:, :, rows:].reshape(PARTS, finer, heads, -1, cols).transpose(0, 2, 1, 3, 4)
        own, wo = own.reshape(PARTS, -1, cols), wo.reshape(PARTS, -1, cols)
        return [jnp.concatenate([own[part], wo[part]], 0) for part in range(PARTS)]

    def spread_parts(self, near, far):
        if self.native:
            return near, far
        parts = jnp.concatenate([near, far], 0)
        count, rows, cols = parts.shape[1:]
        finer = self.rows // PARTS
        parts = parts.reshape(PARTS, count, finer, rows // finer, cols).transpose(0, 2, 1, 3, 4)
        parts = parts.reshape(self.rows, count, rows // finer, cols)
        parts = jnp.take(parts, self.row_slots(), axis=0)
        return parts[: self.rows // 2], parts[self.rows // 2 :]


def add_like(first, second):
    return (first.astype(wide_type) + second.astype(wide_type)).astype(first.dtype)


def estimate(flops, moved, exps=0):
    return pl.CostEstimate(
        flops=flops, bytes_accessed=moved, transcendentals=exps
    )


def like(shape, dtype=low_type):
    return jax.ShapeDtypeStruct(shape, dtype)


def far(value):
    return pltpu.with_memory_space_constraint(value, pltpu.HBM)


def far_like(shape, dtype=low_type):
    return pltpu.HBM(shape, dtype)


def whole_spec(shape, **options):
    return pl.BlockSpec(shape, lambda *ids: (0,) * len(shape), **options)


anywhere = pl.BlockSpec(memory_space=pl.ANY)


def fold_kernel(plan, passed, head_ref, *refs):
    outs = list(refs[len(refs) - passed - sum(job[2] for job in plan) : len(refs) - passed])
    refs = list(refs)
    for count, kind, given in plan:
        terms, refs = refs[:count], refs[count:]
        targets, outs = outs[:given], outs[given:]
        if kind == "packed":
            rest, wo = terms[:2], terms[2:]
            total = sum(term[...].astype(wide_type) for term in wo).astype(low_type)
            targets[-1][...] = total
            for group, target in enumerate(targets[:-1]):
                value = sum(term[group].astype(wide_type) for term in rest).astype(low_type)
                rows, cols = value.shape[0], value.shape[1] // 2
                target[0:rows] = value[:, :cols]
                target[rows : 2 * rows] = value[:, cols:]
                target[2 * rows :] = total
            continue
        if kind == "final":
            (target,) = targets
            rows, cols = terms[0].shape[0], terms[0].shape[1] // 2
            for half in range(2):
                lanes = slice(half * cols, (half + 1) * cols)
                at = slice(half * rows, (half + 1) * rows)
                value = sum(term[:, lanes].astype(wide_type) for term in terms[:2])
                value = value + sum(term[at].astype(wide_type) for term in terms[3:])
                target[at] = value.astype(low_type)
            small = terms[2].shape[0]
            for offset, term in enumerate(terms[2:]):
                piece = term[...] if offset == 0 else term[2 * rows :]
                target[2 * rows + offset * small : 2 * rows + (offset + 1) * small] = piece
            continue
        for out, target in enumerate(targets):
            total = 0.0
            for term in terms:
                if kind == "halves":
                    size = target.shape[0]
                    value = term[out * size : (out + 1) * size]
                elif kind == "slots":
                    value = term[out]
                elif kind == "heads":
                    rows = target.shape[0]
                    value = term[pl.ds(pl.multiple_of((head_ref[0] ^ out) * rows, 16), rows), :]
                else:
                    value = term[...]
                total = total + value.astype(wide_type)
            target[...] = total.astype(target.dtype)


def fold(grid, head, jobs, deps=(), passes=(), tiles=1):
    if not grid.native:
        return [plain_job(grid, head, *job) for job in jobs], list(passes)
    plan, values, shapes = [], [], []
    for terms, kind in jobs:
        kind = "halves" if kind == "core" else kind
        shape, dtype, given = terms[0].shape, low_type, 1
        if kind == "halves":
            shape, given = (shape[0] // 2,) + shape[1:], 2
        elif kind == "slots":
            shape, given = shape[1:], shape[0]
        elif kind == "heads":
            shape, given = (shape[0] // grid.heads,) + shape[1:], grid.heads
        elif kind == "wide":
            dtype = wide_type
        elif kind == "packed":
            small = terms[2].shape
            shape, given = (2 * shape[1] + small[0], small[1]), shape[0]
        elif kind == "final":
            small = terms[2].shape
            shape = (2 * shape[0] + len(terms[2:]) * small[0], small[1])
        kinds = [far_like(shape, dtype)] * given
        if kind == "packed":
            kinds.append(far_like(small))
        plan.append((len(terms), kind, len(kinds)))
        values += terms
        shapes += kinds

    def spec(shape):
        if tiles == 1:
            return whole_spec(shape)
        cut = len(shape) - 2
        block = shape[:cut] + (shape[cut] // tiles, shape[-1])
        return pl.BlockSpec(block, lambda i, *_: (0,) * cut + (i, 0))

    first, sums = 1 + len(values) + len(deps), len(shapes)
    outs = pl.pallas_call(
        functools.partial(fold_kernel, tuple(plan), len(passes)),
        grid_spec=pltpu.PrefetchScalarGridSpec(
            num_scalar_prefetch=1,
            grid=(tiles,),
            in_specs=[spec(value.shape) for value in values]
            + [anywhere] * (len(deps) + len(passes)),
            out_specs=[spec(shape.shape) for shape in shapes] + [anywhere] * len(passes),
        ),
        out_shape=shapes + [like(value.shape) for value in passes],
        input_output_aliases={first + place: sums + place for place in range(len(passes))},
        compiler_params=room,
        cost_estimate=estimate(0, sum(3 * value.size for value in values)),
    )(head, *[far(value) for value in values], *deps, *passes)
    results, place = [], 0
    for _, _, given in plan:
        results.append(outs[place : place + given])
        place += given
    return results, list(outs[sums:])


def plain_job(grid, head, terms, kind):
    if kind == "core":
        held = grid.scatter_wide(*terms)
        return [held[:2], held[2:]]
    if kind == "packed":
        rest = sum(term.astype(wide_type) for term in terms[:2]).astype(low_type)
        wo = sum(term.astype(wide_type) for term in terms[2:]).astype(low_type)
        cols = rest.shape[2] // 2
        return [jnp.concatenate([group[:, :cols], group[:, cols:], wo], 0) for group in rest] + [wo]
    if kind == "final":
        rows, cols = terms[0].shape[0], terms[0].shape[1] // 2
        total = sum(term.astype(wide_type) for term in terms[:2])
        total = jnp.concatenate([total[:, :cols], total[:, cols:]], 0)
        total = total + sum(term[: 2 * rows].astype(wide_type) for term in terms[3:])
        blocks = [terms[2]] + [term[2 * rows :] for term in terms[3:]]
        return [jnp.concatenate([total.astype(low_type)] + blocks, 0)]
    total = sum(term.astype(wide_type) for term in terms)
    if kind == "wide":
        return [total]
    total = total.astype(low_type)
    if kind == "halves":
        half = total.shape[0] // 2
        return [total[:half], total[half:]]
    if kind == "slots":
        return list(total)
    if kind == "heads":
        total = total.reshape((grid.heads, -1) + total.shape[1:])
        return [total[head[0] ^ offset] for offset in range(grid.heads)]
    return [total]


def join_kernel(count, *refs):
    for slot in range(count):
        refs[-1][slot] = refs[slot][...]


def join(values, deps=()):
    shape = (len(values),) + values[0].shape
    return pl.pallas_call(
        functools.partial(join_kernel, len(values)),
        grid=(1,),
        in_specs=[whole_spec(value.shape) for value in values] + [anywhere] * len(deps),
        out_specs=whole_spec(shape),
        out_shape=like(shape),
        compiler_params=room,
        cost_estimate=estimate(0, 4 * values[0].size),
    )(*values, *deps)


def three_parts(values):
    first = values.astype(low_type).astype(wide_type)
    rest = values - first
    second = rest.astype(low_type).astype(wide_type)
    return first, second, (rest - second).astype(low_type).astype(wide_type)


def pair_up(low_lanes, first, second):
    return jnp.where(low_lanes, first, pltpu.roll(second, HD, 1))


def pack_kernel(index_ref, q_ref, k_ref, v_ref, bias_ref, w_ref, piece_ref):
    rows = piece_ref.shape[0]
    w_ref[0, 0:128, :] = q_ref[0:128, :]
    w_ref[0, 128:256, :] = k_ref[0:128, :]
    w_ref[0, 256:384, :] = v_ref[0:128, :]
    w_ref[0, 384:448, :] = q_ref[128:192, :]
    w_ref[0, 448:512, :] = k_ref[128:192, :]
    w_ref[0, 512:576, :] = v_ref[128:192, :]
    row = lax.broadcasted_iota(jnp.int32, (HD, w_ref.shape[2]), 0)
    w_ref[0, 576:640, :] = jnp.where(row == 0, bias_ref[...], 0.0).astype(low_type)
    mine = pl.multiple_of(index_ref[0] * rows, 16)
    piece_ref[...] = w_ref[0, pl.ds(mine, rows), :]


def pack(part, w_query, w_key, w_value, bias):
    width = w_query.shape[1]
    rows = 640 // PARTS
    return pl.pallas_call(
        pack_kernel,
        grid_spec=pltpu.PrefetchScalarGridSpec(
            num_scalar_prefetch=1,
            grid=(1,),
            in_specs=[whole_spec(w_query.shape)] * 3 + [whole_spec(bias.shape)],
            out_specs=[whole_spec((1, 640, width)), whole_spec((rows, width))],
        ),
        out_shape=[like((1, 640, width)), like((rows, width))],
        compiler_params=room,
        cost_estimate=estimate(0, 4 * width * 640),
    )(part, w_query, w_key, w_value, bias)


def attend_body(x_ref, w_ref, seg_ref, q_ref, k_ref, v_ref, ctx_ref):
    seqs, _, length = seg_ref.shape
    lane = lax.broadcasted_iota(jnp.int32, (1, 128), 1)
    low = lane < HD
    row8 = lax.broadcasted_iota(jnp.int32, (8, length), 0)
    bias_row = w_ref[0, 576:592, :][0:1, 0:640].astype(wide_type)
    for seq in range(seqs):
        at = slice(seq * length, (seq + 1) * length)
        qkv = (dot_nt(x_ref[at, :], w_ref[0]) + bias_row).astype(low_type).astype(wide_type)
        q01 = qkv[:, 0:128] * 0.125
        k01 = qkv[:, 128:256]
        v01 = qkv[:, 256:384]
        qk2 = qkv[:, 384:512]
        queries = [q01, pltpu.roll(q01, HD, 1), qk2 * 0.125]
        keys = [k01, pltpu.roll(k01, HD, 1), pltpu.roll(qk2, HD, 1)]
        values = [v01, pltpu.roll(v01, HD, 1), qkv[:, 512:640]]
        seg_rows = jnp.broadcast_to(seg_ref[seq], (8, length)).astype(wide_type)
        seg_col = seg_rows.T[:, 0:1].astype(jnp.int32) + HD
        same = lane == seg_col
        in_seg = (lane >= HD) & (lane < HD + 4)
        extra_q = jnp.where(same, 1.0, 0.0)
        extra_k = jnp.where(
            in_seg & ~same,
            masked_score,
            jnp.where((lane >= HD + 4) & (lane < HD + 7), 1.0, 0.0),
        )
        extra_v = jnp.where((lane >= HD) & (lane < HD + 3), 1.0, 0.0)
        contexts = []
        for head in range(3):
            query = jnp.where(low, queries[head], extra_q)
            key = jnp.where(low, keys[head], extra_k).astype(low_type)
            value = jnp.where(low, values[head], extra_v).astype(low_type)
            k_ref[0, head, at, :] = key
            v_ref[0, head, at, :] = value
            scores = dot_nt(key, query.astype(low_type))
            highest = jnp.max(scores, 0, keepdims=True)
            weights_low = jnp.exp(scores - highest).astype(low_type)
            summed = dot_tn(value, weights_low)
            total = summed[HD : HD + 1, :]
            first, second, third = three_parts(-(highest + jnp.log(total)))
            extra = jnp.where(
                row8 == 4, first, jnp.where(row8 == 5, second, jnp.where(row8 == 6, third, 0.0))
            )
            full = jnp.concatenate(
                [summed[:HD] * (1.0 / total), extra, jnp.zeros((56, length), wide_type)], 0
            ).T
            q_ref[0, head, at, :] = jnp.where(low, query, full + extra_q).astype(low_type)
            contexts.append(full)
        ctx_ref[0, at, 0:128] = pair_up(low, contexts[0], contexts[1]).astype(low_type)
        ctx_ref[0, at, 128:192] = contexts[2][:, :HD].astype(low_type)


def attend_own_kernel(x_ref, w_ref, seg_ref, q_ref, k_ref, v_ref, ctx_ref):
    attend_body(x_ref, w_ref, seg_ref, q_ref, k_ref, v_ref, ctx_ref)


def attend_rest_kernel(parts_ref, x_ref, seg_ref, *refs):
    pieces, (q_ref, k_ref, v_ref, ctx_ref, w_ref) = refs[:PARTS], refs[PARTS:]
    rows = pieces[0].shape[1]
    for slot in range(PARTS):
        at = pl.ds(pl.multiple_of(parts_ref[slot] * rows, 16), rows)
        w_ref[0, at, :] = pieces[slot][0]
    attend_body(x_ref, w_ref, seg_ref, q_ref, k_ref, v_ref, ctx_ref)


def attend_cost(count, tokens, length, width):
    return estimate(
        count * (2 * tokens * width * 576 + 3 * 4 * tokens * length * 128),
        2 * tokens * width + count * 2 * (576 * width + 10 * tokens * 128),
        count * 3 * tokens * length,
    )


def attend_outputs(count, tokens):
    heads = pl.BlockSpec((1, 3, tokens, 128), lambda g, *_: (g, 0, 0, 0))
    specs = [heads, heads, heads, pl.BlockSpec((1, tokens, 192), lambda g, *_: (g, 0, 0))]
    shapes = [far_like((count, 3, tokens, 128))] * 3 + [like((count, tokens, 192))]
    return specs, shapes


def attend_own(layer_in, shard, segments):
    tokens, width = layer_in.shape
    specs, shapes = attend_outputs(1, tokens)
    return pl.pallas_call(
        attend_own_kernel,
        grid=(1,),
        in_specs=[
            whole_spec((tokens, width)),
            whole_spec(shard.shape),
            whole_spec(segments.shape),
        ],
        out_specs=specs,
        out_shape=shapes,
        compiler_params=room,
        cost_estimate=attend_cost(1, tokens, segments.shape[2], width),
    )(layer_in, shard, segments)


def attend_rest(parts, layer_in, pieces, segments):
    tokens, width = layer_in.shape
    count, rows, width = pieces[0].shape
    specs, shapes = attend_outputs(count, tokens)
    piece = pl.BlockSpec((1, rows, width), lambda g, *_: (g, 0, 0))
    return pl.pallas_call(
        attend_rest_kernel,
        grid_spec=pltpu.PrefetchScalarGridSpec(
            num_scalar_prefetch=1,
            grid=(count,),
            in_specs=[whole_spec((tokens, width)), whole_spec(segments.shape)] + [piece] * PARTS,
            out_specs=specs + [pl.BlockSpec((1, 640, width), lambda g, *_: (g, 0, 0))],
        ),
        out_shape=shapes + [far_like((count, 640, width))],
        compiler_params=room,
        cost_estimate=attend_cost(count, tokens, segments.shape[2], width),
    )(parts, layer_in, segments, *pieces)


def attend_back_kernel(
    length,
    slots_ref,
    x_ref,
    q_ref,
    k_ref,
    v_ref,
    ctx_ref,
    dctx_ref,
    *refs,
):
    dqkv_ref, near_ref, far_ref, held = refs[-4:]
    tokens, width = x_ref.shape
    rows = 640 // PARTS
    lane = lax.broadcasted_iota(jnp.int32, (1, 128), 1)
    low = lane < HD
    for seq in range(tokens // length):
        at = slice(seq * length, (seq + 1) * length)
        grad01 = dctx_ref[0, at, 0:128].astype(wide_type)
        grad2 = dctx_ref[0, at, 128:192].astype(wide_type)
        both = grad01 * ctx_ref[0, at, 0:128].astype(wide_type)
        inner = [
            jnp.sum(jnp.where(low, both, 0.0), -1, keepdims=True),
            jnp.sum(jnp.where(low, 0.0, both), -1, keepdims=True),
            jnp.sum(grad2 * ctx_ref[0, at, 128:192].astype(wide_type), -1, keepdims=True),
        ]
        grads = [
            grad01,
            pltpu.roll(grad01, HD, 1),
            jnp.concatenate([grad2, jnp.zeros((length, HD), wide_type)], 1),
        ]
        grad_q, grad_k, grad_v = [], [], []
        for head in range(3):
            first, second, third = three_parts(-inner[head])
            extra = jnp.where(
                lane == HD,
                first,
                jnp.where(lane == HD + 1, second, jnp.where(lane == HD + 2, third, 0.0)),
            )
            grad = jnp.where(low, grads[head], extra).astype(low_type)
            query = q_ref[0, head, at, :]
            key = k_ref[0, head, at, :]
            probs = jnp.exp(dot_nt(key, query))
            grad_scores = (probs * dot_nt(v_ref[0, head, at, :], grad)).astype(low_type)
            grad_v.append(dot_nn(probs.astype(low_type), grad))
            grad_k.append(dot_nn(grad_scores, query))
            grad_q.append(dot_tn(key, grad_scores).T * 0.125)
        dqkv_ref[0, at, 0:128] = pair_up(low, grad_q[0], grad_q[1]).astype(low_type)
        dqkv_ref[0, at, 128:256] = pair_up(low, grad_k[0], grad_k[1]).astype(low_type)
        dqkv_ref[0, at, 256:384] = pair_up(low, grad_v[0], grad_v[1]).astype(low_type)
        dqkv_ref[0, at, 384:512] = pair_up(low, grad_q[2], grad_k[2]).astype(low_type)
        dqkv_ref[0, at, 512:640] = jnp.where(low, grad_v[2], 0.0).astype(low_type)
    grad_all = dqkv_ref[0]
    total = dot_tn(grad_all, x_ref[...])
    sums = jnp.sum(grad_all.astype(wide_type), 0, keepdims=True)
    sums = jnp.concatenate([sums, jnp.zeros((1, width - 640), wide_type)], 1)
    for part in range(PARTS):
        held[part] = total[part * rows : (part + 1) * rows].astype(low_type)
    row = lax.broadcasted_iota(jnp.int32, (HD, width), 0)
    spare = jnp.where(row == 0, sums, 0.0)
    held[PARTS - 1, rows - HD : rows] = spare.astype(low_type)
    for slot in range(PARTS // 2):
        near_ref[slot, 0] = held[slots_ref[slot]]
        far_ref[slot, 0] = held[slots_ref[slot + PARTS // 2]]


def attend_back(
    slots, layer_in, queries, keys, values, context, grad_context, deps, length
):
    tokens, width = layer_in.shape
    count = context.shape[0]
    rows = 640 // PARTS
    heads = pl.BlockSpec((1, 3, tokens, 128), lambda g, *_: (g, 0, 0, 0))
    group = pl.BlockSpec((1, tokens, 192), lambda g, *_: (g, 0, 0))
    half = pl.BlockSpec((PARTS // 2, 1, rows, width), lambda g, *_: (0, g, 0, 0))
    return pl.pallas_call(
        functools.partial(attend_back_kernel, length),
        grid_spec=pltpu.PrefetchScalarGridSpec(
            num_scalar_prefetch=1,
            grid=(count,),
            in_specs=[whole_spec((tokens, width)), heads, heads, heads, group, group]
            + [anywhere] * len(deps),
            out_specs=[pl.BlockSpec((1, tokens, 640), lambda g, *_: (g, 0, 0)), half, half],
            scratch_shapes=[pltpu.VMEM((PARTS, rows, width), low_type)],
        ),
        out_shape=[
            like((count, tokens, 640)),
            far_like((PARTS // 2, count, rows, width)),
            far_like((PARTS // 2, count, rows, width)),
        ],
        compiler_params=room,
        cost_estimate=estimate(
            count * (2 * tokens * width * 576 + 3 * 10 * tokens * length * 128),
            2 * tokens * width + count * 2 * (576 * width + 16 * tokens * 128),
            count * 3 * tokens * length,
        ),
    )(slots, layer_in, queries, keys, values, context, grad_context, *deps)


def mean_last(values):
    return jnp.mean(values, -1, keepdims=True)


def tiles(tokens, size, body):
    def step(index, carry):
        body(pl.ds(pl.multiple_of(index * size, size), size))
        return carry

    lax.fori_loop(0, tokens // size, step, 0)


def gelu_pair(values):
    cumulative = 0.5 * (1.0 + lax.erf(values * 0.7071067811865476))
    density = jnp.exp(-0.5 * values * values) * 0.3989422804014327
    return values * cumulative, cumulative + values * density


class Loads:
    def __init__(self, slots_ref, w_in_hbm, w_out_hbm, w_in, w_out, sems):
        self.count = sems.shape[1]
        self.size = w_out.shape[0] // self.count
        self.copies = []
        for slot in range(self.count):
            source = pl.ds(pl.multiple_of(slots_ref[slot] * self.size, 128), self.size)
            target = pl.ds(slot * self.size, self.size)
            self.copies.append(
                (
                    pltpu.make_async_copy(w_in_hbm.at[:, source], w_in.at[:, target], sems.at[0, slot]),
                    pltpu.make_async_copy(w_out_hbm.at[source], w_out.at[target], sems.at[1, slot]),
                )
            )

    def start(self):
        for copies in self.copies:
            for copy in copies:
                copy.start()

    def wait(self, low, high):
        for slot in range(-(-low // self.size), -(-high // self.size)):
            for copy in self.copies[slot]:
                copy.wait()


def overlaps(size, chunks, block, blocks):
    return [
        [
            (which, max(chunk * size, which * block), min((chunk + 1) * size, (which + 1) * block))
            for which in range(blocks)
            if max(chunk * size, which * block) < min((chunk + 1) * size, (which + 1) * block)
        ]
        for chunk in range(chunks)
    ]


def forward_kernel(
    chunks,
    slots_ref,
    x_ref,
    own_ref,
    rest_ref,
    wo_ref,
    cot_ref,
    vec_ref,
    b_in_ref,
    w_in_hbm,
    w_out_hbm,
    slope_ref,
    rstd_ref,
    sums_ref,
    low_hbm,
    normal_hbm,
    out_hbm,
    grad_hbm,
    near_hbm,
    far_hbm,
    w_in,
    w_out,
    normed,
    outer,
    active,
    low,
    normal_low,
    result_low,
    grad_out,
    sems,
    out_sems,
):
    step = pl.program_id(0)
    tokens = x_ref.shape[0]
    hidden = w_out.shape[0]
    size = hidden // chunks
    loads = Loads(slots_ref, w_in_hbm, w_out_hbm, w_in, w_out, sems)
    head = slots_ref[loads.count]
    b_output, gain_attn, shift_attn = vec_ref[0:1, :], vec_ref[1:2, :], vec_ref[2:3, :]
    b_outer, gain_ffn, shift_ffn = vec_ref[3:4, :], vec_ref[4:5, :], vec_ref[5:6, :]
    small = [
        pltpu.make_async_copy(source, target, out_sems.at[place])
        for place, (source, target) in enumerate(
            ((low, low_hbm), (normal_low, normal_hbm), (result_low, out_hbm), (grad_out, grad_hbm))
        )
    ]
    half = hidden // 2
    count = len(small)
    grads = []
    for cuts in overlaps(size, chunks, half, 2):
        copies = []
        for which, begin, end in cuts:
            copies.append(
                pltpu.make_async_copy(
                    w_out.at[pl.ds(begin, end - begin)],
                    (near_hbm, far_hbm)[which].at[pl.ds(begin - which * half, end - begin)],
                    out_sems.at[count],
                )
            )
            count += 1
        grads.append(copies)

    @pl.when(step == 0)
    def _():
        loads.start()
        outer[...] = jnp.zeros_like(outer)
        branch = dot_nn(own_ref[0], wo_ref[head])
        for offset in range(1, wo_ref.shape[0]):
            branch += dot_nn(rest_ref[offset - 1], wo_ref[head ^ offset])
        normed[...] = branch

        def one(at):
            total = x_ref[at, :].astype(wide_type) + (normed[at, :] + b_output)
            centred = total - mean_last(total)
            rstd = lax.rsqrt(mean_last(centred * centred) + epsilon)
            normal = centred * rstd
            result = normal * gain_attn + shift_attn
            normed[at, :] = result
            low[at, :] = result.astype(low_type)
            normal_low[at, :] = normal.astype(low_type)
            rstd_ref[at, :] = jnp.broadcast_to(rstd, (rstd.shape[0], 128))

        tiles(tokens, 256, one)
        small[0].start()
        small[1].start()

    for chunk in range(chunks):

        @pl.when(step == chunk)
        def _():
            loads.wait(chunk * size, (chunk + 1) * size)

    @pl.when(step < chunks)
    def _():
        at = pl.ds(pl.multiple_of(step * size, 128), size)
        inner = dot_nn(low[...], w_in[:, at]) + b_in_ref[...]
        values, slope = gelu_pair(inner)
        values = values.astype(low_type)
        active[step] = values
        slope_ref[...] = slope.astype(low_type)
        outer[...] += dot_nn(values, w_out[at, :])

    @pl.when(step == chunks - 1)
    def _():
        sums_ref[...] = jnp.zeros_like(sums_ref)

        def one(at):
            total = normed[at, :] + (outer[at, :] + b_outer)
            centred = total - mean_last(total)
            rstd = lax.rsqrt(mean_last(centred * centred) + epsilon)
            normal = centred * rstd
            result_low[at, :] = (normal * gain_ffn + shift_ffn).astype(low_type)
            grad = cot_ref[at, :].astype(wide_type)
            scaled = grad * gain_ffn
            grad_sum = rstd * (scaled - mean_last(scaled) - normal * mean_last(scaled * normal))
            grad_low = grad_sum.astype(low_type)
            grad_out[at, :] = grad_low
            sums_ref[0:1, :] += jnp.sum(grad * normal, 0, keepdims=True)
            sums_ref[1:2, :] += jnp.sum(grad, 0, keepdims=True)
            sums_ref[2:3, :] += jnp.sum(grad_low.astype(wide_type), 0, keepdims=True)

        tiles(tokens, 256, one)
        small[2].start()
        small[3].start()

    @pl.when(step >= chunks)
    def _():
        which = step - chunks
        at = pl.ds(pl.multiple_of(which * size, 128), size)
        w_out[at, :] = dot_tn(active[which], grad_out[...]).astype(low_type)

    for chunk in range(chunks):

        @pl.when(step == chunks + chunk)
        def _():
            for copy in grads[chunk]:
                copy.start()

    @pl.when(step == 2 * chunks - 1)
    def _():
        for copy in small:
            copy.wait()
        for copies in grads:
            for copy in copies:
                copy.wait()


def forward_ffn(slots, layer_in, ctx_own, ctx_rest, w_output, cotangent, vectors, w_in, w_out, b_in):
    tokens, width = layer_in.shape
    hidden = w_out.shape[0]
    chunks = 3
    blocks = slots.shape[0] - 1
    size = hidden // chunks
    wide_chunk = lambda i, *_: (0, jnp.minimum(i, chunks - 1))
    once = dict(pipeline_mode=pl.Buffered(1))
    return pl.pallas_call(
        functools.partial(forward_kernel, chunks),
        grid_spec=pltpu.PrefetchScalarGridSpec(
            num_scalar_prefetch=1,
            grid=(2 * chunks,),
            in_specs=[
                whole_spec((tokens, width), **once),
                whole_spec(ctx_own.shape, **once),
                whole_spec(ctx_rest.shape, **once),
                whole_spec(w_output.shape, **once),
                whole_spec((tokens, width), **once),
                whole_spec(vectors.shape, **once),
                pl.BlockSpec((1, size), wide_chunk),
                anywhere,
                anywhere,
            ],
            out_specs=[
                pl.BlockSpec((tokens, size), wide_chunk),
                whole_spec((tokens, 128)),
                whole_spec((8, width)),
            ]
            + [anywhere] * 6,
            scratch_shapes=[
                pltpu.VMEM((width, hidden), low_type),
                pltpu.VMEM((hidden, width), low_type),
                pltpu.VMEM((tokens, width), wide_type),
                pltpu.VMEM((tokens, width), wide_type),
                pltpu.VMEM((chunks, tokens, size), low_type),
            ]
            + [pltpu.VMEM((tokens, width), low_type)] * 4
            + [pltpu.SemaphoreType.DMA((2, blocks)), pltpu.SemaphoreType.DMA((4 + 2 * chunks,))],
        ),
        out_shape=[
            far_like((tokens, hidden)),
            like((tokens, 128), wide_type),
            like((8, width), wide_type),
        ]
        + [far_like((tokens, width))] * 4
        + [far_like((hidden // 2, width))] * 2,
        compiler_params=large_room,
        cost_estimate=estimate(
            2 * tokens * width * (3 * hidden + width),
            2 * (tokens * (7 * width + hidden) + 3 * hidden * width),
            tokens * hidden,
        ),
    )(slots, layer_in, ctx_own, ctx_rest, w_output, cotangent, vectors, b_in, far(w_in), far(w_out))


def inner_back_kernel(
    chunks,
    slots_ref,
    grad_ref,
    low_ref,
    slope_ref,
    w_in_hbm,
    w_out_hbm,
    sums_ref,
    total_ref,
    near_hbm,
    far_hbm,
    w_in,
    w_out,
    sems,
    out_sems,
):
    step = pl.program_id(0)
    hidden = w_out.shape[0]
    size = hidden // chunks
    half = hidden // 2
    loads = Loads(slots_ref, w_in_hbm, w_out_hbm, w_in, w_out, sems)
    pieces = []
    for chunk in range(chunks):
        begin, end = chunk * size, (chunk + 1) * size
        cuts = [begin, half, end] if begin < half < end else [begin, end]
        for low, high in zip(cuts, cuts[1:]):
            target, offset = (near_hbm, 0) if high <= half else (far_hbm, half)
            copy = pltpu.make_async_copy(
                w_out.at[pl.ds(low, high - low)],
                target.at[pl.ds(low - offset, high - low)],
                out_sems.at[len(pieces)],
            )
            pieces.append((chunk, copy))

    @pl.when(step == 0)
    def _():
        loads.start()

    for chunk in range(chunks):

        @pl.when(step == chunk)
        def _():
            loads.wait(chunk * size, (chunk + 1) * size)

    at = pl.ds(pl.multiple_of(step * size, 128), size)
    grad_inner = (
        dot_nt(grad_ref[...], w_out[at, :]) * slope_ref[...].astype(wide_type)
    ).astype(low_type)
    sums_ref[...] = jnp.sum(grad_inner.astype(wide_type), 0, keepdims=True)
    w_out[at, :] = dot_tn(grad_inner, low_ref[...]).astype(low_type)
    part = dot_nt(grad_inner, w_in[:, at])

    for chunk in range(chunks):

        @pl.when(step == chunk)
        def _():
            for owner, copy in pieces:
                if owner == chunk:
                    copy.start()

    @pl.when(step == 0)
    def _():
        total_ref[...] = part + grad_ref[...].astype(wide_type)

    @pl.when(step > 0)
    def _():
        total_ref[...] += part

    @pl.when(step == chunks - 1)
    def _():
        for _, copy in pieces:
            copy.wait()


def inner_back(slots, grad_outer, normed_low, slope, w_in, w_out):
    tokens, width = grad_outer.shape
    hidden = w_out.shape[0]
    chunks = 3
    blocks = slots.shape[0] - 1
    size = hidden // chunks
    return pl.pallas_call(
        functools.partial(inner_back_kernel, chunks),
        grid_spec=pltpu.PrefetchScalarGridSpec(
            num_scalar_prefetch=1,
            grid=(chunks,),
            in_specs=[
                whole_spec((tokens, width)),
                whole_spec((tokens, width)),
                pl.BlockSpec((tokens, size), lambda i, *_: (0, i)),
                anywhere,
                anywhere,
            ],
            out_specs=[
                pl.BlockSpec((1, size), lambda i, *_: (0, i)),
                whole_spec((tokens, width)),
                anywhere,
                anywhere,
            ],
            scratch_shapes=[
                pltpu.VMEM((width, hidden), low_type),
                pltpu.VMEM((hidden, width), low_type),
                pltpu.SemaphoreType.DMA((2, blocks)),
                pltpu.SemaphoreType.DMA((2 * chunks,)),
            ],
        ),
        out_shape=[
            like((1, hidden), wide_type),
            like((tokens, width), wide_type),
            far_like((hidden // 2, width)),
            far_like((hidden // 2, width)),
        ],
        compiler_params=large_room,
        cost_estimate=estimate(
            6 * tokens * width * hidden, 2 * (tokens * (4 * width + hidden) + 3 * hidden * width)
        ),
    )(slots, grad_outer, normed_low, far(slope), far(w_in), far(w_out))


def norm_back_kernel(
    index_ref,
    total_ref,
    normal_ref,
    rstd_ref,
    own_ref,
    rest_ref,
    wo_ref,
    vec_ref,
    sums_in_ref,
    gb_ref,
    *refs,
):
    branch_ref, down_ref, drest_ref, near_ref, far_ref, sums, acc, held, table = refs[-9:]
    step = pl.program_id(0)
    size = branch_ref.shape[0]
    head = index_ref[PARTS]
    gain_attn = vec_ref[1:2, :]
    heads = wo_ref.shape[0]
    rows = wo_ref.shape[1] // 4
    cols = wo_ref.shape[2] // 2

    @pl.when(step == 0)
    def _():
        sums[...] = sums_in_ref[...]

    def one(at):
        grad = total_ref[at, :]
        normal = normal_ref[at, :].astype(wide_type)
        scaled = grad * gain_attn
        rstd = rstd_ref[at, 0:1]
        grad_sum = rstd * (scaled - mean_last(scaled) - normal * mean_last(scaled * normal))
        grad_low = grad_sum.astype(low_type)
        branch_ref[at, :] = grad_low
        sums[3:4, :] += jnp.sum(grad * normal, 0, keepdims=True)
        sums[4:5, :] += jnp.sum(grad, 0, keepdims=True)
        sums[5:6, :] += jnp.sum(grad_low.astype(wide_type), 0, keepdims=True)

    tiles(size, 256, one)
    branch = branch_ref[...]
    for offset in range(heads):
        context = own_ref[0] if offset == 0 else rest_ref[offset - 1]
        weights = wo_ref[head ^ offset]
        grad_context = dot_nt(branch, weights).astype(low_type)
        if offset == 0:
            down_ref[0] = grad_context
        else:
            drest_ref[offset - 1] = grad_context
        part = dot_tn(context, branch)

        @pl.when(step == 0)
        def _():
            acc[offset] = part

        @pl.when(step > 0)
        def _():
            acc[offset] += part

    @pl.when(step == pl.num_programs(0) - 1)
    def _():
        table[...] = jnp.zeros_like(table)
        for which in range(6):
            for across in range(2):
                place = 2 * which + across
                table[place : place + 1, :] = sums[
                    which : which + 1, across * cols : (across + 1) * cols
                ]
        for slot in range(PARTS):
            table[pl.ds(12 + index_ref[slot], 1), :] = gb_ref[:, slot * cols : (slot + 1) * cols]
        for offset in range(heads):
            for part in range(PARTS):
                across, below = divmod(part, 4)
                held[part, offset, 0:rows] = acc[
                    offset,
                    below * rows : (below + 1) * rows,
                    across * cols : (across + 1) * cols,
                ].astype(low_type)
                row = table[pl.ds(part * heads + (head ^ offset), 1), :]
                held[part, offset, rows : rows + 16] = jnp.broadcast_to(row, (16, cols)).astype(
                    low_type
                )
        for slot in range(PARTS // 2):
            near_ref[slot] = held[index_ref[slot]]
            far_ref[slot] = held[index_ref[slot + PARTS // 2]]


def norm_back(
    index, total, normal, rstd, ctx_own, ctx_rest, w_output, vectors, sums, gb, deps
):
    tokens, width = total.shape
    heads, group = w_output.shape[:2]
    size = tokens // 2
    tile = pl.BlockSpec((size, width), lambda i, *_: (i, 0))
    own = pl.BlockSpec((1, size, group), lambda i, *_: (0, i, 0))
    rest = pl.BlockSpec((heads - 1, size, group), lambda i, *_: (0, i, 0))
    half = (PARTS // 2, heads, group // 4 + 16, width // 2)
    return pl.pallas_call(
        norm_back_kernel,
        grid_spec=pltpu.PrefetchScalarGridSpec(
            num_scalar_prefetch=1,
            grid=(2,),
            in_specs=[
                tile,
                tile,
                pl.BlockSpec((size, 128), lambda i, *_: (i, 0)),
                own,
                rest,
                whole_spec(w_output.shape),
                whole_spec(vectors.shape),
                whole_spec(sums.shape),
                whole_spec(gb.shape),
            ]
            + [anywhere] * len(deps),
            out_specs=[
                tile,
                own,
                rest,
                whole_spec(half),
                whole_spec(half),
            ],
            scratch_shapes=[
                pltpu.VMEM((8, width), wide_type),
                pltpu.VMEM((heads, group, width), wide_type),
                pltpu.VMEM((PARTS,) + half[1:], low_type),
                pltpu.VMEM((PARTS * heads, width // 2), wide_type),
            ],
        ),
        out_shape=[
            like((tokens, width)),
            like(ctx_own.shape),
            like(ctx_rest.shape),
            far_like(half),
            far_like(half),
        ],
        compiler_params=room,
        cost_estimate=estimate(
            4 * tokens * width * width, 2 * tokens * width * 8 + 6 * width * width
        ),
    )(index, total, normal, rstd, ctx_own, ctx_rest, w_output, vectors, sums, gb, *deps)


def input_kernel(branch_ref, own_ref, shard_ref, rest_ref, weights_ref, *refs):
    total = branch_ref[...].astype(wide_type) + dot_nn(own_ref[0], shard_ref[0])
    for group in range(rest_ref.shape[0]):
        total += dot_nn(rest_ref[group], weights_ref[group])
    refs[-1][...] = total


def input_back(branch, own, shard, rest, weights, deps):
    tokens, width = branch.shape
    size = tokens // 2
    tile = pl.BlockSpec((size, width), lambda i: (i, 0))
    group = lambda value: pl.BlockSpec((value.shape[0], size, 640), lambda i: (0, i, 0))
    return pl.pallas_call(
        input_kernel,
        grid=(2,),
        in_specs=[tile, group(own), whole_spec(shard.shape), group(rest), whole_spec(weights.shape)]
        + [anywhere] * len(deps),
        out_specs=tile,
        out_shape=like((tokens, width), wide_type),
        compiler_params=room,
        cost_estimate=estimate(2 * tokens * width * 640 * 4, 16 * tokens * width),
    )(branch, own, shard, rest, weights, *deps)


def finish_kernel(blocks, heads, index_ref, *refs):
    pieces = refs[:PARTS]
    q_ref, k_ref, v_ref, wo_ref, bq_ref, bv_ref, gb_ref = refs[PARTS : PARTS + 7]
    vectors = refs[PARTS + 7 : PARTS + 13]
    held, back, table = refs[-3:]
    rows, cols = held.shape[1], held.shape[2] // 2
    extra = back.shape[2]
    small = extra - 16
    head, row = index_ref[PARTS], index_ref[PARTS + 1]
    for slot in range(PARTS):
        part = index_ref[slot]
        piece = pieces[slot]
        held[part] = jnp.concatenate([piece[0:rows], piece[rows : 2 * rows]], 1)
        for offset in range(heads):
            begin = 2 * rows + offset * extra
            back[part, offset] = piece[begin : begin + extra]
    whole = held[...].reshape(PARTS * rows, 2 * cols)
    for ref, first, second in ((q_ref, 0, 384), (k_ref, 128, 448), (v_ref, 256, 512)):
        ref[0:128, :] = whole[first : first + 128].astype(wide_type)
        ref[128:192, :] = whole[second : second + HD].astype(wide_type)
    sums = whole[576:592].astype(wide_type)[0:1]
    for ref, first, second in ((bq_ref, 0, 384), (bv_ref, 256, 512)):
        joined = jnp.concatenate([sums[:, first : first + 128], sums[:, second : second + HD]], 1)
        ref[...] = joined.reshape(ref.shape)
    for part in range(PARTS):
        across, down = divmod(part, 4)
        for offset in range(heads):
            other = head ^ offset
            block = back[part, offset].astype(wide_type)
            wo_ref[
                other, down * small : (down + 1) * small, across * cols : (across + 1) * cols
            ] = block[:small]
            table[pl.ds(part * heads + other, 1), :] = block[small : small + 1]
    for which, ref in enumerate(vectors):
        ref[...] = jnp.concatenate(
            [table[2 * which : 2 * which + 1], table[2 * which + 1 : 2 * which + 2]], 1
        ).reshape(ref.shape)
    block = gb_ref.shape[0]
    per_row = cols // block
    place = row * heads + head
    sums = table[pl.ds(12 + place // per_row, 1), :]
    total = jnp.zeros((1, block), wide_type)
    for which in range(per_row):
        total = jnp.where(
            place % per_row == which, sums[:, which * block : (which + 1) * block], total
        )
    gb_ref[...] = total.reshape(gb_ref.shape)
    del blocks


def finish(index, pieces, block, heads):
    rows = 640 // PARTS
    cols = pieces[0].shape[1]
    width, group = 2 * cols, 192
    extra = (pieces[0].shape[0] - 2 * rows) // heads
    shapes = (
        [like((group, width), wide_type)] * 3
        + [like((heads, group, width), wide_type)]
        + [like((group,), wide_type)] * 2
        + [like((block,), wide_type)]
        + [like((width,), wide_type)] * 6
    )
    return pl.pallas_call(
        functools.partial(finish_kernel, block, heads),
        grid_spec=pltpu.PrefetchScalarGridSpec(
            num_scalar_prefetch=1,
            grid=(1,),
            in_specs=[whole_spec(piece.shape) for piece in pieces],
            out_specs=[whole_spec(shape.shape) for shape in shapes],
            scratch_shapes=[
                pltpu.VMEM((PARTS, rows, width), low_type),
                pltpu.VMEM((PARTS, heads, extra, cols), low_type),
                pltpu.VMEM((PARTS * heads, cols), wide_type),
            ],
        ),
        out_shape=shapes,
        compiler_params=room,
        cost_estimate=estimate(0, 16 * width * width),
    )(index, *pieces)


def local(
    grid,
    layer_in,
    segment_ids,
    w_query,
    w_key,
    w_value,
    b_query,
    b_value,
    w_output,
    b_output,
    gain_attn,
    shift_attn,
    w_inner,
    b_inner,
    w_outer,
    b_outer,
    gain_ffn,
    shift_ffn,
    cotangent,
):
    tokens, width = layer_in.shape
    length = segment_ids.shape[1]
    seqs = tokens // length
    group = w_query.shape[1]
    hidden = w_inner.shape[1]
    heads = grid.heads
    row = lax.axis_index("rows")
    head = lax.axis_index("heads")
    segments = lax.dynamic_slice_in_dim(segment_ids, head * seqs, seqs, 0)[:, None, :]

    gap = jnp.zeros((128,), b_query.dtype)
    bias = jnp.concatenate(
        [b_query[:128], gap, b_value[:128], b_query[128:], gap[:HD], b_value[128:], gap, gap[:HD]]
    ).astype(wide_type)[None]
    part = grid.part_of(row.astype(jnp.int32))[None]
    shard, piece = pack(part, w_query.T, w_key.T, w_value.T, bias)
    got = [grid.across_heads(piece, offset) for offset in range(1, heads)]
    q_own, k_own, v_own, ctx_own = attend_own(layer_in, shard, segments)
    held = join(got, (ctx_own,))
    held = [held] + grid.across_chips([held] * 4)
    held = held + [grid.across_core(value) for value in held]
    parts = grid.part_of(grid.helper_parts())

    row_slots = grid.row_slots()
    b_in = jnp.take(b_inner.reshape(grid.rows, -1), row_slots, axis=0, mode="clip").reshape(1, hidden)
    w_in, w_out = w_inner, w_outer
    if not grid.native:
        w_in = jnp.take(w_in.reshape(width, grid.rows, -1), row_slots, axis=1).reshape(width, hidden)
        w_out = jnp.take(w_out.reshape(grid.rows, -1, width), row_slots, axis=0).reshape(hidden, width)
    head_index = head.astype(jnp.int32)[None]
    natural = jnp.arange(PARTS, dtype=jnp.int32)
    index = jnp.concatenate([row_slots if grid.native else natural, head_index])
    w_output_heads = w_output.reshape(heads, group, width)
    vectors = jnp.stack(
        [b_output, gain_attn, shift_attn, b_outer, gain_ffn, shift_ffn, b_output, b_output]
    )

    q_rest, k_rest, v_rest, ctx_rest, w_rest = attend_rest(parts, layer_in, held, segments)
    slope, rstd, sums, normed_low, normal, layer_out, grad_outer, outer_near, outer_far = forward_ffn(
        index, layer_in, ctx_own, ctx_rest, w_output_heads, cotangent, vectors, w_in, w_out, b_in
    )
    slot_shape = (grid.rows // 2, hidden // grid.rows, width)
    outer_got = grid.across_core(outer_far.reshape(slot_shape))
    gb_inner, total, inner_near, inner_far = inner_back(
        index, grad_outer, normed_low, slope, w_in, w_out
    )
    if not grid.native:
        gb_inner = jnp.take(gb_inner.reshape(grid.rows, -1), grid.row_places(), axis=0).reshape(1, hidden)
    folded = functools.partial(fold, grid, head_index)
    first, second = grid.steps - 2, grid.steps - 1

    ((outer, outer_send),), (inner_far,) = folded(
        [([outer_near.reshape(slot_shape), outer_got], "core")], (total,), (inner_far,), 4
    )
    outer_got = grid.across_chip(outer_send, first)
    inner_got = grid.across_core(inner_far.reshape(slot_shape))
    branch, dctx_own, dctx_rest, wo_near, wo_far = norm_back(
        index, total, normal, rstd, ctx_own, ctx_rest, w_output_heads, vectors, sums, gb_inner, (outer_send,)
    )
    wo_near, wo_far = grid.spread_parts(wo_near, wo_far)

    ((inner, inner_send), (outer, outer_send)), (wo_far,) = folded(
        [
            ([inner_near.reshape(slot_shape), inner_got], "core"),
            ([outer, outer_got], "halves"),
        ],
        (branch,),
        (wo_far,),
        4,
    )
    outer_got = grid.across_chip(outer_send, second)
    inner_got = grid.across_chip(inner_send, first)
    wo_got = grid.across_core(wo_far)
    dqkv_rest, rest_near, rest_far = attend_back(
        index, layer_in, q_rest, k_rest, v_rest, ctx_rest, dctx_rest, (inner_send,), length
    )
    rest_near, rest_far = grid.spread_parts(rest_near, rest_far)
    (outer, (inner, inner_send), (wo, wo_send)), (rest_far,) = folded(
        [
            ([outer[0], outer_got[0]], "heads"),
            ([inner, inner_got], "halves"),
            ([wo_near, wo_got], "core"),
        ],
        (dqkv_rest,),
        (rest_far,),
    )
    outer_got = [grid.across_heads(outer[offset], offset) for offset in range(1, heads)]
    inner_got = grid.across_chip(inner_send, second)
    wo_got = grid.across_chip(wo_send, first)
    rest_got = grid.across_core(rest_far)
    dqkv_own, own_near, own_far = attend_back(
        index, layer_in, q_own, k_own, v_own, ctx_own, dctx_own, (wo_send,), length
    )
    own_near, own_far = grid.spread_parts(own_near, own_far)
    ((out_w_outer,), inner, (wo, wo_send), (rest, rest_send)), (own_far,) = folded(
        [
            ([outer[0]] + outer_got, "wide"),
            ([inner[0], inner_got[0]], "heads"),
            ([wo, wo_got], "halves"),
            ([rest_near, rest_got], "core"),
        ],
        (dqkv_own,),
        (own_far,),
    )
    inner_got = [grid.across_heads(inner[offset], offset) for offset in range(1, heads)]
    wo_got = grid.across_chip(wo_send, second)
    rest_got = grid.across_chip(rest_send, first)
    own_got = grid.across_core(own_far)
    input_grad = input_back(branch, dqkv_own, shard, dqkv_rest, w_rest, (rest_send,))
    ((out_w_inner,), wo, (rest, rest_send), (own, own_send)), _ = folded(
        [
            ([inner[0]] + inner_got, "wide"),
            ([wo[0], wo_got[0]], "slots"),
            ([rest, rest_got], "halves"),
            ([own_near, own_got], "core"),
        ],
        (input_grad,),
    )
    wo_got = [grid.across_heads(wo[offset], offset) for offset in range(1, heads)]
    rest_got = grid.across_chip(rest_send, second)
    own_got = grid.across_chip(own_send, first)
    (packed, (own, own_send)), _ = folded(
        [
            ([rest[0], rest_got[0], wo[0]] + wo_got, "packed"),
            ([own, own_got], "halves"),
        ],
    )
    packed_got = [grid.across_heads(packed[offset - 1], offset) for offset in range(1, heads)]
    own_got = grid.across_chip(own_send, second)
    ((final,),), _ = folded([([own[0, 0], own_got[0, 0], packed[-1]] + packed_got, "final")])
    pieces = grid.gather(final)
    if not grid.native:
        pieces = grid.coarse(pieces, 2 * 640 // grid.rows, heads)
    block = hidden // (grid.rows * heads)
    gw_query, gw_key, gw_value, gw_output, gb_query, gb_value, gb_inner, *vector = finish(
        jnp.concatenate([index, row.astype(jnp.int32)[None]]), pieces, block, heads
    )
    return (
        layer_out,
        input_grad,
        gw_query.T,
        gw_key.T,
        gw_value.T,
        gb_query,
        gb_value,
        gw_output.reshape(width, width),
        vector[5],
        vector[3],
        vector[4],
        out_w_inner.T,
        gb_inner,
        out_w_outer,
        vector[2],
        vector[0],
        vector[1],
    )


def solution(mesh):
    grid = Grid(mesh)
    return jax.shard_map(
        lambda *values: local(grid, *values),
        mesh=mesh,
        in_specs=(
            P(("rows", "heads"), None),
            P("rows", None),
            P(None, "heads"),
            P(None, "heads"),
            P(None, "heads"),
            P("heads"),
            P("heads"),
            P(),
            P(),
            P(),
            P(),
            P(),
            P(),
            P(),
            P(),
            P(),
            P(),
            P(("rows", "heads"), None),
        ),
        out_specs=(
            P(("rows", "heads"), None),
            P(("rows", "heads"), None),
            P(None, "heads"),
            P(None, "heads"),
            P(None, "heads"),
            P("heads"),
            P("heads"),
            P(),
            P(),
            P(),
            P(),
            P(None, ("rows", "heads")),
            P(("rows", "heads")),
            P(("rows", "heads"), None),
            P(),
            P(),
            P(),
        ),
        check_vma=False,
    )
```

```python
import functools

import jax
import jax.numpy as jnp
from jax import lax
from jax.experimental import pallas as pl
from jax.experimental.pallas import tpu as pltpu
from jax.sharding import PartitionSpec as P

HD = 64
PARTS = 8
epsilon = 1e-06
masked_score = -1000000000.0
low_type = jnp.bfloat16
wide_type = jnp.float32
room = pltpu.CompilerParams(vmem_limit_bytes=32 * 1024 * 1024)
large_room = pltpu.CompilerParams(vmem_limit_bytes=60 * 1024 * 1024)


def contract(left, right, left_dim, right_dim):
    return lax.dot_general(
        left, right, (((left_dim,), (right_dim,)), ((), ())), preferred_element_type=wide_type
    )


def dot_nn(left, right):
    return contract(left, right, 1, 0)


def dot_nt(left, right):
    return contract(left, right, 1, 1)


def dot_tn(left, right):
    return contract(left, right, 0, 0)


class Grid:
    def __init__(self, mesh):
        self.rows = mesh.shape["rows"]
        self.heads = mesh.shape["heads"]
        self.native = self.rows == PARTS
        self.steps = self.rows.bit_length() - 2
        up = list(range(1, self.steps + 1))
        self.orders = (up, up[::-1])

    def permute(self, value, row_masks, head_mask=0):
        pairs = [
            (row * self.heads + head, (row ^ row_masks[row & 1]) * self.heads + (head ^ head_mask))
            for row in range(self.rows)
            for head in range(self.heads)
        ]
        return lax.ppermute(value, ("rows", "heads"), pairs)

    def across_core(self, value):
        return self.permute(value, (1, 1))

    def across_heads(self, value, offset):
        return self.permute(value, (0, 0), offset)

    def across_chip(self, value, step):
        return self.permute(value, [1 << order[step] for order in self.orders])

    def across_chips(self, values):
        masks = [self.slot_masks(core) for core in (0, 1)]
        return [
            self.permute(value, (masks[0][slot], masks[1][slot]))
            for slot, value in enumerate(values)
            if slot
        ]

    def slot_masks(self, core):
        last = self.steps - 1
        masks = []
        for slot in range(1 << self.steps):
            mask = 0
            for step in range(self.steps):
                mask |= ((slot >> (last - step)) & 1) << self.orders[core][step]
            masks.append(mask)
        return masks

    def row_slots(self):
        row = lax.axis_index("rows").astype(jnp.int32)
        masks = jnp.array([self.slot_masks(0), self.slot_masks(1)], jnp.int32)
        core = row & 1
        return jnp.concatenate([row ^ masks[core], (row ^ 1) ^ masks[1 - core]])

    def row_places(self):
        row = lax.axis_index("rows").astype(jnp.int32)
        half = self.rows // 2
        inverse = []
        for core in (0, 1):
            table = [0] * half
            for slot, mask in enumerate(self.slot_masks(core)):
                table[mask >> 1] = slot
            inverse.append(table)
        inverse = jnp.array(inverse, jnp.int32)
        apart = jnp.arange(self.rows, dtype=jnp.int32) ^ row
        other = apart & 1
        return other * half + inverse[(row & 1) ^ other, apart >> 1]

    def helper_parts(self):
        row = lax.axis_index("rows").astype(jnp.int32)
        masks = jnp.array([self.slot_masks(0)[:4], self.slot_masks(1)[:4]], jnp.int32)
        core = row & 1
        return jnp.concatenate([row ^ masks[core], (row ^ 1) ^ masks[1 - core]])

    def part_of(self, row):
        if self.native:
            return row
        low, high = sorted(self.orders[0][-2:])
        return (row & 1) + 2 * ((row >> low) & 1) + 4 * ((row >> high) & 1)

    def scatter_wide(self, mine, got):
        held = add_like(mine, got)
        for step in range(self.steps - 2):
            half = held.shape[0] // 2
            held = add_like(held[:half], self.across_chip(held[half:], step))
        return held

    def gather_wide(self, value):
        held = jnp.stack([value] + self.across_chips([value] * 4))
        for step in reversed(range(self.steps - 2)):
            held = jnp.concatenate([held, self.across_chip(held, step)], 0)
        held = jnp.concatenate([held, self.across_core(held)], 0)
        return jnp.take(held, self.row_places(), axis=0)

    def coarse(self, blocks):
        half = blocks.shape[3] // 2
        blocks = jnp.concatenate([blocks[..., :half], blocks[..., half:]], 2)
        blocks = blocks.reshape((PARTS, -1) + blocks.shape[1:]).transpose(0, 2, 1, 3, 4)
        blocks = blocks.reshape(PARTS, blocks.shape[1], -1, half)
        middle = blocks.shape[2] // 2
        return jnp.concatenate([blocks[:, :, :middle], blocks[:, :, middle:]], 3)

    def spread_parts(self, near, far, paired=False):
        if self.native:
            return near, far
        parts = jnp.concatenate([near, far], 0)
        if paired:
            half = parts.shape[3] // 2
            parts = jnp.concatenate([parts[..., :half], parts[..., half:]], 2)
        count, rows, cols = parts.shape[1:]
        finer = self.rows // PARTS
        parts = parts.reshape(PARTS, count, finer, rows // finer, cols).transpose(0, 2, 1, 3, 4)
        parts = parts.reshape(self.rows, count, rows // finer, cols)
        parts = jnp.take(parts, self.row_slots(), axis=0)
        if paired:
            half = parts.shape[2] // 2
            parts = jnp.concatenate([parts[:, :, :half], parts[:, :, half:]], 3)
        return parts[: self.rows // 2], parts[self.rows // 2 :]


def add_like(first, second):
    return (first.astype(wide_type) + second.astype(wide_type)).astype(first.dtype)


def estimate(flops, moved, exps=0):
    return pl.CostEstimate(
        flops=flops, bytes_accessed=moved, transcendentals=exps
    )


def like(shape, dtype=low_type):
    return jax.ShapeDtypeStruct(shape, dtype)


def far(value):
    return pltpu.with_memory_space_constraint(value, pltpu.HBM)


def far_like(shape, dtype=low_type):
    return pltpu.HBM(shape, dtype)


def whole_spec(shape, **options):
    return pl.BlockSpec(shape, lambda *ids: (0,) * len(shape), **options)


anywhere = pl.BlockSpec(memory_space=pl.ANY)


def total_of(terms, cut):
    return sum(cut(term).astype(wide_type) for term in terms)


def fold_kernel(plan, passed, head_ref, *refs):
    inputs, outputs = sum(job[0] for job in plan), sum(job[2] for job in plan)
    scratch = refs[len(refs) - inputs - outputs - 2 : len(refs) - 2]
    in_sems, out_sems = refs[-2:]
    given = len(refs) - len(scratch) - 2 - passed - outputs
    sources, targets = refs[:inputs], refs[given : given + outputs]

    def copies(source, target, sems, which):
        if len(source.shape) < 3:
            return [pltpu.make_async_copy(source, target, sems.at[which, 0])]
        return [
            pltpu.make_async_copy(source.at[slot], target.at[slot], sems.at[which, slot])
            for slot in range(source.shape[0])
        ]

    arrivals = [
        copies(source, scratch[which], in_sems, which) for which, source in enumerate(sources)
    ]
    leaves = [
        copies(scratch[inputs + which], target, out_sems, which)
        for which, target in enumerate(targets)
    ]
    order = []
    place = out_place = 0
    for count, kind, made in plan:
        mine = range(place, place + count)
        outs = range(out_place, out_place + made)
        place, out_place = place + count, out_place + made
        if kind == "halves":
            size = sources[mine[0]].shape[0] // 2
            pairs = [(out, slot) for out in reversed(range(2)) for slot in range(size)]
            order += [("slot", mine, outs[out], slot, out * size + slot) for out, slot in pairs]
        elif kind == "slots":
            order += [("whole", mine, outs[out], None, out) for out in range(made)]
        else:
            order.append((kind, mine, outs, None, None))
    for kind, mine, out, slot, source in order:
        for which in mine:
            for copy in arrivals[which] if source is None else [arrivals[which][source]]:
                copy.start()
    for kind, mine, out, slot, source in order:
        terms = [scratch[which] for which in mine]
        for which in mine:
            for copy in arrivals[which] if source is None else [arrivals[which][source]]:
                copy.wait()
        if kind == "slot":
            target = scratch[inputs + out]
            target[slot] = total_of(terms, lambda term: term[source]).astype(target.dtype)
            leaves[out][slot].start()
            continue
        if kind == "whole":
            target = scratch[inputs + out]
            target[...] = total_of(terms, lambda term: term[source]).astype(target.dtype)
            for copy in leaves[out]:
                copy.start()
            continue
        made = [scratch[inputs + which] for which in out]
        if kind == "heads" or kind == "zpack":
            cut = terms if kind == "heads" else terms[:2]
            for offset, target in enumerate(made):
                rows = terms[0].shape[0] // len(made)
                at = pl.ds(pl.multiple_of((head_ref[0] ^ offset) * rows, 16), rows)
                target[0:rows] = total_of(cut, lambda term: term[at, :]).astype(target.dtype)
                if kind == "zpack":
                    target[rows:] = total_of(terms[2:], lambda term: term[offset]).astype(target.dtype)
        elif kind == "zsplit":
            rows = made[0].shape[0]
            made[0][...] = total_of(terms, lambda term: term[0:rows])
            made[1][...] = total_of(terms, lambda term: term[rows:]).astype(low_type)
        elif kind == "stack":
            for place, term in enumerate(terms):
                made[0][place] = term[...]
        else:
            made[0][...] = total_of(terms, lambda term: term[...]).astype(made[0].dtype)
        for which in out:
            for copy in leaves[which]:
                copy.start()
    for copies_out in leaves:
        for copy in copies_out:
            copy.wait()


def fold(grid, head, jobs, deps=(), passes=()):
    if not grid.native:
        return [plain_job(grid, head, *job) for job in jobs], list(passes)
    plan, values, shapes = [], [], []
    for terms, kind in jobs:
        kind = {"core": "halves", "spread": "slots"}.get(kind, kind)
        shape = terms[0].shape
        if kind == "halves":
            made = [like((shape[0] // 2,) + shape[1:])] * 2
        elif kind == "slots":
            made = [like(shape[1:])] * shape[0]
        elif kind == "heads":
            made = [like((shape[0] // grid.heads, shape[1]))] * grid.heads
        elif kind == "zpack":
            rows = shape[0] // grid.heads + terms[2].shape[1]
            made = [like((rows, shape[1]))] * grid.heads
        elif kind == "zsplit":
            rows = shape[0] * 3 // 4
            made = [like((rows, shape[1]), wide_type), like((shape[0] - rows, shape[1]))]
        elif kind == "stack":
            made = [like((len(terms),) + shape)]
        else:
            made = [like(shape, wide_type if kind == "wide" else low_type)]
        plan.append((len(terms), kind, len(made)))
        values += terms
        shapes += made
    first, sums = 1 + len(values) + len(deps), len(shapes)
    slots = lambda arrays: max(array.shape[0] if len(array.shape) > 2 else 1 for array in arrays)
    outs = pl.pallas_call(
        functools.partial(fold_kernel, tuple(plan), len(passes)),
        grid_spec=pltpu.PrefetchScalarGridSpec(
            num_scalar_prefetch=1,
            grid=(1,),
            in_specs=[anywhere] * (len(values) + len(deps) + len(passes)),
            out_specs=[anywhere] * (len(shapes) + len(passes)),
            scratch_shapes=[pltpu.VMEM(value.shape, value.dtype) for value in values]
            + [pltpu.VMEM(shape.shape, shape.dtype) for shape in shapes]
            + [
                pltpu.SemaphoreType.DMA((len(values), slots(values))),
                pltpu.SemaphoreType.DMA((len(shapes), slots(shapes))),
            ],
        ),
        out_shape=shapes + [far_like(value.shape) for value in passes],
        input_output_aliases={first + place: sums + place for place in range(len(passes))},
        compiler_params=room,
        cost_estimate=estimate(0, sum(3 * value.size for value in values)),
    )(head, *values, *[far(dep) for dep in deps], *[far(value) for value in passes])
    results, place = [], 0
    for _, _, given in plan:
        results.append(outs[place : place + given])
        place += given
    return results, list(outs[sums:])


def plain_job(grid, head, terms, kind):
    whole = lambda term: term
    if kind in ("core", "spread"):
        held = grid.scatter_wide(*terms)
        return [held[:2], held[2:]] if kind == "core" else list(held)
    if kind == "stack":
        return [jnp.stack(terms)]
    if kind == "zsplit":
        rows = terms[0].shape[0] * 3 // 4
        total = total_of(terms, whole)
        return [total[:rows], total[rows:].astype(low_type)]
    if kind in ("heads", "zpack"):
        total = total_of(terms if kind == "heads" else terms[:2], whole).astype(low_type)
        total = total.reshape((grid.heads, -1) + total.shape[1:])
        made = [total[head[0] ^ offset] for offset in range(grid.heads)]
        if kind == "heads":
            return made
        wo = total_of(terms[2:], whole).astype(low_type)
        return [jnp.concatenate([made[offset], wo[offset]], 0) for offset in range(grid.heads)]
    total = total_of(terms, whole)
    if kind == "wide":
        return [total]
    total = total.astype(low_type)
    if kind == "halves":
        half = total.shape[0] // 2
        return [total[:half], total[half:]]
    return list(total) if kind == "slots" else [total]


def join_kernel(count, *refs):
    for slot in range(count):
        refs[-1][slot] = refs[slot][...]


def join(values, deps=()):
    shape = (len(values),) + values[0].shape
    return pl.pallas_call(
        functools.partial(join_kernel, len(values)),
        grid=(1,),
        in_specs=[whole_spec(value.shape) for value in values] + [anywhere] * len(deps),
        out_specs=whole_spec(shape),
        out_shape=far_like(shape),
        compiler_params=room,
        cost_estimate=estimate(0, 4 * values[0].size),
    )(*values, *[far(dep) for dep in deps])


def three_parts(values):
    first = values.astype(low_type).astype(wide_type)
    rest = values - first
    second = rest.astype(low_type).astype(wide_type)
    return first, second, (rest - second).astype(low_type).astype(wide_type)


def pair_up(low_lanes, first, second):
    return jnp.where(low_lanes, first, pltpu.roll(second, HD, 1))


def pack_kernel(index_ref, q_ref, k_ref, v_ref, bias_ref, w_ref, piece_ref):
    rows = piece_ref.shape[0]
    w_ref[0, 0:128, :] = q_ref[0:128, :]
    w_ref[0, 128:256, :] = k_ref[0:128, :]
    w_ref[0, 256:384, :] = v_ref[0:128, :]
    w_ref[0, 384:448, :] = q_ref[128:192, :]
    w_ref[0, 448:512, :] = k_ref[128:192, :]
    w_ref[0, 512:576, :] = v_ref[128:192, :]
    row = lax.broadcasted_iota(jnp.int32, (HD, w_ref.shape[2]), 0)
    w_ref[0, 576:640, :] = jnp.where(row == 0, bias_ref[...], 0.0).astype(low_type)
    mine = pl.multiple_of(index_ref[0] * rows, 16)
    piece_ref[...] = w_ref[0, pl.ds(mine, rows), :]


def pack(part, w_query, w_key, w_value, bias):
    width = w_query.shape[1]
    rows = 640 // PARTS
    return pl.pallas_call(
        pack_kernel,
        grid_spec=pltpu.PrefetchScalarGridSpec(
            num_scalar_prefetch=1,
            grid=(1,),
            in_specs=[whole_spec(w_query.shape)] * 3 + [whole_spec(bias.shape)],
            out_specs=[whole_spec((1, 640, width)), whole_spec((rows, width))],
        ),
        out_shape=[far_like((1, 640, width)), far_like((rows, width))],
        compiler_params=room,
        cost_estimate=estimate(0, 4 * width * 640),
    )(part, far(w_query), far(w_key), far(w_value), bias)


def attend_body(x_ref, w_ref, seg_ref, q_ref, k_ref, v_ref, ctx_ref):
    seqs, _, length = seg_ref.shape
    lane = lax.broadcasted_iota(jnp.int32, (1, 128), 1)
    low = lane < HD
    row8 = lax.broadcasted_iota(jnp.int32, (8, length), 0)
    bias_row = w_ref[0, 576:592, :][0:1, 0:640].astype(wide_type)
    for seq in range(seqs):
        at = slice(seq * length, (seq + 1) * length)
        qkv = (dot_nt(x_ref[at, :], w_ref[0]) + bias_row).astype(low_type).astype(wide_type)
        q01 = qkv[:, 0:128] * 0.125
        k01 = qkv[:, 128:256]
        v01 = qkv[:, 256:384]
        qk2 = qkv[:, 384:512]
        queries = [q01, pltpu.roll(q01, HD, 1), qk2 * 0.125]
        keys = [k01, pltpu.roll(k01, HD, 1), pltpu.roll(qk2, HD, 1)]
        values = [v01, pltpu.roll(v01, HD, 1), qkv[:, 512:640]]
        seg_rows = jnp.broadcast_to(seg_ref[seq], (8, length)).astype(wide_type)
        seg_col = seg_rows.T[:, 0:1].astype(jnp.int32) + HD
        same = lane == seg_col
        in_seg = (lane >= HD) & (lane < HD + 4)
        extra_q = jnp.where(same, 1.0, 0.0)
        extra_k = jnp.where(
            in_seg & ~same,
            masked_score,
            jnp.where((lane >= HD + 4) & (lane < HD + 7), 1.0, 0.0),
        )
        extra_v = jnp.where((lane >= HD) & (lane < HD + 3), 1.0, 0.0)
        contexts = []
        for head in range(3):
            query = jnp.where(low, queries[head], extra_q)
            key = jnp.where(low, keys[head], extra_k).astype(low_type)
            value = jnp.where(low, values[head], extra_v).astype(low_type)
            k_ref[0, head, at, :] = key
            v_ref[0, head, at, :] = value
            scores = dot_nt(key, query.astype(low_type))
            highest = jnp.max(scores, 0, keepdims=True)
            weights_low = jnp.exp(scores - highest).astype(low_type)
            summed = dot_tn(value, weights_low)
            total = summed[HD : HD + 1, :]
            first, second, third = three_parts(-(highest + jnp.log(total)))
            extra = jnp.where(
                row8 == 4, first, jnp.where(row8 == 5, second, jnp.where(row8 == 6, third, 0.0))
            )
            full = jnp.concatenate(
                [summed[:HD] * (1.0 / total), extra, jnp.zeros((56, length), wide_type)], 0
            ).T
            q_ref[0, head, at, :] = jnp.where(low, query, full + extra_q).astype(low_type)
            contexts.append(full)
        ctx_ref[0, at, 0:128] = pair_up(low, contexts[0], contexts[1]).astype(low_type)
        ctx_ref[0, at, 128:192] = contexts[2][:, :HD].astype(low_type)


def attend_own_kernel(x_ref, w_ref, seg_ref, q_ref, k_ref, v_ref, ctx_ref):
    attend_body(x_ref, w_ref, seg_ref, q_ref, k_ref, v_ref, ctx_ref)


def attend_rest_kernel(parts_ref, x_ref, seg_ref, *refs):
    pieces, (q_ref, k_ref, v_ref, ctx_ref, w_ref) = refs[:PARTS], refs[PARTS:]
    rows = pieces[0].shape[1]
    for slot in range(PARTS):
        at = pl.ds(pl.multiple_of(parts_ref[slot] * rows, 16), rows)
        w_ref[0, at, :] = pieces[slot][0]
    attend_body(x_ref, w_ref, seg_ref, q_ref, k_ref, v_ref, ctx_ref)


def attend_cost(count, tokens, length, width):
    return estimate(
        count * (2 * tokens * width * 576 + 3 * 4 * tokens * length * 128),
        2 * tokens * width + count * 2 * (576 * width + 10 * tokens * 128),
        count * 3 * tokens * length,
    )


def attend_outputs(count, tokens):
    heads = pl.BlockSpec((1, 3, tokens, 128), lambda g, *_: (g, 0, 0, 0))
    specs = [heads, heads, heads, pl.BlockSpec((1, tokens, 192), lambda g, *_: (g, 0, 0))]
    shapes = [far_like((count, 3, tokens, 128))] * 3 + [like((count, tokens, 192))]
    return specs, shapes


def attend_own(layer_in, shard, segments):
    tokens, width = layer_in.shape
    specs, shapes = attend_outputs(1, tokens)
    return pl.pallas_call(
        attend_own_kernel,
        grid=(1,),
        in_specs=[
            whole_spec((tokens, width)),
            whole_spec(shard.shape),
            whole_spec(segments.shape),
        ],
        out_specs=specs,
        out_shape=shapes,
        compiler_params=room,
        cost_estimate=attend_cost(1, tokens, segments.shape[2], width),
    )(far(layer_in), far(shard), segments)


def attend_rest(parts, layer_in, pieces, segments):
    tokens, width = layer_in.shape
    count, rows, width = pieces[0].shape
    specs, shapes = attend_outputs(count, tokens)
    piece = pl.BlockSpec((1, rows, width), lambda g, *_: (g, 0, 0))
    return pl.pallas_call(
        attend_rest_kernel,
        grid_spec=pltpu.PrefetchScalarGridSpec(
            num_scalar_prefetch=1,
            grid=(count,),
            in_specs=[whole_spec((tokens, width)), whole_spec(segments.shape)] + [piece] * PARTS,
            out_specs=specs + [pl.BlockSpec((1, 640, width), lambda g, *_: (g, 0, 0))],
        ),
        out_shape=shapes + [far_like((count, 640, width))],
        compiler_params=room,
        cost_estimate=attend_cost(count, tokens, segments.shape[2], width),
    )(parts, far(layer_in), segments, *pieces)


def attend_back_kernel(
    length,
    slots_ref,
    x_ref,
    q_ref,
    k_ref,
    v_ref,
    ctx_ref,
    dctx_ref,
    *refs,
):
    dqkv_ref, near_ref, far_ref, held = refs[-4:]
    tokens, width = x_ref.shape
    rows = 640 // PARTS
    lane = lax.broadcasted_iota(jnp.int32, (1, 128), 1)
    low = lane < HD
    for seq in range(tokens // length):
        at = slice(seq * length, (seq + 1) * length)
        grad01 = dctx_ref[0, at, 0:128].astype(wide_type)
        grad2 = dctx_ref[0, at, 128:192].astype(wide_type)
        both = grad01 * ctx_ref[0, at, 0:128].astype(wide_type)
        inner = [
            jnp.sum(jnp.where(low, both, 0.0), -1, keepdims=True),
            jnp.sum(jnp.where(low, 0.0, both), -1, keepdims=True),
            jnp.sum(grad2 * ctx_ref[0, at, 128:192].astype(wide_type), -1, keepdims=True),
        ]
        grads = [
            grad01,
            pltpu.roll(grad01, HD, 1),
            jnp.concatenate([grad2, jnp.zeros((length, HD), wide_type)], 1),
        ]
        grad_q, grad_k, grad_v = [], [], []
        for head in range(3):
            first, second, third = three_parts(-inner[head])
            extra = jnp.where(
                lane == HD,
                first,
                jnp.where(lane == HD + 1, second, jnp.where(lane == HD + 2, third, 0.0)),
            )
            grad = jnp.where(low, grads[head], extra).astype(low_type)
            query = q_ref[0, head, at, :]
            key = k_ref[0, head, at, :]
            probs = jnp.exp(dot_nt(key, query))
            grad_scores = (probs * dot_nt(v_ref[0, head, at, :], grad)).astype(low_type)
            grad_v.append(dot_nn(probs.astype(low_type), grad))
            grad_k.append(dot_nn(grad_scores, query))
            grad_q.append(dot_tn(key, grad_scores).T * 0.125)
        dqkv_ref[0, at, 0:128] = pair_up(low, grad_q[0], grad_q[1]).astype(low_type)
        dqkv_ref[0, at, 128:256] = pair_up(low, grad_k[0], grad_k[1]).astype(low_type)
        dqkv_ref[0, at, 256:384] = pair_up(low, grad_v[0], grad_v[1]).astype(low_type)
        dqkv_ref[0, at, 384:512] = pair_up(low, grad_q[2], grad_k[2]).astype(low_type)
        dqkv_ref[0, at, 512:640] = jnp.where(low, grad_v[2], 0.0).astype(low_type)
    grad_all = dqkv_ref[0]
    total = dot_tn(grad_all, x_ref[...])
    sums = jnp.sum(grad_all.astype(wide_type), 0, keepdims=True)
    sums = jnp.concatenate([sums, jnp.zeros((1, width - 640), wide_type)], 1)
    for part in range(PARTS):
        held[part] = total[part * rows : (part + 1) * rows].astype(low_type)
    row = lax.broadcasted_iota(jnp.int32, (HD, width), 0)
    spare = jnp.where(row == 0, sums, 0.0)
    held[PARTS - 1, rows - HD : rows] = spare.astype(low_type)
    for slot in range(PARTS // 2):
        near_ref[slot, 0] = held[slots_ref[slot]]
        far_ref[slot, 0] = held[slots_ref[slot + PARTS // 2]]


def attend_back(
    slots, layer_in, queries, keys, values, context, grad_context, deps, length
):
    tokens, width = layer_in.shape
    count = context.shape[0]
    rows = 640 // PARTS
    heads = pl.BlockSpec((1, 3, tokens, 128), lambda g, *_: (g, 0, 0, 0))
    group = pl.BlockSpec((1, tokens, 192), lambda g, *_: (g, 0, 0))
    half = pl.BlockSpec((PARTS // 2, 1, rows, width), lambda g, *_: (0, g, 0, 0))
    return pl.pallas_call(
        functools.partial(attend_back_kernel, length),
        grid_spec=pltpu.PrefetchScalarGridSpec(
            num_scalar_prefetch=1,
            grid=(count,),
            in_specs=[whole_spec((tokens, width)), heads, heads, heads, group, group]
            + [anywhere] * len(deps),
            out_specs=[pl.BlockSpec((1, tokens, 640), lambda g, *_: (g, 0, 0)), half, half],
            scratch_shapes=[pltpu.VMEM((PARTS, rows, width), low_type)],
        ),
        out_shape=[
            like((count, tokens, 640)),
            far_like((PARTS // 2, count, rows, width)),
            far_like((PARTS // 2, count, rows, width)),
        ],
        compiler_params=room,
        cost_estimate=estimate(
            count * (2 * tokens * width * 576 + 3 * 10 * tokens * length * 128),
            2 * tokens * width + count * 2 * (576 * width + 16 * tokens * 128),
            count * 3 * tokens * length,
        ),
    )(slots, far(layer_in), queries, keys, values, context, grad_context, *[far(dep) for dep in deps])


def mean_last(values):
    return jnp.mean(values, -1, keepdims=True)


def tiles(tokens, size, body):
    def step(index, carry):
        body(pl.ds(pl.multiple_of(index * size, size), size))
        return carry

    lax.fori_loop(0, tokens // size, step, 0)


def gelu_pair(values):
    cumulative = 0.5 * (1.0 + lax.erf(values * 0.7071067811865476))
    density = jnp.exp(-0.5 * values * values) * 0.3989422804014327
    return values * cumulative, cumulative + values * density


class Loads:
    def __init__(self, slots_ref, w_in_hbm, w_out_hbm, w_in, w_out, sems):
        self.count = sems.shape[1]
        self.size = w_out.shape[0] // self.count
        self.copies = []
        for slot in range(self.count):
            source = pl.ds(pl.multiple_of(slots_ref[slot] * self.size, 128), self.size)
            target = pl.ds(slot * self.size, self.size)
            self.copies.append(
                (
                    pltpu.make_async_copy(w_in_hbm.at[:, source], w_in.at[:, target], sems.at[0, slot]),
                    pltpu.make_async_copy(w_out_hbm.at[source], w_out.at[target], sems.at[1, slot]),
                )
            )

    def start(self):
        for copies in self.copies:
            for copy in copies:
                copy.start()

    def wait(self, low, high):
        for slot in range(-(-low // self.size), -(-high // self.size)):
            for copy in self.copies[slot]:
                copy.wait()


def overlaps(size, chunks, block, blocks):
    return [
        [
            (which, max(chunk * size, which * block), min((chunk + 1) * size, (which + 1) * block))
            for which in range(blocks)
            if max(chunk * size, which * block) < min((chunk + 1) * size, (which + 1) * block)
        ]
        for chunk in range(chunks)
    ]


def ffn_kernel(
    chunks,
    slots_ref,
    x_ref,
    own_ref,
    rest_ref,
    wo_ref,
    cot_ref,
    vec_ref,
    b_in_ref,
    w_in_hbm,
    w_out_hbm,
    rstd_ref,
    sums_ref,
    gb_ref,
    normal_hbm,
    out_hbm,
    total_hbm,
    outer_near_hbm,
    outer_far_hbm,
    near_hbm,
    far_hbm,
    w_in,
    w_out,
    normed,
    outer,
    active,
    slope,
    low,
    normal_low,
    result_low,
    grad_out,
    sems,
    out_sems,
):
    step = pl.program_id(0)
    tokens, width = x_ref.shape
    hidden = w_out.shape[0]
    size = hidden // chunks
    half = hidden // 2
    loads = Loads(slots_ref, w_in_hbm, w_out_hbm, w_in, w_out, sems)
    head = slots_ref[loads.count]
    b_output, gain_attn, shift_attn = vec_ref[0:1, :], vec_ref[1:2, :], vec_ref[2:3, :]
    b_outer, gain_ffn, shift_ffn = vec_ref[3:4, :], vec_ref[4:5, :], vec_ref[5:6, :]
    small = [
        pltpu.make_async_copy(source, target, out_sems.at[place])
        for place, (source, target) in enumerate(
            ((normal_low, normal_hbm), (result_low, out_hbm), (outer, total_hbm))
        )
    ]
    count = len(small)
    outer_copies, inner_copies = [], []
    for chunk, cuts in enumerate(overlaps(size, chunks, half, 2)):
        from_active, from_out = [], []
        for which, begin, end in cuts:
            at = pl.ds(begin - which * half, end - begin)
            from_active.append(
                pltpu.make_async_copy(
                    active.at[chunk, pl.ds(begin - chunk * size, end - begin), pl.ds(0, width)],
                    (outer_near_hbm, outer_far_hbm)[which].at[at],
                    out_sems.at[count],
                )
            )
            from_out.append(
                pltpu.make_async_copy(
                    w_out.at[pl.ds(begin, end - begin)],
                    (near_hbm, far_hbm)[which].at[at],
                    out_sems.at[count + 1],
                )
            )
            count += 2
        outer_copies.append(from_active)
        inner_copies.append(from_out)

    @pl.when(step == 0)
    def _():
        loads.start()
        outer[...] = jnp.zeros_like(outer)
        branch = dot_nn(own_ref[0], wo_ref[head])
        for offset in range(1, wo_ref.shape[0]):
            branch += dot_nn(rest_ref[offset - 1], wo_ref[head ^ offset])
        normed[...] = branch

        def one(at):
            total = x_ref[at, :].astype(wide_type) + (normed[at, :] + b_output)
            centred = total - mean_last(total)
            rstd = lax.rsqrt(mean_last(centred * centred) + epsilon)
            normal = centred * rstd
            result = normal * gain_attn + shift_attn
            normed[at, :] = result
            low[at, :] = result.astype(low_type)
            normal_low[at, :] = normal.astype(low_type)
            rstd_ref[at, :] = jnp.broadcast_to(rstd, (rstd.shape[0], 128))

        tiles(tokens, 256, one)
        small[0].start()

    for chunk in range(chunks):

        @pl.when(step == chunk)
        def _():
            loads.wait(chunk * size, (chunk + 1) * size)

    @pl.when(step < chunks)
    def _():
        at = pl.ds(pl.multiple_of(step * size, 128), size)
        inner = dot_nn(low[...], w_in[:, at]) + b_in_ref[...]
        values, gradient = gelu_pair(inner)
        values = values.astype(low_type)
        active[step] = values
        slope[step] = gradient.astype(low_type)
        outer[...] += dot_nn(values, w_out[at, :])

    @pl.when(step == chunks - 1)
    def _():
        sums_ref[...] = jnp.zeros_like(sums_ref)

        def one(at):
            total = normed[at, :] + (outer[at, :] + b_outer)
            centred = total - mean_last(total)
            rstd = lax.rsqrt(mean_last(centred * centred) + epsilon)
            normal = centred * rstd
            result_low[at, :] = (normal * gain_ffn + shift_ffn).astype(low_type)
            grad = cot_ref[at, :].astype(wide_type)
            scaled = grad * gain_ffn
            grad_sum = rstd * (scaled - mean_last(scaled) - normal * mean_last(scaled * normal))
            grad_low = grad_sum.astype(low_type)
            grad_out[at, :] = grad_low
            outer[at, :] = grad_low.astype(wide_type)
            sums_ref[0:1, :] += jnp.sum(grad * normal, 0, keepdims=True)
            sums_ref[1:2, :] += jnp.sum(grad, 0, keepdims=True)
            sums_ref[2:3, :] += jnp.sum(grad_low.astype(wide_type), 0, keepdims=True)

        tiles(tokens, 256, one)
        small[1].start()

    @pl.when(step >= chunks)
    def _():
        which = step - chunks
        at = pl.ds(pl.multiple_of(which * size, 128), size)
        grad = grad_out[...]
        active[which, :, 0:width] = dot_tn(active[which], grad).astype(low_type)
        grad_inner = (dot_nt(grad, w_out[at, :]) * slope[which].astype(wide_type)).astype(low_type)
        gb_ref[...] = jnp.sum(grad_inner.astype(wide_type), 0, keepdims=True)
        w_out[at, :] = dot_tn(grad_inner, low[...]).astype(low_type)
        outer[...] += dot_nt(grad_inner, w_in[:, at])

    for chunk in range(chunks):

        @pl.when(step == chunks + chunk)
        def _():
            for copy in outer_copies[chunk] + inner_copies[chunk]:
                copy.start()

    @pl.when(step == 2 * chunks - 1)
    def _():
        small[2].start()
        for copy in small:
            copy.wait()
        for copies in outer_copies + inner_copies:
            for copy in copies:
                copy.wait()


def ffn(slots, layer_in, ctx_own, ctx_rest, w_output, cotangent, vectors, w_in, w_out, b_in):
    tokens, width = layer_in.shape
    hidden = w_out.shape[0]
    chunks = 3
    blocks = slots.shape[0] - 1
    size = hidden // chunks
    forth = lambda i, *_: (0, jnp.minimum(i, chunks - 1))
    back = lambda i, *_: (0, jnp.maximum(i - chunks, 0))
    once = dict(pipeline_mode=pl.Buffered(1))
    copies = 3 + 4 * chunks
    return pl.pallas_call(
        functools.partial(ffn_kernel, chunks),
        grid_spec=pltpu.PrefetchScalarGridSpec(
            num_scalar_prefetch=1,
            grid=(2 * chunks,),
            in_specs=[
                whole_spec((tokens, width), **once),
                whole_spec(ctx_own.shape, **once),
                whole_spec(ctx_rest.shape, **once),
                whole_spec(w_output.shape, **once),
                whole_spec((tokens, width), **once),
                whole_spec(vectors.shape, **once),
                pl.BlockSpec((1, size), forth),
                anywhere,
                anywhere,
            ],
            out_specs=[
                whole_spec((tokens, 128)),
                whole_spec((8, width)),
                pl.BlockSpec((1, size), back),
            ]
            + [anywhere] * 7,
            scratch_shapes=[
                pltpu.VMEM((width, hidden), low_type),
                pltpu.VMEM((hidden, width), low_type),
                pltpu.VMEM((tokens, width), wide_type),
                pltpu.VMEM((tokens, width), wide_type),
                pltpu.VMEM((chunks, tokens, size), low_type),
                pltpu.VMEM((chunks, tokens, size), low_type),
            ]
            + [pltpu.VMEM((tokens, width), low_type)] * 4
            + [pltpu.SemaphoreType.DMA((2, blocks)), pltpu.SemaphoreType.DMA((copies,))],
        ),
        out_shape=[
            like((tokens, 128), wide_type),
            like((8, width), wide_type),
            like((1, hidden), wide_type),
            far_like((tokens, width)),
            far_like((tokens, width)),
            far_like((tokens, width), wide_type),
        ]
        + [far_like((hidden // 2, width))] * 4,
        compiler_params=large_room,
        cost_estimate=estimate(
            2 * tokens * width * (6 * hidden + width),
            2 * (tokens * 10 * width + 4 * hidden * width),
            tokens * hidden,
        ),
    )(slots, layer_in, ctx_own, ctx_rest, w_output, cotangent, vectors, b_in, far(w_in), far(w_out))


def norm_back_kernel(
    index_ref,
    total_ref,
    normal_ref,
    rstd_ref,
    own_ref,
    rest_ref,
    wo_ref,
    vec_ref,
    sums_in_ref,
    gb_ref,
    *refs,
):
    branch_ref, down_ref, drest_ref, near_ref, far_ref, sums, acc, held, table = refs[-9:]
    step = pl.program_id(0)
    size = branch_ref.shape[0]
    head = index_ref[PARTS]
    gain_attn = vec_ref[1:2, :]
    heads = wo_ref.shape[0]
    rows = wo_ref.shape[1] // 4
    cols = wo_ref.shape[2] // 2

    @pl.when(step == 0)
    def _():
        sums[...] = sums_in_ref[...]

    def one(at):
        grad = total_ref[at, :]
        normal = normal_ref[at, :].astype(wide_type)
        scaled = grad * gain_attn
        rstd = rstd_ref[at, 0:1]
        grad_sum = rstd * (scaled - mean_last(scaled) - normal * mean_last(scaled * normal))
        grad_low = grad_sum.astype(low_type)
        branch_ref[at, :] = grad_low
        sums[3:4, :] += jnp.sum(grad * normal, 0, keepdims=True)
        sums[4:5, :] += jnp.sum(grad, 0, keepdims=True)
        sums[5:6, :] += jnp.sum(grad_low.astype(wide_type), 0, keepdims=True)

    tiles(size, 256, one)
    branch = branch_ref[...]
    for offset in range(heads):
        context = own_ref[0] if offset == 0 else rest_ref[offset - 1]
        weights = wo_ref[head ^ offset]
        grad_context = dot_nt(branch, weights).astype(low_type)
        if offset == 0:
            down_ref[0] = grad_context
        else:
            drest_ref[offset - 1] = grad_context
        part = dot_tn(context, branch)

        @pl.when(step == 0)
        def _():
            acc[offset] = part

        @pl.when(step > 0)
        def _():
            acc[offset] += part

    @pl.when(step == pl.num_programs(0) - 1)
    def _():
        table[...] = jnp.zeros_like(table)
        for which in range(6):
            for across in range(2):
                place = 2 * which + across
                table[place : place + 1, :] = sums[
                    which : which + 1, across * cols : (across + 1) * cols
                ]
        for slot in range(PARTS):
            table[pl.ds(12 + index_ref[slot], 1), :] = gb_ref[:, slot * cols : (slot + 1) * cols]
        for offset in range(heads):
            for part in range(PARTS):
                across, below = divmod(part, 4)
                block = acc[
                    offset,
                    below * rows : (below + 1) * rows,
                    across * cols : (across + 1) * cols,
                ].astype(low_type)
                row = table[pl.ds(part * heads + (head ^ offset), 1), :]
                held[part, offset, :, 0:cols] = block[0:32]
                held[part, offset, 0:16, cols:] = block[32:48]
                held[part, offset, 16:32, cols:] = jnp.broadcast_to(row, (16, cols)).astype(low_type)
        for slot in range(PARTS // 2):
            near_ref[slot] = held[index_ref[slot]]
            far_ref[slot] = held[index_ref[slot + PARTS // 2]]


def norm_back(
    index, total, normal, rstd, ctx_own, ctx_rest, w_output, vectors, sums, gb, deps
):
    tokens, width = total.shape
    heads, group = w_output.shape[:2]
    size = tokens // 2
    tile = pl.BlockSpec((size, width), lambda i, *_: (i, 0))
    own = pl.BlockSpec((1, size, group), lambda i, *_: (0, i, 0))
    rest = pl.BlockSpec((heads - 1, size, group), lambda i, *_: (0, i, 0))
    half = (PARTS // 2, heads, (group // 4 + 16) // 2, width)
    return pl.pallas_call(
        norm_back_kernel,
        grid_spec=pltpu.PrefetchScalarGridSpec(
            num_scalar_prefetch=1,
            grid=(2,),
            in_specs=[
                tile,
                tile,
                pl.BlockSpec((size, 128), lambda i, *_: (i, 0)),
                own,
                rest,
                whole_spec(w_output.shape),
                whole_spec(vectors.shape),
                whole_spec(sums.shape),
                whole_spec(gb.shape),
            ]
            + [anywhere] * len(deps),
            out_specs=[
                tile,
                own,
                rest,
                whole_spec(half),
                whole_spec(half),
            ],
            scratch_shapes=[
                pltpu.VMEM((8, width), wide_type),
                pltpu.VMEM((heads, group, width), wide_type),
                pltpu.VMEM((PARTS,) + half[1:], low_type),
                pltpu.VMEM((PARTS * heads, width // 2), wide_type),
            ],
        ),
        out_shape=[
            like((tokens, width)),
            like(ctx_own.shape),
            like(ctx_rest.shape),
            far_like(half),
            far_like(half),
        ],
        compiler_params=room,
        cost_estimate=estimate(
            4 * tokens * width * width, 2 * tokens * width * 8 + 6 * width * width
        ),
    )(index, far(total), far(normal), far(rstd), ctx_own, ctx_rest, w_output, vectors, sums, gb, *[far(dep) for dep in deps])


def input_kernel(branch_ref, own_ref, shard_ref, rest_ref, weights_ref, *refs):
    total = branch_ref[...].astype(wide_type) + dot_nn(own_ref[0], shard_ref[0])
    for group in range(rest_ref.shape[0]):
        total += dot_nn(rest_ref[group], weights_ref[group])
    refs[-1][...] = total


def input_back(branch, own, shard, rest, weights, deps):
    tokens, width = branch.shape
    size = tokens // 2
    tile = pl.BlockSpec((size, width), lambda i: (i, 0))
    group = lambda value: pl.BlockSpec((value.shape[0], size, 640), lambda i: (0, i, 0))
    return pl.pallas_call(
        input_kernel,
        grid=(2,),
        in_specs=[tile, group(own), whole_spec(shard.shape), group(rest), whole_spec(weights.shape)]
        + [anywhere] * len(deps),
        out_specs=tile,
        out_shape=far_like((tokens, width), wide_type),
        compiler_params=room,
        cost_estimate=estimate(2 * tokens * width * 640 * 4, 16 * tokens * width),
    )(branch, own, shard, rest, weights, *[far(dep) for dep in deps])


def finish_kernel(heads, index_ref, *refs):
    owns, blocks = refs[0:2], refs[2:4]
    q_ref, k_ref, v_ref, wo_ref, bq_ref, bv_ref, gb_ref = refs[4:11]
    vectors = refs[11:17]
    held, back, table = refs[-3:]
    rows, cols = held.shape[1], held.shape[2] // 2
    head, row = index_ref[PARTS], index_ref[PARTS + 1]
    for slot in range(PARTS):
        part = index_ref[slot]
        half, place = divmod(slot, PARTS // 2)
        held[part] = owns[half][place]
        back[part] = blocks[half][place]
    whole = held[...].reshape(PARTS * rows, 2 * cols)
    for ref, first, second in ((q_ref, 0, 384), (k_ref, 128, 448), (v_ref, 256, 512)):
        ref[0:128, :] = whole[first : first + 128].astype(wide_type)
        ref[128:192, :] = whole[second : second + HD].astype(wide_type)
    sums = whole[576:592].astype(wide_type)[0:1]
    for ref, first, second in ((bq_ref, 0, 384), (bv_ref, 256, 512)):
        joined = jnp.concatenate([sums[:, first : first + 128], sums[:, second : second + HD]], 1)
        ref[...] = joined.reshape(ref.shape)
    for part in range(PARTS):
        across, down = divmod(part, 4)
        lanes = slice(across * cols, (across + 1) * cols)
        for offset in range(heads):
            other = head ^ offset
            block = back[part, offset].astype(wide_type)
            wo_ref[other, down * 48 : down * 48 + 32, lanes] = block[:, :cols]
            wo_ref[other, down * 48 + 32 : down * 48 + 48, lanes] = block[0:16, cols:]
            table[pl.ds(part * heads + other, 1), :] = block[16:17, cols:]
    for which, ref in enumerate(vectors):
        ref[...] = jnp.concatenate(
            [table[2 * which : 2 * which + 1], table[2 * which + 1 : 2 * which + 2]], 1
        ).reshape(ref.shape)
    block = gb_ref.shape[0]
    per_row = cols // block
    place = row * heads + head
    sums = table[pl.ds(12 + place // per_row, 1), :]
    total = jnp.zeros((1, block), wide_type)
    for which in range(per_row):
        total = jnp.where(
            place % per_row == which, sums[:, which * block : (which + 1) * block], total
        )
    gb_ref[...] = total.reshape(gb_ref.shape)


def finish(index, owns, blocks, block):
    rows = 640 // PARTS
    heads, extra, width = blocks[0].shape[1:]
    cols, group = width // 2, 192
    pieces = owns + blocks
    shapes = (
        [like((group, width), wide_type)] * 3
        + [like((heads, group, width), wide_type)]
        + [like((group,), wide_type)] * 2
        + [like((block,), wide_type)]
        + [like((width,), wide_type)] * 6
    )
    return pl.pallas_call(
        functools.partial(finish_kernel, heads),
        grid_spec=pltpu.PrefetchScalarGridSpec(
            num_scalar_prefetch=1,
            grid=(1,),
            in_specs=[whole_spec(piece.shape) for piece in pieces],
            out_specs=[whole_spec(shape.shape) for shape in shapes],
            scratch_shapes=[
                pltpu.VMEM((PARTS, rows, width), low_type),
                pltpu.VMEM((PARTS, heads, extra, width), low_type),
                pltpu.VMEM((PARTS * heads, cols), wide_type),
            ],
        ),
        out_shape=shapes,
        compiler_params=room,
        cost_estimate=estimate(0, 16 * width * width),
    )(index, *pieces)


def local(
    grid,
    layer_in,
    segment_ids,
    w_query,
    w_key,
    w_value,
    b_query,
    b_value,
    w_output,
    b_output,
    gain_attn,
    shift_attn,
    w_inner,
    b_inner,
    w_outer,
    b_outer,
    gain_ffn,
    shift_ffn,
    cotangent,
):
    tokens, width = layer_in.shape
    length = segment_ids.shape[1]
    seqs = tokens // length
    group = w_query.shape[1]
    hidden = w_inner.shape[1]
    heads = grid.heads
    row = lax.axis_index("rows")
    head = lax.axis_index("heads")
    segments = lax.dynamic_slice_in_dim(segment_ids, head * seqs, seqs, 0)[:, None, :]

    gap = jnp.zeros((128,), b_query.dtype)
    bias = jnp.concatenate(
        [b_query[:128], gap, b_value[:128], b_query[128:], gap[:HD], b_value[128:], gap, gap[:HD]]
    ).astype(wide_type)[None]
    part = grid.part_of(row.astype(jnp.int32))[None]
    shard, piece = pack(part, w_query.T, w_key.T, w_value.T, bias)
    got = [grid.across_heads(piece, offset) for offset in range(1, heads)]
    q_own, k_own, v_own, ctx_own = attend_own(layer_in, shard, segments)
    parts = grid.part_of(grid.helper_parts())

    row_slots = grid.row_slots()
    b_in = jnp.take(b_inner.reshape(grid.rows, -1), row_slots, axis=0, mode="clip").reshape(1, hidden)
    w_in, w_out = w_inner, w_outer
    if not grid.native:
        w_in = jnp.take(w_in.reshape(width, grid.rows, -1), row_slots, axis=1).reshape(width, hidden)
        w_out = jnp.take(w_out.reshape(grid.rows, -1, width), row_slots, axis=0).reshape(hidden, width)
    head_index = head.astype(jnp.int32)[None]
    natural = jnp.arange(PARTS, dtype=jnp.int32)
    index = jnp.concatenate([row_slots if grid.native else natural, head_index])
    w_output_heads = w_output.reshape(heads, group, width)
    vectors = jnp.stack(
        [b_output, gain_attn, shift_attn, b_outer, gain_ffn, shift_ffn, b_output, b_output]
    )

    held = join(got, (ctx_own, b_in, vectors, index, parts))
    held = [held] + grid.across_chips([held] * 4)
    held = held + [grid.across_core(value) for value in held]
    q_rest, k_rest, v_rest, ctx_rest, w_rest = attend_rest(parts, layer_in, held, segments)
    rstd, sums, gb_inner, normal, layer_out, total, outer_near, outer_far, inner_near, inner_far = ffn(
        index, layer_in, ctx_own, ctx_rest, w_output_heads, cotangent, vectors, w_in, w_out, b_in
    )
    slot_shape = (grid.rows // 2, hidden // grid.rows, width)
    outer_got = grid.across_core(outer_far.reshape(slot_shape))
    inner_got = grid.across_core(inner_far.reshape(slot_shape))
    if not grid.native:
        gb_inner = jnp.take(gb_inner.reshape(grid.rows, -1), grid.row_places(), axis=0).reshape(1, hidden)
    folded = functools.partial(fold, grid, head_index)
    first, second = grid.steps - 2, grid.steps - 1

    branch, dctx_own, dctx_rest, wo_near, wo_far = norm_back(
        index, total, normal, rstd, ctx_own, ctx_rest, w_output_heads, vectors, sums, gb_inner, ()
    )
    wo_near, wo_far = grid.spread_parts(wo_near, wo_far, True)

    ((outer, outer_send), (inner, inner_send)), (wo_far,) = folded(
        [
            ([outer_near.reshape(slot_shape), outer_got], "core"),
            ([inner_near.reshape(slot_shape), inner_got], "core"),
        ],
        (branch,),
        (wo_far,),
    )
    outer_got = grid.across_chip(outer_send, first)
    inner_got = grid.across_chip(inner_send, first)
    wo_got = grid.across_core(wo_far)
    dqkv_rest, rest_near, rest_far = attend_back(
        index, layer_in, q_rest, k_rest, v_rest, ctx_rest, dctx_rest, (inner_send,), length
    )
    rest_near, rest_far = grid.spread_parts(rest_near, rest_far)
    ((outer, outer_send), (inner, inner_send), wo), (rest_far,) = folded(
        [
            ([outer, outer_got], "halves"),
            ([inner, inner_got], "halves"),
            ([wo_near, wo_got], "spread"),
        ],
        (dqkv_rest,),
        (rest_far,),
    )
    outer_got = grid.across_chip(outer_send, second)
    wo_got = grid.across_chips(wo)
    rest_got = grid.across_core(rest_far)
    dqkv_own, own_near, own_far = attend_back(
        index, layer_in, q_own, k_own, v_own, ctx_own, dctx_own, (wo[3],), length
    )
    own_near, own_far = grid.spread_parts(own_near, own_far)
    (outer, (rest, rest_send)), (own_far, inner_send) = folded(
        [
            ([outer[0], outer_got[0], wo[0]] + wo_got, "zpack"),
            ([rest_near, rest_got], "core"),
        ],
        (dqkv_own,),
        (own_far, inner_send),
    )
    outer_got = [grid.across_heads(outer[offset], offset) for offset in range(1, heads)]
    inner_got = grid.across_chip(inner_send, second)
    rest_got = grid.across_chip(rest_send, first)
    input_grad = input_back(branch, dqkv_own, shard, dqkv_rest, w_rest, (rest_send,))
    ((out_w_outer, wo), (rest, rest_send), (inner,)), (own_far,) = folded(
        [
            ([outer[0]] + outer_got, "zsplit"),
            ([rest, rest_got], "halves"),
            ([inner[0], inner_got[0]], "sum"),
        ],
        (input_grad,),
        (own_far,),
    )
    wo_got = [grid.across_heads(wo, offset) for offset in range(1, heads)]
    rest_got = grid.across_chip(rest_send, second)
    own_got = grid.across_core(own_far)
    (rest, (wo,), own), _ = folded(
        [
            ([rest[0], rest_got[0]], "slots"),
            ([wo] + wo_got, "stack"),
            ([own_near, own_got], "spread"),
        ],
    )
    rest_got = [grid.across_heads(rest[offset - 1], offset) for offset in range(1, heads)]
    own_got = grid.across_chips(own)
    if grid.native:
        wo_got = grid.across_chips([wo] * 4)
    own = [value[0] for value in [own[0]] + own_got]
    ((own,), inner), _ = folded([(own + rest_got, "sum"), ([inner], "heads")])
    inner_got = [grid.across_heads(inner[offset], offset) for offset in range(1, heads)]
    if grid.native:
        own_got = grid.across_chips([own] * 4)
        ((out_w_inner,), (own,), (wo,)), _ = folded(
            [
                ([inner[0]] + inner_got, "wide"),
                ([own] + own_got, "stack"),
                ([wo] + wo_got, "stack"),
            ]
        )
        owns, blocks = [own, grid.across_core(own)], [wo, grid.across_core(wo)]
    else:
        ((out_w_inner,),), _ = folded([([inner[0]] + inner_got, "wide")])
        own = grid.gather_wide(own).reshape(PARTS, -1, width)
        wo = grid.coarse(grid.gather_wide(wo))
        owns, blocks = [own[: PARTS // 2], own[PARTS // 2 :]], [wo[: PARTS // 2], wo[PARTS // 2 :]]
    block = hidden // (grid.rows * heads)
    gw_query, gw_key, gw_value, gw_output, gb_query, gb_value, gb_inner, *vector = finish(
        jnp.concatenate([index, row.astype(jnp.int32)[None]]), owns, blocks, block
    )
    return (
        layer_out,
        input_grad,
        gw_query.T,
        gw_key.T,
        gw_value.T,
        gb_query,
        gb_value,
        gw_output.reshape(width, width),
        vector[5],
        vector[3],
        vector[4],
        out_w_inner.T,
        gb_inner,
        out_w_outer,
        vector[2],
        vector[0],
        vector[1],
    )


def solution(mesh):
    grid = Grid(mesh)
    return jax.shard_map(
        lambda *values: local(grid, *values),
        mesh=mesh,
        in_specs=(
            P(("rows", "heads"), None),
            P("rows", None),
            P(None, "heads"),
            P(None, "heads"),
            P(None, "heads"),
            P("heads"),
            P("heads"),
            P(),
            P(),
            P(),
            P(),
            P(),
            P(),
            P(),
            P(),
            P(),
            P(),
            P(("rows", "heads"), None),
        ),
        out_specs=(
            P(("rows", "heads"), None),
            P(("rows", "heads"), None),
            P(None, "heads"),
            P(None, "heads"),
            P(None, "heads"),
            P("heads"),
            P("heads"),
            P(),
            P(),
            P(),
            P(),
            P(None, ("rows", "heads")),
            P(("rows", "heads")),
            P(("rows", "heads"), None),
            P(),
            P(),
            P(),
        ),
        check_vma=False,
    )
```

```python
import functools

import jax
import jax.numpy as jnp
from jax import lax
from jax.experimental import pallas as pl
from jax.experimental.pallas import tpu as pltpu
from jax.sharding import PartitionSpec as P

HD = 64
PARTS = 8
epsilon = 1e-06
masked_score = -1000000000.0
low_type = jnp.bfloat16
wide_type = jnp.float32
room = pltpu.CompilerParams(vmem_limit_bytes=32 * 1024 * 1024)
large_room = pltpu.CompilerParams(vmem_limit_bytes=60 * 1024 * 1024)


def contract(left, right, left_dim, right_dim):
    return lax.dot_general(
        left, right, (((left_dim,), (right_dim,)), ((), ())), preferred_element_type=wide_type
    )


def dot_nn(left, right):
    return contract(left, right, 1, 0)


def dot_nt(left, right):
    return contract(left, right, 1, 1)


def dot_tn(left, right):
    return contract(left, right, 0, 0)


class Grid:
    def __init__(self, mesh):
        self.rows = mesh.shape["rows"]
        self.heads = mesh.shape["heads"]
        self.native = self.rows == PARTS
        self.steps = self.rows.bit_length() - 2
        up = list(range(1, self.steps + 1))
        self.orders = (up, up[::-1])

    def permute(self, value, row_masks, head_mask=0):
        pairs = [
            (row * self.heads + head, (row ^ row_masks[row & 1]) * self.heads + (head ^ head_mask))
            for row in range(self.rows)
            for head in range(self.heads)
        ]
        return lax.ppermute(value, ("rows", "heads"), pairs)

    def across_core(self, value):
        return self.permute(value, (1, 1))

    def across_heads(self, value, offset):
        return self.permute(value, (0, 0), offset)

    def across_chip(self, value, step):
        return self.permute(value, [1 << order[step] for order in self.orders])

    def across_chips(self, values):
        masks = [self.slot_masks(core) for core in (0, 1)]
        return [
            self.permute(value, (masks[0][slot], masks[1][slot]))
            for slot, value in enumerate(values)
            if slot
        ]

    def slot_masks(self, core):
        last = self.steps - 1
        masks = []
        for slot in range(1 << self.steps):
            mask = 0
            for step in range(self.steps):
                mask |= ((slot >> (last - step)) & 1) << self.orders[core][step]
            masks.append(mask)
        return masks

    def row_slots(self):
        row = lax.axis_index("rows").astype(jnp.int32)
        masks = jnp.array([self.slot_masks(0), self.slot_masks(1)], jnp.int32)
        core = row & 1
        return jnp.concatenate([row ^ masks[core], (row ^ 1) ^ masks[1 - core]])

    def row_places(self):
        row = lax.axis_index("rows").astype(jnp.int32)
        half = self.rows // 2
        inverse = []
        for core in (0, 1):
            table = [0] * half
            for slot, mask in enumerate(self.slot_masks(core)):
                table[mask >> 1] = slot
            inverse.append(table)
        inverse = jnp.array(inverse, jnp.int32)
        apart = jnp.arange(self.rows, dtype=jnp.int32) ^ row
        other = apart & 1
        return other * half + inverse[(row & 1) ^ other, apart >> 1]

    def helper_parts(self):
        row = lax.axis_index("rows").astype(jnp.int32)
        masks = jnp.array([self.slot_masks(0)[:4], self.slot_masks(1)[:4]], jnp.int32)
        core = row & 1
        return jnp.concatenate([row ^ masks[core], (row ^ 1) ^ masks[1 - core]])

    def part_of(self, row):
        if self.native:
            return row
        low, high = sorted(self.orders[0][-2:])
        return (row & 1) + 2 * ((row >> low) & 1) + 4 * ((row >> high) & 1)

    def scatter_wide(self, mine, got):
        held = add_like(mine, got)
        for step in range(self.steps - 2):
            half = held.shape[0] // 2
            held = add_like(held[:half], self.across_chip(held[half:], step))
        return held

    def gather_wide(self, value):
        held = jnp.stack([value] + self.across_chips([value] * 4))
        for step in reversed(range(self.steps - 2)):
            held = jnp.concatenate([held, self.across_chip(held, step)], 0)
        held = jnp.concatenate([held, self.across_core(held)], 0)
        return jnp.take(held, self.row_places(), axis=0)

    def coarse(self, blocks):
        half = blocks.shape[3] // 2
        blocks = jnp.concatenate([blocks[..., :half], blocks[..., half:]], 2)
        blocks = blocks.reshape((PARTS, -1) + blocks.shape[1:]).transpose(0, 2, 1, 3, 4)
        blocks = blocks.reshape(PARTS, blocks.shape[1], -1, half)
        middle = blocks.shape[2] // 2
        return jnp.concatenate([blocks[:, :, :middle], blocks[:, :, middle:]], 3)

    def spread_parts(self, near, far, paired=False):
        if self.native:
            return near, far
        parts = jnp.concatenate([near, far], 0)
        if paired:
            half = parts.shape[3] // 2
            parts = jnp.concatenate([parts[..., :half], parts[..., half:]], 2)
        count, rows, cols = parts.shape[1:]
        finer = self.rows // PARTS
        parts = parts.reshape(PARTS, count, finer, rows // finer, cols).transpose(0, 2, 1, 3, 4)
        parts = parts.reshape(self.rows, count, rows // finer, cols)
        parts = jnp.take(parts, self.row_slots(), axis=0)
        if paired:
            half = parts.shape[2] // 2
            parts = jnp.concatenate([parts[:, :, :half], parts[:, :, half:]], 3)
        return parts[: self.rows // 2], parts[self.rows // 2 :]


def add_like(first, second):
    return (first.astype(wide_type) + second.astype(wide_type)).astype(first.dtype)


def estimate(flops, moved, exps=0):
    return pl.CostEstimate(
        flops=flops, bytes_accessed=moved, transcendentals=exps
    )


def like(shape, dtype=low_type):
    return jax.ShapeDtypeStruct(shape, dtype)


def far(value):
    return pltpu.with_memory_space_constraint(value, pltpu.HBM)


def far_like(shape, dtype=low_type):
    return pltpu.HBM(shape, dtype)


def whole_spec(shape, **options):
    return pl.BlockSpec(shape, lambda *ids: (0,) * len(shape), **options)


anywhere = pl.BlockSpec(memory_space=pl.ANY)


def total_of(terms, cut):
    return sum(cut(term).astype(wide_type) for term in terms)


def fold_kernel(plan, passed, head_ref, *refs):
    outs = list(refs[len(refs) - passed - sum(job[2] for job in plan) : len(refs) - passed])
    refs = list(refs)
    for count, kind, given in plan:
        terms, refs = refs[:count], refs[count:]
        made, outs = outs[:given], outs[given:]
        if kind == "halves":
            size = made[0].shape[0]
            for half, target in enumerate(made):
                at = slice(half * size, (half + 1) * size)
                target[...] = total_of(terms, lambda term: term[at]).astype(target.dtype)
        elif kind == "slots":
            for slot, target in enumerate(made):
                target[...] = total_of(terms, lambda term: term[slot]).astype(target.dtype)
        elif kind == "heads" or kind == "zpack":
            heads = len(made) if kind == "heads" else len(made) // 2
            rows = terms[0].shape[0] // heads
            for offset in range(heads):
                begin = (head_ref[0] ^ offset) * rows
                if kind == "heads":
                    at = pl.ds(pl.multiple_of(begin, 16), rows)
                    made[offset][...] = total_of(terms, lambda term: term[at, :]).astype(low_type)
                    continue
                half = rows // 2
                upper = pl.ds(pl.multiple_of(begin, 16), half)
                lower = pl.ds(pl.multiple_of(begin + half, 16), half)
                target, other = made[offset], made[heads + offset]
                target[0:half] = total_of(terms[:2], lambda term: term[upper, :]).astype(low_type)
                target[half:] = total_of(terms[2:], lambda term: term[offset]).astype(low_type)
                other[...] = total_of(terms[:2], lambda term: term[lower, :]).astype(low_type)
        elif kind == "zsplit":
            rows = made[0].shape[0]
            made[0][...] = total_of(terms[:4], lambda term: term[0:rows])
            total = total_of(terms[:4], lambda term: term[rows:]).astype(low_type)
            made[1][...] = total
            for term, target in zip(terms[4:], made[2:]):
                target[0:rows] = term[...]
                target[rows:] = total
        elif kind == "zlast":
            rows = terms[0].shape[0]
            made[0][0:rows] = terms[0][...]
            made[0][rows:] = total_of(terms[1:2] + terms[3:], lambda term: term[0:rows])
            made[1][0] = terms[2][...]
            for place, term in enumerate(terms[3:]):
                made[1][place + 1] = term[rows:]
        elif kind == "stack":
            for place, term in enumerate(terms):
                made[0][place] = term[...]
        else:
            made[0][...] = total_of(terms, lambda term: term[...]).astype(made[0].dtype)


def fold(grid, head, jobs, deps=(), passes=()):
    if not grid.native:
        return [plain_job(grid, head, *job) for job in jobs], list(passes)
    plan, values, shapes = [], [], []
    for terms, kind in jobs:
        kind = {"core": "halves", "spread": "slots"}.get(kind, kind)
        shape = terms[0].shape
        if kind == "halves":
            made = [like((shape[0] // 2,) + shape[1:])] * 2
        elif kind == "slots":
            made = [like(shape[1:])] * shape[0]
        elif kind == "heads":
            made = [like((shape[0] // grid.heads, shape[1]))] * grid.heads
        elif kind == "zpack":
            rows = shape[0] // grid.heads // 2
            made = [like((rows + terms[2].shape[1], shape[1]))] * grid.heads
            made = made + [like((rows, shape[1]))] * grid.heads
        elif kind == "zsplit":
            rows = terms[4].shape[0]
            made = [like((rows, shape[1]), wide_type), like((shape[0] - rows, shape[1]))]
            made = made + [like(shape)] * 3
        elif kind == "zlast":
            made = [
                like((2 * shape[0], shape[1]), wide_type),
                like((len(terms) - 2,) + terms[2].shape),
            ]
        elif kind == "stack":
            made = [like((len(terms),) + shape)]
        else:
            made = [like(shape, wide_type if kind == "wide" else low_type)]
        plan.append((len(terms), kind, len(made)))
        values += terms
        shapes += made
    first, sums = 1 + len(values) + len(deps), len(shapes)
    outs = pl.pallas_call(
        functools.partial(fold_kernel, tuple(plan), len(passes)),
        grid_spec=pltpu.PrefetchScalarGridSpec(
            num_scalar_prefetch=1,
            grid=(1,),
            in_specs=[whole_spec(value.shape) for value in values]
            + [anywhere] * (len(deps) + len(passes)),
            out_specs=[whole_spec(shape.shape) for shape in shapes] + [anywhere] * len(passes),
        ),
        out_shape=shapes + [like(value.shape) for value in passes],
        input_output_aliases={first + place: sums + place for place in range(len(passes))},
        compiler_params=room,
        cost_estimate=estimate(0, sum(3 * value.size for value in values)),
    )(head, *values, *[far(dep) for dep in deps], *passes)
    results, place = [], 0
    for _, _, given in plan:
        results.append(outs[place : place + given])
        place += given
    return results, list(outs[sums:])


def plain_job(grid, head, terms, kind):
    whole = lambda term: term
    if kind in ("core", "spread"):
        held = grid.scatter_wide(*terms)
        return [held[:2], held[2:]] if kind == "core" else list(held)
    if kind == "stack":
        return [jnp.stack(terms)]
    if kind == "zsplit":
        rows = terms[4].shape[0]
        total = total_of(terms[:4], whole)
        small = total[rows:].astype(low_type)
        return [total[:rows], small] + [jnp.concatenate([term, small], 0) for term in terms[4:]]
    if kind == "zlast":
        rows = terms[0].shape[0]
        lower = total_of(terms[1:2] + terms[3:], lambda term: term[:rows])
        blocks = jnp.stack([terms[2]] + [term[rows:] for term in terms[3:]])
        return [jnp.concatenate([terms[0], lower], 0), blocks]
    if kind in ("heads", "zpack"):
        total = total_of(terms if kind == "heads" else terms[:2], whole).astype(low_type)
        total = total.reshape((grid.heads, -1) + total.shape[1:])
        made = [total[head[0] ^ offset] for offset in range(grid.heads)]
        if kind == "heads":
            return made
        wo = total_of(terms[2:], whole).astype(low_type)
        half = made[0].shape[0] // 2
        upper = [jnp.concatenate([made[offset][:half], wo[offset]], 0) for offset in range(grid.heads)]
        return upper + [block[half:] for block in made]
    total = total_of(terms, whole)
    if kind == "wide":
        return [total]
    total = total.astype(low_type)
    if kind == "halves":
        half = total.shape[0] // 2
        return [total[:half], total[half:]]
    return list(total) if kind == "slots" else [total]


def join_kernel(count, *refs):
    for slot in range(count):
        refs[-1][slot] = refs[slot][...]


def join(values, deps=()):
    shape = (len(values),) + values[0].shape
    return pl.pallas_call(
        functools.partial(join_kernel, len(values)),
        grid=(1,),
        in_specs=[whole_spec(value.shape) for value in values] + [anywhere] * len(deps),
        out_specs=whole_spec(shape),
        out_shape=like(shape),
        compiler_params=room,
        cost_estimate=estimate(0, 4 * values[0].size),
    )(*values, *[far(dep) for dep in deps])


def three_parts(values):
    first = values.astype(low_type).astype(wide_type)
    rest = values - first
    second = rest.astype(low_type).astype(wide_type)
    return first, second, (rest - second).astype(low_type).astype(wide_type)


def pair_up(low_lanes, first, second):
    return jnp.where(low_lanes, first, pltpu.roll(second, HD, 1))


def pack_kernel(index_ref, q_ref, k_ref, v_ref, bq_ref, bv_ref, w_ref, piece_ref):
    rows = piece_ref.shape[0]
    w_ref[0, 0:128, :] = q_ref[0:128, :]
    w_ref[0, 128:256, :] = k_ref[0:128, :]
    w_ref[0, 256:384, :] = v_ref[0:128, :]
    w_ref[0, 384:448, :] = q_ref[128:192, :]
    w_ref[0, 448:512, :] = k_ref[128:192, :]
    w_ref[0, 512:576, :] = v_ref[128:192, :]
    row = lax.broadcasted_iota(jnp.int32, (HD, w_ref.shape[2]), 0)
    bias_q = bq_ref[...].astype(wide_type).reshape(1, 192)
    bias_v = bv_ref[...].astype(wide_type).reshape(1, 192)
    gap = jnp.zeros((1, 128), wide_type)
    bias = [bias_q[:, 0:128], gap, bias_v[:, 0:128]]
    bias.append(jnp.concatenate([bias_q[:, 128:192], gap[:, :HD]], 1))
    bias.append(jnp.concatenate([bias_v[:, 128:192], gap[:, :HD]], 1))
    bias = jnp.concatenate(bias + [gap] * (w_ref.shape[2] // 128 - 5), 1)
    w_ref[0, 576:640, :] = jnp.where(row == 0, bias, 0.0).astype(low_type)
    mine = pl.multiple_of(index_ref[0] * rows, 16)
    piece_ref[...] = w_ref[0, pl.ds(mine, rows), :]


def pack(part, w_query, w_key, w_value, b_query, b_value):
    width = w_query.shape[1]
    rows = 640 // PARTS
    return pl.pallas_call(
        pack_kernel,
        grid_spec=pltpu.PrefetchScalarGridSpec(
            num_scalar_prefetch=1,
            grid=(1,),
            in_specs=[whole_spec(w_query.shape)] * 3 + [whole_spec(b_query.shape)] * 2,
            out_specs=[whole_spec((1, 640, width)), whole_spec((rows, width))],
        ),
        out_shape=[far_like((1, 640, width)), far_like((rows, width))],
        compiler_params=room,
        cost_estimate=estimate(0, 4 * width * 640),
    )(part, far(w_query), far(w_key), far(w_value), b_query, b_value)


def attend_body(device_head, x_ref, w_ref, seg_ref, q_ref, k_ref, v_ref, ctx_ref):
    length = seg_ref.shape[1]
    seqs = x_ref.shape[0] // length
    lane = lax.broadcasted_iota(jnp.int32, (1, 128), 1)
    low = lane < HD
    row8 = lax.broadcasted_iota(jnp.int32, (8, length), 0)
    bias_row = w_ref[0, 576:592, :][0:1, 0:640].astype(wide_type)
    for seq in range(seqs):
        at = slice(seq * length, (seq + 1) * length)
        qkv = (dot_nt(x_ref[at, :], w_ref[0]) + bias_row).astype(low_type).astype(wide_type)
        q01 = qkv[:, 0:128] * 0.125
        k01 = qkv[:, 128:256]
        v01 = qkv[:, 256:384]
        qk2 = qkv[:, 384:512]
        queries = [q01, pltpu.roll(q01, HD, 1), qk2 * 0.125]
        keys = [k01, pltpu.roll(k01, HD, 1), pltpu.roll(qk2, HD, 1)]
        values = [v01, pltpu.roll(v01, HD, 1), qkv[:, 512:640]]
        seg_row = seg_ref[pl.ds(device_head * seqs + seq, 1), :]
        seg_rows = jnp.broadcast_to(seg_row.astype(wide_type), (8, length))
        seg_col = seg_rows.T[:, 0:1].astype(jnp.int32) + HD
        same = lane == seg_col
        in_seg = (lane >= HD) & (lane < HD + 4)
        extra_q = jnp.where(same, 1.0, 0.0)
        extra_k = jnp.where(
            in_seg & ~same,
            masked_score,
            jnp.where((lane >= HD + 4) & (lane < HD + 7), 1.0, 0.0),
        )
        extra_v = jnp.where((lane >= HD) & (lane < HD + 3), 1.0, 0.0)
        contexts = []
        for head in range(3):
            query = jnp.where(low, queries[head], extra_q)
            key = jnp.where(low, keys[head], extra_k).astype(low_type)
            value = jnp.where(low, values[head], extra_v).astype(low_type)
            k_ref[0, head, at, :] = key
            v_ref[0, head, at, :] = value
            scores = dot_nt(key, query.astype(low_type))
            highest = jnp.max(scores, 0, keepdims=True)
            weights_low = jnp.exp(scores - highest).astype(low_type)
            summed = dot_tn(value, weights_low)
            total = summed[HD : HD + 1, :]
            first, second, third = three_parts(-(highest + jnp.log(total)))
            extra = jnp.where(
                row8 == 4, first, jnp.where(row8 == 5, second, jnp.where(row8 == 6, third, 0.0))
            )
            full = jnp.concatenate(
                [summed[:HD] * (1.0 / total), extra, jnp.zeros((56, length), wide_type)], 0
            ).T
            q_ref[0, head, at, :] = jnp.where(low, query, full + extra_q).astype(low_type)
            contexts.append(full)
        ctx_ref[0, at, 0:128] = pair_up(low, contexts[0], contexts[1]).astype(low_type)
        ctx_ref[0, at, 128:192] = contexts[2][:, :HD].astype(low_type)


def attend_own_kernel(head_ref, x_ref, w_ref, seg_ref, q_ref, k_ref, v_ref, ctx_ref):
    attend_body(head_ref[0], x_ref, w_ref, seg_ref, q_ref, k_ref, v_ref, ctx_ref)


def attend_rest_kernel(parts_ref, x_ref, seg_ref, *refs):
    pieces, (q_ref, k_ref, v_ref, ctx_ref, w_ref) = refs[:PARTS], refs[PARTS:]
    rows = pieces[0].shape[1]
    for slot in range(PARTS):
        at = pl.ds(pl.multiple_of(parts_ref[slot] * rows, 16), rows)
        w_ref[0, at, :] = pieces[slot][0]
    attend_body(parts_ref[PARTS], x_ref, w_ref, seg_ref, q_ref, k_ref, v_ref, ctx_ref)


def attend_cost(count, tokens, length, width):
    return estimate(
        count * (2 * tokens * width * 576 + 3 * 4 * tokens * length * 128),
        2 * tokens * width + count * 2 * (576 * width + 10 * tokens * 128),
        count * 3 * tokens * length,
    )


def attend_outputs(count, tokens):
    heads = pl.BlockSpec((1, 3, tokens, 128), lambda g, *_: (g, 0, 0, 0))
    specs = [heads, heads, heads, pl.BlockSpec((1, tokens, 192), lambda g, *_: (g, 0, 0))]
    shapes = [far_like((count, 3, tokens, 128))] * 3 + [far_like((count, tokens, 192))]
    return specs, shapes


def attend_own(head, layer_in, shard, segments):
    tokens, width = layer_in.shape
    specs, shapes = attend_outputs(1, tokens)
    return pl.pallas_call(
        attend_own_kernel,
        grid_spec=pltpu.PrefetchScalarGridSpec(
            num_scalar_prefetch=1,
            grid=(1,),
            in_specs=[
                whole_spec((tokens, width)),
                whole_spec(shard.shape),
                whole_spec(segments.shape),
            ],
            out_specs=specs,
        ),
        out_shape=shapes,
        compiler_params=room,
        cost_estimate=attend_cost(1, tokens, segments.shape[1], width),
    )(head, far(layer_in), far(shard), segments)


def attend_rest(parts, layer_in, pieces, segments):
    tokens, width = layer_in.shape
    count, rows, width = pieces[0].shape
    specs, shapes = attend_outputs(count, tokens)
    piece = pl.BlockSpec((1, rows, width), lambda g, *_: (g, 0, 0))
    return pl.pallas_call(
        attend_rest_kernel,
        grid_spec=pltpu.PrefetchScalarGridSpec(
            num_scalar_prefetch=1,
            grid=(count,),
            in_specs=[whole_spec((tokens, width)), whole_spec(segments.shape)] + [piece] * PARTS,
            out_specs=specs + [pl.BlockSpec((1, 640, width), lambda g, *_: (g, 0, 0))],
        ),
        out_shape=shapes + [far_like((count, 640, width))],
        compiler_params=room,
        cost_estimate=attend_cost(count, tokens, segments.shape[1], width),
    )(parts, far(layer_in), segments, *pieces)


def attend_back_kernel(
    length,
    slots_ref,
    x_ref,
    q_ref,
    k_ref,
    v_ref,
    ctx_ref,
    dctx_ref,
    *refs,
):
    dqkv_ref, near_ref, far_ref, held = refs[-4:]
    tokens, width = x_ref.shape
    rows = 640 // PARTS
    lane = lax.broadcasted_iota(jnp.int32, (1, 128), 1)
    low = lane < HD
    for seq in range(tokens // length):
        at = slice(seq * length, (seq + 1) * length)
        grad01 = dctx_ref[0, at, 0:128].astype(wide_type)
        grad2 = dctx_ref[0, at, 128:192].astype(wide_type)
        both = grad01 * ctx_ref[0, at, 0:128].astype(wide_type)
        inner = [
            jnp.sum(jnp.where(low, both, 0.0), -1, keepdims=True),
            jnp.sum(jnp.where(low, 0.0, both), -1, keepdims=True),
            jnp.sum(grad2 * ctx_ref[0, at, 128:192].astype(wide_type), -1, keepdims=True),
        ]
        grads = [
            grad01,
            pltpu.roll(grad01, HD, 1),
            jnp.concatenate([grad2, jnp.zeros((length, HD), wide_type)], 1),
        ]
        grad_q, grad_k, grad_v = [], [], []
        for head in range(3):
            first, second, third = three_parts(-inner[head])
            extra = jnp.where(
                lane == HD,
                first,
                jnp.where(lane == HD + 1, second, jnp.where(lane == HD + 2, third, 0.0)),
            )
            grad = jnp.where(low, grads[head], extra).astype(low_type)
            query = q_ref[0, head, at, :]
            key = k_ref[0, head, at, :]
            probs = jnp.exp(dot_nt(key, query))
            grad_scores = (probs * dot_nt(v_ref[0, head, at, :], grad)).astype(low_type)
            grad_v.append(dot_nn(probs.astype(low_type), grad))
            grad_k.append(dot_nn(grad_scores, query))
            grad_q.append(dot_tn(key, grad_scores).T * 0.125)
        dqkv_ref[0, at, 0:128] = pair_up(low, grad_q[0], grad_q[1]).astype(low_type)
        dqkv_ref[0, at, 128:256] = pair_up(low, grad_k[0], grad_k[1]).astype(low_type)
        dqkv_ref[0, at, 256:384] = pair_up(low, grad_v[0], grad_v[1]).astype(low_type)
        dqkv_ref[0, at, 384:512] = pair_up(low, grad_q[2], grad_k[2]).astype(low_type)
        dqkv_ref[0, at, 512:640] = jnp.where(low, grad_v[2], 0.0).astype(low_type)
    grad_all = dqkv_ref[0]
    total = dot_tn(grad_all, x_ref[...])
    sums = jnp.sum(grad_all.astype(wide_type), 0, keepdims=True)
    sums = jnp.concatenate([sums, jnp.zeros((1, width - 640), wide_type)], 1)
    for part in range(PARTS):
        held[part] = total[part * rows : (part + 1) * rows].astype(low_type)
    row = lax.broadcasted_iota(jnp.int32, (HD, width), 0)
    spare = jnp.where(row == 0, sums, 0.0)
    held[PARTS - 1, rows - HD : rows] = spare.astype(low_type)
    for slot in range(PARTS // 2):
        near_ref[slot, 0] = held[slots_ref[slot]]
        far_ref[slot, 0] = held[slots_ref[slot + PARTS // 2]]


def attend_back(
    slots, layer_in, queries, keys, values, context, grad_context, deps, length
):
    tokens, width = layer_in.shape
    count = context.shape[0]
    rows = 640 // PARTS
    heads = pl.BlockSpec((1, 3, tokens, 128), lambda g, *_: (g, 0, 0, 0))
    group = pl.BlockSpec((1, tokens, 192), lambda g, *_: (g, 0, 0))
    half = pl.BlockSpec((PARTS // 2, 1, rows, width), lambda g, *_: (0, g, 0, 0))
    return pl.pallas_call(
        functools.partial(attend_back_kernel, length),
        grid_spec=pltpu.PrefetchScalarGridSpec(
            num_scalar_prefetch=1,
            grid=(count,),
            in_specs=[whole_spec((tokens, width)), heads, heads, heads, group, group]
            + [anywhere] * len(deps),
            out_specs=[pl.BlockSpec((1, tokens, 640), lambda g, *_: (g, 0, 0)), half, half],
            scratch_shapes=[pltpu.VMEM((PARTS, rows, width), low_type)],
        ),
        out_shape=[
            like((count, tokens, 640)),
            like((PARTS // 2, count, rows, width)),
            like((PARTS // 2, count, rows, width)),
        ],
        compiler_params=room,
        cost_estimate=estimate(
            count * (2 * tokens * width * 576 + 3 * 10 * tokens * length * 128),
            2 * tokens * width + count * 2 * (576 * width + 16 * tokens * 128),
            count * 3 * tokens * length,
        ),
    )(slots, far(layer_in), queries, keys, values, context, grad_context, *[far(dep) for dep in deps])


def mean_last(values):
    return jnp.mean(values, -1, keepdims=True)


def tiles(tokens, size, body):
    def step(index, carry):
        body(pl.ds(pl.multiple_of(index * size, size), size))
        return carry

    lax.fori_loop(0, tokens // size, step, 0)


def gelu_pair(values):
    cumulative = 0.5 * (1.0 + lax.erf(values * 0.7071067811865476))
    density = jnp.exp(-0.5 * values * values) * 0.3989422804014327
    return values * cumulative, cumulative + values * density


class Loads:
    def __init__(self, slots_ref, w_in_hbm, w_out_hbm, w_in, w_out, sems):
        self.count = sems.shape[1]
        self.size = w_out.shape[0] // self.count
        self.copies = []
        for slot in range(self.count):
            source = pl.ds(pl.multiple_of(slots_ref[slot] * self.size, 128), self.size)
            target = pl.ds(slot * self.size, self.size)
            self.copies.append(
                (
                    pltpu.make_async_copy(w_in_hbm.at[:, source], w_in.at[:, target], sems.at[0, slot]),
                    pltpu.make_async_copy(w_out_hbm.at[source], w_out.at[target], sems.at[1, slot]),
                )
            )

    def start(self):
        for copies in self.copies:
            for copy in copies:
                copy.start()

    def wait(self, low, high):
        for slot in range(-(-low // self.size), -(-high // self.size)):
            for copy in self.copies[slot]:
                copy.wait()


def overlaps(size, chunks, block, blocks):
    return [
        [
            (which, max(chunk * size, which * block), min((chunk + 1) * size, (which + 1) * block))
            for which in range(blocks)
            if max(chunk * size, which * block) < min((chunk + 1) * size, (which + 1) * block)
        ]
        for chunk in range(chunks)
    ]


def ffn_kernel(
    chunks,
    slots_ref,
    x_ref,
    own_ref,
    rest_ref,
    wo_ref,
    cot_ref,
    b_output_ref,
    gain_attn_ref,
    shift_attn_ref,
    b_outer_ref,
    gain_ffn_ref,
    shift_ffn_ref,
    b_in_ref,
    w_in_hbm,
    w_out_hbm,
    rstd_ref,
    sums_ref,
    gb_ref,
    normal_hbm,
    out_hbm,
    total_hbm,
    outer_near_hbm,
    outer_far_hbm,
    near_hbm,
    far_hbm,
    w_in,
    w_out,
    normed,
    outer,
    active,
    slope,
    low,
    normal_low,
    result_low,
    grad_out,
    b_row,
    sems,
    out_sems,
):
    step = pl.program_id(0)
    tokens, width = x_ref.shape
    hidden = w_out.shape[0]
    size = hidden // chunks
    half = hidden // 2
    loads = Loads(slots_ref, w_in_hbm, w_out_hbm, w_in, w_out, sems)
    head = slots_ref[loads.count]
    b_output, gain_attn, shift_attn, b_outer, gain_ffn, shift_ffn = (
        ref[...].reshape(1, width)
        for ref in (
            b_output_ref,
            gain_attn_ref,
            shift_attn_ref,
            b_outer_ref,
            gain_ffn_ref,
            shift_ffn_ref,
        )
    )
    small = [
        pltpu.make_async_copy(source, target, out_sems.at[place])
        for place, (source, target) in enumerate(
            ((normal_low, normal_hbm), (result_low, out_hbm), (outer, total_hbm))
        )
    ]
    count = len(small)
    outer_copies, inner_copies = [], []
    for chunk, cuts in enumerate(overlaps(size, chunks, half, 2)):
        from_active, from_out = [], []
        for which, begin, end in cuts:
            at = pl.ds(begin - which * half, end - begin)
            from_active.append(
                pltpu.make_async_copy(
                    active.at[chunk, pl.ds(begin - chunk * size, end - begin), pl.ds(0, width)],
                    (outer_near_hbm, outer_far_hbm)[which].at[at],
                    out_sems.at[count],
                )
            )
            from_out.append(
                pltpu.make_async_copy(
                    w_out.at[pl.ds(begin, end - begin)],
                    (near_hbm, far_hbm)[which].at[at],
                    out_sems.at[count + 1],
                )
            )
            count += 2
        outer_copies.append(from_active)
        inner_copies.append(from_out)

    @pl.when(step == 0)
    def _():
        loads.start()
        b_row[1:2, :] = b_in_ref[...].reshape(1, hidden)
        for slot in range(loads.count):
            source = pl.ds(pl.multiple_of(slots_ref[slot] * loads.size, 128), loads.size)
            b_row[0:1, slot * loads.size : (slot + 1) * loads.size] = b_row[1:2, source]
        outer[...] = jnp.zeros_like(outer)
        branch = dot_nn(own_ref[0], wo_ref[head])
        for offset in range(1, wo_ref.shape[0]):
            branch += dot_nn(rest_ref[offset - 1], wo_ref[head ^ offset])
        normed[...] = branch

        def one(at):
            total = x_ref[at, :].astype(wide_type) + (normed[at, :] + b_output)
            centred = total - mean_last(total)
            rstd = lax.rsqrt(mean_last(centred * centred) + epsilon)
            normal = centred * rstd
            result = normal * gain_attn + shift_attn
            normed[at, :] = result
            low[at, :] = result.astype(low_type)
            normal_low[at, :] = normal.astype(low_type)
            rstd_ref[at, :] = jnp.broadcast_to(rstd, (rstd.shape[0], 128))

        tiles(tokens, 256, one)
        small[0].start()

    for chunk in range(chunks):

        @pl.when(step == chunk)
        def _():
            loads.wait(chunk * size, (chunk + 1) * size)

    @pl.when(step < chunks)
    def _():
        at = pl.ds(pl.multiple_of(step * size, 128), size)
        inner = dot_nn(low[...], w_in[:, at]) + b_row[0:1, at]
        values, gradient = gelu_pair(inner)
        values = values.astype(low_type)
        active[step] = values
        slope[step] = gradient.astype(low_type)
        outer[...] += dot_nn(values, w_out[at, :])

    @pl.when(step == chunks - 1)
    def _():
        sums_ref[...] = jnp.zeros_like(sums_ref)

        def one(at):
            total = normed[at, :] + (outer[at, :] + b_outer)
            centred = total - mean_last(total)
            rstd = lax.rsqrt(mean_last(centred * centred) + epsilon)
            normal = centred * rstd
            result_low[at, :] = (normal * gain_ffn + shift_ffn).astype(low_type)
            grad = cot_ref[at, :].astype(wide_type)
            scaled = grad * gain_ffn
            grad_sum = rstd * (scaled - mean_last(scaled) - normal * mean_last(scaled * normal))
            grad_low = grad_sum.astype(low_type)
            grad_out[at, :] = grad_low
            outer[at, :] = grad_low.astype(wide_type)
            sums_ref[0:1, :] += jnp.sum(grad * normal, 0, keepdims=True)
            sums_ref[1:2, :] += jnp.sum(grad, 0, keepdims=True)
            sums_ref[2:3, :] += jnp.sum(grad_low.astype(wide_type), 0, keepdims=True)

        tiles(tokens, 256, one)
        small[1].start()

    @pl.when(step >= chunks)
    def _():
        which = step - chunks
        at = pl.ds(pl.multiple_of(which * size, 128), size)
        grad = grad_out[...]
        active[which, :, 0:width] = dot_tn(active[which], grad).astype(low_type)
        grad_inner = (dot_nt(grad, w_out[at, :]) * slope[which].astype(wide_type)).astype(low_type)
        gb_ref[...] = jnp.sum(grad_inner.astype(wide_type), 0, keepdims=True)
        w_out[at, :] = dot_tn(grad_inner, low[...]).astype(low_type)
        outer[...] += dot_nt(grad_inner, w_in[:, at])

    for chunk in range(chunks):

        @pl.when(step == chunks + chunk)
        def _():
            for copy in outer_copies[chunk] + inner_copies[chunk]:
                copy.start()

    @pl.when(step == 2 * chunks - 1)
    def _():
        small[2].start()
        for copy in small:
            copy.wait()
        for copies in outer_copies + inner_copies:
            for copy in copies:
                copy.wait()


def ffn(slots, layer_in, ctx_own, ctx_rest, w_output, cotangent, vectors, w_in, w_out, b_in):
    tokens, width = layer_in.shape
    hidden = w_out.shape[0]
    chunks = 3
    blocks = slots.shape[0] - 1
    size = hidden // chunks
    back = lambda i, *_: (0, jnp.maximum(i - chunks, 0))
    once = dict(pipeline_mode=pl.Buffered(1))
    copies = 3 + 4 * chunks
    return pl.pallas_call(
        functools.partial(ffn_kernel, chunks),
        grid_spec=pltpu.PrefetchScalarGridSpec(
            num_scalar_prefetch=1,
            grid=(2 * chunks,),
            in_specs=[
                whole_spec((tokens, width), **once),
                whole_spec(ctx_own.shape, **once),
                whole_spec(ctx_rest.shape, **once),
                whole_spec(w_output.shape, **once),
                whole_spec((tokens, width), **once),
            ]
            + [whole_spec(vector.shape, **once) for vector in vectors]
            + [whole_spec(b_in.shape, **once), anywhere, anywhere],
            out_specs=[
                whole_spec((tokens, 128)),
                whole_spec((8, width)),
                pl.BlockSpec((1, size), back),
            ]
            + [anywhere] * 7,
            scratch_shapes=[
                pltpu.VMEM((width, hidden), low_type),
                pltpu.VMEM((hidden, width), low_type),
                pltpu.VMEM((tokens, width), wide_type),
                pltpu.VMEM((tokens, width), wide_type),
                pltpu.VMEM((chunks, tokens, size), low_type),
                pltpu.VMEM((chunks, tokens, size), low_type),
            ]
            + [pltpu.VMEM((tokens, width), low_type)] * 4
            + [pltpu.VMEM((8, hidden), wide_type)]
            + [pltpu.SemaphoreType.DMA((2, blocks)), pltpu.SemaphoreType.DMA((copies,))],
        ),
        out_shape=[
            like((tokens, 128), wide_type),
            like((8, width), wide_type),
            like((1, hidden), wide_type),
            far_like((tokens, width)),
            far_like((tokens, width)),
            far_like((tokens, width), wide_type),
        ]
        + [far_like((hidden // 2, width))] * 4,
        compiler_params=large_room,
        cost_estimate=estimate(
            2 * tokens * width * (6 * hidden + width),
            2 * (tokens * 10 * width + 4 * hidden * width),
            tokens * hidden,
        ),
    )(slots, layer_in, ctx_own, ctx_rest, w_output, cotangent, *vectors, b_in, far(w_in), far(w_out))


def norm_back_kernel(
    index_ref,
    total_ref,
    normal_ref,
    rstd_ref,
    own_ref,
    rest_ref,
    wo_ref,
    gain_ref,
    sums_in_ref,
    gb_ref,
    *refs,
):
    branch_ref, down_ref, drest_ref, near_ref, far_ref, sums, acc, held, table = refs[-9:]
    step = pl.program_id(0)
    size = branch_ref.shape[0]
    head = index_ref[PARTS]
    gain_attn = gain_ref[...].reshape(1, total_ref.shape[1])
    heads = wo_ref.shape[0]
    rows = wo_ref.shape[1] // 4
    cols = wo_ref.shape[2] // 2

    @pl.when(step == 0)
    def _():
        sums[...] = sums_in_ref[...]

    def one(at):
        grad = total_ref[at, :]
        normal = normal_ref[at, :].astype(wide_type)
        scaled = grad * gain_attn
        rstd = rstd_ref[at, 0:1]
        grad_sum = rstd * (scaled - mean_last(scaled) - normal * mean_last(scaled * normal))
        grad_low = grad_sum.astype(low_type)
        branch_ref[at, :] = grad_low
        sums[3:4, :] += jnp.sum(grad * normal, 0, keepdims=True)
        sums[4:5, :] += jnp.sum(grad, 0, keepdims=True)
        sums[5:6, :] += jnp.sum(grad_low.astype(wide_type), 0, keepdims=True)

    tiles(size, 256, one)
    branch = branch_ref[...]
    for offset in range(heads):
        context = own_ref[0] if offset == 0 else rest_ref[offset - 1]
        weights = wo_ref[head ^ offset]
        grad_context = dot_nt(branch, weights).astype(low_type)
        if offset == 0:
            down_ref[0] = grad_context
        else:
            drest_ref[offset - 1] = grad_context
        part = dot_tn(context, branch)

        @pl.when(step == 0)
        def _():
            acc[offset] = part

        @pl.when(step > 0)
        def _():
            acc[offset] += part

    @pl.when(step == pl.num_programs(0) - 1)
    def _():
        table[...] = jnp.zeros_like(table)
        for which in range(6):
            for across in range(2):
                place = 2 * which + across
                table[place : place + 1, :] = sums[
                    which : which + 1, across * cols : (across + 1) * cols
                ]
        for slot in range(PARTS):
            table[pl.ds(12 + index_ref[slot], 1), :] = gb_ref[:, slot * cols : (slot + 1) * cols]
        for offset in range(heads):
            for part in range(PARTS):
                across, below = divmod(part, 4)
                block = acc[
                    offset,
                    below * rows : (below + 1) * rows,
                    across * cols : (across + 1) * cols,
                ].astype(low_type)
                row = table[pl.ds(part * heads + (head ^ offset), 1), :]
                held[part, offset, :, 0:cols] = block[0:32]
                held[part, offset, 0:16, cols:] = block[32:48]
                held[part, offset, 16:32, cols:] = jnp.broadcast_to(row, (16, cols)).astype(low_type)
        for slot in range(PARTS // 2):
            near_ref[slot] = held[index_ref[slot]]
            far_ref[slot] = held[index_ref[slot + PARTS // 2]]


def norm_back(
    index, total, normal, rstd, ctx_own, ctx_rest, w_output, gain, sums, gb, deps
):
    tokens, width = total.shape
    heads, group = w_output.shape[:2]
    size = tokens // 2
    tile = pl.BlockSpec((size, width), lambda i, *_: (i, 0))
    own = pl.BlockSpec((1, size, group), lambda i, *_: (0, i, 0))
    rest = pl.BlockSpec((heads - 1, size, group), lambda i, *_: (0, i, 0))
    half = (PARTS // 2, heads, (group // 4 + 16) // 2, width)
    return pl.pallas_call(
        norm_back_kernel,
        grid_spec=pltpu.PrefetchScalarGridSpec(
            num_scalar_prefetch=1,
            grid=(2,),
            in_specs=[
                tile,
                tile,
                pl.BlockSpec((size, 128), lambda i, *_: (i, 0)),
                own,
                rest,
                whole_spec(w_output.shape),
                whole_spec(gain.shape),
                whole_spec(sums.shape),
                whole_spec(gb.shape),
            ]
            + [anywhere] * len(deps),
            out_specs=[
                tile,
                own,
                rest,
                whole_spec(half),
                whole_spec(half),
            ],
            scratch_shapes=[
                pltpu.VMEM((8, width), wide_type),
                pltpu.VMEM((heads, group, width), wide_type),
                pltpu.VMEM((PARTS,) + half[1:], low_type),
                pltpu.VMEM((PARTS * heads, width // 2), wide_type),
            ],
        ),
        out_shape=[
            like((tokens, width)),
            like(ctx_own.shape),
            like(ctx_rest.shape),
            like(half),
            like(half),
        ],
        compiler_params=room,
        cost_estimate=estimate(
            4 * tokens * width * width, 2 * tokens * width * 8 + 6 * width * width
        ),
    )(index, far(total), far(normal), far(rstd), ctx_own, ctx_rest, w_output, gain, far(sums), far(gb), *[far(dep) for dep in deps])


def input_kernel(branch_ref, own_ref, shard_ref, rest_ref, weights_ref, *refs):
    total = branch_ref[...].astype(wide_type) + dot_nn(own_ref[0], shard_ref[0])
    for group in range(rest_ref.shape[0]):
        total += dot_nn(rest_ref[group], weights_ref[group])
    refs[-1][...] = total


def input_back(branch, own, shard, rest, weights, deps):
    tokens, width = branch.shape
    size = tokens // 2
    tile = pl.BlockSpec((size, width), lambda i: (i, 0))
    group = lambda value: pl.BlockSpec((value.shape[0], size, 640), lambda i: (0, i, 0))
    return pl.pallas_call(
        input_kernel,
        grid=(2,),
        in_specs=[tile, group(own), whole_spec(shard.shape), group(rest), whole_spec(weights.shape)]
        + [anywhere] * len(deps),
        out_specs=tile,
        out_shape=far_like((tokens, width), wide_type),
        compiler_params=room,
        cost_estimate=estimate(2 * tokens * width * 640 * 4, 16 * tokens * width),
    )(branch, own, shard, rest, weights, *[far(dep) for dep in deps])


def finish_kernel(heads, index_ref, *refs):
    owns, blocks = refs[0:2], refs[2:4]
    q_ref, k_ref, v_ref, wo_ref, bq_ref, bv_ref, gb_ref = refs[4:11]
    vectors = refs[11:17]
    held, back, table = refs[-3:]
    rows, cols = held.shape[1], held.shape[2] // 2
    head, row = index_ref[PARTS], index_ref[PARTS + 1]
    for slot in range(PARTS):
        part = index_ref[slot]
        half, place = divmod(slot, PARTS // 2)
        held[part] = owns[half][place]
        back[part] = blocks[half][place]
    whole = held[...].reshape(PARTS * rows, 2 * cols)
    for ref, first, second in ((q_ref, 0, 384), (k_ref, 128, 448), (v_ref, 256, 512)):
        ref[0:128, :] = whole[first : first + 128].astype(wide_type)
        ref[128:192, :] = whole[second : second + HD].astype(wide_type)
    sums = whole[576:592].astype(wide_type)[0:1]
    for ref, first, second in ((bq_ref, 0, 384), (bv_ref, 256, 512)):
        joined = jnp.concatenate([sums[:, first : first + 128], sums[:, second : second + HD]], 1)
        ref[...] = joined.reshape(ref.shape)
    for part in range(PARTS):
        across, down = divmod(part, 4)
        lanes = slice(across * cols, (across + 1) * cols)
        for offset in range(heads):
            other = head ^ offset
            block = back[part, offset].astype(wide_type)
            wo_ref[other, down * 48 : down * 48 + 32, lanes] = block[:, :cols]
            wo_ref[other, down * 48 + 32 : down * 48 + 48, lanes] = block[0:16, cols:]
            table[pl.ds(part * heads + other, 1), :] = block[16:17, cols:]
    for which, ref in enumerate(vectors):
        ref[...] = jnp.concatenate(
            [table[2 * which : 2 * which + 1], table[2 * which + 1 : 2 * which + 2]], 1
        ).reshape(ref.shape)
    block = gb_ref.shape[0]
    per_row = cols // block
    place = row * heads + head
    sums = table[pl.ds(12 + place // per_row, 1), :]
    total = jnp.zeros((1, block), wide_type)
    for which in range(per_row):
        total = jnp.where(
            place % per_row == which, sums[:, which * block : (which + 1) * block], total
        )
    gb_ref[...] = total.reshape(gb_ref.shape)


def finish(index, owns, blocks, block):
    rows = 640 // PARTS
    heads, extra, width = blocks[0].shape[1:]
    cols, group = width // 2, 192
    pieces = owns + blocks
    shapes = (
        [like((group, width), wide_type)] * 3
        + [like((heads, group, width), wide_type)]
        + [like((group,), wide_type)] * 2
        + [like((block,), wide_type)]
        + [like((width,), wide_type)] * 6
    )
    return pl.pallas_call(
        functools.partial(finish_kernel, heads),
        grid_spec=pltpu.PrefetchScalarGridSpec(
            num_scalar_prefetch=1,
            grid=(1,),
            in_specs=[whole_spec(piece.shape) for piece in pieces],
            out_specs=[whole_spec(shape.shape) for shape in shapes],
            scratch_shapes=[
                pltpu.VMEM((PARTS, rows, width), low_type),
                pltpu.VMEM((PARTS, heads, extra, width), low_type),
                pltpu.VMEM((PARTS * heads, cols), wide_type),
            ],
        ),
        out_shape=shapes,
        compiler_params=room,
        cost_estimate=estimate(0, 16 * width * width),
    )(index, *pieces)


def local(
    grid,
    layer_in,
    segment_ids,
    w_query,
    w_key,
    w_value,
    b_query,
    b_value,
    w_output,
    b_output,
    gain_attn,
    shift_attn,
    w_inner,
    b_inner,
    w_outer,
    b_outer,
    gain_ffn,
    shift_ffn,
    cotangent,
):
    tokens, width = layer_in.shape
    length = segment_ids.shape[1]
    group = w_query.shape[1]
    hidden = w_inner.shape[1]
    heads = grid.heads
    row = lax.axis_index("rows")
    head = lax.axis_index("heads")

    head_index = head.astype(jnp.int32)[None]
    part = grid.part_of(row.astype(jnp.int32))[None]
    shard, piece = pack(part, w_query.T, w_key.T, w_value.T, b_query, b_value)
    got = [grid.across_heads(piece, offset) for offset in range(1, heads)]
    q_own, k_own, v_own, ctx_own = attend_own(head_index, layer_in, shard, segment_ids)
    parts = jnp.concatenate([grid.part_of(grid.helper_parts()), head_index])

    row_slots = grid.row_slots()
    w_in, w_out, b_in = w_inner, w_outer, b_inner
    if not grid.native:
        w_in = jnp.take(w_in.reshape(width, grid.rows, -1), row_slots, axis=1).reshape(width, hidden)
        w_out = jnp.take(w_out.reshape(grid.rows, -1, width), row_slots, axis=0).reshape(hidden, width)
        b_in = jnp.take(b_in.reshape(grid.rows, -1), row_slots, axis=0).reshape(hidden)
    natural = jnp.arange(PARTS, dtype=jnp.int32)
    index = jnp.concatenate([row_slots if grid.native else natural, head_index])
    w_output_heads = w_output.reshape(heads, group, width)
    vectors = [b_output, gain_attn, shift_attn, b_outer, gain_ffn, shift_ffn]
    held = join(got, (k_own,))
    held = [held] + grid.across_chips([held] * 4)
    held = held + [grid.across_core(value) for value in held]

    q_rest, k_rest, v_rest, ctx_rest, w_rest = attend_rest(parts, layer_in, held, segment_ids)
    rstd, sums, gb_inner, normal, layer_out, total, outer_near, outer_far, inner_near, inner_far = ffn(
        index, layer_in, ctx_own, ctx_rest, w_output_heads, cotangent, vectors, w_in, w_out, b_in
    )
    slot_shape = (grid.rows // 2, hidden // grid.rows, width)
    outer_got = grid.across_core(outer_far.reshape(slot_shape))
    inner_got = grid.across_core(inner_far.reshape(slot_shape))
    if not grid.native:
        gb_inner = jnp.take(gb_inner.reshape(grid.rows, -1), grid.row_places(), axis=0).reshape(1, hidden)
    folded = functools.partial(fold, grid, head_index)
    first, second = grid.steps - 2, grid.steps - 1

    branch, dctx_own, dctx_rest, wo_near, wo_far = norm_back(
        index, total, normal, rstd, ctx_own, ctx_rest, w_output_heads, gain_attn, sums, gb_inner, ()
    )
    wo_near, wo_far = grid.spread_parts(wo_near, wo_far, True)

    ((outer, outer_send), (inner, inner_send)), (wo_far,) = folded(
        [
            ([outer_near.reshape(slot_shape), outer_got], "core"),
            ([inner_near.reshape(slot_shape), inner_got], "core"),
        ],
        (),
        (wo_far,),
    )
    outer_got = grid.across_chip(outer_send, first)
    inner_got = grid.across_chip(inner_send, first)
    wo_got = grid.across_core(wo_far)
    dqkv_rest, rest_near, rest_far = attend_back(
        index, layer_in, q_rest, k_rest, v_rest, ctx_rest, dctx_rest, (inner_send,), length
    )
    rest_near, rest_far = grid.spread_parts(rest_near, rest_far)
    ((outer, outer_send), (inner, inner_send), wo), (rest_far,) = folded(
        [
            ([outer, outer_got], "halves"),
            ([inner, inner_got], "halves"),
            ([wo_near, wo_got], "spread"),
        ],
        (),
        (rest_far,),
    )
    outer_got = grid.across_chip(outer_send, second)
    wo_got = grid.across_chips(wo)
    rest_got = grid.across_core(rest_far)
    dqkv_own, own_near, own_far = attend_back(
        index, layer_in, q_own, k_own, v_own, ctx_own, dctx_own, (wo[3],), length
    )
    own_near, own_far = grid.spread_parts(own_near, own_far)
    (outer, (rest, rest_send)), (own_far, inner_send) = folded(
        [
            ([outer[0], outer_got[0], wo[0]] + wo_got, "zpack"),
            ([rest_near, rest_got], "core"),
        ],
        (),
        (own_far, inner_send),
    )
    outer_got = [grid.across_heads(outer[offset], offset) for offset in range(1, heads)]
    inner_got = grid.across_chip(inner_send, second)
    rest_got = grid.across_chip(rest_send, first)
    input_grad = input_back(branch, dqkv_own, shard, dqkv_rest, w_rest, (rest_send,))
    ((upper, wo, *outer_send), (rest, rest_send), (inner,)), (own_far,) = folded(
        [
            ([outer[0]] + outer_got + list(outer[heads + 1 :]), "zsplit"),
            ([rest, rest_got], "halves"),
            ([inner[0], inner_got[0]], "sum"),
        ],
        (input_grad,),
        (own_far,),
    )
    outer_got = [grid.across_heads(outer_send[offset - 1], offset) for offset in range(1, heads)]
    rest_got = grid.across_chip(rest_send, second)
    own_got = grid.across_core(own_far)
    (rest, (out_w_outer, wo), own), _ = folded(
        [
            ([rest[0], rest_got[0]], "slots"),
            ([upper, outer[heads], wo] + outer_got, "zlast"),
            ([own_near, own_got], "spread"),
        ],
    )
    rest_got = [grid.across_heads(rest[offset - 1], offset) for offset in range(1, heads)]
    own_got = grid.across_chips(own)
    if grid.native:
        wo_got = grid.across_chips([wo] * 4)
    own = [value[0] for value in [own[0]] + own_got]
    ((own,), inner), _ = folded([(own + rest_got, "sum"), ([inner], "heads")])
    inner_got = [grid.across_heads(inner[offset], offset) for offset in range(1, heads)]
    if grid.native:
        own_got = grid.across_chips([own] * 4)
        ((out_w_inner,), (own,), (wo,)), _ = folded(
            [
                ([inner[0]] + inner_got, "wide"),
                ([own] + own_got, "stack"),
                ([wo] + wo_got, "stack"),
            ]
        )
        owns, blocks = [own, grid.across_core(own)], [wo, grid.across_core(wo)]
    else:
        ((out_w_inner,),), _ = folded([([inner[0]] + inner_got, "wide")])
        own = grid.gather_wide(own).reshape(PARTS, -1, width)
        wo = grid.coarse(grid.gather_wide(wo))
        owns, blocks = [own[: PARTS // 2], own[PARTS // 2 :]], [wo[: PARTS // 2], wo[PARTS // 2 :]]
    block = hidden // (grid.rows * heads)
    gw_query, gw_key, gw_value, gw_output, gb_query, gb_value, gb_inner, *vector = finish(
        jnp.concatenate([index, row.astype(jnp.int32)[None]]), owns, blocks, block
    )
    return (
        layer_out,
        input_grad,
        gw_query.T,
        gw_key.T,
        gw_value.T,
        gb_query,
        gb_value,
        gw_output.reshape(width, width),
        vector[5],
        vector[3],
        vector[4],
        out_w_inner.T,
        gb_inner,
        out_w_outer,
        vector[2],
        vector[0],
        vector[1],
    )


def solution(mesh):
    grid = Grid(mesh)
    return jax.shard_map(
        lambda *values: local(grid, *values),
        mesh=mesh,
        in_specs=(
            P(("rows", "heads"), None),
            P("rows", None),
            P(None, "heads"),
            P(None, "heads"),
            P(None, "heads"),
            P("heads"),
            P("heads"),
            P(),
            P(),
            P(),
            P(),
            P(),
            P(),
            P(),
            P(),
            P(),
            P(),
            P(("rows", "heads"), None),
        ),
        out_specs=(
            P(("rows", "heads"), None),
            P(("rows", "heads"), None),
            P(None, "heads"),
            P(None, "heads"),
            P(None, "heads"),
            P("heads"),
            P("heads"),
            P(),
            P(),
            P(),
            P(),
            P(None, ("rows", "heads")),
            P(("rows", "heads")),
            P(("rows", "heads"), None),
            P(),
            P(),
            P(),
        ),
        check_vma=False,
    )
```

```python
import functools

import jax
import jax.numpy as jnp
from jax import lax
from jax.experimental import pallas as pl
from jax.experimental.pallas import tpu as pltpu
from jax.sharding import PartitionSpec as P

HD = 64
PARTS = 8
epsilon = 1e-06
masked_score = -1000000000.0
low_type = jnp.bfloat16
wide_type = jnp.float32
room = pltpu.CompilerParams(vmem_limit_bytes=32 * 1024 * 1024)
large_room = pltpu.CompilerParams(vmem_limit_bytes=60 * 1024 * 1024)


def contract(left, right, left_dim, right_dim):
    return lax.dot_general(
        left, right, (((left_dim,), (right_dim,)), ((), ())), preferred_element_type=wide_type
    )


def dot_nn(left, right):
    return contract(left, right, 1, 0)


def dot_nt(left, right):
    return contract(left, right, 1, 1)


def dot_tn(left, right):
    return contract(left, right, 0, 0)


class Grid:
    def __init__(self, mesh):
        self.rows = mesh.shape["rows"]
        self.heads = mesh.shape["heads"]
        self.native = self.rows == PARTS
        self.steps = self.rows.bit_length() - 2
        up = list(range(1, self.steps + 1))
        self.orders = (up, up[::-1])

    def permute(self, value, row_masks, head_mask=0):
        pairs = [
            (row * self.heads + head, (row ^ row_masks[row & 1]) * self.heads + (head ^ head_mask))
            for row in range(self.rows)
            for head in range(self.heads)
        ]
        return lax.ppermute(value, ("rows", "heads"), pairs)

    def across_core(self, value):
        return self.permute(value, (1, 1))

    def across_heads(self, value, offset):
        return self.permute(value, (0, 0), offset)

    def across_chip(self, value, step):
        return self.permute(value, [1 << order[step] for order in self.orders])

    def across_chips(self, values):
        masks = [self.slot_masks(core) for core in (0, 1)]
        return [
            self.permute(value, (masks[0][slot], masks[1][slot]))
            for slot, value in enumerate(values)
            if slot
        ]

    def slot_masks(self, core):
        last = self.steps - 1
        masks = []
        for slot in range(1 << self.steps):
            mask = 0
            for step in range(self.steps):
                mask |= ((slot >> (last - step)) & 1) << self.orders[core][step]
            masks.append(mask)
        return masks

    def row_slots(self):
        row = lax.axis_index("rows").astype(jnp.int32)
        masks = jnp.array([self.slot_masks(0), self.slot_masks(1)], jnp.int32)
        core = row & 1
        return jnp.concatenate([row ^ masks[core], (row ^ 1) ^ masks[1 - core]])

    def row_places(self):
        row = lax.axis_index("rows").astype(jnp.int32)
        half = self.rows // 2
        inverse = []
        for core in (0, 1):
            table = [0] * half
            for slot, mask in enumerate(self.slot_masks(core)):
                table[mask >> 1] = slot
            inverse.append(table)
        inverse = jnp.array(inverse, jnp.int32)
        apart = jnp.arange(self.rows, dtype=jnp.int32) ^ row
        other = apart & 1
        return other * half + inverse[(row & 1) ^ other, apart >> 1]

    def helper_parts(self):
        row = lax.axis_index("rows").astype(jnp.int32)
        masks = jnp.array([self.slot_masks(0)[:4], self.slot_masks(1)[:4]], jnp.int32)
        core = row & 1
        return jnp.concatenate([row ^ masks[core], (row ^ 1) ^ masks[1 - core]])

    def part_of(self, row):
        if self.native:
            return row
        low, high = sorted(self.orders[0][-2:])
        return (row & 1) + 2 * ((row >> low) & 1) + 4 * ((row >> high) & 1)

    def scatter_wide(self, mine, got):
        held = add_like(mine, got)
        for step in range(self.steps - 2):
            half = held.shape[0] // 2
            held = add_like(held[:half], self.across_chip(held[half:], step))
        return held

    def gather_wide(self, value):
        held = jnp.stack([value] + self.across_chips([value] * 4))
        for step in reversed(range(self.steps - 2)):
            held = jnp.concatenate([held, self.across_chip(held, step)], 0)
        held = jnp.concatenate([held, self.across_core(held)], 0)
        return jnp.take(held, self.row_places(), axis=0)

    def coarse(self, blocks):
        half = blocks.shape[3] // 2
        blocks = jnp.concatenate([blocks[..., :half], blocks[..., half:]], 2)
        blocks = blocks.reshape((PARTS, -1) + blocks.shape[1:]).transpose(0, 2, 1, 3, 4)
        blocks = blocks.reshape(PARTS, blocks.shape[1], -1, half)
        middle = blocks.shape[2] // 2
        return jnp.concatenate([blocks[:, :, :middle], blocks[:, :, middle:]], 3)

    def spread_parts(self, near, far, paired=False):
        if self.native:
            return near, far
        parts = jnp.concatenate([near, far], 0)
        if paired:
            half = parts.shape[3] // 2
            parts = jnp.concatenate([parts[..., :half], parts[..., half:]], 2)
        count, rows, cols = parts.shape[1:]
        finer = self.rows // PARTS
        parts = parts.reshape(PARTS, count, finer, rows // finer, cols).transpose(0, 2, 1, 3, 4)
        parts = parts.reshape(self.rows, count, rows // finer, cols)
        parts = jnp.take(parts, self.row_slots(), axis=0)
        if paired:
            half = parts.shape[2] // 2
            parts = jnp.concatenate([parts[:, :, :half], parts[:, :, half:]], 3)
        return parts[: self.rows // 2], parts[self.rows // 2 :]


def add_like(first, second):
    return (first.astype(wide_type) + second.astype(wide_type)).astype(first.dtype)


def estimate(flops, moved, exps=0):
    return pl.CostEstimate(
        flops=flops, bytes_accessed=moved, transcendentals=exps
    )


def like(shape, dtype=low_type):
    return jax.ShapeDtypeStruct(shape, dtype)


def far(value):
    return pltpu.with_memory_space_constraint(value, pltpu.HBM)


def far_like(shape, dtype=low_type):
    return pltpu.HBM(shape, dtype)


def whole_spec(shape, **options):
    return pl.BlockSpec(shape, lambda *ids: (0,) * len(shape), **options)


anywhere = pl.BlockSpec(memory_space=pl.ANY)


def total_of(terms, cut):
    return sum(cut(term).astype(wide_type) for term in terms)


def fold_kernel(plan, passed, head_ref, *refs):
    outs = list(refs[len(refs) - passed - sum(job[2] for job in plan) : len(refs) - passed])
    refs = list(refs)
    for count, kind, given in plan:
        terms, refs = refs[:count], refs[count:]
        made, outs = outs[:given], outs[given:]
        if kind == "halves":
            size = made[0].shape[0]
            for half, target in enumerate(made):
                at = slice(half * size, (half + 1) * size)
                target[...] = total_of(terms, lambda term: term[at]).astype(target.dtype)
        elif kind == "slots":
            for slot, target in enumerate(made):
                target[...] = total_of(terms, lambda term: term[slot]).astype(target.dtype)
        elif kind == "heads" or kind == "zpack":
            heads = len(made) if kind == "heads" else len(made) // 2
            rows = terms[0].shape[0] // heads
            for offset in range(heads):
                begin = (head_ref[0] ^ offset) * rows
                if kind == "heads":
                    at = pl.ds(pl.multiple_of(begin, 16), rows)
                    made[offset][...] = total_of(terms, lambda term: term[at, :]).astype(low_type)
                    continue
                half = rows // 2
                upper = pl.ds(pl.multiple_of(begin, 16), half)
                lower = pl.ds(pl.multiple_of(begin + half, 16), half)
                target, other = made[offset], made[heads + offset]
                target[0:half] = total_of(terms[:2], lambda term: term[upper, :]).astype(low_type)
                target[half:] = total_of(terms[2:], lambda term: term[offset]).astype(low_type)
                other[...] = total_of(terms[:2], lambda term: term[lower, :]).astype(low_type)
        elif kind == "zsplit":
            rows = made[0].shape[0]
            made[0][...] = total_of(terms[:4], lambda term: term[0:rows])
            total = total_of(terms[:4], lambda term: term[rows:]).astype(low_type)
            made[1][...] = total
            for term, target in zip(terms[4:], made[2:]):
                target[0:rows] = term[...]
                target[rows:] = total
        elif kind == "zlast":
            rows = terms[0].shape[0]
            made[0][0:rows] = terms[0][...]
            made[0][rows:] = total_of(terms[1:2] + terms[3:], lambda term: term[0:rows])
            made[1][0] = terms[2][...]
            for place, term in enumerate(terms[3:]):
                made[1][place + 1] = term[rows:]
        elif kind == "stack":
            for place, term in enumerate(terms):
                made[0][place] = term[...]
        else:
            made[0][...] = total_of(terms, lambda term: term[...]).astype(made[0].dtype)


def fold(grid, head, jobs, deps=(), passes=()):
    if not grid.native:
        return [plain_job(grid, head, *job) for job in jobs], list(passes)
    plan, values, shapes = [], [], []
    for terms, kind in jobs:
        kind = {"core": "halves", "spread": "slots"}.get(kind, kind)
        shape = terms[0].shape
        if kind == "halves":
            made = [like((shape[0] // 2,) + shape[1:])] * 2
        elif kind == "slots":
            made = [like(shape[1:])] * shape[0]
        elif kind == "heads":
            made = [like((shape[0] // grid.heads, shape[1]))] * grid.heads
        elif kind == "zpack":
            rows = shape[0] // grid.heads // 2
            made = [like((rows + terms[2].shape[1], shape[1]))] * grid.heads
            made = made + [like((rows, shape[1]))] * grid.heads
        elif kind == "zsplit":
            rows = terms[4].shape[0]
            made = [like((rows, shape[1]), wide_type), like((shape[0] - rows, shape[1]))]
            made = made + [like(shape)] * 3
        elif kind == "zlast":
            made = [
                like((2 * shape[0], shape[1]), wide_type),
                like((len(terms) - 2,) + terms[2].shape),
            ]
        elif kind == "stack":
            made = [like((len(terms),) + shape)]
        else:
            made = [like(shape, wide_type if kind == "wide" else low_type)]
        plan.append((len(terms), kind, len(made)))
        values += terms
        shapes += made
    first, sums = 1 + len(values) + len(deps), len(shapes)
    outs = pl.pallas_call(
        functools.partial(fold_kernel, tuple(plan), len(passes)),
        grid_spec=pltpu.PrefetchScalarGridSpec(
            num_scalar_prefetch=1,
            grid=(1,),
            in_specs=[whole_spec(value.shape) for value in values]
            + [anywhere] * (len(deps) + len(passes)),
            out_specs=[whole_spec(shape.shape) for shape in shapes] + [anywhere] * len(passes),
        ),
        out_shape=shapes + [like(value.shape) for value in passes],
        input_output_aliases={first + place: sums + place for place in range(len(passes))},
        compiler_params=room,
        cost_estimate=estimate(0, sum(3 * value.size for value in values)),
    )(head, *values, *[far(dep) for dep in deps], *passes)
    results, place = [], 0
    for _, _, given in plan:
        results.append(outs[place : place + given])
        place += given
    return results, list(outs[sums:])


def plain_job(grid, head, terms, kind):
    whole = lambda term: term
    if kind in ("core", "spread"):
        held = grid.scatter_wide(*terms)
        return [held[:2], held[2:]] if kind == "core" else list(held)
    if kind == "stack":
        return [jnp.stack(terms)]
    if kind == "zsplit":
        rows = terms[4].shape[0]
        total = total_of(terms[:4], whole)
        small = total[rows:].astype(low_type)
        return [total[:rows], small] + [jnp.concatenate([term, small], 0) for term in terms[4:]]
    if kind == "zlast":
        rows = terms[0].shape[0]
        lower = total_of(terms[1:2] + terms[3:], lambda term: term[:rows])
        blocks = jnp.stack([terms[2]] + [term[rows:] for term in terms[3:]])
        return [jnp.concatenate([terms[0], lower], 0), blocks]
    if kind in ("heads", "zpack"):
        total = total_of(terms if kind == "heads" else terms[:2], whole).astype(low_type)
        total = total.reshape((grid.heads, -1) + total.shape[1:])
        made = [total[head[0] ^ offset] for offset in range(grid.heads)]
        if kind == "heads":
            return made
        wo = total_of(terms[2:], whole).astype(low_type)
        half = made[0].shape[0] // 2
        upper = [jnp.concatenate([made[offset][:half], wo[offset]], 0) for offset in range(grid.heads)]
        return upper + [block[half:] for block in made]
    total = total_of(terms, whole)
    if kind == "wide":
        return [total]
    total = total.astype(low_type)
    if kind == "halves":
        half = total.shape[0] // 2
        return [total[:half], total[half:]]
    return list(total) if kind == "slots" else [total]


def join_kernel(count, *refs):
    for slot in range(count):
        refs[-1][slot] = refs[slot][...]


def join(values, deps=()):
    shape = (len(values),) + values[0].shape
    return pl.pallas_call(
        functools.partial(join_kernel, len(values)),
        grid=(1,),
        in_specs=[whole_spec(value.shape) for value in values] + [anywhere] * len(deps),
        out_specs=whole_spec(shape),
        out_shape=like(shape),
        compiler_params=room,
        cost_estimate=estimate(0, 4 * values[0].size),
    )(*values, *[far(dep) for dep in deps])


def three_parts(values):
    first = values.astype(low_type).astype(wide_type)
    rest = values - first
    second = rest.astype(low_type).astype(wide_type)
    return first, second, (rest - second).astype(low_type).astype(wide_type)


def pair_up(low_lanes, first, second):
    return jnp.where(low_lanes, first, pltpu.roll(second, HD, 1))


def pack_kernel(index_ref, q_ref, k_ref, v_ref, bq_ref, bv_ref, w_ref, piece_ref):
    rows = piece_ref.shape[0]
    w_ref[0, 0:128, :] = q_ref[0:128, :]
    w_ref[0, 128:256, :] = k_ref[0:128, :]
    w_ref[0, 256:384, :] = v_ref[0:128, :]
    w_ref[0, 384:448, :] = q_ref[128:192, :]
    w_ref[0, 448:512, :] = k_ref[128:192, :]
    w_ref[0, 512:576, :] = v_ref[128:192, :]
    row = lax.broadcasted_iota(jnp.int32, (HD, w_ref.shape[2]), 0)
    bias_q = bq_ref[...].astype(wide_type).reshape(1, 192)
    bias_v = bv_ref[...].astype(wide_type).reshape(1, 192)
    gap = jnp.zeros((1, 128), wide_type)
    bias = [bias_q[:, 0:128], gap, bias_v[:, 0:128]]
    bias.append(jnp.concatenate([bias_q[:, 128:192], gap[:, :HD]], 1))
    bias.append(jnp.concatenate([bias_v[:, 128:192], gap[:, :HD]], 1))
    bias = jnp.concatenate(bias + [gap] * (w_ref.shape[2] // 128 - 5), 1)
    w_ref[0, 576:640, :] = jnp.where(row == 0, bias, 0.0).astype(low_type)
    mine = pl.multiple_of(index_ref[0] * rows, 16)
    piece_ref[...] = w_ref[0, pl.ds(mine, rows), :]


def pack(part, w_query, w_key, w_value, b_query, b_value):
    width = w_query.shape[1]
    rows = 640 // PARTS
    return pl.pallas_call(
        pack_kernel,
        grid_spec=pltpu.PrefetchScalarGridSpec(
            num_scalar_prefetch=1,
            grid=(1,),
            in_specs=[whole_spec(w_query.shape)] * 3 + [whole_spec(b_query.shape)] * 2,
            out_specs=[whole_spec((1, 640, width)), whole_spec((rows, width))],
        ),
        out_shape=[far_like((1, 640, width)), far_like((rows, width))],
        compiler_params=room,
        cost_estimate=estimate(0, 4 * width * 640),
    )(part, far(w_query), far(w_key), far(w_value), far(b_query), far(b_value))


def attend_body(device_head, x_ref, w_ref, seg_ref, q_ref, k_ref, v_ref, ctx_ref):
    length = seg_ref.shape[1]
    seqs = x_ref.shape[0] // length
    lane = lax.broadcasted_iota(jnp.int32, (1, 128), 1)
    low = lane < HD
    row8 = lax.broadcasted_iota(jnp.int32, (8, length), 0)
    bias_row = w_ref[0, 576:592, :][0:1, 0:640].astype(wide_type)
    for seq in range(seqs):
        at = slice(seq * length, (seq + 1) * length)
        qkv = (dot_nt(x_ref[at, :], w_ref[0]) + bias_row).astype(low_type).astype(wide_type)
        q01 = qkv[:, 0:128] * 0.125
        k01 = qkv[:, 128:256]
        v01 = qkv[:, 256:384]
        qk2 = qkv[:, 384:512]
        queries = [q01, pltpu.roll(q01, HD, 1), qk2 * 0.125]
        keys = [k01, pltpu.roll(k01, HD, 1), pltpu.roll(qk2, HD, 1)]
        values = [v01, pltpu.roll(v01, HD, 1), qkv[:, 512:640]]
        seg_row = seg_ref[pl.ds(device_head * seqs + seq, 1), :]
        seg_rows = jnp.broadcast_to(seg_row.astype(wide_type), (8, length))
        seg_col = seg_rows.T[:, 0:1].astype(jnp.int32) + HD
        same = lane == seg_col
        in_seg = (lane >= HD) & (lane < HD + 4)
        extra_q = jnp.where(same, 1.0, 0.0)
        extra_k = jnp.where(
            in_seg & ~same,
            masked_score,
            jnp.where((lane >= HD + 4) & (lane < HD + 7), 1.0, 0.0),
        )
        extra_v = jnp.where((lane >= HD) & (lane < HD + 3), 1.0, 0.0)
        contexts = []
        for head in range(3):
            query = jnp.where(low, queries[head], extra_q)
            key = jnp.where(low, keys[head], extra_k).astype(low_type)
            value = jnp.where(low, values[head], extra_v).astype(low_type)
            k_ref[0, head, at, :] = key
            v_ref[0, head, at, :] = value
            scores = dot_nt(key, query.astype(low_type))
            highest = jnp.max(scores, 0, keepdims=True)
            weights_low = jnp.exp(scores - highest).astype(low_type)
            summed = dot_tn(value, weights_low)
            total = summed[HD : HD + 1, :]
            first, second, third = three_parts(-(highest + jnp.log(total)))
            extra = jnp.where(
                row8 == 4, first, jnp.where(row8 == 5, second, jnp.where(row8 == 6, third, 0.0))
            )
            full = jnp.concatenate(
                [summed[:HD] * (1.0 / total), extra, jnp.zeros((56, length), wide_type)], 0
            ).T
            q_ref[0, head, at, :] = jnp.where(low, query, full + extra_q).astype(low_type)
            contexts.append(full)
        ctx_ref[0, at, 0:128] = pair_up(low, contexts[0], contexts[1]).astype(low_type)
        ctx_ref[0, at, 128:192] = contexts[2][:, :HD].astype(low_type)


def attend_own_kernel(head_ref, x_ref, w_ref, seg_ref, q_ref, k_ref, v_ref, ctx_ref):
    attend_body(head_ref[0], x_ref, w_ref, seg_ref, q_ref, k_ref, v_ref, ctx_ref)


def attend_rest_kernel(parts_ref, x_ref, seg_ref, *refs):
    pieces, (q_ref, k_ref, v_ref, ctx_ref, w_ref) = refs[:PARTS], refs[-5:]
    rows = pieces[0].shape[1]
    for slot in range(PARTS):
        at = pl.ds(pl.multiple_of(parts_ref[slot] * rows, 16), rows)
        w_ref[0, at, :] = pieces[slot][0]
    attend_body(parts_ref[PARTS], x_ref, w_ref, seg_ref, q_ref, k_ref, v_ref, ctx_ref)


def attend_cost(count, tokens, length, width):
    return estimate(
        count * (2 * tokens * width * 576 + 3 * 4 * tokens * length * 128),
        2 * tokens * width + count * 2 * (576 * width + 10 * tokens * 128),
        count * 3 * tokens * length,
    )


def attend_outputs(groups, tokens, start):
    heads = pl.BlockSpec((1, 3, tokens, 128), lambda g, *_: (g + start, 0, 0, 0))
    specs = [heads, heads, heads, pl.BlockSpec((1, tokens, 192), lambda g, *_: (g + start, 0, 0))]
    shapes = [far_like((groups, 3, tokens, 128))] * 3 + [far_like((groups, tokens, 192))]
    return specs, shapes


def attend_own(head, layer_in, shard, segments, groups):
    tokens, width = layer_in.shape
    specs, shapes = attend_outputs(groups, tokens, 0)
    return pl.pallas_call(
        attend_own_kernel,
        grid_spec=pltpu.PrefetchScalarGridSpec(
            num_scalar_prefetch=1,
            grid=(1,),
            in_specs=[
                whole_spec((tokens, width)),
                whole_spec(shard.shape),
                whole_spec(segments.shape),
            ],
            out_specs=specs,
        ),
        out_shape=shapes,
        compiler_params=room,
        cost_estimate=attend_cost(1, tokens, segments.shape[1], width),
    )(head, far(layer_in), far(shard), far(segments))


def attend_rest(parts, layer_in, pieces, segments, own):
    tokens, width = layer_in.shape
    count, rows, width = pieces[0].shape
    specs, shapes = attend_outputs(count + 1, tokens, 1)
    piece = pl.BlockSpec((1, rows, width), lambda g, *_: (g, 0, 0))
    return pl.pallas_call(
        attend_rest_kernel,
        grid_spec=pltpu.PrefetchScalarGridSpec(
            num_scalar_prefetch=1,
            grid=(count,),
            in_specs=[whole_spec((tokens, width)), whole_spec(segments.shape)]
            + [piece] * PARTS
            + [anywhere] * len(own),
            out_specs=specs + [pl.BlockSpec((1, 640, width), lambda g, *_: (g, 0, 0))],
        ),
        out_shape=shapes + [far_like((count, 640, width))],
        input_output_aliases={3 + PARTS + place: place for place in range(len(own))},
        compiler_params=room,
        cost_estimate=attend_cost(count, tokens, segments.shape[1], width),
    )(parts, far(layer_in), segments, *pieces, *[far(value) for value in own])


def attend_back_kernel(
    length,
    slots_ref,
    x_ref,
    q_ref,
    k_ref,
    v_ref,
    ctx_ref,
    dctx_ref,
    *refs,
):
    dqkv_ref, near_ref, far_ref, held = refs[-4:]
    tokens, width = x_ref.shape
    rows = 640 // PARTS
    lane = lax.broadcasted_iota(jnp.int32, (1, 128), 1)
    low = lane < HD
    for seq in range(tokens // length):
        at = slice(seq * length, (seq + 1) * length)
        grad01 = dctx_ref[0, at, 0:128].astype(wide_type)
        grad2 = dctx_ref[0, at, 128:192].astype(wide_type)
        both = grad01 * ctx_ref[0, at, 0:128].astype(wide_type)
        inner = [
            jnp.sum(jnp.where(low, both, 0.0), -1, keepdims=True),
            jnp.sum(jnp.where(low, 0.0, both), -1, keepdims=True),
            jnp.sum(grad2 * ctx_ref[0, at, 128:192].astype(wide_type), -1, keepdims=True),
        ]
        grads = [
            grad01,
            pltpu.roll(grad01, HD, 1),
            jnp.concatenate([grad2, jnp.zeros((length, HD), wide_type)], 1),
        ]
        grad_q, grad_k, grad_v = [], [], []
        for head in range(3):
            first, second, third = three_parts(-inner[head])
            extra = jnp.where(
                lane == HD,
                first,
                jnp.where(lane == HD + 1, second, jnp.where(lane == HD + 2, third, 0.0)),
            )
            grad = jnp.where(low, grads[head], extra).astype(low_type)
            query = q_ref[0, head, at, :]
            key = k_ref[0, head, at, :]
            probs = jnp.exp(dot_nt(key, query))
            grad_scores = (probs * dot_nt(v_ref[0, head, at, :], grad)).astype(low_type)
            grad_v.append(dot_nn(probs.astype(low_type), grad))
            grad_k.append(dot_nn(grad_scores, query))
            grad_q.append(dot_tn(key, grad_scores).T * 0.125)
        dqkv_ref[0, at, 0:128] = pair_up(low, grad_q[0], grad_q[1]).astype(low_type)
        dqkv_ref[0, at, 128:256] = pair_up(low, grad_k[0], grad_k[1]).astype(low_type)
        dqkv_ref[0, at, 256:384] = pair_up(low, grad_v[0], grad_v[1]).astype(low_type)
        dqkv_ref[0, at, 384:512] = pair_up(low, grad_q[2], grad_k[2]).astype(low_type)
        dqkv_ref[0, at, 512:640] = jnp.where(low, grad_v[2], 0.0).astype(low_type)
    grad_all = dqkv_ref[0]
    total = dot_tn(grad_all, x_ref[...])
    sums = jnp.sum(grad_all.astype(wide_type), 0, keepdims=True)
    sums = jnp.concatenate([sums, jnp.zeros((1, width - 640), wide_type)], 1)
    for part in range(PARTS):
        held[part] = total[part * rows : (part + 1) * rows].astype(low_type)
    row = lax.broadcasted_iota(jnp.int32, (HD, width), 0)
    spare = jnp.where(row == 0, sums, 0.0)
    held[PARTS - 1, rows - HD : rows] = spare.astype(low_type)
    for slot in range(PARTS // 2):
        near_ref[slot, 0] = held[slots_ref[slot]]
        far_ref[slot, 0] = held[slots_ref[slot + PARTS // 2]]


def attend_back(
    slots, layer_in, queries, keys, values, context, grad_context, deps, length
):
    tokens, width = layer_in.shape
    count = context.shape[0]
    rows = 640 // PARTS
    heads = pl.BlockSpec((1, 3, tokens, 128), lambda g, *_: (g, 0, 0, 0))
    group = pl.BlockSpec((1, tokens, 192), lambda g, *_: (g, 0, 0))
    half = pl.BlockSpec((PARTS // 2, 1, rows, width), lambda g, *_: (0, g, 0, 0))
    return pl.pallas_call(
        functools.partial(attend_back_kernel, length),
        grid_spec=pltpu.PrefetchScalarGridSpec(
            num_scalar_prefetch=1,
            grid=(count,),
            in_specs=[whole_spec((tokens, width)), heads, heads, heads, group, group]
            + [anywhere] * len(deps),
            out_specs=[pl.BlockSpec((1, tokens, 640), lambda g, *_: (g, 0, 0)), half, half],
            scratch_shapes=[pltpu.VMEM((PARTS, rows, width), low_type)],
        ),
        out_shape=[
            (far_like if count > 1 else like)((count, tokens, 640)),
            like((PARTS // 2, count, rows, width)),
            like((PARTS // 2, count, rows, width)),
        ],
        compiler_params=room,
        cost_estimate=estimate(
            count * (2 * tokens * width * 576 + 3 * 10 * tokens * length * 128),
            2 * tokens * width + count * 2 * (576 * width + 16 * tokens * 128),
            count * 3 * tokens * length,
        ),
    )(slots, far(layer_in), queries, keys, far(values), context, grad_context, *[far(dep) for dep in deps])


def mean_last(values):
    return jnp.mean(values, -1, keepdims=True)


def tiles(tokens, size, body):
    def step(index, carry):
        body(pl.ds(pl.multiple_of(index * size, size), size))
        return carry

    lax.fori_loop(0, tokens // size, step, 0)


def gelu_pair(values):
    cumulative = 0.5 * (1.0 + lax.erf(values * 0.7071067811865476))
    density = jnp.exp(-0.5 * values * values) * 0.3989422804014327
    return values * cumulative, cumulative + values * density


class Loads:
    def __init__(self, slots_ref, w_in_hbm, w_out_hbm, w_in, w_out, sems):
        self.count = sems.shape[1]
        self.size = w_out.shape[0] // self.count
        self.copies = []
        for slot in range(self.count):
            source = pl.ds(pl.multiple_of(slots_ref[slot] * self.size, 128), self.size)
            target = pl.ds(slot * self.size, self.size)
            self.copies.append(
                (
                    pltpu.make_async_copy(w_in_hbm.at[:, source], w_in.at[:, target], sems.at[0, slot]),
                    pltpu.make_async_copy(w_out_hbm.at[source], w_out.at[target], sems.at[1, slot]),
                )
            )

    def start(self):
        for copies in self.copies:
            for copy in copies:
                copy.start()

    def wait(self, low, high):
        for slot in range(-(-low // self.size), -(-high // self.size)):
            for copy in self.copies[slot]:
                copy.wait()


def overlaps(size, chunks, block, blocks):
    return [
        [
            (which, max(chunk * size, which * block), min((chunk + 1) * size, (which + 1) * block))
            for which in range(blocks)
            if max(chunk * size, which * block) < min((chunk + 1) * size, (which + 1) * block)
        ]
        for chunk in range(chunks)
    ]


def ffn_kernel(
    chunks,
    slots_ref,
    x_ref,
    ctx_ref,
    wo_ref,
    cot_ref,
    b_output_ref,
    gain_attn_ref,
    shift_attn_ref,
    b_outer_ref,
    gain_ffn_ref,
    shift_ffn_ref,
    b_in_ref,
    w_in_hbm,
    w_out_hbm,
    rstd_ref,
    sums_ref,
    gb_ref,
    normal_hbm,
    out_hbm,
    total_hbm,
    outer_near_hbm,
    outer_far_hbm,
    near_hbm,
    far_hbm,
    w_in,
    w_out,
    normed,
    outer,
    active,
    slope,
    low,
    normal_low,
    result_low,
    grad_out,
    b_row,
    sems,
    out_sems,
):
    step = pl.program_id(0)
    tokens, width = x_ref.shape
    hidden = w_out.shape[0]
    size = hidden // chunks
    half = hidden // 2
    loads = Loads(slots_ref, w_in_hbm, w_out_hbm, w_in, w_out, sems)
    head = slots_ref[loads.count]
    b_output, gain_attn, shift_attn, b_outer, gain_ffn, shift_ffn = (
        ref[...].reshape(1, width)
        for ref in (
            b_output_ref,
            gain_attn_ref,
            shift_attn_ref,
            b_outer_ref,
            gain_ffn_ref,
            shift_ffn_ref,
        )
    )
    small = [
        pltpu.make_async_copy(source, target, out_sems.at[place])
        for place, (source, target) in enumerate(
            ((normal_low, normal_hbm), (result_low, out_hbm), (outer, total_hbm))
        )
    ]
    count = len(small)
    outer_copies, inner_copies = [], []
    for chunk, cuts in enumerate(overlaps(size, chunks, half, 2)):
        from_active, from_out = [], []
        for which, begin, end in cuts:
            at = pl.ds(begin - which * half, end - begin)
            from_active.append(
                pltpu.make_async_copy(
                    active.at[chunk, pl.ds(begin - chunk * size, end - begin), pl.ds(0, width)],
                    (outer_near_hbm, outer_far_hbm)[which].at[at],
                    out_sems.at[count],
                )
            )
            from_out.append(
                pltpu.make_async_copy(
                    w_out.at[pl.ds(begin, end - begin)],
                    (near_hbm, far_hbm)[which].at[at],
                    out_sems.at[count + 1],
                )
            )
            count += 2
        outer_copies.append(from_active)
        inner_copies.append(from_out)

    @pl.when(step == 0)
    def _():
        loads.start()
        b_row[1:2, :] = b_in_ref[...].reshape(1, hidden)
        for slot in range(loads.count):
            source = pl.ds(pl.multiple_of(slots_ref[slot] * loads.size, 128), loads.size)
            b_row[0:1, slot * loads.size : (slot + 1) * loads.size] = b_row[1:2, source]
        outer[...] = jnp.zeros_like(outer)
        branch = dot_nn(ctx_ref[0], wo_ref[head])
        for offset in range(1, wo_ref.shape[0]):
            branch += dot_nn(ctx_ref[offset], wo_ref[head ^ offset])
        normed[...] = branch

        def one(at):
            total = x_ref[at, :].astype(wide_type) + (normed[at, :] + b_output)
            centred = total - mean_last(total)
            rstd = lax.rsqrt(mean_last(centred * centred) + epsilon)
            normal = centred * rstd
            result = normal * gain_attn + shift_attn
            normed[at, :] = result
            low[at, :] = result.astype(low_type)
            normal_low[at, :] = normal.astype(low_type)
            rstd_ref[at, :] = jnp.broadcast_to(rstd, (rstd.shape[0], 128))

        tiles(tokens, 256, one)
        small[0].start()

    for chunk in range(chunks):

        @pl.when(step == chunk)
        def _():
            loads.wait(chunk * size, (chunk + 1) * size)

    @pl.when(step < chunks)
    def _():
        at = pl.ds(pl.multiple_of(step * size, 128), size)
        inner = dot_nn(low[...], w_in[:, at]) + b_row[0:1, at]
        values, gradient = gelu_pair(inner)
        values = values.astype(low_type)
        active[step] = values
        slope[step] = gradient.astype(low_type)
        outer[...] += dot_nn(values, w_out[at, :])

    @pl.when(step == chunks - 1)
    def _():
        sums_ref[...] = jnp.zeros_like(sums_ref)

        def one(at):
            total = normed[at, :] + (outer[at, :] + b_outer)
            centred = total - mean_last(total)
            rstd = lax.rsqrt(mean_last(centred * centred) + epsilon)
            normal = centred * rstd
            result_low[at, :] = (normal * gain_ffn + shift_ffn).astype(low_type)
            grad = cot_ref[at, :].astype(wide_type)
            scaled = grad * gain_ffn
            grad_sum = rstd * (scaled - mean_last(scaled) - normal * mean_last(scaled * normal))
            grad_low = grad_sum.astype(low_type)
            grad_out[at, :] = grad_low
            outer[at, :] = grad_low.astype(wide_type)
            sums_ref[0:1, :] += jnp.sum(grad * normal, 0, keepdims=True)
            sums_ref[1:2, :] += jnp.sum(grad, 0, keepdims=True)
            sums_ref[2:3, :] += jnp.sum(grad_low.astype(wide_type), 0, keepdims=True)

        tiles(tokens, 256, one)
        small[1].start()

    @pl.when(step >= chunks)
    def _():
        which = step - chunks
        at = pl.ds(pl.multiple_of(which * size, 128), size)
        grad = grad_out[...]
        active[which, :, 0:width] = dot_tn(active[which], grad).astype(low_type)
        grad_inner = (dot_nt(grad, w_out[at, :]) * slope[which].astype(wide_type)).astype(low_type)
        gb_ref[...] = jnp.sum(grad_inner.astype(wide_type), 0, keepdims=True)
        w_out[at, :] = dot_tn(grad_inner, low[...]).astype(low_type)
        outer[...] += dot_nt(grad_inner, w_in[:, at])

    for chunk in range(chunks):

        @pl.when(step == chunks + chunk)
        def _():
            for copy in outer_copies[chunk] + inner_copies[chunk]:
                copy.start()

    @pl.when(step == 2 * chunks - 1)
    def _():
        small[2].start()
        for copy in small:
            copy.wait()
        for copies in outer_copies + inner_copies:
            for copy in copies:
                copy.wait()


def ffn(slots, layer_in, context, w_output, cotangent, vectors, w_in, w_out, b_in):
    tokens, width = layer_in.shape
    hidden = w_out.shape[0]
    chunks = 3
    blocks = slots.shape[0] - 1
    size = hidden // chunks
    back = lambda i, *_: (0, jnp.maximum(i - chunks, 0))
    once = dict(pipeline_mode=pl.Buffered(1))
    copies = 3 + 4 * chunks
    return pl.pallas_call(
        functools.partial(ffn_kernel, chunks),
        grid_spec=pltpu.PrefetchScalarGridSpec(
            num_scalar_prefetch=1,
            grid=(2 * chunks,),
            in_specs=[
                whole_spec((tokens, width), **once),
                whole_spec(context.shape, **once),
                whole_spec(w_output.shape, **once),
                whole_spec((tokens, width), **once),
            ]
            + [whole_spec(vector.shape, **once) for vector in vectors]
            + [whole_spec(b_in.shape, **once), anywhere, anywhere],
            out_specs=[
                whole_spec((tokens, 128)),
                whole_spec((8, width)),
                pl.BlockSpec((1, size), back),
            ]
            + [anywhere] * 7,
            scratch_shapes=[
                pltpu.VMEM((width, hidden), low_type),
                pltpu.VMEM((hidden, width), low_type),
                pltpu.VMEM((tokens, width), wide_type),
                pltpu.VMEM((tokens, width), wide_type),
                pltpu.VMEM((chunks, tokens, size), low_type),
                pltpu.VMEM((chunks, tokens, size), low_type),
            ]
            + [pltpu.VMEM((tokens, width), low_type)] * 4
            + [pltpu.VMEM((8, hidden), wide_type)]
            + [pltpu.SemaphoreType.DMA((2, blocks)), pltpu.SemaphoreType.DMA((copies,))],
        ),
        out_shape=[
            like((tokens, 128), wide_type),
            like((8, width), wide_type),
            like((1, hidden), wide_type),
            far_like((tokens, width)),
            far_like((tokens, width)),
            far_like((tokens, width), wide_type),
        ]
        + [far_like((hidden // 2, width))] * 4,
        compiler_params=large_room,
        cost_estimate=estimate(
            2 * tokens * width * (6 * hidden + width),
            2 * (tokens * 10 * width + 4 * hidden * width),
            tokens * hidden,
        ),
    )(slots, layer_in, context, w_output, cotangent, *vectors, b_in, far(w_in), far(w_out))


def norm_back_kernel(
    index_ref,
    total_ref,
    normal_ref,
    rstd_ref,
    ctx_ref,
    wo_ref,
    gain_ref,
    sums_in_ref,
    gb_ref,
    *refs,
):
    branch_ref, dctx_ref, near_ref, far_ref, sums, acc, held, table = refs[-8:]
    step = pl.program_id(0)
    size = branch_ref.shape[0]
    head = index_ref[PARTS]
    gain_attn = gain_ref[...].reshape(1, total_ref.shape[1])
    heads = wo_ref.shape[0]
    rows = wo_ref.shape[1] // 4
    cols = wo_ref.shape[2] // 2

    @pl.when(step == 0)
    def _():
        sums[...] = sums_in_ref[...]

    def one(at):
        grad = total_ref[at, :]
        normal = normal_ref[at, :].astype(wide_type)
        scaled = grad * gain_attn
        rstd = rstd_ref[at, 0:1]
        grad_sum = rstd * (scaled - mean_last(scaled) - normal * mean_last(scaled * normal))
        grad_low = grad_sum.astype(low_type)
        branch_ref[at, :] = grad_low
        sums[3:4, :] += jnp.sum(grad * normal, 0, keepdims=True)
        sums[4:5, :] += jnp.sum(grad, 0, keepdims=True)
        sums[5:6, :] += jnp.sum(grad_low.astype(wide_type), 0, keepdims=True)

    tiles(size, 256, one)
    branch = branch_ref[...]
    for offset in range(heads):
        context = ctx_ref[offset]
        weights = wo_ref[head ^ offset]
        grad_context = dot_nt(branch, weights).astype(low_type)
        dctx_ref[offset] = grad_context
        part = dot_tn(context, branch)

        @pl.when(step == 0)
        def _():
            acc[offset] = part

        @pl.when(step > 0)
        def _():
            acc[offset] += part

    @pl.when(step == pl.num_programs(0) - 1)
    def _():
        table[...] = jnp.zeros_like(table)
        for which in range(6):
            for across in range(2):
                place = 2 * which + across
                table[place : place + 1, :] = sums[
                    which : which + 1, across * cols : (across + 1) * cols
                ]
        for slot in range(PARTS):
            table[pl.ds(12 + index_ref[slot], 1), :] = gb_ref[:, slot * cols : (slot + 1) * cols]
        for offset in range(heads):
            for part in range(PARTS):
                across, below = divmod(part, 4)
                block = acc[
                    offset,
                    below * rows : (below + 1) * rows,
                    across * cols : (across + 1) * cols,
                ].astype(low_type)
                row = table[pl.ds(part * heads + (head ^ offset), 1), :]
                held[part, offset, :, 0:cols] = block[0:32]
                held[part, offset, 0:16, cols:] = block[32:48]
                held[part, offset, 16:32, cols:] = jnp.broadcast_to(row, (16, cols)).astype(low_type)
        for slot in range(PARTS // 2):
            near_ref[slot] = held[index_ref[slot]]
            far_ref[slot] = held[index_ref[slot + PARTS // 2]]


def norm_back(
    index, total, normal, rstd, context, w_output, gain, sums, gb, deps
):
    tokens, width = total.shape
    heads, group = w_output.shape[:2]
    size = tokens
    tile = pl.BlockSpec((size, width), lambda i, *_: (i, 0))
    groups = pl.BlockSpec((heads, size, group), lambda i, *_: (0, i, 0))
    half = (PARTS // 2, heads, (group // 4 + 16) // 2, width)
    return pl.pallas_call(
        norm_back_kernel,
        grid_spec=pltpu.PrefetchScalarGridSpec(
            num_scalar_prefetch=1,
            grid=(1,),
            in_specs=[
                tile,
                tile,
                pl.BlockSpec((size, 128), lambda i, *_: (i, 0)),
                groups,
                whole_spec(w_output.shape),
                whole_spec(gain.shape),
                whole_spec(sums.shape),
                whole_spec(gb.shape),
            ]
            + [anywhere] * len(deps),
            out_specs=[
                tile,
                groups,
                whole_spec(half),
                whole_spec(half),
            ],
            scratch_shapes=[
                pltpu.VMEM((8, width), wide_type),
                pltpu.VMEM((heads, group, width), wide_type),
                pltpu.VMEM((PARTS,) + half[1:], low_type),
                pltpu.VMEM((PARTS * heads, width // 2), wide_type),
            ],
        ),
        out_shape=[
            like((tokens, width)),
            like(context.shape),
            like(half),
            like(half),
        ],
        compiler_params=room,
        cost_estimate=estimate(
            4 * tokens * width * width, 2 * tokens * width * 8 + 6 * width * width
        ),
    )(index, far(total), far(normal), far(rstd), far(context), far(w_output), gain, far(sums), far(gb), *[far(dep) for dep in deps])


def input_kernel(branch_ref, grads_ref, shard_ref, weights_ref, *refs):
    total = branch_ref[...].astype(wide_type) + dot_nn(grads_ref[0], shard_ref[0])
    for group in range(weights_ref.shape[0]):
        total += dot_nn(grads_ref[group + 1], weights_ref[group])
    refs[-1][...] = total


def input_back(branch, grads, shard, weights, deps):
    tokens, width = branch.shape
    size = tokens // 2
    tile = pl.BlockSpec((size, width), lambda i: (i, 0))
    groups = pl.BlockSpec((grads.shape[0], size, 640), lambda i: (0, i, 0))
    return pl.pallas_call(
        input_kernel,
        grid=(2,),
        in_specs=[tile, groups, whole_spec(shard.shape), whole_spec(weights.shape)]
        + [anywhere] * len(deps),
        out_specs=tile,
        out_shape=far_like((tokens, width), wide_type),
        compiler_params=room,
        cost_estimate=estimate(2 * tokens * width * 640 * 4, 16 * tokens * width),
    )(branch, grads, shard, weights, *[far(dep) for dep in deps])


def finish_kernel(heads, index_ref, *refs):
    owns, blocks = refs[0:2], refs[2:4]
    q_ref, k_ref, v_ref, wo_ref, bq_ref, bv_ref, gb_ref = refs[4:11]
    vectors = refs[11:17]
    held, back, table = refs[-3:]
    rows, cols = held.shape[1], held.shape[2] // 2
    head, row = index_ref[PARTS], index_ref[PARTS + 1]
    for slot in range(PARTS):
        part = index_ref[slot]
        half, place = divmod(slot, PARTS // 2)
        held[part] = owns[half][place]
        back[part] = blocks[half][place]
    whole = held[...].reshape(PARTS * rows, 2 * cols)
    for ref, first, second in ((q_ref, 0, 384), (k_ref, 128, 448), (v_ref, 256, 512)):
        ref[0:128, :] = whole[first : first + 128].astype(wide_type)
        ref[128:192, :] = whole[second : second + HD].astype(wide_type)
    sums = whole[576:592].astype(wide_type)[0:1]
    for ref, first, second in ((bq_ref, 0, 384), (bv_ref, 256, 512)):
        joined = jnp.concatenate([sums[:, first : first + 128], sums[:, second : second + HD]], 1)
        ref[...] = joined.reshape(ref.shape)
    for part in range(PARTS):
        across, down = divmod(part, 4)
        lanes = slice(across * cols, (across + 1) * cols)
        for offset in range(heads):
            other = head ^ offset
            block = back[part, offset].astype(wide_type)
            wo_ref[other, down * 48 : down * 48 + 32, lanes] = block[:, :cols]
            wo_ref[other, down * 48 + 32 : down * 48 + 48, lanes] = block[0:16, cols:]
            table[pl.ds(part * heads + other, 1), :] = block[16:17, cols:]
    for which, ref in enumerate(vectors):
        ref[...] = jnp.concatenate(
            [table[2 * which : 2 * which + 1], table[2 * which + 1 : 2 * which + 2]], 1
        ).reshape(ref.shape)
    block = gb_ref.shape[0]
    per_row = cols // block
    place = row * heads + head
    sums = table[pl.ds(12 + place // per_row, 1), :]
    total = jnp.zeros((1, block), wide_type)
    for which in range(per_row):
        total = jnp.where(
            place % per_row == which, sums[:, which * block : (which + 1) * block], total
        )
    gb_ref[...] = total.reshape(gb_ref.shape)


def finish(index, owns, blocks, block):
    rows = 640 // PARTS
    heads, extra, width = blocks[0].shape[1:]
    cols, group = width // 2, 192
    pieces = owns + blocks
    shapes = (
        [like((group, width), wide_type)] * 3
        + [like((heads, group, width), wide_type)]
        + [like((group,), wide_type)] * 2
        + [like((block,), wide_type)]
        + [like((width,), wide_type)] * 6
    )
    return pl.pallas_call(
        functools.partial(finish_kernel, heads),
        grid_spec=pltpu.PrefetchScalarGridSpec(
            num_scalar_prefetch=1,
            grid=(1,),
            in_specs=[whole_spec(piece.shape) for piece in pieces],
            out_specs=[whole_spec(shape.shape) for shape in shapes],
            scratch_shapes=[
                pltpu.VMEM((PARTS, rows, width), low_type),
                pltpu.VMEM((PARTS, heads, extra, width), low_type),
                pltpu.VMEM((PARTS * heads, cols), wide_type),
            ],
        ),
        out_shape=shapes,
        compiler_params=room,
        cost_estimate=estimate(0, 16 * width * width),
    )(index, *pieces)


def local(
    grid,
    layer_in,
    segment_ids,
    w_query,
    w_key,
    w_value,
    b_query,
    b_value,
    w_output,
    b_output,
    gain_attn,
    shift_attn,
    w_inner,
    b_inner,
    w_outer,
    b_outer,
    gain_ffn,
    shift_ffn,
    cotangent,
):
    tokens, width = layer_in.shape
    length = segment_ids.shape[1]
    group = w_query.shape[1]
    hidden = w_inner.shape[1]
    heads = grid.heads
    row = lax.axis_index("rows")
    head = lax.axis_index("heads")

    head_index = head.astype(jnp.int32)[None]
    part = grid.part_of(row.astype(jnp.int32))[None]
    shard, piece = pack(part, w_query.T, w_key.T, w_value.T, b_query, b_value)
    got = [grid.across_heads(piece, offset) for offset in range(1, heads)]
    own = attend_own(head_index, layer_in, shard, segment_ids, heads)
    parts = jnp.concatenate([grid.part_of(grid.helper_parts()), head_index])

    row_slots = grid.row_slots()
    w_in, w_out, b_in = w_inner, w_outer, b_inner
    if not grid.native:
        w_in = jnp.take(w_in.reshape(width, grid.rows, -1), row_slots, axis=1).reshape(width, hidden)
        w_out = jnp.take(w_out.reshape(grid.rows, -1, width), row_slots, axis=0).reshape(hidden, width)
        b_in = jnp.take(b_in.reshape(grid.rows, -1), row_slots, axis=0).reshape(hidden)
    natural = jnp.arange(PARTS, dtype=jnp.int32)
    index = jnp.concatenate([row_slots if grid.native else natural, head_index])
    w_output_heads = w_output.reshape(heads, group, width)
    vectors = [b_output, gain_attn, shift_attn, b_outer, gain_ffn, shift_ffn]
    held = join(got, (own[1],))
    held = [held] + grid.across_chips([held] * 4)
    held = held + [grid.across_core(value) for value in held]

    queries, keys, values, context, w_rest = attend_rest(parts, layer_in, held, segment_ids, own)
    rstd, sums, gb_inner, normal, layer_out, total, outer_near, outer_far, inner_near, inner_far = ffn(
        index, layer_in, context, w_output_heads, cotangent, vectors, w_in, w_out, b_in
    )
    slot_shape = (grid.rows // 2, hidden // grid.rows, width)
    outer_got = grid.across_core(outer_far.reshape(slot_shape))
    inner_got = grid.across_core(inner_far.reshape(slot_shape))
    if not grid.native:
        gb_inner = jnp.take(gb_inner.reshape(grid.rows, -1), grid.row_places(), axis=0).reshape(1, hidden)
    folded = functools.partial(fold, grid, head_index)
    first, second = grid.steps - 2, grid.steps - 1

    branch, grad_context, wo_near, wo_far = norm_back(
        index, total, normal, rstd, context, w_output_heads, gain_attn, sums, gb_inner, ()
    )
    wo_near, wo_far = grid.spread_parts(wo_near, wo_far, True)

    ((outer, outer_send), (inner, inner_send)), (wo_far,) = folded(
        [
            ([outer_near.reshape(slot_shape), outer_got], "core"),
            ([inner_near.reshape(slot_shape), inner_got], "core"),
        ],
        (),
        (wo_far,),
    )
    outer_got = grid.across_chip(outer_send, first)
    inner_got = grid.across_chip(inner_send, first)
    wo_got = grid.across_core(wo_far)
    grads, near, far_half = attend_back(
        index, layer_in, queries, keys, values, context, grad_context, (inner_send,), length
    )
    near, far_half = grid.spread_parts(near, far_half)
    ((outer, outer_send), (inner, inner_send), wo), (far_half,) = folded(
        [
            ([outer, outer_got], "halves"),
            ([inner, inner_got], "halves"),
            ([wo_near, wo_got], "spread"),
        ],
        (),
        (far_half,),
    )
    outer_got = grid.across_chip(outer_send, second)
    wo_got = grid.across_chips(wo)
    got = grid.across_core(far_half)
    input_grad = input_back(branch, grads, shard, w_rest, (wo[3],))
    (outer, (near, send)), (inner_send,) = folded(
        [
            ([outer[0], outer_got[0], wo[0]] + wo_got, "zpack"),
            ([near, got], "core"),
        ],
        (input_grad,),
        (inner_send,),
    )
    outer_got = [grid.across_heads(outer[offset], offset) for offset in range(1, heads)]
    got = grid.across_chip(send, first)
    ((upper, wo, *outer_send), (near, send)), (inner_send,) = folded(
        [
            ([outer[0]] + outer_got + list(outer[heads + 1 :]), "zsplit"),
            ([near, got], "halves"),
        ],
        (),
        (inner_send,),
    )
    outer_got = [grid.across_heads(outer_send[offset - 1], offset) for offset in range(1, heads)]
    got = grid.across_chip(send, second)
    inner_got = grid.across_chip(inner_send, second)
    (groups, (out_w_outer, wo), inner), _ = folded(
        [
            ([near[0], got[0]], "slots"),
            ([upper, outer[heads], wo] + outer_got, "zlast"),
            ([inner[0], inner_got[0]], "heads"),
        ],
    )
    got = [grid.across_heads(groups[offset], offset) for offset in range(1, heads)]
    if grid.native:
        wo_got = grid.across_chips([wo] * 4)
    ((own,),), inner = folded([([groups[0]] + got, "sum")], (), inner)
    inner_got = [grid.across_heads(inner[offset], offset) for offset in range(1, heads)]
    if grid.native:
        own_got = grid.across_chips([own] * 4)
        ((out_w_inner,), (own,), (wo,)), _ = folded(
            [
                ([inner[0]] + inner_got, "wide"),
                ([own] + own_got, "stack"),
                ([wo] + wo_got, "stack"),
            ]
        )
        owns, blocks = [own, grid.across_core(own)], [wo, grid.across_core(wo)]
    else:
        ((out_w_inner,),), _ = folded([([inner[0]] + inner_got, "wide")])
        own = grid.gather_wide(own).reshape(PARTS, -1, width)
        wo = grid.coarse(grid.gather_wide(wo))
        owns, blocks = [own[: PARTS // 2], own[PARTS // 2 :]], [wo[: PARTS // 2], wo[PARTS // 2 :]]
    block = hidden // (grid.rows * heads)
    gw_query, gw_key, gw_value, gw_output, gb_query, gb_value, gb_inner, *vector = finish(
        jnp.concatenate([index, row.astype(jnp.int32)[None]]), owns, blocks, block
    )
    return (
        layer_out,
        input_grad,
        gw_query.T,
        gw_key.T,
        gw_value.T,
        gb_query,
        gb_value,
        gw_output.reshape(width, width),
        vector[5],
        vector[3],
        vector[4],
        out_w_inner.T,
        gb_inner,
        out_w_outer,
        vector[2],
        vector[0],
        vector[1],
    )


def solution(mesh):
    grid = Grid(mesh)
    return jax.shard_map(
        lambda *values: local(grid, *values),
        mesh=mesh,
        in_specs=(
            P(("rows", "heads"), None),
            P("rows", None),
            P(None, "heads"),
            P(None, "heads"),
            P(None, "heads"),
            P("heads"),
            P("heads"),
            P(),
            P(),
            P(),
            P(),
            P(),
            P(),
            P(),
            P(),
            P(),
            P(),
            P(("rows", "heads"), None),
        ),
        out_specs=(
            P(("rows", "heads"), None),
            P(("rows", "heads"), None),
            P(None, "heads"),
            P(None, "heads"),
            P(None, "heads"),
            P("heads"),
            P("heads"),
            P(),
            P(),
            P(),
            P(),
            P(None, ("rows", "heads")),
            P(("rows", "heads")),
            P(("rows", "heads"), None),
            P(),
            P(),
            P(),
        ),
        check_vma=False,
    )
```

```python
import functools

import jax
import jax.numpy as jnp
from jax import lax
from jax.experimental import pallas as pl
from jax.experimental.pallas import tpu as pltpu
from jax.sharding import PartitionSpec as P

HD = 64
PARTS = 8
epsilon = 1e-06
masked_score = -1000000000.0
low_type = jnp.bfloat16
wide_type = jnp.float32
room = pltpu.CompilerParams(vmem_limit_bytes=32 * 1024 * 1024)
large_room = pltpu.CompilerParams(vmem_limit_bytes=60 * 1024 * 1024)


def contract(left, right, left_dim, right_dim):
    return lax.dot_general(
        left, right, (((left_dim,), (right_dim,)), ((), ())), preferred_element_type=wide_type
    )


def dot_nn(left, right):
    return contract(left, right, 1, 0)


def dot_nt(left, right):
    return contract(left, right, 1, 1)


def dot_tn(left, right):
    return contract(left, right, 0, 0)


class Grid:
    def __init__(self, mesh):
        self.rows = mesh.shape["rows"]
        self.heads = mesh.shape["heads"]
        self.native = self.rows == PARTS
        self.steps = self.rows.bit_length() - 2
        up = list(range(1, self.steps + 1))
        self.orders = (up, up[::-1])

    def permute(self, value, row_masks, head_mask=0):
        pairs = [
            (row * self.heads + head, (row ^ row_masks[row & 1]) * self.heads + (head ^ head_mask))
            for row in range(self.rows)
            for head in range(self.heads)
        ]
        return lax.ppermute(value, ("rows", "heads"), pairs)

    def across_core(self, value):
        return self.permute(value, (1, 1))

    def across_heads(self, value, offset):
        return self.permute(value, (0, 0), offset)

    def across_chip(self, value, step):
        return self.permute(value, [1 << order[step] for order in self.orders])

    def across_chips(self, values):
        masks = [self.slot_masks(core) for core in (0, 1)]
        return [
            self.permute(value, (masks[0][slot], masks[1][slot]))
            for slot, value in enumerate(values)
            if slot
        ]

    def slot_masks(self, core):
        last = self.steps - 1
        masks = []
        for slot in range(1 << self.steps):
            mask = 0
            for step in range(self.steps):
                mask |= ((slot >> (last - step)) & 1) << self.orders[core][step]
            masks.append(mask)
        return masks

    def row_slots(self):
        row = lax.axis_index("rows").astype(jnp.int32)
        masks = jnp.array([self.slot_masks(0), self.slot_masks(1)], jnp.int32)
        core = row & 1
        return jnp.concatenate([row ^ masks[core], (row ^ 1) ^ masks[1 - core]])

    def row_places(self):
        row = lax.axis_index("rows").astype(jnp.int32)
        half = self.rows // 2
        inverse = []
        for core in (0, 1):
            table = [0] * half
            for slot, mask in enumerate(self.slot_masks(core)):
                table[mask >> 1] = slot
            inverse.append(table)
        inverse = jnp.array(inverse, jnp.int32)
        apart = jnp.arange(self.rows, dtype=jnp.int32) ^ row
        other = apart & 1
        return other * half + inverse[(row & 1) ^ other, apart >> 1]

    def helper_parts(self):
        row = lax.axis_index("rows").astype(jnp.int32)
        masks = jnp.array([self.slot_masks(0)[:4], self.slot_masks(1)[:4]], jnp.int32)
        core = row & 1
        return jnp.concatenate([row ^ masks[core], (row ^ 1) ^ masks[1 - core]])

    def part_of(self, row):
        if self.native:
            return row
        low, high = sorted(self.orders[0][-2:])
        return (row & 1) + 2 * ((row >> low) & 1) + 4 * ((row >> high) & 1)

    def scatter_wide(self, mine, got):
        held = add_like(mine, got)
        for step in range(self.steps - 2):
            half = held.shape[0] // 2
            held = add_like(held[:half], self.across_chip(held[half:], step))
        return held

    def gather_wide(self, value):
        held = jnp.stack([value] + self.across_chips([value] * 4))
        for step in reversed(range(self.steps - 2)):
            held = jnp.concatenate([held, self.across_chip(held, step)], 0)
        held = jnp.concatenate([held, self.across_core(held)], 0)
        return jnp.take(held, self.row_places(), axis=0)

    def coarse(self, blocks):
        blocks = blocks.reshape((PARTS, -1) + blocks.shape[1:]).transpose(0, 2, 1, 3, 4)
        return blocks.reshape(PARTS, blocks.shape[1], -1, blocks.shape[4])

    def spread_parts(self, near, far):
        if self.native:
            return near, far
        parts = jnp.concatenate([near, far], 0)
        count, rows, cols = parts.shape[1:]
        finer = self.rows // PARTS
        parts = parts.reshape(PARTS, count, finer, rows // finer, cols).transpose(0, 2, 1, 3, 4)
        parts = parts.reshape(self.rows, count, rows // finer, cols)
        parts = jnp.take(parts, self.row_slots(), axis=0)
        return parts[: self.rows // 2], parts[self.rows // 2 :]


def add_like(first, second):
    return (first.astype(wide_type) + second.astype(wide_type)).astype(first.dtype)


def estimate(flops, moved, exps=0):
    return pl.CostEstimate(
        flops=flops, bytes_accessed=moved, transcendentals=exps
    )


def like(shape, dtype=low_type):
    return jax.ShapeDtypeStruct(shape, dtype)


def far(value):
    return pltpu.with_memory_space_constraint(value, pltpu.HBM)


def far_like(shape, dtype=low_type):
    return pltpu.HBM(shape, dtype)


def whole_spec(shape, **options):
    return pl.BlockSpec(shape, lambda *ids: (0,) * len(shape), **options)


anywhere = pl.BlockSpec(memory_space=pl.ANY)


def total_of(terms, cut):
    return sum(cut(term).astype(wide_type) for term in terms)


def fold_kernel(plan, passed, head_ref, *refs):
    outs = list(refs[len(refs) - passed - sum(job[2] for job in plan) : len(refs) - passed])
    refs = list(refs)
    for count, kind, given in plan:
        terms, refs = refs[:count], refs[count:]
        made, outs = outs[:given], outs[given:]
        if kind == "halves":
            size = made[0].shape[0]
            for half, target in enumerate(made):
                at = slice(half * size, (half + 1) * size)
                target[...] = total_of(terms, lambda term: term[at]).astype(target.dtype)
        elif kind == "slots":
            for slot, target in enumerate(made):
                target[...] = total_of(terms, lambda term: term[slot]).astype(target.dtype)
        elif kind == "heads" or kind == "zpack":
            heads = len(made) if kind == "heads" else len(made) // 2
            rows = terms[0].shape[0] // heads
            for offset in range(heads):
                begin = (head_ref[0] ^ offset) * rows
                if kind == "heads":
                    at = pl.ds(pl.multiple_of(begin, 16), rows)
                    made[offset][...] = total_of(terms, lambda term: term[at, :]).astype(low_type)
                    continue
                half = rows // 2
                upper = pl.ds(pl.multiple_of(begin, 16), half)
                lower = pl.ds(pl.multiple_of(begin + half, 16), half)
                target, other = made[offset], made[heads + offset]
                target[0:half] = total_of(terms[:2], lambda term: term[upper, :]).astype(low_type)
                target[half:] = total_of(terms[2:], lambda term: term[offset]).astype(low_type)
                other[...] = total_of(terms[:2], lambda term: term[lower, :]).astype(low_type)
        elif kind == "zsplit":
            rows = made[0].shape[0]
            made[0][...] = total_of(terms[:4], lambda term: term[0:rows])
            total = total_of(terms[:4], lambda term: term[rows:]).astype(low_type)
            made[1][...] = total
            for term, target in zip(terms[4:], made[2:]):
                target[0:rows] = term[...]
                target[rows:] = total
        elif kind == "zlast":
            rows = terms[0].shape[0]
            made[0][0:rows] = terms[0][...]
            made[0][rows:] = total_of(terms[1:2] + terms[3:], lambda term: term[0:rows])
            made[1][0] = terms[2][...]
            for place, term in enumerate(terms[3:]):
                made[1][place + 1] = term[rows:]
        elif kind == "stack":
            for place, term in enumerate(terms):
                made[0][place] = term[...]
        else:
            made[0][...] = total_of(terms, lambda term: term[...]).astype(made[0].dtype)


def fold(grid, head, jobs, deps=(), passes=()):
    if not grid.native:
        return [plain_job(grid, head, *job) for job in jobs], list(passes)
    plan, values, shapes = [], [], []
    for terms, kind in jobs:
        kind = {"core": "halves", "spread": "slots"}.get(kind, kind)
        shape = terms[0].shape
        if kind == "halves":
            made = [like((shape[0] // 2,) + shape[1:])] * 2
        elif kind == "slots":
            made = [like(shape[1:])] * shape[0]
        elif kind == "heads":
            made = [like((shape[0] // grid.heads, shape[1]))] * grid.heads
        elif kind == "zpack":
            rows = shape[0] // grid.heads // 2
            made = [like((rows + terms[2].shape[1], shape[1]))] * grid.heads
            made = made + [like((rows, shape[1]))] * grid.heads
        elif kind == "zsplit":
            rows = terms[4].shape[0]
            made = [like((rows, shape[1]), wide_type), like((shape[0] - rows, shape[1]))]
            made = made + [like(shape)] * 3
        elif kind == "zlast":
            made = [
                like((2 * shape[0], shape[1]), wide_type),
                like((len(terms) - 2,) + terms[2].shape),
            ]
        elif kind == "stack":
            made = [like((len(terms),) + shape)]
        else:
            made = [like(shape, wide_type if kind == "wide" else low_type)]
        plan.append((len(terms), kind, len(made)))
        values += terms
        shapes += made
    first, sums = 1 + len(values) + len(deps), len(shapes)
    outs = pl.pallas_call(
        functools.partial(fold_kernel, tuple(plan), len(passes)),
        grid_spec=pltpu.PrefetchScalarGridSpec(
            num_scalar_prefetch=1,
            grid=(1,),
            in_specs=[whole_spec(value.shape) for value in values]
            + [anywhere] * (len(deps) + len(passes)),
            out_specs=[whole_spec(shape.shape) for shape in shapes] + [anywhere] * len(passes),
        ),
        out_shape=shapes + [like(value.shape) for value in passes],
        input_output_aliases={first + place: sums + place for place in range(len(passes))},
        compiler_params=room,
        cost_estimate=estimate(0, sum(3 * value.size for value in values)),
    )(head, *values, *[far(dep) for dep in deps], *passes)
    results, place = [], 0
    for _, _, given in plan:
        results.append(outs[place : place + given])
        place += given
    return results, list(outs[sums:])


def plain_job(grid, head, terms, kind):
    whole = lambda term: term
    if kind in ("core", "spread"):
        held = grid.scatter_wide(*terms)
        return [held[:2], held[2:]] if kind == "core" else list(held)
    if kind == "stack":
        return [jnp.stack(terms)]
    if kind == "zsplit":
        rows = terms[4].shape[0]
        total = total_of(terms[:4], whole)
        small = total[rows:].astype(low_type)
        return [total[:rows], small] + [jnp.concatenate([term, small], 0) for term in terms[4:]]
    if kind == "zlast":
        rows = terms[0].shape[0]
        lower = total_of(terms[1:2] + terms[3:], lambda term: term[:rows])
        blocks = jnp.stack([terms[2]] + [term[rows:] for term in terms[3:]])
        return [jnp.concatenate([terms[0], lower], 0), blocks]
    if kind in ("heads", "zpack"):
        total = total_of(terms if kind == "heads" else terms[:2], whole).astype(low_type)
        total = total.reshape((grid.heads, -1) + total.shape[1:])
        made = [total[head[0] ^ offset] for offset in range(grid.heads)]
        if kind == "heads":
            return made
        wo = total_of(terms[2:], whole).astype(low_type)
        half = made[0].shape[0] // 2
        upper = [jnp.concatenate([made[offset][:half], wo[offset]], 0) for offset in range(grid.heads)]
        return upper + [block[half:] for block in made]
    total = total_of(terms, whole)
    if kind == "wide":
        return [total]
    total = total.astype(low_type)
    if kind == "halves":
        half = total.shape[0] // 2
        return [total[:half], total[half:]]
    return list(total) if kind == "slots" else [total]


def join_kernel(count, *refs):
    for slot in range(count):
        refs[-1][slot] = refs[slot][...]


def join(values, deps=()):
    shape = (len(values),) + values[0].shape
    return pl.pallas_call(
        functools.partial(join_kernel, len(values)),
        grid=(1,),
        in_specs=[whole_spec(value.shape) for value in values] + [anywhere] * len(deps),
        out_specs=whole_spec(shape),
        out_shape=like(shape),
        compiler_params=room,
        cost_estimate=estimate(0, 4 * values[0].size),
    )(*values, *[far(dep) for dep in deps])


def three_parts(values):
    first = values.astype(low_type).astype(wide_type)
    rest = values - first
    second = rest.astype(low_type).astype(wide_type)
    return first, second, (rest - second).astype(low_type).astype(wide_type)


def pair_up(low_lanes, first, second):
    return jnp.where(low_lanes, first, pltpu.roll(second, HD, 1))


def pack_kernel(index_ref, q_ref, k_ref, v_ref, bq_ref, bv_ref, w_ref, piece_ref):
    rows = piece_ref.shape[0]
    w_ref[0, 0:128, :] = q_ref[0:128, :]
    w_ref[0, 128:256, :] = k_ref[0:128, :]
    w_ref[0, 256:384, :] = v_ref[0:128, :]
    w_ref[0, 384:448, :] = q_ref[128:192, :]
    w_ref[0, 448:512, :] = k_ref[128:192, :]
    w_ref[0, 512:576, :] = v_ref[128:192, :]
    row = lax.broadcasted_iota(jnp.int32, (HD, w_ref.shape[2]), 0)
    bias_q = bq_ref[...].astype(wide_type).reshape(1, 192)
    bias_v = bv_ref[...].astype(wide_type).reshape(1, 192)
    gap = jnp.zeros((1, 128), wide_type)
    bias = [bias_q[:, 0:128], gap, bias_v[:, 0:128]]
    bias.append(jnp.concatenate([bias_q[:, 128:192], gap[:, :HD]], 1))
    bias.append(jnp.concatenate([bias_v[:, 128:192], gap[:, :HD]], 1))
    bias = jnp.concatenate(bias + [gap] * (w_ref.shape[2] // 128 - 5), 1)
    w_ref[0, 576:640, :] = jnp.where(row == 0, bias, 0.0).astype(low_type)
    mine = pl.multiple_of(index_ref[0] * rows, 16)
    piece_ref[...] = w_ref[0, pl.ds(mine, rows), :]


def pack(part, w_query, w_key, w_value, b_query, b_value):
    width = w_query.shape[1]
    rows = 640 // PARTS
    return pl.pallas_call(
        pack_kernel,
        grid_spec=pltpu.PrefetchScalarGridSpec(
            num_scalar_prefetch=1,
            grid=(1,),
            in_specs=[whole_spec(w_query.shape)] * 3 + [whole_spec(b_query.shape)] * 2,
            out_specs=[whole_spec((1, 640, width)), whole_spec((rows, width))],
        ),
        out_shape=[far_like((1, 640, width)), far_like((rows, width))],
        compiler_params=room,
        cost_estimate=estimate(0, 4 * width * 640),
    )(part, far(w_query), far(w_key), far(w_value), far(b_query), far(b_value))


def attend_body(device_head, x_ref, w_ref, seg_ref, q_ref, k_ref, v_ref, ctx_ref):
    length = seg_ref.shape[1]
    seqs = x_ref.shape[0] // length
    lane = lax.broadcasted_iota(jnp.int32, (1, 128), 1)
    low = lane < HD
    row8 = lax.broadcasted_iota(jnp.int32, (8, length), 0)
    bias_row = w_ref[0, 576:592, :][0:1, 0:640].astype(wide_type)
    for seq in range(seqs):
        at = slice(seq * length, (seq + 1) * length)
        qkv = (dot_nt(x_ref[at, :], w_ref[0]) + bias_row).astype(low_type).astype(wide_type)
        q01 = qkv[:, 0:128] * 0.125
        k01 = qkv[:, 128:256]
        v01 = qkv[:, 256:384]
        qk2 = qkv[:, 384:512]
        queries = [q01, pltpu.roll(q01, HD, 1), qk2 * 0.125]
        keys = [k01, pltpu.roll(k01, HD, 1), pltpu.roll(qk2, HD, 1)]
        values = [v01, pltpu.roll(v01, HD, 1), qkv[:, 512:640]]
        seg_row = seg_ref[pl.ds(device_head * seqs + seq, 1), :]
        seg_rows = jnp.broadcast_to(seg_row.astype(wide_type), (8, length))
        seg_col = seg_rows.T[:, 0:1].astype(jnp.int32) + HD
        same = lane == seg_col
        in_seg = (lane >= HD) & (lane < HD + 4)
        extra_q = jnp.where(same, 1.0, 0.0)
        extra_k = jnp.where(
            in_seg & ~same,
            masked_score,
            jnp.where((lane >= HD + 4) & (lane < HD + 7), 1.0, 0.0),
        )
        extra_v = jnp.where((lane >= HD) & (lane < HD + 3), 1.0, 0.0)
        contexts = []
        for head in range(3):
            query = jnp.where(low, queries[head], extra_q)
            key = jnp.where(low, keys[head], extra_k).astype(low_type)
            value = jnp.where(low, values[head], extra_v).astype(low_type)
            k_ref[0, head, at, :] = key
            v_ref[0, head, at, :] = value
            scores = dot_nt(key, query.astype(low_type))
            highest = jnp.max(scores, 0, keepdims=True)
            weights_low = jnp.exp(scores - highest).astype(low_type)
            summed = dot_tn(value, weights_low)
            total = summed[HD : HD + 1, :]
            first, second, third = three_parts(-(highest + jnp.log(total)))
            extra = jnp.where(
                row8 == 4, first, jnp.where(row8 == 5, second, jnp.where(row8 == 6, third, 0.0))
            )
            full = jnp.concatenate(
                [summed[:HD] * (1.0 / total), extra, jnp.zeros((56, length), wide_type)], 0
            ).T
            q_ref[0, head, at, :] = jnp.where(low, query, full + extra_q).astype(low_type)
            contexts.append(full)
        ctx_ref[0, at, 0:128] = pair_up(low, contexts[0], contexts[1]).astype(low_type)
        ctx_ref[0, at, 128:192] = contexts[2][:, :HD].astype(low_type)


def attend_own_kernel(head_ref, x_ref, w_ref, seg_ref, q_ref, k_ref, v_ref, ctx_ref):
    attend_body(head_ref[0], x_ref, w_ref, seg_ref, q_ref, k_ref, v_ref, ctx_ref)


def attend_rest_kernel(parts_ref, x_ref, seg_ref, *refs):
    pieces, (q_ref, k_ref, v_ref, ctx_ref, w_ref) = refs[:PARTS], refs[-5:]
    rows = pieces[0].shape[1]
    for slot in range(PARTS):
        at = pl.ds(pl.multiple_of(parts_ref[slot] * rows, 16), rows)
        w_ref[0, at, :] = pieces[slot][0]
    attend_body(parts_ref[PARTS], x_ref, w_ref, seg_ref, q_ref, k_ref, v_ref, ctx_ref)


def attend_cost(count, tokens, length, width):
    return estimate(
        count * (2 * tokens * width * 576 + 3 * 4 * tokens * length * 128),
        2 * tokens * width + count * 2 * (576 * width + 10 * tokens * 128),
        count * 3 * tokens * length,
    )


def attend_outputs(groups, tokens, start):
    heads = pl.BlockSpec((1, 3, tokens, 128), lambda g, *_: (g + start, 0, 0, 0))
    specs = [heads, heads, heads, pl.BlockSpec((1, tokens, 192), lambda g, *_: (g + start, 0, 0))]
    shapes = [far_like((groups, 3, tokens, 128))] * 3 + [far_like((groups, tokens, 192))]
    return specs, shapes


def attend_own(head, layer_in, shard, segments, groups):
    tokens, width = layer_in.shape
    specs, shapes = attend_outputs(groups, tokens, 0)
    return pl.pallas_call(
        attend_own_kernel,
        grid_spec=pltpu.PrefetchScalarGridSpec(
            num_scalar_prefetch=1,
            grid=(1,),
            in_specs=[
                whole_spec((tokens, width)),
                whole_spec(shard.shape),
                whole_spec(segments.shape),
            ],
            out_specs=specs,
        ),
        out_shape=shapes,
        compiler_params=room,
        cost_estimate=attend_cost(1, tokens, segments.shape[1], width),
    )(head, far(layer_in), far(shard), far(segments))


def attend_rest(parts, layer_in, pieces, segments, own):
    tokens, width = layer_in.shape
    count, rows, width = pieces[0].shape
    specs, shapes = attend_outputs(count + 1, tokens, 1)
    piece = pl.BlockSpec((1, rows, width), lambda g, *_: (g, 0, 0))
    return pl.pallas_call(
        attend_rest_kernel,
        grid_spec=pltpu.PrefetchScalarGridSpec(
            num_scalar_prefetch=1,
            grid=(count,),
            in_specs=[whole_spec((tokens, width)), whole_spec(segments.shape)]
            + [piece] * PARTS
            + [anywhere] * len(own),
            out_specs=specs + [pl.BlockSpec((1, 640, width), lambda g, *_: (g, 0, 0))],
        ),
        out_shape=shapes + [far_like((count, 640, width))],
        input_output_aliases={3 + PARTS + place: place for place in range(len(own))},
        compiler_params=room,
        cost_estimate=attend_cost(count, tokens, segments.shape[1], width),
    )(parts, far(layer_in), segments, *pieces, *[far(value) for value in own])


def attend_back_kernel(
    length,
    slots_ref,
    x_ref,
    q_ref,
    k_ref,
    v_ref,
    ctx_ref,
    dctx_ref,
    spare_ref,
    *refs,
):
    dqkv_ref, near_ref, far_ref, held = refs[-4:]
    tokens, width = x_ref.shape
    rows = 640 // PARTS
    lane = lax.broadcasted_iota(jnp.int32, (1, 128), 1)
    low = lane < HD
    for seq in range(tokens // length):
        at = slice(seq * length, (seq + 1) * length)
        grad01 = dctx_ref[0, at, 0:128].astype(wide_type)
        grad2 = dctx_ref[0, at, 128:192].astype(wide_type)
        both = grad01 * ctx_ref[0, at, 0:128].astype(wide_type)
        inner = [
            jnp.sum(jnp.where(low, both, 0.0), -1, keepdims=True),
            jnp.sum(jnp.where(low, 0.0, both), -1, keepdims=True),
            jnp.sum(grad2 * ctx_ref[0, at, 128:192].astype(wide_type), -1, keepdims=True),
        ]
        grads = [
            grad01,
            pltpu.roll(grad01, HD, 1),
            jnp.concatenate([grad2, jnp.zeros((length, HD), wide_type)], 1),
        ]
        grad_q, grad_k, grad_v = [], [], []
        for head in range(3):
            first, second, third = three_parts(-inner[head])
            extra = jnp.where(
                lane == HD,
                first,
                jnp.where(lane == HD + 1, second, jnp.where(lane == HD + 2, third, 0.0)),
            )
            grad = jnp.where(low, grads[head], extra).astype(low_type)
            query = q_ref[0, head, at, :]
            key = k_ref[0, head, at, :]
            probs = jnp.exp(dot_nt(key, query))
            grad_scores = (probs * dot_nt(v_ref[0, head, at, :], grad)).astype(low_type)
            grad_v.append(dot_nn(probs.astype(low_type), grad))
            grad_k.append(dot_nn(grad_scores, query))
            grad_q.append(dot_tn(key, grad_scores).T * 0.125)
        dqkv_ref[0, at, 0:128] = pair_up(low, grad_q[0], grad_q[1]).astype(low_type)
        dqkv_ref[0, at, 128:256] = pair_up(low, grad_k[0], grad_k[1]).astype(low_type)
        dqkv_ref[0, at, 256:384] = pair_up(low, grad_v[0], grad_v[1]).astype(low_type)
        dqkv_ref[0, at, 384:512] = pair_up(low, grad_q[2], grad_k[2]).astype(low_type)
        dqkv_ref[0, at, 512:640] = jnp.where(low, grad_v[2], 0.0).astype(low_type)
    grad_all = dqkv_ref[0]
    total = dot_tn(grad_all, x_ref[...])
    sums = jnp.sum(grad_all.astype(wide_type), 0, keepdims=True)
    sums = jnp.concatenate([sums, jnp.zeros((1, width - 640), wide_type)], 1)
    for part in range(PARTS):
        held[part] = total[part * rows : (part + 1) * rows].astype(low_type)
    row = lax.broadcasted_iota(jnp.int32, (HD, width), 0)
    spare = jnp.where(row == 0, sums, spare_ref[...].astype(wide_type))
    held[PARTS - 1, rows - HD : rows] = spare.astype(low_type)
    for slot in range(PARTS // 2):
        near_ref[slot, 0] = held[slots_ref[slot]]
        far_ref[slot, 0] = held[slots_ref[slot + PARTS // 2]]


def attend_back(
    slots, layer_in, queries, keys, values, context, grad_context, spare, deps, length
):
    tokens, width = layer_in.shape
    count = context.shape[0]
    rows = 640 // PARTS
    heads = pl.BlockSpec((1, 3, tokens, 128), lambda g, *_: (g, 0, 0, 0))
    group = pl.BlockSpec((1, tokens, 192), lambda g, *_: (g, 0, 0))
    half = pl.BlockSpec((PARTS // 2, 1, rows, width), lambda g, *_: (0, g, 0, 0))
    return pl.pallas_call(
        functools.partial(attend_back_kernel, length),
        grid_spec=pltpu.PrefetchScalarGridSpec(
            num_scalar_prefetch=1,
            grid=(count,),
            in_specs=[whole_spec((tokens, width)), heads, heads, heads, group, group]
            + [whole_spec(spare.shape)]
            + [anywhere] * len(deps),
            out_specs=[pl.BlockSpec((1, tokens, 640), lambda g, *_: (g, 0, 0)), half, half],
            scratch_shapes=[pltpu.VMEM((PARTS, rows, width), low_type)],
        ),
        out_shape=[
            (far_like if count > 1 else like)((count, tokens, 640)),
            like((PARTS // 2, count, rows, width)),
            like((PARTS // 2, count, rows, width)),
        ],
        compiler_params=room,
        cost_estimate=estimate(
            count * (2 * tokens * width * 576 + 3 * 10 * tokens * length * 128),
            2 * tokens * width + count * 2 * (576 * width + 16 * tokens * 128),
            count * 3 * tokens * length,
        ),
    )(slots, far(layer_in), queries, keys, far(values), context, grad_context, spare, *[far(dep) for dep in deps])


def mean_last(values):
    return jnp.mean(values, -1, keepdims=True)


def tiles(tokens, size, body):
    def step(index, carry):
        body(pl.ds(pl.multiple_of(index * size, size), size))
        return carry

    lax.fori_loop(0, tokens // size, step, 0)


def gelu_pair(values):
    cumulative = 0.5 * (1.0 + lax.erf(values * 0.7071067811865476))
    density = jnp.exp(-0.5 * values * values) * 0.3989422804014327
    return values * cumulative, cumulative + values * density


class Loads:
    def __init__(self, slots_ref, w_in_hbm, w_out_hbm, w_in, w_out, sems):
        self.count = sems.shape[1]
        self.size = w_out.shape[0] // self.count
        self.copies = []
        for slot in range(self.count):
            source = pl.ds(pl.multiple_of(slots_ref[slot] * self.size, 128), self.size)
            target = pl.ds(slot * self.size, self.size)
            self.copies.append(
                (
                    pltpu.make_async_copy(w_in_hbm.at[:, source], w_in.at[:, target], sems.at[0, slot]),
                    pltpu.make_async_copy(w_out_hbm.at[source], w_out.at[target], sems.at[1, slot]),
                )
            )

    def start(self):
        for copies in self.copies:
            for copy in copies:
                copy.start()

    def wait(self, low, high):
        for slot in range(-(-low // self.size), -(-high // self.size)):
            for copy in self.copies[slot]:
                copy.wait()


def overlaps(size, chunks, block, blocks):
    return [
        [
            (which, max(chunk * size, which * block), min((chunk + 1) * size, (which + 1) * block))
            for which in range(blocks)
            if max(chunk * size, which * block) < min((chunk + 1) * size, (which + 1) * block)
        ]
        for chunk in range(chunks)
    ]


def ffn_kernel(
    chunks,
    slots_ref,
    x_ref,
    ctx_ref,
    wo_ref,
    cot_ref,
    b_output_ref,
    gain_attn_ref,
    shift_attn_ref,
    b_outer_ref,
    gain_ffn_ref,
    shift_ffn_ref,
    b_in_ref,
    w_in_hbm,
    w_out_hbm,
    rstd_ref,
    sums_ref,
    gb_ref,
    normal_hbm,
    out_hbm,
    total_hbm,
    outer_near_hbm,
    outer_far_hbm,
    near_hbm,
    far_hbm,
    w_in,
    w_out,
    normed,
    outer,
    active,
    slope,
    low,
    normal_low,
    result_low,
    grad_out,
    b_row,
    sems,
    out_sems,
):
    step = pl.program_id(0)
    tokens, width = x_ref.shape
    hidden = w_out.shape[0]
    size = hidden // chunks
    half = hidden // 2
    loads = Loads(slots_ref, w_in_hbm, w_out_hbm, w_in, w_out, sems)
    head = slots_ref[loads.count]
    b_output, gain_attn, shift_attn, b_outer, gain_ffn, shift_ffn = (
        ref[...].reshape(1, width)
        for ref in (
            b_output_ref,
            gain_attn_ref,
            shift_attn_ref,
            b_outer_ref,
            gain_ffn_ref,
            shift_ffn_ref,
        )
    )
    small = [
        pltpu.make_async_copy(source, target, out_sems.at[place])
        for place, (source, target) in enumerate(
            ((normal_low, normal_hbm), (result_low, out_hbm), (outer, total_hbm))
        )
    ]
    count = len(small)
    outer_copies, inner_copies = [], []
    for chunk, cuts in enumerate(overlaps(size, chunks, half, 2)):
        from_active, from_out = [], []
        for which, begin, end in cuts:
            at = pl.ds(begin - which * half, end - begin)
            from_active.append(
                pltpu.make_async_copy(
                    active.at[chunk, pl.ds(begin - chunk * size, end - begin), pl.ds(0, width)],
                    (outer_near_hbm, outer_far_hbm)[which].at[at],
                    out_sems.at[count],
                )
            )
            from_out.append(
                pltpu.make_async_copy(
                    w_out.at[pl.ds(begin, end - begin)],
                    (near_hbm, far_hbm)[which].at[at],
                    out_sems.at[count + 1],
                )
            )
            count += 2
        outer_copies.append(from_active)
        inner_copies.append(from_out)

    @pl.when(step == 0)
    def _():
        loads.start()
        b_row[1:2, :] = b_in_ref[...].reshape(1, hidden)
        for slot in range(loads.count):
            source = pl.ds(pl.multiple_of(slots_ref[slot] * loads.size, 128), loads.size)
            b_row[0:1, slot * loads.size : (slot + 1) * loads.size] = b_row[1:2, source]
        outer[...] = jnp.zeros_like(outer)
        branch = dot_nn(ctx_ref[0], wo_ref[head])
        for offset in range(1, wo_ref.shape[0]):
            branch += dot_nn(ctx_ref[offset], wo_ref[head ^ offset])
        normed[...] = branch

        def one(at):
            total = x_ref[at, :].astype(wide_type) + (normed[at, :] + b_output)
            centred = total - mean_last(total)
            rstd = lax.rsqrt(mean_last(centred * centred) + epsilon)
            normal = centred * rstd
            result = normal * gain_attn + shift_attn
            normed[at, :] = result
            low[at, :] = result.astype(low_type)
            normal_low[at, :] = normal.astype(low_type)
            rstd_ref[at, :] = jnp.broadcast_to(rstd, (rstd.shape[0], 128))

        tiles(tokens, 256, one)
        small[0].start()

    for chunk in range(chunks):

        @pl.when(step == chunk)
        def _():
            loads.wait(chunk * size, (chunk + 1) * size)

    @pl.when(step < chunks)
    def _():
        at = pl.ds(pl.multiple_of(step * size, 128), size)
        inner = dot_nn(low[...], w_in[:, at]) + b_row[0:1, at]
        values, gradient = gelu_pair(inner)
        values = values.astype(low_type)
        active[step] = values
        slope[step] = gradient.astype(low_type)
        outer[...] += dot_nn(values, w_out[at, :])

    @pl.when(step == chunks - 1)
    def _():
        sums_ref[...] = jnp.zeros_like(sums_ref)

        def one(at):
            total = normed[at, :] + (outer[at, :] + b_outer)
            centred = total - mean_last(total)
            rstd = lax.rsqrt(mean_last(centred * centred) + epsilon)
            normal = centred * rstd
            result_low[at, :] = (normal * gain_ffn + shift_ffn).astype(low_type)
            grad = cot_ref[at, :].astype(wide_type)
            scaled = grad * gain_ffn
            grad_sum = rstd * (scaled - mean_last(scaled) - normal * mean_last(scaled * normal))
            grad_low = grad_sum.astype(low_type)
            grad_out[at, :] = grad_low
            outer[at, :] = grad_low.astype(wide_type)
            sums_ref[0:1, :] += jnp.sum(grad * normal, 0, keepdims=True)
            sums_ref[1:2, :] += jnp.sum(grad, 0, keepdims=True)
            sums_ref[2:3, :] += jnp.sum(grad_low.astype(wide_type), 0, keepdims=True)

        tiles(tokens, 256, one)
        small[1].start()

    @pl.when(step >= chunks)
    def _():
        which = step - chunks
        at = pl.ds(pl.multiple_of(which * size, 128), size)
        grad = grad_out[...]
        active[which, :, 0:width] = dot_tn(active[which], grad).astype(low_type)
        grad_inner = (dot_nt(grad, w_out[at, :]) * slope[which].astype(wide_type)).astype(low_type)
        gb_ref[...] = jnp.sum(grad_inner.astype(wide_type), 0, keepdims=True)
        w_out[at, :] = dot_tn(grad_inner, low[...]).astype(low_type)
        outer[...] += dot_nt(grad_inner, w_in[:, at])

    for chunk in range(chunks):

        @pl.when(step == chunks + chunk)
        def _():
            for copy in outer_copies[chunk] + inner_copies[chunk]:
                copy.start()

    @pl.when(step == 2 * chunks - 1)
    def _():
        small[2].start()
        for copy in small:
            copy.wait()
        for copies in outer_copies + inner_copies:
            for copy in copies:
                copy.wait()


def ffn(slots, layer_in, context, w_output, cotangent, vectors, w_in, w_out, b_in):
    tokens, width = layer_in.shape
    hidden = w_out.shape[0]
    chunks = 3
    blocks = slots.shape[0] - 1
    size = hidden // chunks
    back = lambda i, *_: (0, jnp.maximum(i - chunks, 0))
    once = dict(pipeline_mode=pl.Buffered(1))
    copies = 3 + 4 * chunks
    return pl.pallas_call(
        functools.partial(ffn_kernel, chunks),
        grid_spec=pltpu.PrefetchScalarGridSpec(
            num_scalar_prefetch=1,
            grid=(2 * chunks,),
            in_specs=[
                whole_spec((tokens, width), **once),
                whole_spec(context.shape, **once),
                whole_spec(w_output.shape, **once),
                whole_spec((tokens, width), **once),
            ]
            + [whole_spec(vector.shape, **once) for vector in vectors]
            + [whole_spec(b_in.shape, **once), anywhere, anywhere],
            out_specs=[
                whole_spec((tokens, 128)),
                whole_spec((8, width)),
                pl.BlockSpec((1, size), back),
            ]
            + [anywhere] * 7,
            scratch_shapes=[
                pltpu.VMEM((width, hidden), low_type),
                pltpu.VMEM((hidden, width), low_type),
                pltpu.VMEM((tokens, width), wide_type),
                pltpu.VMEM((tokens, width), wide_type),
                pltpu.VMEM((chunks, tokens, size), low_type),
                pltpu.VMEM((chunks, tokens, size), low_type),
            ]
            + [pltpu.VMEM((tokens, width), low_type)] * 4
            + [pltpu.VMEM((8, hidden), wide_type)]
            + [pltpu.SemaphoreType.DMA((2, blocks)), pltpu.SemaphoreType.DMA((copies,))],
        ),
        out_shape=[
            like((tokens, 128), wide_type),
            like((8, width), wide_type),
            like((1, hidden), wide_type),
            far_like((tokens, width)),
            far_like((tokens, width)),
            far_like((tokens, width), wide_type),
        ]
        + [far_like((hidden // 2, width))] * 4,
        compiler_params=large_room,
        cost_estimate=estimate(
            2 * tokens * width * (6 * hidden + width),
            2 * (tokens * 10 * width + 4 * hidden * width),
            tokens * hidden,
        ),
    )(slots, layer_in, context, w_output, cotangent, *vectors, b_in, far(w_in), far(w_out))


def norm_back_kernel(
    index_ref,
    total_ref,
    normal_ref,
    rstd_ref,
    ctx_ref,
    wo_ref,
    gain_ref,
    sums_in_ref,
    gb_ref,
    *refs,
):
    branch_ref, dctx_ref, near_ref, far_ref, spare_ref, sums, acc, held, inner_sums = refs[-9:]
    step = pl.program_id(0)
    size = branch_ref.shape[0]
    head = index_ref[PARTS]
    gain_attn = gain_ref[...].reshape(1, total_ref.shape[1])
    heads = wo_ref.shape[0]
    rows = wo_ref.shape[1] // PARTS

    @pl.when(step == 0)
    def _():
        sums[...] = sums_in_ref[...]

    def one(at):
        grad = total_ref[at, :]
        normal = normal_ref[at, :].astype(wide_type)
        scaled = grad * gain_attn
        rstd = rstd_ref[at, 0:1]
        grad_sum = rstd * (scaled - mean_last(scaled) - normal * mean_last(scaled * normal))
        grad_low = grad_sum.astype(low_type)
        branch_ref[at, :] = grad_low
        sums[3:4, :] += jnp.sum(grad * normal, 0, keepdims=True)
        sums[4:5, :] += jnp.sum(grad, 0, keepdims=True)
        sums[5:6, :] += jnp.sum(grad_low.astype(wide_type), 0, keepdims=True)

    tiles(size, 256, one)
    branch = branch_ref[...]
    for offset in range(heads):
        context = ctx_ref[offset]
        weights = wo_ref[head ^ offset]
        grad_context = dot_nt(branch, weights).astype(low_type)
        dctx_ref[offset] = grad_context
        part = dot_tn(context, branch)

        @pl.when(step == 0)
        def _():
            acc[offset] = part

        @pl.when(step > 0)
        def _():
            acc[offset] += part

    @pl.when(step == pl.num_programs(0) - 1)
    def _():
        for offset in range(heads):
            for part in range(PARTS):
                held[part, offset] = acc[offset, part * rows : (part + 1) * rows, :].astype(low_type)
        for slot in range(PARTS // 2):
            near_ref[slot] = held[index_ref[slot]]
            far_ref[slot] = held[index_ref[slot + PARTS // 2]]
        block = gb_ref.shape[1] // PARTS
        for slot in range(PARTS):
            inner_sums[pl.ds(index_ref[slot], 1), :] = gb_ref[:, slot * block : (slot + 1) * block]
        lines = [jnp.zeros((1, 2 * block), wide_type), sums[0:6, :]]
        for pair in range(PARTS // 2):
            both = [inner_sums[2 * pair + half : 2 * pair + half + 1, :] for half in range(2)]
            lines.append(jnp.concatenate(both, 1))
        lines.append(jnp.zeros((5, 2 * block), wide_type))
        spare_ref[...] = jnp.zeros_like(spare_ref)
        spare_ref[0:16, :] = jnp.concatenate(lines, 0).astype(low_type)


def norm_back(
    index, total, normal, rstd, context, w_output, gain, sums, gb, deps
):
    tokens, width = total.shape
    heads, group = w_output.shape[:2]
    size = tokens
    tile = pl.BlockSpec((size, width), lambda i, *_: (i, 0))
    groups = pl.BlockSpec((heads, size, group), lambda i, *_: (0, i, 0))
    half = (PARTS // 2, heads, group // PARTS, width)
    return pl.pallas_call(
        norm_back_kernel,
        grid_spec=pltpu.PrefetchScalarGridSpec(
            num_scalar_prefetch=1,
            grid=(1,),
            in_specs=[
                tile,
                tile,
                pl.BlockSpec((size, 128), lambda i, *_: (i, 0)),
                groups,
                whole_spec(w_output.shape),
                whole_spec(gain.shape),
                whole_spec(sums.shape),
                whole_spec(gb.shape),
            ]
            + [anywhere] * len(deps),
            out_specs=[
                tile,
                groups,
                whole_spec(half),
                whole_spec(half),
                whole_spec((HD, width)),
            ],
            scratch_shapes=[
                pltpu.VMEM((8, width), wide_type),
                pltpu.VMEM((heads, group, width), wide_type),
                pltpu.VMEM((PARTS,) + half[1:], low_type),
                pltpu.VMEM((PARTS, gb.shape[1] // PARTS), wide_type),
            ],
        ),
        out_shape=[
            like((tokens, width)),
            like(context.shape),
            like(half),
            like(half),
            like((HD, width)),
        ],
        compiler_params=room,
        cost_estimate=estimate(
            4 * tokens * width * width, 2 * tokens * width * 8 + 6 * width * width
        ),
    )(index, far(total), far(normal), far(rstd), far(context), far(w_output), gain, far(sums), far(gb), *[far(dep) for dep in deps])


def input_kernel(branch_ref, grads_ref, shard_ref, weights_ref, *refs):
    total = branch_ref[...].astype(wide_type) + dot_nn(grads_ref[0], shard_ref[0])
    for group in range(weights_ref.shape[0]):
        total += dot_nn(grads_ref[group + 1], weights_ref[group])
    refs[-1][...] = total


def input_back(branch, grads, shard, weights, deps):
    tokens, width = branch.shape
    size = tokens // 2
    tile = pl.BlockSpec((size, width), lambda i: (i, 0))
    groups = pl.BlockSpec((grads.shape[0], size, 640), lambda i: (0, i, 0))
    return pl.pallas_call(
        input_kernel,
        grid=(2,),
        in_specs=[tile, groups, whole_spec(shard.shape), whole_spec(weights.shape)]
        + [anywhere] * len(deps),
        out_specs=tile,
        out_shape=far_like((tokens, width), wide_type),
        compiler_params=room,
        cost_estimate=estimate(2 * tokens * width * 640 * 4, 16 * tokens * width),
    )(branch, grads, shard, weights, *[far(dep) for dep in deps])


def finish_kernel(index_ref, *refs):
    owns, blocks = refs[0:2], refs[2:4]
    q_ref, k_ref, v_ref, wo_ref, bq_ref, bv_ref, gb_ref = refs[4:11]
    vectors = refs[11:17]
    held, small_rows = refs[-2:]
    rows = held.shape[1]
    heads, extra, width = blocks[0].shape[1:]
    head, row = index_ref[PARTS], index_ref[PARTS + 1]
    for slot in range(PARTS):
        part = index_ref[slot]
        half, place = divmod(slot, PARTS // 2)
        held[part] = owns[half][place]
        for offset in range(heads):
            at = pl.ds(pl.multiple_of(part * extra, 8), extra)
            wo_ref[head ^ offset, at, :] = blocks[half][place, offset].astype(wide_type)
    whole = held[...].reshape(PARTS * rows, width)
    for ref, first, second in ((q_ref, 0, 384), (k_ref, 128, 448), (v_ref, 256, 512)):
        ref[0:128, :] = whole[first : first + 128].astype(wide_type)
        ref[128:192, :] = whole[second : second + HD].astype(wide_type)
    small_rows[...] = whole[576:592].astype(wide_type)
    sums = small_rows[0:1, :]
    for ref, first, second in ((bq_ref, 0, 384), (bv_ref, 256, 512)):
        joined = jnp.concatenate([sums[:, first : first + 128], sums[:, second : second + HD]], 1)
        ref[...] = joined.reshape(ref.shape)
    for which, ref in enumerate(vectors):
        ref[...] = small_rows[1 + which : 2 + which, :].reshape(ref.shape)
    block = gb_ref.shape[0]
    per_row = width // block
    place = row * heads + head
    sums = small_rows[pl.ds(7 + place // per_row, 1), :]
    total = jnp.zeros((1, block), wide_type)
    for which in range(per_row):
        total = jnp.where(
            place % per_row == which, sums[:, which * block : (which + 1) * block], total
        )
    gb_ref[...] = total.reshape(gb_ref.shape)


def finish(index, owns, blocks, block):
    rows = 640 // PARTS
    heads, extra, width = blocks[0].shape[1:]
    group = PARTS * extra
    pieces = owns + blocks
    shapes = (
        [like((group, width), wide_type)] * 3
        + [like((heads, group, width), wide_type)]
        + [like((group,), wide_type)] * 2
        + [like((block,), wide_type)]
        + [like((width,), wide_type)] * 6
    )
    return pl.pallas_call(
        finish_kernel,
        grid_spec=pltpu.PrefetchScalarGridSpec(
            num_scalar_prefetch=1,
            grid=(1,),
            in_specs=[whole_spec(piece.shape) for piece in pieces],
            out_specs=[whole_spec(shape.shape) for shape in shapes],
            scratch_shapes=[
                pltpu.VMEM((PARTS, rows, width), low_type),
                pltpu.VMEM((16, width), wide_type),
            ],
        ),
        out_shape=shapes,
        compiler_params=room,
        cost_estimate=estimate(0, 16 * width * width),
    )(index, *pieces)


def local(
    grid,
    layer_in,
    segment_ids,
    w_query,
    w_key,
    w_value,
    b_query,
    b_value,
    w_output,
    b_output,
    gain_attn,
    shift_attn,
    w_inner,
    b_inner,
    w_outer,
    b_outer,
    gain_ffn,
    shift_ffn,
    cotangent,
):
    tokens, width = layer_in.shape
    length = segment_ids.shape[1]
    group = w_query.shape[1]
    hidden = w_inner.shape[1]
    heads = grid.heads
    row = lax.axis_index("rows")
    head = lax.axis_index("heads")

    head_index = head.astype(jnp.int32)[None]
    part = grid.part_of(row.astype(jnp.int32))[None]
    shard, piece = pack(part, w_query.T, w_key.T, w_value.T, b_query, b_value)
    got = [grid.across_heads(piece, offset) for offset in range(1, heads)]
    own = attend_own(head_index, layer_in, shard, segment_ids, heads)
    parts = jnp.concatenate([grid.part_of(grid.helper_parts()), head_index])

    row_slots = grid.row_slots()
    w_in, w_out, b_in = w_inner, w_outer, b_inner
    if not grid.native:
        w_in = jnp.take(w_in.reshape(width, grid.rows, -1), row_slots, axis=1).reshape(width, hidden)
        w_out = jnp.take(w_out.reshape(grid.rows, -1, width), row_slots, axis=0).reshape(hidden, width)
        b_in = jnp.take(b_in.reshape(grid.rows, -1), row_slots, axis=0).reshape(hidden)
    natural = jnp.arange(PARTS, dtype=jnp.int32)
    index = jnp.concatenate([row_slots if grid.native else natural, head_index])
    w_output_heads = w_output.reshape(heads, group, width)
    vectors = [b_output, gain_attn, shift_attn, b_outer, gain_ffn, shift_ffn]
    held = join(got, (own[1],))
    held = [held] + grid.across_chips([held] * 4)
    held = held + [grid.across_core(value) for value in held]

    queries, keys, values, context, w_rest = attend_rest(parts, layer_in, held, segment_ids, own)
    rstd, sums, gb_inner, normal, layer_out, total, outer_near, outer_far, inner_near, inner_far = ffn(
        index, layer_in, context, w_output_heads, cotangent, vectors, w_in, w_out, b_in
    )
    slot_shape = (grid.rows // 2, hidden // grid.rows, width)
    outer_got = grid.across_core(outer_far.reshape(slot_shape))
    inner_got = grid.across_core(inner_far.reshape(slot_shape))
    if not grid.native:
        gb_inner = jnp.take(gb_inner.reshape(grid.rows, -1), grid.row_places(), axis=0).reshape(1, hidden)
    folded = functools.partial(fold, grid, head_index)
    first, second = grid.steps - 2, grid.steps - 1

    branch, grad_context, wo_near, wo_far, spare = norm_back(
        index, total, normal, rstd, context, w_output_heads, gain_attn, sums, gb_inner, ()
    )
    wo_near, wo_far = grid.spread_parts(wo_near, wo_far)

    ((outer, outer_send), (inner, inner_send)), (wo_far,) = folded(
        [
            ([outer_near.reshape(slot_shape), outer_got], "core"),
            ([inner_near.reshape(slot_shape), inner_got], "core"),
        ],
        (),
        (wo_far,),
    )
    outer_got = grid.across_chip(outer_send, first)
    inner_got = grid.across_chip(inner_send, first)
    wo_got = grid.across_core(wo_far)
    grads, near, far_half = attend_back(
        index, layer_in, queries, keys, values, context, grad_context, spare, (inner_send,), length
    )
    near, far_half = grid.spread_parts(near, far_half)
    ((outer, outer_send), (inner, inner_send), wo), (far_half,) = folded(
        [
            ([outer, outer_got], "halves"),
            ([inner, inner_got], "halves"),
            ([wo_near, wo_got], "spread"),
        ],
        (),
        (far_half,),
    )
    outer_got = grid.across_chip(outer_send, second)
    wo_got = grid.across_chips(wo)
    got = grid.across_core(far_half)
    input_grad = input_back(branch, grads, shard, w_rest, (wo[3],))
    (outer, (near, send)), (inner_send,) = folded(
        [
            ([outer[0], outer_got[0], wo[0]] + wo_got, "zpack"),
            ([near, got], "core"),
        ],
        (input_grad,),
        (inner_send,),
    )
    outer_got = [grid.across_heads(outer[offset], offset) for offset in range(1, heads)]
    got = grid.across_chip(send, first)
    ((upper, wo, *outer_send), (near, send)), (inner_send,) = folded(
        [
            ([outer[0]] + outer_got + list(outer[heads + 1 :]), "zsplit"),
            ([near, got], "halves"),
        ],
        (),
        (inner_send,),
    )
    outer_got = [grid.across_heads(outer_send[offset - 1], offset) for offset in range(1, heads)]
    got = grid.across_chip(send, second)
    inner_got = grid.across_chip(inner_send, second)
    (groups, (out_w_outer, wo), inner), _ = folded(
        [
            ([near[0], got[0]], "slots"),
            ([upper, outer[heads], wo] + outer_got, "zlast"),
            ([inner[0], inner_got[0]], "heads"),
        ],
    )
    got = [grid.across_heads(groups[offset], offset) for offset in range(1, heads)]
    if grid.native:
        wo_got = grid.across_chips([wo] * 4)
    ((own,),), inner = folded([([groups[0]] + got, "sum")], (), inner)
    inner_got = [grid.across_heads(inner[offset], offset) for offset in range(1, heads)]
    if grid.native:
        own_got = grid.across_chips([own] * 4)
        ((out_w_inner,), (own,), (wo,)), _ = folded(
            [
                ([inner[0]] + inner_got, "wide"),
                ([own] + own_got, "stack"),
                ([wo] + wo_got, "stack"),
            ]
        )
        owns, blocks = [own, grid.across_core(own)], [wo, grid.across_core(wo)]
    else:
        ((out_w_inner,),), _ = folded([([inner[0]] + inner_got, "wide")])
        own = grid.gather_wide(own).reshape(PARTS, -1, width)
        wo = grid.coarse(grid.gather_wide(wo))
        owns, blocks = [own[: PARTS // 2], own[PARTS // 2 :]], [wo[: PARTS // 2], wo[PARTS // 2 :]]
    block = hidden // (grid.rows * heads)
    gw_query, gw_key, gw_value, gw_output, gb_query, gb_value, gb_inner, *vector = finish(
        jnp.concatenate([index, row.astype(jnp.int32)[None]]), owns, blocks, block
    )
    return (
        layer_out,
        input_grad,
        gw_query.T,
        gw_key.T,
        gw_value.T,
        gb_query,
        gb_value,
        gw_output.reshape(width, width),
        vector[5],
        vector[3],
        vector[4],
        out_w_inner.T,
        gb_inner,
        out_w_outer,
        vector[2],
        vector[0],
        vector[1],
    )


def solution(mesh):
    grid = Grid(mesh)
    return jax.shard_map(
        lambda *values: local(grid, *values),
        mesh=mesh,
        in_specs=(
            P(("rows", "heads"), None),
            P("rows", None),
            P(None, "heads"),
            P(None, "heads"),
            P(None, "heads"),
            P("heads"),
            P("heads"),
            P(),
            P(),
            P(),
            P(),
            P(),
            P(),
            P(),
            P(),
            P(),
            P(),
            P(("rows", "heads"), None),
        ),
        out_specs=(
            P(("rows", "heads"), None),
            P(("rows", "heads"), None),
            P(None, "heads"),
            P(None, "heads"),
            P(None, "heads"),
            P("heads"),
            P("heads"),
            P(),
            P(),
            P(),
            P(),
            P(None, ("rows", "heads")),
            P(("rows", "heads")),
            P(("rows", "heads"), None),
            P(),
            P(),
            P(),
        ),
        check_vma=False,
    )
```

```python
import functools

import jax
import jax.numpy as jnp
from jax import lax
from jax.experimental import pallas as pl
from jax.experimental.pallas import tpu as pltpu
from jax.sharding import PartitionSpec as P

HD = 64
PARTS = 8
epsilon = 1e-06
masked_score = -1000000000.0
low_type = jnp.bfloat16
wide_type = jnp.float32
room = pltpu.CompilerParams(vmem_limit_bytes=32 * 1024 * 1024)
large_room = pltpu.CompilerParams(vmem_limit_bytes=60 * 1024 * 1024)


def contract(left, right, left_dim, right_dim):
    return lax.dot_general(
        left, right, (((left_dim,), (right_dim,)), ((), ())), preferred_element_type=wide_type
    )


def dot_nn(left, right):
    return contract(left, right, 1, 0)


def dot_nt(left, right):
    return contract(left, right, 1, 1)


def dot_tn(left, right):
    return contract(left, right, 0, 0)


class Grid:
    def __init__(self, mesh):
        self.rows = mesh.shape["rows"]
        self.heads = mesh.shape["heads"]
        self.native = self.rows == PARTS
        self.steps = self.rows.bit_length() - 2
        up = list(range(1, self.steps + 1))
        self.orders = (up, up[::-1])

    def permute(self, value, row_masks, head_mask=0):
        pairs = [
            (row * self.heads + head, (row ^ row_masks[row & 1]) * self.heads + (head ^ head_mask))
            for row in range(self.rows)
            for head in range(self.heads)
        ]
        return lax.ppermute(value, ("rows", "heads"), pairs)

    def across_core(self, value):
        return self.permute(value, (1, 1))

    def across_heads(self, value, offset):
        return self.permute(value, (0, 0), offset)

    def across_chip(self, value, step):
        return self.permute(value, [1 << order[step] for order in self.orders])

    def across_chips(self, values):
        masks = [self.slot_masks(core) for core in (0, 1)]
        return [
            self.permute(value, (masks[0][slot], masks[1][slot]))
            for slot, value in enumerate(values)
            if slot
        ]

    def slot_masks(self, core):
        last = self.steps - 1
        masks = []
        for slot in range(1 << self.steps):
            mask = 0
            for step in range(self.steps):
                mask |= ((slot >> (last - step)) & 1) << self.orders[core][step]
            masks.append(mask)
        return masks

    def row_slots(self):
        row = lax.axis_index("rows").astype(jnp.int32)
        masks = jnp.array([self.slot_masks(0), self.slot_masks(1)], jnp.int32)
        core = row & 1
        return jnp.concatenate([row ^ masks[core], (row ^ 1) ^ masks[1 - core]])

    def row_places(self):
        row = lax.axis_index("rows").astype(jnp.int32)
        half = self.rows // 2
        inverse = []
        for core in (0, 1):
            table = [0] * half
            for slot, mask in enumerate(self.slot_masks(core)):
                table[mask >> 1] = slot
            inverse.append(table)
        inverse = jnp.array(inverse, jnp.int32)
        apart = jnp.arange(self.rows, dtype=jnp.int32) ^ row
        other = apart & 1
        return other * half + inverse[(row & 1) ^ other, apart >> 1]

    def helper_parts(self):
        row = lax.axis_index("rows").astype(jnp.int32)
        masks = jnp.array([self.slot_masks(0)[:4], self.slot_masks(1)[:4]], jnp.int32)
        core = row & 1
        return jnp.concatenate([row ^ masks[core], (row ^ 1) ^ masks[1 - core]])

    def part_of(self, row):
        if self.native:
            return row
        low, high = sorted(self.orders[0][-2:])
        return (row & 1) + 2 * ((row >> low) & 1) + 4 * ((row >> high) & 1)

    def scatter_wide(self, mine, got):
        held = add_like(mine, got)
        for step in range(self.steps - 2):
            half = held.shape[0] // 2
            held = add_like(held[:half], self.across_chip(held[half:], step))
        return held

    def gather_wide(self, value):
        held = jnp.stack([value] + self.across_chips([value] * 4))
        for step in reversed(range(self.steps - 2)):
            held = jnp.concatenate([held, self.across_chip(held, step)], 0)
        held = jnp.concatenate([held, self.across_core(held)], 0)
        return jnp.take(held, self.row_places(), axis=0)

    def coarse(self, blocks):
        blocks = blocks.reshape((PARTS, -1) + blocks.shape[1:]).transpose(0, 2, 1, 3, 4)
        return blocks.reshape(PARTS, blocks.shape[1], -1, blocks.shape[4])

    def spread_parts(self, near, far):
        if self.native:
            return near, far
        parts = jnp.concatenate([near, far], 0)
        count, rows, cols = parts.shape[1:]
        finer = self.rows // PARTS
        parts = parts.reshape(PARTS, count, finer, rows // finer, cols).transpose(0, 2, 1, 3, 4)
        parts = parts.reshape(self.rows, count, rows // finer, cols)
        parts = jnp.take(parts, self.row_slots(), axis=0)
        return parts[: self.rows // 2], parts[self.rows // 2 :]


def add_like(first, second):
    return (first.astype(wide_type) + second.astype(wide_type)).astype(first.dtype)


def estimate(flops, moved, exps=0):
    return pl.CostEstimate(
        flops=flops, bytes_accessed=moved, transcendentals=exps
    )


def like(shape, dtype=low_type):
    return jax.ShapeDtypeStruct(shape, dtype)


def far(value):
    return pltpu.with_memory_space_constraint(value, pltpu.HBM)


def far_like(shape, dtype=low_type):
    return pltpu.HBM(shape, dtype)


def whole_spec(shape, **options):
    return pl.BlockSpec(shape, lambda *ids: (0,) * len(shape), **options)


anywhere = pl.BlockSpec(memory_space=pl.ANY)


def total_of(terms, cut):
    return sum(cut(term).astype(wide_type) for term in terms)


def fold_kernel(plan, passed, head_ref, *refs):
    outs = list(refs[len(refs) - passed - sum(job[2] for job in plan) : len(refs) - passed])
    refs = list(refs)
    for count, kind, given in plan:
        terms, refs = refs[:count], refs[count:]
        made, outs = outs[:given], outs[given:]
        if kind == "halves":
            size = made[0].shape[0]
            for half, target in enumerate(made):
                at = slice(half * size, (half + 1) * size)
                target[...] = total_of(terms, lambda term: term[at]).astype(target.dtype)
        elif kind == "slots":
            for slot, target in enumerate(made):
                target[...] = total_of(terms, lambda term: term[slot]).astype(target.dtype)
        elif kind == "heads" or kind == "zpack":
            heads = len(made) if kind == "heads" else len(made) // 2
            rows = terms[0].shape[0] // heads
            for offset in range(heads):
                begin = (head_ref[0] ^ offset) * rows
                if kind == "heads":
                    at = pl.ds(pl.multiple_of(begin, 16), rows)
                    made[offset][...] = total_of(terms, lambda term: term[at, :]).astype(low_type)
                    continue
                half = rows // 2
                upper = pl.ds(pl.multiple_of(begin, 16), half)
                lower = pl.ds(pl.multiple_of(begin + half, 16), half)
                target, other = made[offset], made[heads + offset]
                target[0:half] = total_of(terms[:2], lambda term: term[upper, :]).astype(low_type)
                target[half:] = total_of(terms[2:], lambda term: term[offset]).astype(low_type)
                other[...] = total_of(terms[:2], lambda term: term[lower, :]).astype(low_type)
        elif kind == "zsplit":
            rows = made[0].shape[0]
            made[0][...] = total_of(terms[:4], lambda term: term[0:rows])
            total = total_of(terms[:4], lambda term: term[rows:]).astype(low_type)
            made[1][...] = total
            for term, target in zip(terms[4:], made[2:]):
                target[0:rows] = term[...]
                target[rows:] = total
        elif kind == "zlast":
            rows = terms[0].shape[0]
            made[0][0:rows] = terms[0][...]
            made[0][rows:] = total_of(terms[1:2] + terms[3:], lambda term: term[0:rows])
            made[1][0] = terms[2][...]
            for place, term in enumerate(terms[3:]):
                made[1][place + 1] = term[rows:]
        elif kind == "stack":
            for place, term in enumerate(terms):
                made[0][place] = term[...]
        else:
            made[0][...] = total_of(terms, lambda term: term[...]).astype(made[0].dtype)


def fold(grid, head, jobs, deps=(), passes=()):
    if not grid.native:
        return [plain_job(grid, head, *job) for job in jobs], list(passes)
    plan, values, shapes = [], [], []
    for terms, kind in jobs:
        kind = {"core": "halves", "spread": "slots"}.get(kind, kind)
        shape = terms[0].shape
        if kind == "halves":
            made = [like((shape[0] // 2,) + shape[1:])] * 2
        elif kind == "slots":
            made = [like(shape[1:])] * shape[0]
        elif kind == "heads":
            made = [like((shape[0] // grid.heads, shape[1]))] * grid.heads
        elif kind == "zpack":
            rows = shape[0] // grid.heads // 2
            made = [like((rows + terms[2].shape[1], shape[1]))] * grid.heads
            made = made + [like((rows, shape[1]))] * grid.heads
        elif kind == "zsplit":
            rows = terms[4].shape[0]
            made = [like((rows, shape[1]), wide_type), like((shape[0] - rows, shape[1]))]
            made = made + [like(shape)] * 3
        elif kind == "zlast":
            made = [
                like((2 * shape[0], shape[1]), wide_type),
                like((len(terms) - 2,) + terms[2].shape),
            ]
        elif kind == "stack":
            made = [like((len(terms),) + shape)]
        else:
            made = [like(shape, wide_type if kind == "wide" else low_type)]
        plan.append((len(terms), kind, len(made)))
        values += terms
        shapes += made
    first, sums = 1 + len(values) + len(deps), len(shapes)
    outs = pl.pallas_call(
        functools.partial(fold_kernel, tuple(plan), len(passes)),
        grid_spec=pltpu.PrefetchScalarGridSpec(
            num_scalar_prefetch=1,
            grid=(1,),
            in_specs=[whole_spec(value.shape) for value in values]
            + [anywhere] * (len(deps) + len(passes)),
            out_specs=[whole_spec(shape.shape) for shape in shapes] + [anywhere] * len(passes),
        ),
        out_shape=shapes + [like(value.shape) for value in passes],
        input_output_aliases={first + place: sums + place for place in range(len(passes))},
        compiler_params=room,
        cost_estimate=estimate(0, sum(3 * value.size for value in values)),
    )(head, *values, *[far(dep) for dep in deps], *passes)
    results, place = [], 0
    for _, _, given in plan:
        results.append(outs[place : place + given])
        place += given
    return results, list(outs[sums:])


def plain_job(grid, head, terms, kind):
    whole = lambda term: term
    if kind in ("core", "spread"):
        held = grid.scatter_wide(*terms)
        return [held[:2], held[2:]] if kind == "core" else list(held)
    if kind == "stack":
        return [jnp.stack(terms)]
    if kind == "zsplit":
        rows = terms[4].shape[0]
        total = total_of(terms[:4], whole)
        small = total[rows:].astype(low_type)
        return [total[:rows], small] + [jnp.concatenate([term, small], 0) for term in terms[4:]]
    if kind == "zlast":
        rows = terms[0].shape[0]
        lower = total_of(terms[1:2] + terms[3:], lambda term: term[:rows])
        blocks = jnp.stack([terms[2]] + [term[rows:] for term in terms[3:]])
        return [jnp.concatenate([terms[0], lower], 0), blocks]
    if kind in ("heads", "zpack"):
        total = total_of(terms if kind == "heads" else terms[:2], whole).astype(low_type)
        total = total.reshape((grid.heads, -1) + total.shape[1:])
        made = [total[head[0] ^ offset] for offset in range(grid.heads)]
        if kind == "heads":
            return made
        wo = total_of(terms[2:], whole).astype(low_type)
        half = made[0].shape[0] // 2
        upper = [jnp.concatenate([made[offset][:half], wo[offset]], 0) for offset in range(grid.heads)]
        return upper + [block[half:] for block in made]
    total = total_of(terms, whole)
    if kind == "wide":
        return [total]
    total = total.astype(low_type)
    if kind == "halves":
        half = total.shape[0] // 2
        return [total[:half], total[half:]]
    return list(total) if kind == "slots" else [total]


def join_kernel(count, *refs):
    for slot in range(count):
        refs[-1][slot] = refs[slot][...]


def join(values, deps=()):
    shape = (len(values),) + values[0].shape
    return pl.pallas_call(
        functools.partial(join_kernel, len(values)),
        grid=(1,),
        in_specs=[whole_spec(value.shape) for value in values] + [anywhere] * len(deps),
        out_specs=whole_spec(shape),
        out_shape=like(shape),
        compiler_params=room,
        cost_estimate=estimate(0, 4 * values[0].size),
    )(*values, *[far(dep) for dep in deps])


def three_parts(values):
    first = values.astype(low_type).astype(wide_type)
    rest = values - first
    second = rest.astype(low_type).astype(wide_type)
    return first, second, (rest - second).astype(low_type).astype(wide_type)


def pack_kernel(index_ref, q_ref, k_ref, v_ref, bq_ref, bv_ref, w_ref, piece_ref):
    rows = piece_ref.shape[0]
    w_ref[0, 0:128, :] = q_ref[0:128, :]
    w_ref[0, 128:256, :] = k_ref[0:128, :]
    w_ref[0, 256:384, :] = v_ref[0:128, :]
    w_ref[0, 384:448, :] = q_ref[128:192, :]
    w_ref[0, 448:512, :] = v_ref[128:192, :]
    w_ref[0, 512:576, :] = k_ref[128:192, :]
    row = lax.broadcasted_iota(jnp.int32, (HD, w_ref.shape[2]), 0)
    bias_q = bq_ref[...].astype(wide_type).reshape(1, 192)
    bias_v = bv_ref[...].astype(wide_type).reshape(1, 192)
    gap = jnp.zeros((1, 128), wide_type)
    bias = [bias_q[:, 0:128], gap, bias_v[:, 0:128]]
    bias.append(jnp.concatenate([bias_q[:, 128:192], bias_v[:, 128:192]], 1))
    bias = jnp.concatenate(bias + [gap] * (w_ref.shape[2] // 128 - 4), 1)
    w_ref[0, 576:640, :] = jnp.where(row == 0, bias, 0.0).astype(low_type)
    mine = pl.multiple_of(index_ref[0] * rows, 16)
    piece_ref[...] = w_ref[0, pl.ds(mine, rows), :]


def pack(part, w_query, w_key, w_value, b_query, b_value):
    width = w_query.shape[1]
    rows = 640 // PARTS
    return pl.pallas_call(
        pack_kernel,
        grid_spec=pltpu.PrefetchScalarGridSpec(
            num_scalar_prefetch=1,
            grid=(1,),
            in_specs=[whole_spec(w_query.shape)] * 3 + [whole_spec(b_query.shape)] * 2,
            out_specs=[whole_spec((1, 640, width)), whole_spec((rows, width))],
        ),
        out_shape=[far_like((1, 640, width)), far_like((rows, width))],
        compiler_params=room,
        cost_estimate=estimate(0, 4 * width * 640),
    )(part, far(w_query), far(w_key), far(w_value), far(b_query), far(b_value))


def attend_body(device_head, x_ref, w_ref, seg_ref, q_ref, k_ref, v_ref, ctx_ref):
    length = seg_ref.shape[1]
    seqs = x_ref.shape[0] // length
    lane = lax.broadcasted_iota(jnp.int32, (1, 128), 1)
    low = lane < HD
    half_lane = lane % HD
    row8 = lax.broadcasted_iota(jnp.int32, (8, length), 0)
    bias_row = w_ref[0, 576:592, :][0:1, 0:640].astype(wide_type)
    sums_at = [HD + 4, 20, HD + 12]
    extra_v = jnp.where(half_lane < 3, 1.0, 0.0)
    kept = []
    for seq in range(seqs):
        at = slice(seq * length, (seq + 1) * length)
        qkv = (dot_nt(x_ref[at, :], w_ref[0]) + bias_row).astype(low_type).astype(wide_type)
        q01 = qkv[:, 0:128] * 0.125
        k01 = qkv[:, 128:256]
        v01 = qkv[:, 256:384]
        qv2 = qkv[:, 384:512]
        queries = [q01, q01, qv2 * 0.125]
        keys = [k01, k01, qkv[:, 512:640]]
        values = [v01, v01, qv2]
        seg_row = seg_ref[pl.ds(device_head * seqs + seq, 1), :]
        seg_rows = jnp.broadcast_to(seg_row.astype(wide_type), (8, length))
        same = half_lane == seg_rows.T[:, 0:1].astype(jnp.int32)
        extra_q = jnp.where(same, 1.0, 0.0)
        mask = jnp.where((half_lane < 4) & ~same, masked_score, 0.0)
        for head in range(3):
            mine = ~low if head == 1 else low
            values_mine = low if head == 0 else ~low
            begin = sums_at[head]
            ones = (lane >= begin) & (lane < begin + 3)
            query = jnp.where(mine, queries[head], extra_q)
            key = jnp.where(mine, keys[head], jnp.where(ones, 1.0, mask)).astype(low_type)
            value = jnp.where(values_mine, values[head], extra_v).astype(low_type)
            k_ref[0, head, at, :] = key
            v_ref[0, head, at, :] = value
            kept.append((at, query, value, dot_nt(key, query.astype(low_type))))
    for seq in range(seqs):
        contexts, sums, plain = [], [], []
        for head in range(3):
            at, query, value, scores = kept[3 * seq + head]
            highest = jnp.max(scores, 0, keepdims=True)
            weights_low = jnp.exp(scores - highest).astype(low_type)
            summed = dot_tn(value, weights_low)
            total = summed[HD : HD + 1, :] if head == 0 else summed[0:1, :]
            context = summed[:HD] if head == 0 else summed[HD:]
            first, second, third = three_parts(-(highest + jnp.log(total)))
            sums.append(
                jnp.where(
                    row8 == 4, first, jnp.where(row8 == 5, second, jnp.where(row8 == 6, third, 0.0))
                )
            )
            contexts.append(context * (1.0 / total))
            plain.append(query)
        pair = jnp.concatenate(contexts[:2], 0).astype(low_type)
        ctx_ref[0, at, 0:128] = pair.T
        other = [contexts[2], sums[0], sums[2], sums[1], jnp.zeros((40, length), wide_type)]
        other = jnp.concatenate(other, 0).T
        ctx_ref[0, at, 128:192] = other[:, :HD].astype(low_type)
        turned = pltpu.roll(other, HD, 1)
        for head in range(3):
            begin = sums_at[head]
            ones = (lane >= begin) & (lane < begin + 3)
            given = turned if head == 1 else other
            q_ref[0, head, at, :] = jnp.where(ones, given, plain[head]).astype(low_type)


def attend_own_kernel(head_ref, x_ref, w_ref, seg_ref, q_ref, k_ref, v_ref, ctx_ref):
    attend_body(head_ref[0], x_ref, w_ref, seg_ref, q_ref, k_ref, v_ref, ctx_ref)


def attend_rest_kernel(parts_ref, x_ref, seg_ref, *refs):
    pieces, (q_ref, k_ref, v_ref, ctx_ref, w_ref) = refs[:PARTS], refs[-5:]
    rows = pieces[0].shape[1]
    for slot in range(PARTS):
        at = pl.ds(pl.multiple_of(parts_ref[slot] * rows, 16), rows)
        w_ref[0, at, :] = pieces[slot][0]
    attend_body(parts_ref[PARTS], x_ref, w_ref, seg_ref, q_ref, k_ref, v_ref, ctx_ref)


def attend_cost(count, tokens, length, width):
    return estimate(
        count * (2 * tokens * width * 576 + 3 * 4 * tokens * length * 128),
        2 * tokens * width + count * 2 * (576 * width + 10 * tokens * 128),
        count * 3 * tokens * length,
    )


def attend_outputs(groups, tokens, start):
    heads = pl.BlockSpec((1, 3, tokens, 128), lambda g, *_: (g + start, 0, 0, 0))
    specs = [heads, heads, heads, pl.BlockSpec((1, tokens, 192), lambda g, *_: (g + start, 0, 0))]
    shapes = [far_like((groups, 3, tokens, 128))] * 3 + [far_like((groups, tokens, 192))]
    return specs, shapes


def attend_own(head, layer_in, shard, segments, groups):
    tokens, width = layer_in.shape
    specs, shapes = attend_outputs(groups, tokens, 0)
    return pl.pallas_call(
        attend_own_kernel,
        grid_spec=pltpu.PrefetchScalarGridSpec(
            num_scalar_prefetch=1,
            grid=(1,),
            in_specs=[
                whole_spec((tokens, width)),
                whole_spec(shard.shape),
                whole_spec(segments.shape),
            ],
            out_specs=specs,
        ),
        out_shape=shapes,
        compiler_params=room,
        cost_estimate=attend_cost(1, tokens, segments.shape[1], width),
    )(head, far(layer_in), far(shard), far(segments))


def attend_rest(parts, layer_in, pieces, segments, own):
    tokens, width = layer_in.shape
    count, rows, width = pieces[0].shape
    specs, shapes = attend_outputs(count + 1, tokens, 1)
    piece = pl.BlockSpec((1, rows, width), lambda g, *_: (g, 0, 0))
    return pl.pallas_call(
        attend_rest_kernel,
        grid_spec=pltpu.PrefetchScalarGridSpec(
            num_scalar_prefetch=1,
            grid=(count,),
            in_specs=[whole_spec((tokens, width)), whole_spec(segments.shape)]
            + [piece] * PARTS
            + [anywhere] * len(own),
            out_specs=specs + [pl.BlockSpec((1, 640, width), lambda g, *_: (g, 0, 0))],
        ),
        out_shape=shapes + [far_like((count, 640, width))],
        input_output_aliases={3 + PARTS + place: place for place in range(len(own))},
        compiler_params=room,
        cost_estimate=attend_cost(count, tokens, segments.shape[1], width),
    )(parts, far(layer_in), segments, *pieces, *[far(value) for value in own])


def attend_back_kernel(
    length,
    slots_ref,
    x_ref,
    q_ref,
    k_ref,
    v_ref,
    ctx_ref,
    dctx_ref,
    spare_ref,
    *refs,
):
    dqkv_ref, near_ref, far_ref, held = refs[-4:]
    tokens, width = x_ref.shape
    rows = 640 // PARTS
    lane = lax.broadcasted_iota(jnp.int32, (1, 128), 1)
    low = lane < HD
    half_lane = lane % HD
    for seq in range(tokens // length):
        at = slice(seq * length, (seq + 1) * length)
        grad01 = dctx_ref[0, at, 0:128].astype(wide_type)
        grad2 = dctx_ref[0, at, 128:192].astype(wide_type)
        both = grad01 * ctx_ref[0, at, 0:128].astype(wide_type)
        inner = [
            jnp.sum(jnp.where(low, both, 0.0), -1, keepdims=True),
            jnp.sum(jnp.where(low, 0.0, both), -1, keepdims=True),
            jnp.sum(grad2 * ctx_ref[0, at, 128:192].astype(wide_type), -1, keepdims=True),
        ]
        grads = [grad01, grad01, jnp.concatenate([jnp.zeros((length, HD), wide_type), grad2], 1)]
        grad_q, grad_k, grad_v = [], [], []
        for head in range(3):
            first, second, third = three_parts(-inner[head])
            extra = jnp.where(
                half_lane == 0,
                first,
                jnp.where(half_lane == 1, second, jnp.where(half_lane == 2, third, 0.0)),
            )
            grad = jnp.where(low if head == 0 else ~low, grads[head], extra).astype(low_type)
            query = q_ref[0, head, at, :]
            key = k_ref[0, head, at, :]
            probs = jnp.exp(dot_nt(key, query))
            grad_scores = (probs * dot_nt(v_ref[0, head, at, :], grad)).astype(low_type)
            grad_v.append(dot_nn(probs.astype(low_type), grad))
            grad_k.append(dot_nn(grad_scores, query))
            grad_q.append(dot_tn(key, grad_scores) * 0.125)
        pair = jnp.concatenate([grad_q[0][:HD], grad_q[1][HD:]], 0).astype(low_type)
        dqkv_ref[0, at, 0:128] = pair.T
        dqkv_ref[0, at, 128:256] = jnp.where(low, grad_k[0], grad_k[1]).astype(low_type)
        dqkv_ref[0, at, 256:384] = jnp.where(low, grad_v[0], grad_v[1]).astype(low_type)
        single = grad_q[2].astype(low_type).T
        dqkv_ref[0, at, 384:512] = jnp.where(low, single, grad_v[2].astype(low_type))
        dqkv_ref[0, at, 512:640] = jnp.where(low, grad_k[2], 0.0).astype(low_type)
    grad_all = dqkv_ref[0]
    total = dot_tn(grad_all, x_ref[...])
    sums = jnp.sum(grad_all.astype(wide_type), 0, keepdims=True)
    sums = jnp.concatenate([sums, jnp.zeros((1, width - 640), wide_type)], 1)
    for part in range(PARTS):
        held[part] = total[part * rows : (part + 1) * rows].astype(low_type)
    row = lax.broadcasted_iota(jnp.int32, (HD, width), 0)
    spare = jnp.where(row == 0, sums, spare_ref[...].astype(wide_type))
    held[PARTS - 1, rows - HD : rows] = spare.astype(low_type)
    for slot in range(PARTS // 2):
        near_ref[slot, 0] = held[slots_ref[slot]]
        far_ref[slot, 0] = held[slots_ref[slot + PARTS // 2]]


def attend_back(
    slots, layer_in, queries, keys, values, context, grad_context, spare, deps, length
):
    tokens, width = layer_in.shape
    count = context.shape[0]
    rows = 640 // PARTS
    heads = pl.BlockSpec((1, 3, tokens, 128), lambda g, *_: (g, 0, 0, 0))
    group = pl.BlockSpec((1, tokens, 192), lambda g, *_: (g, 0, 0))
    half = pl.BlockSpec((PARTS // 2, 1, rows, width), lambda g, *_: (0, g, 0, 0))
    return pl.pallas_call(
        functools.partial(attend_back_kernel, length),
        grid_spec=pltpu.PrefetchScalarGridSpec(
            num_scalar_prefetch=1,
            grid=(count,),
            in_specs=[whole_spec((tokens, width)), heads, heads, heads, group, group]
            + [whole_spec(spare.shape)]
            + [anywhere] * len(deps),
            out_specs=[pl.BlockSpec((1, tokens, 640), lambda g, *_: (g, 0, 0)), half, half],
            scratch_shapes=[pltpu.VMEM((PARTS, rows, width), low_type)],
        ),
        out_shape=[
            (far_like if count > 1 else like)((count, tokens, 640)),
            like((PARTS // 2, count, rows, width)),
            like((PARTS // 2, count, rows, width)),
        ],
        compiler_params=room,
        cost_estimate=estimate(
            count * (2 * tokens * width * 576 + 3 * 10 * tokens * length * 128),
            2 * tokens * width + count * 2 * (576 * width + 16 * tokens * 128),
            count * 3 * tokens * length,
        ),
    )(slots, far(layer_in), queries, keys, far(values), context, grad_context, spare, *[far(dep) for dep in deps])


def mean_last(values):
    return jnp.mean(values, -1, keepdims=True)


def tiles(tokens, size, body):
    def step(index, carry):
        body(pl.ds(pl.multiple_of(index * size, size), size))
        return carry

    lax.fori_loop(0, tokens // size, step, 0)


def gelu_pair(values):
    cumulative = 0.5 * (1.0 + lax.erf(values * 0.7071067811865476))
    density = jnp.exp(-0.5 * values * values) * 0.3989422804014327
    return values * cumulative, cumulative + values * density


class Loads:
    def __init__(self, slots_ref, w_in_hbm, w_out_hbm, w_in, w_out, sems):
        self.count = sems.shape[1]
        self.size = w_out.shape[0] // self.count
        self.copies = []
        for slot in range(self.count):
            source = pl.ds(pl.multiple_of(slots_ref[slot] * self.size, 128), self.size)
            target = pl.ds(slot * self.size, self.size)
            self.copies.append(
                (
                    pltpu.make_async_copy(w_in_hbm.at[:, source], w_in.at[:, target], sems.at[0, slot]),
                    pltpu.make_async_copy(w_out_hbm.at[source], w_out.at[target], sems.at[1, slot]),
                )
            )

    def start(self):
        for copies in self.copies:
            for copy in copies:
                copy.start()

    def wait(self, low, high):
        for slot in range(-(-low // self.size), -(-high // self.size)):
            for copy in self.copies[slot]:
                copy.wait()


def overlaps(size, chunks, block, blocks):
    return [
        [
            (which, max(chunk * size, which * block), min((chunk + 1) * size, (which + 1) * block))
            for which in range(blocks)
            if max(chunk * size, which * block) < min((chunk + 1) * size, (which + 1) * block)
        ]
        for chunk in range(chunks)
    ]


def ffn_kernel(
    chunks,
    slots_ref,
    x_ref,
    ctx_ref,
    wo_ref,
    b_output_ref,
    gain_attn_ref,
    shift_attn_ref,
    b_outer_ref,
    gain_ffn_ref,
    shift_ffn_ref,
    b_in_ref,
    cot_hbm,
    w_in_hbm,
    w_out_hbm,
    rstd_ref,
    sums_ref,
    gb_ref,
    normal_hbm,
    out_hbm,
    total_hbm,
    outer_near_hbm,
    outer_far_hbm,
    near_hbm,
    far_hbm,
    w_in,
    w_out,
    normed,
    outer,
    active,
    slope,
    low,
    normal_low,
    result_low,
    grad_out,
    cot_in,
    b_row,
    sems,
    cot_sem,
    out_sems,
):
    step = pl.program_id(0)
    tokens, width = x_ref.shape
    hidden = w_out.shape[0]
    size = hidden // chunks
    half = hidden // 2
    loads = Loads(slots_ref, w_in_hbm, w_out_hbm, w_in, w_out, sems)
    head = slots_ref[loads.count]
    b_output, gain_attn, shift_attn, b_outer, gain_ffn, shift_ffn = (
        ref[...].reshape(1, width)
        for ref in (
            b_output_ref,
            gain_attn_ref,
            shift_attn_ref,
            b_outer_ref,
            gain_ffn_ref,
            shift_ffn_ref,
        )
    )
    load_cot = pltpu.make_async_copy(cot_hbm, cot_in, cot_sem.at[0])
    small = [
        pltpu.make_async_copy(source, target, out_sems.at[place])
        for place, (source, target) in enumerate(
            ((normal_low, normal_hbm), (result_low, out_hbm), (outer, total_hbm))
        )
    ]
    count = len(small)
    outer_copies, inner_copies = [], []
    for chunk, cuts in enumerate(overlaps(size, chunks, half, 2)):
        from_active, from_out = [], []
        for which, begin, end in cuts:
            at = pl.ds(begin - which * half, end - begin)
            from_active.append(
                pltpu.make_async_copy(
                    active.at[chunk, pl.ds(begin - chunk * size, end - begin), pl.ds(0, width)],
                    (outer_near_hbm, outer_far_hbm)[which].at[at],
                    out_sems.at[count],
                )
            )
            from_out.append(
                pltpu.make_async_copy(
                    w_out.at[pl.ds(begin, end - begin)],
                    (near_hbm, far_hbm)[which].at[at],
                    out_sems.at[count + 1],
                )
            )
            count += 2
        outer_copies.append(from_active)
        inner_copies.append(from_out)

    @pl.when(step == 0)
    def _():
        loads.start()
        b_row[1:2, :] = b_in_ref[...].reshape(1, hidden)
        for slot in range(loads.count):
            source = pl.ds(pl.multiple_of(slots_ref[slot] * loads.size, 128), loads.size)
            b_row[0:1, slot * loads.size : (slot + 1) * loads.size] = b_row[1:2, source]
        outer[...] = jnp.zeros_like(outer)
        branch = dot_nn(ctx_ref[0], wo_ref[head])
        for offset in range(1, wo_ref.shape[0]):
            branch += dot_nn(ctx_ref[offset], wo_ref[head ^ offset])
        normed[...] = branch

        def one(at):
            total = x_ref[at, :].astype(wide_type) + (normed[at, :] + b_output)
            centred = total - mean_last(total)
            rstd = lax.rsqrt(mean_last(centred * centred) + epsilon)
            normal = centred * rstd
            result = normal * gain_attn + shift_attn
            normed[at, :] = result
            low[at, :] = result.astype(low_type)
            normal_low[at, :] = normal.astype(low_type)
            rstd_ref[at, :] = jnp.broadcast_to(rstd, (rstd.shape[0], 128))

        tiles(tokens, 256, one)
        small[0].start()
        load_cot.start()

    for chunk in range(chunks):

        @pl.when(step == chunk)
        def _():
            loads.wait(chunk * size, (chunk + 1) * size)

    @pl.when(step < chunks)
    def _():
        at = pl.ds(pl.multiple_of(step * size, 128), size)
        inner = dot_nn(low[...], w_in[:, at]) + b_row[0:1, at]
        values, gradient = gelu_pair(inner)
        values = values.astype(low_type)
        active[step] = values
        slope[step] = gradient.astype(low_type)
        outer[...] += dot_nn(values, w_out[at, :])

    @pl.when(step == chunks - 1)
    def _():
        sums_ref[...] = jnp.zeros_like(sums_ref)
        load_cot.wait()

        def one(at):
            total = normed[at, :] + (outer[at, :] + b_outer)
            centred = total - mean_last(total)
            rstd = lax.rsqrt(mean_last(centred * centred) + epsilon)
            normal = centred * rstd
            result_low[at, :] = (normal * gain_ffn + shift_ffn).astype(low_type)
            grad = cot_in[at, :].astype(wide_type)
            scaled = grad * gain_ffn
            grad_sum = rstd * (scaled - mean_last(scaled) - normal * mean_last(scaled * normal))
            grad_low = grad_sum.astype(low_type)
            grad_out[at, :] = grad_low
            outer[at, :] = grad_low.astype(wide_type)
            sums_ref[0:1, :] += jnp.sum(grad * normal, 0, keepdims=True)
            sums_ref[1:2, :] += jnp.sum(grad, 0, keepdims=True)
            sums_ref[2:3, :] += jnp.sum(grad_low.astype(wide_type), 0, keepdims=True)

        tiles(tokens, 256, one)
        small[1].start()

    @pl.when(step >= chunks)
    def _():
        which = step - chunks
        at = pl.ds(pl.multiple_of(which * size, 128), size)
        grad = grad_out[...]
        active[which, :, 0:width] = dot_tn(active[which], grad).astype(low_type)
        grad_inner = (dot_nt(grad, w_out[at, :]) * slope[which].astype(wide_type)).astype(low_type)
        gb_ref[...] = jnp.sum(grad_inner.astype(wide_type), 0, keepdims=True)
        w_out[at, :] = dot_tn(grad_inner, low[...]).astype(low_type)
        outer[...] += dot_nt(grad_inner, w_in[:, at])

    for chunk in range(chunks):

        @pl.when(step == chunks + chunk)
        def _():
            for copy in outer_copies[chunk] + inner_copies[chunk]:
                copy.start()

    @pl.when(step == 2 * chunks - 1)
    def _():
        small[2].start()
        for copy in small:
            copy.wait()
        for copies in outer_copies + inner_copies:
            for copy in copies:
                copy.wait()


def ffn(slots, layer_in, context, w_output, cotangent, vectors, w_in, w_out, b_in):
    tokens, width = layer_in.shape
    hidden = w_out.shape[0]
    chunks = 3
    blocks = slots.shape[0] - 1
    size = hidden // chunks
    back = lambda i, *_: (0, jnp.maximum(i - chunks, 0))
    once = dict(pipeline_mode=pl.Buffered(1))
    copies = 3 + 4 * chunks
    return pl.pallas_call(
        functools.partial(ffn_kernel, chunks),
        grid_spec=pltpu.PrefetchScalarGridSpec(
            num_scalar_prefetch=1,
            grid=(2 * chunks,),
            in_specs=[
                whole_spec((tokens, width), **once),
                whole_spec(context.shape, **once),
                whole_spec(w_output.shape, **once),
            ]
            + [whole_spec(vector.shape, **once) for vector in vectors]
            + [whole_spec(b_in.shape, **once), anywhere, anywhere, anywhere],
            out_specs=[
                whole_spec((tokens, 128)),
                whole_spec((8, width)),
                pl.BlockSpec((1, size), back),
            ]
            + [anywhere] * 7,
            scratch_shapes=[
                pltpu.VMEM((width, hidden), low_type),
                pltpu.VMEM((hidden, width), low_type),
                pltpu.VMEM((tokens, width), wide_type),
                pltpu.VMEM((tokens, width), wide_type),
                pltpu.VMEM((chunks, tokens, size), low_type),
                pltpu.VMEM((chunks, tokens, size), low_type),
            ]
            + [pltpu.VMEM((tokens, width), low_type)] * 5
            + [pltpu.VMEM((8, hidden), wide_type)]
            + [pltpu.SemaphoreType.DMA((2, blocks)), pltpu.SemaphoreType.DMA((1,)), pltpu.SemaphoreType.DMA((copies,))],
        ),
        out_shape=[
            like((tokens, 128), wide_type),
            like((8, width), wide_type),
            like((1, hidden), wide_type),
            far_like((tokens, width)),
            far_like((tokens, width)),
            far_like((tokens, width), wide_type),
        ]
        + [far_like((hidden // 2, width))] * 4,
        compiler_params=large_room,
        cost_estimate=estimate(
            2 * tokens * width * (6 * hidden + width),
            2 * (tokens * 10 * width + 4 * hidden * width),
            tokens * hidden,
        ),
    )(slots, layer_in, context, w_output, *vectors, b_in, far(cotangent), far(w_in), far(w_out))


def norm_back_kernel(
    index_ref,
    total_ref,
    normal_ref,
    rstd_ref,
    ctx_ref,
    wo_ref,
    gain_ref,
    sums_in_ref,
    gb_ref,
    *refs,
):
    branch_ref, dctx_ref, near_ref, far_ref, spare_ref, sums, acc, held, inner_sums = refs[-9:]
    step = pl.program_id(0)
    size = branch_ref.shape[0]
    head = index_ref[PARTS]
    gain_attn = gain_ref[...].reshape(1, total_ref.shape[1])
    heads = wo_ref.shape[0]
    rows = wo_ref.shape[1] // PARTS

    @pl.when(step == 0)
    def _():
        sums[...] = sums_in_ref[...]

    def one(at):
        grad = total_ref[at, :]
        normal = normal_ref[at, :].astype(wide_type)
        scaled = grad * gain_attn
        rstd = rstd_ref[at, 0:1]
        grad_sum = rstd * (scaled - mean_last(scaled) - normal * mean_last(scaled * normal))
        grad_low = grad_sum.astype(low_type)
        branch_ref[at, :] = grad_low
        sums[3:4, :] += jnp.sum(grad * normal, 0, keepdims=True)
        sums[4:5, :] += jnp.sum(grad, 0, keepdims=True)
        sums[5:6, :] += jnp.sum(grad_low.astype(wide_type), 0, keepdims=True)

    tiles(size, 256, one)
    branch = branch_ref[...]
    for offset in range(heads):
        context = ctx_ref[offset]
        weights = wo_ref[head ^ offset]
        grad_context = dot_nt(branch, weights).astype(low_type)
        dctx_ref[offset] = grad_context
        part = dot_tn(context, branch)

        @pl.when(step == 0)
        def _():
            acc[offset] = part

        @pl.when(step > 0)
        def _():
            acc[offset] += part

    @pl.when(step == pl.num_programs(0) - 1)
    def _():
        for offset in range(heads):
            for part in range(PARTS):
                held[part, offset] = acc[offset, part * rows : (part + 1) * rows, :].astype(low_type)
        for slot in range(PARTS // 2):
            near_ref[slot] = held[index_ref[slot]]
            far_ref[slot] = held[index_ref[slot + PARTS // 2]]
        block = gb_ref.shape[1] // PARTS
        for slot in range(PARTS):
            inner_sums[pl.ds(index_ref[slot], 1), :] = gb_ref[:, slot * block : (slot + 1) * block]
        lines = [jnp.zeros((1, 2 * block), wide_type), sums[0:6, :]]
        for pair in range(PARTS // 2):
            both = [inner_sums[2 * pair + half : 2 * pair + half + 1, :] for half in range(2)]
            lines.append(jnp.concatenate(both, 1))
        lines.append(jnp.zeros((5, 2 * block), wide_type))
        spare_ref[...] = jnp.zeros_like(spare_ref)
        spare_ref[0:16, :] = jnp.concatenate(lines, 0).astype(low_type)


def norm_back(
    index, total, normal, rstd, context, w_output, gain, sums, gb, deps
):
    tokens, width = total.shape
    heads, group = w_output.shape[:2]
    size = tokens
    tile = pl.BlockSpec((size, width), lambda i, *_: (i, 0))
    groups = pl.BlockSpec((heads, size, group), lambda i, *_: (0, i, 0))
    half = (PARTS // 2, heads, group // PARTS, width)
    return pl.pallas_call(
        norm_back_kernel,
        grid_spec=pltpu.PrefetchScalarGridSpec(
            num_scalar_prefetch=1,
            grid=(1,),
            in_specs=[
                tile,
                tile,
                pl.BlockSpec((size, 128), lambda i, *_: (i, 0)),
                groups,
                whole_spec(w_output.shape),
                whole_spec(gain.shape),
                whole_spec(sums.shape),
                whole_spec(gb.shape),
            ]
            + [anywhere] * len(deps),
            out_specs=[
                tile,
                groups,
                whole_spec(half),
                whole_spec(half),
                whole_spec((HD, width)),
            ],
            scratch_shapes=[
                pltpu.VMEM((8, width), wide_type),
                pltpu.VMEM((heads, group, width), wide_type),
                pltpu.VMEM((PARTS,) + half[1:], low_type),
                pltpu.VMEM((PARTS, gb.shape[1] // PARTS), wide_type),
            ],
        ),
        out_shape=[
            like((tokens, width)),
            like(context.shape),
            like(half),
            like(half),
            like((HD, width)),
        ],
        compiler_params=room,
        cost_estimate=estimate(
            4 * tokens * width * width, 2 * tokens * width * 8 + 6 * width * width
        ),
    )(index, far(total), far(normal), far(rstd), far(context), far(w_output), gain, far(sums), far(gb), *[far(dep) for dep in deps])


def input_kernel(branch_ref, grads_ref, shard_ref, weights_ref, *refs):
    total = branch_ref[...].astype(wide_type) + dot_nn(grads_ref[0], shard_ref[0])
    for group in range(weights_ref.shape[0]):
        total += dot_nn(grads_ref[group + 1], weights_ref[group])
    refs[-1][...] = total


def input_back(branch, grads, shard, weights, deps):
    tokens, width = branch.shape
    size = tokens // 2
    tile = pl.BlockSpec((size, width), lambda i: (i, 0))
    groups = pl.BlockSpec((grads.shape[0], size, 640), lambda i: (0, i, 0))
    return pl.pallas_call(
        input_kernel,
        grid=(2,),
        in_specs=[tile, groups, whole_spec(shard.shape), whole_spec(weights.shape)]
        + [anywhere] * len(deps),
        out_specs=tile,
        out_shape=far_like((tokens, width), wide_type),
        compiler_params=room,
        cost_estimate=estimate(2 * tokens * width * 640 * 4, 16 * tokens * width),
    )(branch, grads, shard, weights, *[far(dep) for dep in deps])


def finish_kernel(index_ref, *refs):
    owns, blocks = refs[0:2], refs[2:4]
    q_ref, k_ref, v_ref, wo_ref, bq_ref, bv_ref, gb_ref = refs[4:11]
    vectors = refs[11:17]
    held, small_rows = refs[-2:]
    rows = held.shape[1]
    heads, extra, width = blocks[0].shape[1:]
    head, row = index_ref[PARTS], index_ref[PARTS + 1]
    for slot in range(PARTS):
        part = index_ref[slot]
        half, place = divmod(slot, PARTS // 2)
        held[part] = owns[half][place]
        for offset in range(heads):
            at = pl.ds(pl.multiple_of(part * extra, 8), extra)
            wo_ref[head ^ offset, at, :] = blocks[half][place, offset].astype(wide_type)
    whole = held[...].reshape(PARTS * rows, width)
    for ref, first, second in ((q_ref, 0, 384), (k_ref, 128, 512), (v_ref, 256, 448)):
        ref[0:128, :] = whole[first : first + 128].astype(wide_type)
        ref[128:192, :] = whole[second : second + HD].astype(wide_type)
    small_rows[...] = whole[576:592].astype(wide_type)
    sums = small_rows[0:1, :]
    for ref, first, second in ((bq_ref, 0, 384), (bv_ref, 256, 448)):
        joined = jnp.concatenate([sums[:, first : first + 128], sums[:, second : second + HD]], 1)
        ref[...] = joined.reshape(ref.shape)
    for which, ref in enumerate(vectors):
        ref[...] = small_rows[1 + which : 2 + which, :].reshape(ref.shape)
    block = gb_ref.shape[0]
    per_row = width // block
    place = row * heads + head
    sums = small_rows[pl.ds(7 + place // per_row, 1), :]
    total = jnp.zeros((1, block), wide_type)
    for which in range(per_row):
        total = jnp.where(
            place % per_row == which, sums[:, which * block : (which + 1) * block], total
        )
    gb_ref[...] = total.reshape(gb_ref.shape)


def finish(index, owns, blocks, block):
    rows = 640 // PARTS
    heads, extra, width = blocks[0].shape[1:]
    group = PARTS * extra
    pieces = owns + blocks
    shapes = (
        [like((group, width), wide_type)] * 3
        + [like((heads, group, width), wide_type)]
        + [like((group,), wide_type)] * 2
        + [like((block,), wide_type)]
        + [like((width,), wide_type)] * 6
    )
    return pl.pallas_call(
        finish_kernel,
        grid_spec=pltpu.PrefetchScalarGridSpec(
            num_scalar_prefetch=1,
            grid=(1,),
            in_specs=[whole_spec(piece.shape) for piece in pieces],
            out_specs=[whole_spec(shape.shape) for shape in shapes],
            scratch_shapes=[
                pltpu.VMEM((PARTS, rows, width), low_type),
                pltpu.VMEM((16, width), wide_type),
            ],
        ),
        out_shape=shapes,
        compiler_params=room,
        cost_estimate=estimate(0, 16 * width * width),
    )(index, *pieces)


def local(
    grid,
    layer_in,
    segment_ids,
    w_query,
    w_key,
    w_value,
    b_query,
    b_value,
    w_output,
    b_output,
    gain_attn,
    shift_attn,
    w_inner,
    b_inner,
    w_outer,
    b_outer,
    gain_ffn,
    shift_ffn,
    cotangent,
):
    tokens, width = layer_in.shape
    length = segment_ids.shape[1]
    group = w_query.shape[1]
    hidden = w_inner.shape[1]
    heads = grid.heads
    row = lax.axis_index("rows")
    head = lax.axis_index("heads")

    head_index = head.astype(jnp.int32)[None]
    part = grid.part_of(row.astype(jnp.int32))[None]
    shard, piece = pack(part, w_query.T, w_key.T, w_value.T, b_query, b_value)
    got = [grid.across_heads(piece, offset) for offset in range(1, heads)]
    own = attend_own(head_index, layer_in, shard, segment_ids, heads)
    parts = jnp.concatenate([grid.part_of(grid.helper_parts()), head_index])

    row_slots = grid.row_slots()
    w_in, w_out, b_in = w_inner, w_outer, b_inner
    if not grid.native:
        w_in = jnp.take(w_in.reshape(width, grid.rows, -1), row_slots, axis=1).reshape(width, hidden)
        w_out = jnp.take(w_out.reshape(grid.rows, -1, width), row_slots, axis=0).reshape(hidden, width)
        b_in = jnp.take(b_in.reshape(grid.rows, -1), row_slots, axis=0).reshape(hidden)
    natural = jnp.arange(PARTS, dtype=jnp.int32)
    index = jnp.concatenate([row_slots if grid.native else natural, head_index])
    w_output_heads = w_output.reshape(heads, group, width)
    vectors = [b_output, gain_attn, shift_attn, b_outer, gain_ffn, shift_ffn]
    held = join(got, (own[1],))
    held = [held] + grid.across_chips([held] * 4)
    held = held + [grid.across_core(value) for value in held]

    queries, keys, values, context, w_rest = attend_rest(parts, layer_in, held, segment_ids, own)
    rstd, sums, gb_inner, normal, layer_out, total, outer_near, outer_far, inner_near, inner_far = ffn(
        index, layer_in, context, w_output_heads, cotangent, vectors, w_in, w_out, b_in
    )
    slot_shape = (grid.rows // 2, hidden // grid.rows, width)
    outer_got = grid.across_core(outer_far.reshape(slot_shape))
    inner_got = grid.across_core(inner_far.reshape(slot_shape))
    if not grid.native:
        gb_inner = jnp.take(gb_inner.reshape(grid.rows, -1), grid.row_places(), axis=0).reshape(1, hidden)
    folded = functools.partial(fold, grid, head_index)
    first, second = grid.steps - 2, grid.steps - 1

    branch, grad_context, wo_near, wo_far, spare = norm_back(
        index, total, normal, rstd, context, w_output_heads, gain_attn, sums, gb_inner, ()
    )
    wo_near, wo_far = grid.spread_parts(wo_near, wo_far)

    ((outer, outer_send), (inner, inner_send)), (wo_far,) = folded(
        [
            ([outer_near.reshape(slot_shape), outer_got], "core"),
            ([inner_near.reshape(slot_shape), inner_got], "core"),
        ],
        (),
        (wo_far,),
    )
    outer_got = grid.across_chip(outer_send, first)
    inner_got = grid.across_chip(inner_send, first)
    wo_got = grid.across_core(wo_far)
    grads, near, far_half = attend_back(
        index, layer_in, queries, keys, values, context, grad_context, spare, (inner_send,), length
    )
    near, far_half = grid.spread_parts(near, far_half)
    ((outer, outer_send), (inner, inner_send), wo), (far_half,) = folded(
        [
            ([outer, outer_got], "halves"),
            ([inner, inner_got], "halves"),
            ([wo_near, wo_got], "spread"),
        ],
        (),
        (far_half,),
    )
    outer_got = grid.across_chip(outer_send, second)
    wo_got = grid.across_chips(wo)
    got = grid.across_core(far_half)
    input_grad = input_back(branch, grads, shard, w_rest, (wo[3],))
    (outer, (near, send)), (inner_send,) = folded(
        [
            ([outer[0], outer_got[0], wo[0]] + wo_got, "zpack"),
            ([near, got], "core"),
        ],
        (input_grad,),
        (inner_send,),
    )
    outer_got = [grid.across_heads(outer[offset], offset) for offset in range(1, heads)]
    got = grid.across_chip(send, first)
    ((upper, wo, *outer_send), (near, send)), (inner_send,) = folded(
        [
            ([outer[0]] + outer_got + list(outer[heads + 1 :]), "zsplit"),
            ([near, got], "halves"),
        ],
        (),
        (inner_send,),
    )
    outer_got = [grid.across_heads(outer_send[offset - 1], offset) for offset in range(1, heads)]
    got = grid.across_chip(send, second)
    inner_got = grid.across_chip(inner_send, second)
    (groups, (out_w_outer, wo), inner), _ = folded(
        [
            ([near[0], got[0]], "slots"),
            ([upper, outer[heads], wo] + outer_got, "zlast"),
            ([inner[0], inner_got[0]], "heads"),
        ],
    )
    got = [grid.across_heads(groups[offset], offset) for offset in range(1, heads)]
    if grid.native:
        wo_got = grid.across_chips([wo] * 4)
    ((own,),), inner = folded([([groups[0]] + got, "sum")], (), inner)
    inner_got = [grid.across_heads(inner[offset], offset) for offset in range(1, heads)]
    if grid.native:
        own_got = grid.across_chips([own] * 4)
        ((out_w_inner,), (own,), (wo,)), _ = folded(
            [
                ([inner[0]] + inner_got, "wide"),
                ([own] + own_got, "stack"),
                ([wo] + wo_got, "stack"),
            ]
        )
        owns, blocks = [own, grid.across_core(own)], [wo, grid.across_core(wo)]
    else:
        ((out_w_inner,),), _ = folded([([inner[0]] + inner_got, "wide")])
        own = grid.gather_wide(own).reshape(PARTS, -1, width)
        wo = grid.coarse(grid.gather_wide(wo))
        owns, blocks = [own[: PARTS // 2], own[PARTS // 2 :]], [wo[: PARTS // 2], wo[PARTS // 2 :]]
    block = hidden // (grid.rows * heads)
    gw_query, gw_key, gw_value, gw_output, gb_query, gb_value, gb_inner, *vector = finish(
        jnp.concatenate([index, row.astype(jnp.int32)[None]]), owns, blocks, block
    )
    return (
        layer_out,
        input_grad,
        gw_query.T,
        gw_key.T,
        gw_value.T,
        gb_query,
        gb_value,
        gw_output.reshape(width, width),
        vector[5],
        vector[3],
        vector[4],
        out_w_inner.T,
        gb_inner,
        out_w_outer,
        vector[2],
        vector[0],
        vector[1],
    )


def solution(mesh):
    grid = Grid(mesh)
    return jax.shard_map(
        lambda *values: local(grid, *values),
        mesh=mesh,
        in_specs=(
            P(("rows", "heads"), None),
            P("rows", None),
            P(None, "heads"),
            P(None, "heads"),
            P(None, "heads"),
            P("heads"),
            P("heads"),
            P(),
            P(),
            P(),
            P(),
            P(),
            P(),
            P(),
            P(),
            P(),
            P(),
            P(("rows", "heads"), None),
        ),
        out_specs=(
            P(("rows", "heads"), None),
            P(("rows", "heads"), None),
            P(None, "heads"),
            P(None, "heads"),
            P(None, "heads"),
            P("heads"),
            P("heads"),
            P(),
            P(),
            P(),
            P(),
            P(None, ("rows", "heads")),
            P(("rows", "heads")),
            P(("rows", "heads"), None),
            P(),
            P(),
            P(),
        ),
        check_vma=False,
    )
```

```python
import functools

import jax
import jax.numpy as jnp
from jax import lax
from jax.experimental import pallas as pl
from jax.experimental.pallas import tpu as pltpu
from jax.sharding import PartitionSpec as P

HD = 64
PARTS = 8
epsilon = 1e-06
masked_score = -1000000000.0
low_type = jnp.bfloat16
wide_type = jnp.float32
room = pltpu.CompilerParams(vmem_limit_bytes=32 * 1024 * 1024)
large_room = pltpu.CompilerParams(vmem_limit_bytes=60 * 1024 * 1024)


def contract(left, right, left_dim, right_dim):
    return lax.dot_general(
        left, right, (((left_dim,), (right_dim,)), ((), ())), preferred_element_type=wide_type
    )


def dot_nn(left, right):
    return contract(left, right, 1, 0)


def dot_nt(left, right):
    return contract(left, right, 1, 1)


def dot_tn(left, right):
    return contract(left, right, 0, 0)


class Grid:
    def __init__(self, mesh):
        self.rows = mesh.shape["rows"]
        self.heads = mesh.shape["heads"]
        self.native = self.rows == PARTS
        self.steps = self.rows.bit_length() - 2
        up = list(range(1, self.steps + 1))
        self.orders = (up, up[::-1])

    def permute(self, value, row_masks, head_mask=0):
        pairs = [
            (row * self.heads + head, (row ^ row_masks[row & 1]) * self.heads + (head ^ head_mask))
            for row in range(self.rows)
            for head in range(self.heads)
        ]
        return lax.ppermute(value, ("rows", "heads"), pairs)

    def across_core(self, value):
        return self.permute(value, (1, 1))

    def across_heads(self, value, offset):
        return self.permute(value, (0, 0), offset)

    def across_chip(self, value, step):
        return self.permute(value, [1 << order[step] for order in self.orders])

    def across_chips(self, values):
        masks = [self.slot_masks(core) for core in (0, 1)]
        return [
            self.permute(value, (masks[0][slot], masks[1][slot]))
            for slot, value in enumerate(values)
            if slot
        ]

    def slot_masks(self, core):
        last = self.steps - 1
        masks = []
        for slot in range(1 << self.steps):
            mask = 0
            for step in range(self.steps):
                mask |= ((slot >> (last - step)) & 1) << self.orders[core][step]
            masks.append(mask)
        return masks

    def row_slots(self):
        row = lax.axis_index("rows").astype(jnp.int32)
        masks = jnp.array([self.slot_masks(0), self.slot_masks(1)], jnp.int32)
        core = row & 1
        return jnp.concatenate([row ^ masks[core], (row ^ 1) ^ masks[1 - core]])

    def row_places(self):
        row = lax.axis_index("rows").astype(jnp.int32)
        half = self.rows // 2
        inverse = []
        for core in (0, 1):
            table = [0] * half
            for slot, mask in enumerate(self.slot_masks(core)):
                table[mask >> 1] = slot
            inverse.append(table)
        inverse = jnp.array(inverse, jnp.int32)
        apart = jnp.arange(self.rows, dtype=jnp.int32) ^ row
        other = apart & 1
        return other * half + inverse[(row & 1) ^ other, apart >> 1]

    def helper_parts(self):
        row = lax.axis_index("rows").astype(jnp.int32)
        masks = jnp.array([self.slot_masks(0)[:4], self.slot_masks(1)[:4]], jnp.int32)
        core = row & 1
        return jnp.concatenate([row ^ masks[core], (row ^ 1) ^ masks[1 - core]])

    def part_of(self, row):
        if self.native:
            return row
        low, high = sorted(self.orders[0][-2:])
        return (row & 1) + 2 * ((row >> low) & 1) + 4 * ((row >> high) & 1)

    def scatter_wide(self, mine, got):
        held = add_like(mine, got)
        for step in range(self.steps - 2):
            half = held.shape[0] // 2
            held = add_like(held[:half], self.across_chip(held[half:], step))
        return held

    def gather_wide(self, value):
        held = jnp.stack([value] + self.across_chips([value] * 4))
        for step in reversed(range(self.steps - 2)):
            held = jnp.concatenate([held, self.across_chip(held, step)], 0)
        held = jnp.concatenate([held, self.across_core(held)], 0)
        return jnp.take(held, self.row_places(), axis=0)

    def coarse(self, blocks):
        blocks = blocks.reshape((PARTS, -1) + blocks.shape[1:]).transpose(0, 2, 1, 3, 4)
        return blocks.reshape(PARTS, blocks.shape[1], -1, blocks.shape[4])

    def spread_parts(self, near, far):
        if self.native:
            return near, far
        parts = jnp.concatenate([near, far], 0)
        count, rows, cols = parts.shape[1:]
        finer = self.rows // PARTS
        parts = parts.reshape(PARTS, count, finer, rows // finer, cols).transpose(0, 2, 1, 3, 4)
        parts = parts.reshape(self.rows, count, rows // finer, cols)
        parts = jnp.take(parts, self.row_slots(), axis=0)
        return parts[: self.rows // 2], parts[self.rows // 2 :]


def add_like(first, second):
    return (first.astype(wide_type) + second.astype(wide_type)).astype(first.dtype)


def estimate(flops, moved, exps=0):
    return pl.CostEstimate(
        flops=flops, bytes_accessed=moved, transcendentals=exps
    )


def like(shape, dtype=low_type):
    return jax.ShapeDtypeStruct(shape, dtype)


def far(value):
    return pltpu.with_memory_space_constraint(value, pltpu.HBM)


def far_like(shape, dtype=low_type):
    return pltpu.HBM(shape, dtype)


def whole_spec(shape, **options):
    return pl.BlockSpec(shape, lambda *ids: (0,) * len(shape), **options)


anywhere = pl.BlockSpec(memory_space=pl.ANY)


def total_of(terms, cut):
    return sum(cut(term).astype(wide_type) for term in terms)


def fold_kernel(plan, passed, head_ref, *refs):
    outs = list(refs[len(refs) - passed - sum(job[2] for job in plan) : len(refs) - passed])
    refs = list(refs)
    for count, kind, given in plan:
        terms, refs = refs[:count], refs[count:]
        made, outs = outs[:given], outs[given:]
        if kind == "halves":
            size = made[0].shape[0]
            for half, target in enumerate(made):
                at = slice(half * size, (half + 1) * size)
                target[...] = total_of(terms, lambda term: term[at]).astype(target.dtype)
        elif kind == "slots":
            for slot, target in enumerate(made):
                target[...] = total_of(terms, lambda term: term[slot]).astype(target.dtype)
        elif kind == "heads" or kind == "zpack":
            heads = len(made) if kind == "heads" else len(made) // 2
            rows = terms[0].shape[0] // heads
            for offset in range(heads):
                begin = (head_ref[0] ^ offset) * rows
                if kind == "heads":
                    at = pl.ds(pl.multiple_of(begin, 16), rows)
                    made[offset][...] = total_of(terms, lambda term: term[at, :]).astype(low_type)
                    continue
                half = rows // 2
                upper = pl.ds(pl.multiple_of(begin, 16), half)
                lower = pl.ds(pl.multiple_of(begin + half, 16), half)
                target, other = made[offset], made[heads + offset]
                target[0:half] = total_of(terms[:2], lambda term: term[upper, :]).astype(low_type)
                target[half:] = total_of(terms[2:], lambda term: term[offset]).astype(low_type)
                other[...] = total_of(terms[:2], lambda term: term[lower, :]).astype(low_type)
        elif kind == "zsplit":
            rows = made[0].shape[0]
            made[0][...] = total_of(terms[:4], lambda term: term[0:rows])
            total = total_of(terms[:4], lambda term: term[rows:]).astype(low_type)
            made[1][...] = total
            for term, target in zip(terms[4:], made[2:]):
                target[0:rows] = term[...]
                target[rows:] = total
        elif kind == "zlast":
            rows = terms[0].shape[0]
            made[0][0:rows] = terms[0][...]
            made[0][rows:] = total_of(terms[1:2] + terms[3:], lambda term: term[0:rows])
            made[1][0] = terms[2][...]
            for place, term in enumerate(terms[3:]):
                made[1][place + 1] = term[rows:]
        elif kind == "stack":
            for place, term in enumerate(terms):
                made[0][place] = term[...]
        else:
            made[0][...] = total_of(terms, lambda term: term[...]).astype(made[0].dtype)


def fold(grid, head, jobs, deps=(), passes=()):
    if not grid.native:
        return [plain_job(grid, head, *job) for job in jobs], list(passes)
    plan, values, shapes = [], [], []
    for terms, kind in jobs:
        kind = {"core": "halves", "spread": "slots"}.get(kind, kind)
        shape = terms[0].shape
        if kind == "halves":
            made = [like((shape[0] // 2,) + shape[1:])] * 2
        elif kind == "slots":
            made = [like(shape[1:])] * shape[0]
        elif kind == "heads":
            made = [like((shape[0] // grid.heads, shape[1]))] * grid.heads
        elif kind == "zpack":
            rows = shape[0] // grid.heads // 2
            made = [like((rows + terms[2].shape[1], shape[1]))] * grid.heads
            made = made + [like((rows, shape[1]))] * grid.heads
        elif kind == "zsplit":
            rows = terms[4].shape[0]
            made = [like((rows, shape[1]), wide_type), like((shape[0] - rows, shape[1]))]
            made = made + [like(shape)] * 3
        elif kind == "zlast":
            made = [
                like((2 * shape[0], shape[1]), wide_type),
                like((len(terms) - 2,) + terms[2].shape),
            ]
        elif kind == "stack":
            made = [like((len(terms),) + shape)]
        else:
            made = [like(shape, wide_type if kind == "wide" else low_type)]
        plan.append((len(terms), kind, len(made)))
        values += terms
        shapes += made
    first, sums = 1 + len(values) + len(deps), len(shapes)
    outs = pl.pallas_call(
        functools.partial(fold_kernel, tuple(plan), len(passes)),
        grid_spec=pltpu.PrefetchScalarGridSpec(
            num_scalar_prefetch=1,
            grid=(1,),
            in_specs=[whole_spec(value.shape) for value in values]
            + [anywhere] * (len(deps) + len(passes)),
            out_specs=[whole_spec(shape.shape) for shape in shapes] + [anywhere] * len(passes),
        ),
        out_shape=shapes + [like(value.shape) for value in passes],
        input_output_aliases={first + place: sums + place for place in range(len(passes))},
        compiler_params=room,
        cost_estimate=estimate(0, sum(3 * value.size for value in values)),
    )(head, *values, *[far(dep) for dep in deps], *passes)
    results, place = [], 0
    for _, _, given in plan:
        results.append(outs[place : place + given])
        place += given
    return results, list(outs[sums:])


def plain_job(grid, head, terms, kind):
    whole = lambda term: term
    if kind in ("core", "spread"):
        held = grid.scatter_wide(*terms)
        return [held[:2], held[2:]] if kind == "core" else list(held)
    if kind == "stack":
        return [jnp.stack(terms)]
    if kind == "zsplit":
        rows = terms[4].shape[0]
        total = total_of(terms[:4], whole)
        small = total[rows:].astype(low_type)
        return [total[:rows], small] + [jnp.concatenate([term, small], 0) for term in terms[4:]]
    if kind == "zlast":
        rows = terms[0].shape[0]
        lower = total_of(terms[1:2] + terms[3:], lambda term: term[:rows])
        blocks = jnp.stack([terms[2]] + [term[rows:] for term in terms[3:]])
        return [jnp.concatenate([terms[0], lower], 0), blocks]
    if kind in ("heads", "zpack"):
        total = total_of(terms if kind == "heads" else terms[:2], whole).astype(low_type)
        total = total.reshape((grid.heads, -1) + total.shape[1:])
        made = [total[head[0] ^ offset] for offset in range(grid.heads)]
        if kind == "heads":
            return made
        wo = total_of(terms[2:], whole).astype(low_type)
        half = made[0].shape[0] // 2
        upper = [jnp.concatenate([made[offset][:half], wo[offset]], 0) for offset in range(grid.heads)]
        return upper + [block[half:] for block in made]
    total = total_of(terms, whole)
    if kind == "wide":
        return [total]
    total = total.astype(low_type)
    if kind == "halves":
        half = total.shape[0] // 2
        return [total[:half], total[half:]]
    return list(total) if kind == "slots" else [total]


def join_kernel(count, *refs):
    for slot in range(count):
        refs[-1][slot] = refs[slot][...]


def join(values, deps=()):
    shape = (len(values),) + values[0].shape
    return pl.pallas_call(
        functools.partial(join_kernel, len(values)),
        grid=(1,),
        in_specs=[whole_spec(value.shape) for value in values] + [anywhere] * len(deps),
        out_specs=whole_spec(shape),
        out_shape=like(shape),
        compiler_params=room,
        cost_estimate=estimate(0, 4 * values[0].size),
    )(*values, *[far(dep) for dep in deps])


def three_parts(values):
    first = values.astype(low_type).astype(wide_type)
    rest = values - first
    second = rest.astype(low_type).astype(wide_type)
    return first, second, (rest - second).astype(low_type).astype(wide_type)


def pack_kernel(index_ref, q_ref, k_ref, v_ref, bq_ref, bv_ref, w_ref, piece_ref):
    rows = piece_ref.shape[0]
    w_ref[0, 0:128, :] = q_ref[0:128, :]
    w_ref[0, 128:256, :] = k_ref[0:128, :]
    w_ref[0, 256:384, :] = v_ref[0:128, :]
    w_ref[0, 384:448, :] = q_ref[128:192, :]
    w_ref[0, 448:512, :] = v_ref[128:192, :]
    w_ref[0, 512:576, :] = k_ref[128:192, :]
    row = lax.broadcasted_iota(jnp.int32, (HD, w_ref.shape[2]), 0)
    bias_q = bq_ref[...].astype(wide_type).reshape(1, 192)
    bias_v = bv_ref[...].astype(wide_type).reshape(1, 192)
    gap = jnp.zeros((1, 128), wide_type)
    bias = [bias_q[:, 0:128], gap, bias_v[:, 0:128]]
    bias.append(jnp.concatenate([bias_q[:, 128:192], bias_v[:, 128:192]], 1))
    bias = jnp.concatenate(bias + [gap] * (w_ref.shape[2] // 128 - 4), 1)
    w_ref[0, 576:640, :] = jnp.where(row == 0, bias, 0.0).astype(low_type)
    mine = pl.multiple_of(index_ref[0] * rows, 16)
    piece_ref[...] = w_ref[0, pl.ds(mine, rows), :]


def pack(part, w_query, w_key, w_value, b_query, b_value):
    width = w_query.shape[1]
    rows = 640 // PARTS
    return pl.pallas_call(
        pack_kernel,
        grid_spec=pltpu.PrefetchScalarGridSpec(
            num_scalar_prefetch=1,
            grid=(1,),
            in_specs=[whole_spec(w_query.shape)] * 3 + [whole_spec(b_query.shape)] * 2,
            out_specs=[whole_spec((1, 640, width)), whole_spec((rows, width))],
        ),
        out_shape=[far_like((1, 640, width)), far_like((rows, width))],
        compiler_params=room,
        cost_estimate=estimate(0, 4 * width * 640),
    )(part, far(w_query), far(w_key), far(w_value), far(b_query), far(b_value))


def attend_body(device_head, x_ref, w_ref, seg_ref, q_ref, k_ref, v_ref, ctx_ref):
    length = seg_ref.shape[1]
    seqs = x_ref.shape[0] // length
    lane = lax.broadcasted_iota(jnp.int32, (1, 128), 1)
    low = lane < HD
    half_lane = lane % HD
    row8 = lax.broadcasted_iota(jnp.int32, (8, length), 0)
    bias_row = w_ref[0, 576:592, :][0:1, 0:640].astype(wide_type)
    sums_at = [HD + 4, 20, HD + 12]
    extra_v = jnp.where(half_lane < 3, 1.0, 0.0)
    kept = []
    for seq in range(seqs):
        at = slice(seq * length, (seq + 1) * length)
        qkv = (dot_nt(x_ref[at, :], w_ref[0]) + bias_row).astype(low_type).astype(wide_type)
        q01 = qkv[:, 0:128] * 0.125
        k01 = qkv[:, 128:256]
        v01 = qkv[:, 256:384]
        qv2 = qkv[:, 384:512]
        queries = [q01, q01, qv2 * 0.125]
        keys = [k01, k01, qkv[:, 512:640]]
        values = [v01, v01, qv2]
        seg_row = seg_ref[pl.ds(device_head * seqs + seq, 1), :]
        seg_rows = jnp.broadcast_to(seg_row.astype(wide_type), (8, length))
        same = half_lane == seg_rows.T[:, 0:1].astype(jnp.int32)
        extra_q = jnp.where(same, 1.0, 0.0)
        mask = jnp.where((half_lane < 4) & ~same, masked_score, 0.0)
        for head in range(3):
            mine = ~low if head == 1 else low
            values_mine = low if head == 0 else ~low
            begin = sums_at[head]
            ones = (lane >= begin) & (lane < begin + 3)
            query = jnp.where(mine, queries[head], extra_q)
            key = jnp.where(mine, keys[head], jnp.where(ones, 1.0, mask)).astype(low_type)
            value = jnp.where(values_mine, values[head], extra_v).astype(low_type)
            k_ref[0, head, at, :] = key
            v_ref[0, head, at, :] = value
            kept.append((at, query, value, dot_nt(key, query.astype(low_type))))
    for seq in range(seqs):
        contexts, sums, plain = [], [], []
        for head in range(3):
            at, query, value, scores = kept[3 * seq + head]
            highest = jnp.max(scores, 0, keepdims=True)
            weights_low = jnp.exp(scores - highest).astype(low_type)
            summed = dot_tn(value, weights_low)
            total = summed[HD : HD + 1, :] if head == 0 else summed[0:1, :]
            context = summed[:HD] if head == 0 else summed[HD:]
            first, second, third = three_parts(-(highest + jnp.log(total)))
            sums.append(
                jnp.where(
                    row8 == 4, first, jnp.where(row8 == 5, second, jnp.where(row8 == 6, third, 0.0))
                )
            )
            contexts.append(context * (1.0 / total))
            plain.append(query)
        pair = jnp.concatenate(contexts[:2], 0).astype(low_type)
        ctx_ref[0, at, 0:128] = pair.T
        other = [contexts[2], sums[0], sums[2], sums[1], jnp.zeros((40, length), wide_type)]
        other = jnp.concatenate(other, 0).T
        ctx_ref[0, at, 128:192] = other[:, :HD].astype(low_type)
        turned = pltpu.roll(other, HD, 1)
        for head in range(3):
            begin = sums_at[head]
            ones = (lane >= begin) & (lane < begin + 3)
            given = turned if head == 1 else other
            q_ref[0, head, at, :] = jnp.where(ones, given, plain[head]).astype(low_type)


def attend_own_kernel(head_ref, x_ref, w_ref, seg_ref, q_ref, k_ref, v_ref, ctx_ref):
    attend_body(head_ref[0], x_ref, w_ref, seg_ref, q_ref, k_ref, v_ref, ctx_ref)


def attend_rest_kernel(parts_ref, x_ref, seg_ref, *refs):
    pieces, (q_ref, k_ref, v_ref, ctx_ref, w_ref) = refs[:PARTS], refs[-5:]
    rows = pieces[0].shape[1]
    for slot in range(PARTS):
        at = pl.ds(pl.multiple_of(parts_ref[slot] * rows, 16), rows)
        w_ref[0, at, :] = pieces[slot][0]
    attend_body(parts_ref[PARTS], x_ref, w_ref, seg_ref, q_ref, k_ref, v_ref, ctx_ref)


def attend_cost(count, tokens, length, width):
    return estimate(
        count * (2 * tokens * width * 576 + 3 * 4 * tokens * length * 128),
        2 * tokens * width + count * 2 * (576 * width + 10 * tokens * 128),
        count * 3 * tokens * length,
    )


def attend_outputs(groups, tokens, start):
    heads = pl.BlockSpec((1, 3, tokens, 128), lambda g, *_: (g + start, 0, 0, 0))
    specs = [heads, heads, heads, pl.BlockSpec((1, tokens, 192), lambda g, *_: (g + start, 0, 0))]
    shapes = [far_like((groups, 3, tokens, 128))] * 3 + [far_like((groups, tokens, 192))]
    return specs, shapes


def attend_own(head, layer_in, shard, segments, groups):
    tokens, width = layer_in.shape
    specs, shapes = attend_outputs(groups, tokens, 0)
    return pl.pallas_call(
        attend_own_kernel,
        grid_spec=pltpu.PrefetchScalarGridSpec(
            num_scalar_prefetch=1,
            grid=(1,),
            in_specs=[
                whole_spec((tokens, width)),
                whole_spec(shard.shape),
                whole_spec(segments.shape),
            ],
            out_specs=specs,
        ),
        out_shape=shapes,
        compiler_params=room,
        cost_estimate=attend_cost(1, tokens, segments.shape[1], width),
    )(head, far(layer_in), far(shard), far(segments))


def attend_rest(parts, layer_in, pieces, segments, own):
    tokens, width = layer_in.shape
    count, rows, width = pieces[0].shape
    specs, shapes = attend_outputs(count + 1, tokens, 1)
    piece = pl.BlockSpec((1, rows, width), lambda g, *_: (g, 0, 0))
    return pl.pallas_call(
        attend_rest_kernel,
        grid_spec=pltpu.PrefetchScalarGridSpec(
            num_scalar_prefetch=1,
            grid=(count,),
            in_specs=[whole_spec((tokens, width)), whole_spec(segments.shape)]
            + [piece] * PARTS
            + [anywhere] * len(own),
            out_specs=specs + [pl.BlockSpec((1, 640, width), lambda g, *_: (g, 0, 0))],
        ),
        out_shape=shapes + [far_like((count, 640, width))],
        input_output_aliases={3 + PARTS + place: place for place in range(len(own))},
        compiler_params=room,
        cost_estimate=attend_cost(count, tokens, segments.shape[1], width),
    )(parts, far(layer_in), segments, *pieces, *[far(value) for value in own])


def attend_back_kernel(
    length,
    slots_ref,
    x_ref,
    q_ref,
    k_ref,
    v_ref,
    ctx_ref,
    dctx_ref,
    spare_ref,
    *refs,
):
    dqkv_ref, near_ref, far_ref, held = refs[-4:]
    tokens, width = x_ref.shape
    rows = 640 // PARTS
    lane = lax.broadcasted_iota(jnp.int32, (1, 128), 1)
    low = lane < HD
    half_lane = lane % HD
    for seq in range(tokens // length):
        at = slice(seq * length, (seq + 1) * length)
        grad01 = dctx_ref[0, at, 0:128].astype(wide_type)
        grad2 = dctx_ref[0, at, 128:192].astype(wide_type)
        both = grad01 * ctx_ref[0, at, 0:128].astype(wide_type)
        inner = [
            jnp.sum(jnp.where(low, both, 0.0), -1, keepdims=True),
            jnp.sum(jnp.where(low, 0.0, both), -1, keepdims=True),
            jnp.sum(grad2 * ctx_ref[0, at, 128:192].astype(wide_type), -1, keepdims=True),
        ]
        grads = [grad01, grad01, jnp.concatenate([jnp.zeros((length, HD), wide_type), grad2], 1)]
        grad_q, grad_k, grad_v = [], [], []
        for head in range(3):
            first, second, third = three_parts(-inner[head])
            extra = jnp.where(
                half_lane == 0,
                first,
                jnp.where(half_lane == 1, second, jnp.where(half_lane == 2, third, 0.0)),
            )
            grad = jnp.where(low if head == 0 else ~low, grads[head], extra).astype(low_type)
            query = q_ref[0, head, at, :]
            key = k_ref[0, head, at, :]
            value = v_ref[0, head, at, :]
            total_q, parts_k, parts_v = 0.0, [], []
            for tile in range(0, length, length // 2):
                key_tile = key[tile : tile + length // 2]
                probs = jnp.exp(dot_nt(key_tile, query))
                grad_probs = dot_nt(value[tile : tile + length // 2], grad)
                grad_scores = (probs * grad_probs).astype(low_type)
                parts_v.append(dot_nn(probs.astype(low_type), grad))
                parts_k.append(dot_nn(grad_scores, query))
                total_q += dot_tn(key_tile, grad_scores)
            grad_v.append(jnp.concatenate(parts_v, 0))
            grad_k.append(jnp.concatenate(parts_k, 0))
            grad_q.append(total_q * 0.125)
        pair = jnp.concatenate([grad_q[0][:HD], grad_q[1][HD:]], 0).astype(low_type)
        dqkv_ref[0, at, 0:128] = pair.T
        dqkv_ref[0, at, 128:256] = jnp.where(low, grad_k[0], grad_k[1]).astype(low_type)
        dqkv_ref[0, at, 256:384] = jnp.where(low, grad_v[0], grad_v[1]).astype(low_type)
        single = grad_q[2].astype(low_type).T
        dqkv_ref[0, at, 384:512] = jnp.where(low, single, grad_v[2].astype(low_type))
        dqkv_ref[0, at, 512:640] = jnp.where(low, grad_k[2], 0.0).astype(low_type)
    grad_all = dqkv_ref[0]
    total = dot_tn(grad_all, x_ref[...])
    sums = jnp.sum(grad_all.astype(wide_type), 0, keepdims=True)
    sums = jnp.concatenate([sums, jnp.zeros((1, width - 640), wide_type)], 1)
    for part in range(PARTS):
        held[part] = total[part * rows : (part + 1) * rows].astype(low_type)
    row = lax.broadcasted_iota(jnp.int32, (HD, width), 0)
    spare = jnp.where(row == 0, sums, spare_ref[...].astype(wide_type))
    held[PARTS - 1, rows - HD : rows] = spare.astype(low_type)
    for slot in range(PARTS // 2):
        near_ref[slot, 0] = held[slots_ref[slot]]
        far_ref[slot, 0] = held[slots_ref[slot + PARTS // 2]]


def attend_back(
    slots, layer_in, queries, keys, values, context, grad_context, spare, deps, length
):
    tokens, width = layer_in.shape
    count = context.shape[0]
    rows = 640 // PARTS
    heads = pl.BlockSpec((1, 3, tokens, 128), lambda g, *_: (g, 0, 0, 0))
    group = pl.BlockSpec((1, tokens, 192), lambda g, *_: (g, 0, 0))
    half = pl.BlockSpec((PARTS // 2, 1, rows, width), lambda g, *_: (0, g, 0, 0))
    return pl.pallas_call(
        functools.partial(attend_back_kernel, length),
        grid_spec=pltpu.PrefetchScalarGridSpec(
            num_scalar_prefetch=1,
            grid=(count,),
            in_specs=[whole_spec((tokens, width)), heads, heads, heads, group, group]
            + [whole_spec(spare.shape)]
            + [anywhere] * len(deps),
            out_specs=[pl.BlockSpec((1, tokens, 640), lambda g, *_: (g, 0, 0)), half, half],
            scratch_shapes=[pltpu.VMEM((PARTS, rows, width), low_type)],
        ),
        out_shape=[
            (far_like if count > 1 else like)((count, tokens, 640)),
            like((PARTS // 2, count, rows, width)),
            like((PARTS // 2, count, rows, width)),
        ],
        compiler_params=room,
        cost_estimate=estimate(
            count * (2 * tokens * width * 576 + 3 * 10 * tokens * length * 128),
            2 * tokens * width + count * 2 * (576 * width + 16 * tokens * 128),
            count * 3 * tokens * length,
        ),
    )(slots, far(layer_in), queries, keys, far(values), context, grad_context, spare, *[far(dep) for dep in deps])


def mean_last(values):
    return jnp.mean(values, -1, keepdims=True)


def tiles(tokens, size, body):
    def step(index, carry):
        body(pl.ds(pl.multiple_of(index * size, size), size))
        return carry

    lax.fori_loop(0, tokens // size, step, 0)


def gelu_pair(values):
    cumulative = 0.5 * (1.0 + lax.erf(values * 0.7071067811865476))
    density = jnp.exp(-0.5 * values * values) * 0.3989422804014327
    return values * cumulative, cumulative + values * density


class Loads:
    def __init__(self, slots_ref, w_in_hbm, w_out_hbm, w_in, w_out, sems):
        self.count = sems.shape[1]
        self.size = w_out.shape[0] // self.count
        self.copies = []
        for slot in range(self.count):
            source = pl.ds(pl.multiple_of(slots_ref[slot] * self.size, 128), self.size)
            target = pl.ds(slot * self.size, self.size)
            self.copies.append(
                (
                    pltpu.make_async_copy(w_in_hbm.at[:, source], w_in.at[:, target], sems.at[0, slot]),
                    pltpu.make_async_copy(w_out_hbm.at[source], w_out.at[target], sems.at[1, slot]),
                )
            )

    def start(self):
        for copies in self.copies:
            for copy in copies:
                copy.start()

    def wait(self, low, high):
        for slot in range(-(-low // self.size), -(-high // self.size)):
            for copy in self.copies[slot]:
                copy.wait()


def overlaps(size, chunks, block, blocks):
    return [
        [
            (which, max(chunk * size, which * block), min((chunk + 1) * size, (which + 1) * block))
            for which in range(blocks)
            if max(chunk * size, which * block) < min((chunk + 1) * size, (which + 1) * block)
        ]
        for chunk in range(chunks)
    ]


def ffn_kernel(
    chunks,
    slots_ref,
    x_ref,
    ctx_ref,
    wo_ref,
    b_output_ref,
    gain_attn_ref,
    shift_attn_ref,
    b_outer_ref,
    gain_ffn_ref,
    shift_ffn_ref,
    b_in_ref,
    cot_hbm,
    w_in_hbm,
    w_out_hbm,
    rstd_ref,
    sums_ref,
    gb_ref,
    normal_hbm,
    out_hbm,
    total_hbm,
    outer_near_hbm,
    outer_far_hbm,
    near_hbm,
    far_hbm,
    w_in,
    w_out,
    normed,
    outer,
    active,
    slope,
    low,
    normal_low,
    result_low,
    grad_out,
    cot_in,
    b_row,
    sems,
    cot_sem,
    out_sems,
):
    step = pl.program_id(0)
    tokens, width = x_ref.shape
    hidden = w_out.shape[0]
    size = hidden // chunks
    half = hidden // 2
    loads = Loads(slots_ref, w_in_hbm, w_out_hbm, w_in, w_out, sems)
    head = slots_ref[loads.count]
    b_output, gain_attn, shift_attn, b_outer, gain_ffn, shift_ffn = (
        ref[...].reshape(1, width)
        for ref in (
            b_output_ref,
            gain_attn_ref,
            shift_attn_ref,
            b_outer_ref,
            gain_ffn_ref,
            shift_ffn_ref,
        )
    )
    load_cot = pltpu.make_async_copy(cot_hbm, cot_in, cot_sem.at[0])
    small = [
        pltpu.make_async_copy(source, target, out_sems.at[place])
        for place, (source, target) in enumerate(
            ((normal_low, normal_hbm), (result_low, out_hbm), (outer, total_hbm))
        )
    ]
    count = len(small)
    outer_copies, inner_copies = [], []
    for chunk, cuts in enumerate(overlaps(size, chunks, half, 2)):
        from_active, from_out = [], []
        for which, begin, end in cuts:
            at = pl.ds(begin - which * half, end - begin)
            from_active.append(
                pltpu.make_async_copy(
                    active.at[chunk, pl.ds(begin - chunk * size, end - begin), pl.ds(0, width)],
                    (outer_near_hbm, outer_far_hbm)[which].at[at],
                    out_sems.at[count],
                )
            )
            from_out.append(
                pltpu.make_async_copy(
                    w_out.at[pl.ds(begin, end - begin)],
                    (near_hbm, far_hbm)[which].at[at],
                    out_sems.at[count + 1],
                )
            )
            count += 2
        outer_copies.append(from_active)
        inner_copies.append(from_out)

    @pl.when(step == 0)
    def _():
        loads.start()
        b_row[1:2, :] = b_in_ref[...].reshape(1, hidden)
        for slot in range(loads.count):
            source = pl.ds(pl.multiple_of(slots_ref[slot] * loads.size, 128), loads.size)
            b_row[0:1, slot * loads.size : (slot + 1) * loads.size] = b_row[1:2, source]
        outer[...] = jnp.zeros_like(outer)
        branch = dot_nn(ctx_ref[0], wo_ref[head])
        for offset in range(1, wo_ref.shape[0]):
            branch += dot_nn(ctx_ref[offset], wo_ref[head ^ offset])
        normed[...] = branch

        def one(at):
            total = x_ref[at, :].astype(wide_type) + (normed[at, :] + b_output)
            centred = total - mean_last(total)
            rstd = lax.rsqrt(mean_last(centred * centred) + epsilon)
            normal = centred * rstd
            result = normal * gain_attn + shift_attn
            normed[at, :] = result
            low[at, :] = result.astype(low_type)
            normal_low[at, :] = normal.astype(low_type)
            rstd_ref[at, :] = jnp.broadcast_to(rstd, (rstd.shape[0], 128))

        tiles(tokens, 256, one)
        small[0].start()
        load_cot.start()

    for chunk in range(chunks):

        @pl.when(step == chunk)
        def _():
            loads.wait(chunk * size, (chunk + 1) * size)

    @pl.when(step < chunks)
    def _():
        at = pl.ds(pl.multiple_of(step * size, 128), size)
        inner = dot_nn(low[...], w_in[:, at]) + b_row[0:1, at]
        values, gradient = gelu_pair(inner)
        values = values.astype(low_type)
        active[step] = values
        slope[step] = gradient.astype(low_type)
        outer[...] += dot_nn(values, w_out[at, :])

    @pl.when(step == chunks - 1)
    def _():
        sums_ref[...] = jnp.zeros_like(sums_ref)
        load_cot.wait()

        def one(at):
            total = normed[at, :] + (outer[at, :] + b_outer)
            centred = total - mean_last(total)
            rstd = lax.rsqrt(mean_last(centred * centred) + epsilon)
            normal = centred * rstd
            result_low[at, :] = (normal * gain_ffn + shift_ffn).astype(low_type)
            grad = cot_in[at, :].astype(wide_type)
            scaled = grad * gain_ffn
            grad_sum = rstd * (scaled - mean_last(scaled) - normal * mean_last(scaled * normal))
            grad_low = grad_sum.astype(low_type)
            grad_out[at, :] = grad_low
            outer[at, :] = grad_low.astype(wide_type)
            sums_ref[0:1, :] += jnp.sum(grad * normal, 0, keepdims=True)
            sums_ref[1:2, :] += jnp.sum(grad, 0, keepdims=True)
            sums_ref[2:3, :] += jnp.sum(grad_low.astype(wide_type), 0, keepdims=True)

        tiles(tokens, 256, one)
        small[1].start()

    @pl.when(step >= chunks)
    def _():
        which = step - chunks
        at = pl.ds(pl.multiple_of(which * size, 128), size)
        grad = grad_out[...]
        active[which, :, 0:width] = dot_tn(active[which], grad).astype(low_type)
        grad_inner = (dot_nt(grad, w_out[at, :]) * slope[which].astype(wide_type)).astype(low_type)
        gb_ref[...] = jnp.sum(grad_inner.astype(wide_type), 0, keepdims=True)
        w_out[at, :] = dot_tn(grad_inner, low[...]).astype(low_type)
        outer[...] += dot_nt(grad_inner, w_in[:, at])

    for chunk in range(chunks):

        @pl.when(step == chunks + chunk)
        def _():
            for copy in outer_copies[chunk] + inner_copies[chunk]:
                copy.start()

    @pl.when(step == 2 * chunks - 1)
    def _():
        small[2].start()
        for copy in small:
            copy.wait()
        for copies in outer_copies + inner_copies:
            for copy in copies:
                copy.wait()


def ffn(slots, layer_in, context, w_output, cotangent, vectors, w_in, w_out, b_in):
    tokens, width = layer_in.shape
    hidden = w_out.shape[0]
    chunks = 3
    blocks = slots.shape[0] - 1
    size = hidden // chunks
    back = lambda i, *_: (0, jnp.maximum(i - chunks, 0))
    once = dict(pipeline_mode=pl.Buffered(1))
    copies = 3 + 4 * chunks
    return pl.pallas_call(
        functools.partial(ffn_kernel, chunks),
        grid_spec=pltpu.PrefetchScalarGridSpec(
            num_scalar_prefetch=1,
            grid=(2 * chunks,),
            in_specs=[
                whole_spec((tokens, width), **once),
                whole_spec(context.shape, **once),
                whole_spec(w_output.shape, **once),
            ]
            + [whole_spec(vector.shape, **once) for vector in vectors]
            + [whole_spec(b_in.shape, **once), anywhere, anywhere, anywhere],
            out_specs=[
                whole_spec((tokens, 128)),
                whole_spec((8, width)),
                pl.BlockSpec((1, size), back),
            ]
            + [anywhere] * 7,
            scratch_shapes=[
                pltpu.VMEM((width, hidden), low_type),
                pltpu.VMEM((hidden, width), low_type),
                pltpu.VMEM((tokens, width), wide_type),
                pltpu.VMEM((tokens, width), wide_type),
                pltpu.VMEM((chunks, tokens, size), low_type),
                pltpu.VMEM((chunks, tokens, size), low_type),
            ]
            + [pltpu.VMEM((tokens, width), low_type)] * 5
            + [pltpu.VMEM((8, hidden), wide_type)]
            + [pltpu.SemaphoreType.DMA((2, blocks)), pltpu.SemaphoreType.DMA((1,)), pltpu.SemaphoreType.DMA((copies,))],
        ),
        out_shape=[
            like((tokens, 128), wide_type),
            like((8, width), wide_type),
            like((1, hidden), wide_type),
            far_like((tokens, width)),
            far_like((tokens, width)),
            far_like((tokens, width), wide_type),
        ]
        + [far_like((hidden // 2, width))] * 4,
        compiler_params=large_room,
        cost_estimate=estimate(
            2 * tokens * width * (6 * hidden + width),
            2 * (tokens * 10 * width + 4 * hidden * width),
            tokens * hidden,
        ),
    )(slots, layer_in, context, w_output, *vectors, b_in, far(cotangent), far(w_in), far(w_out))


def norm_back_kernel(
    index_ref,
    total_ref,
    normal_ref,
    rstd_ref,
    ctx_ref,
    wo_ref,
    gain_ref,
    sums_in_ref,
    gb_ref,
    *refs,
):
    branch_ref, dctx_ref, near_ref, far_ref, spare_ref, sums, acc, held, inner_sums = refs[-9:]
    step = pl.program_id(0)
    size = branch_ref.shape[0]
    head = index_ref[PARTS]
    gain_attn = gain_ref[...].reshape(1, total_ref.shape[1])
    heads = wo_ref.shape[0]
    rows = wo_ref.shape[1] // PARTS

    @pl.when(step == 0)
    def _():
        sums[...] = sums_in_ref[...]

    def one(at):
        grad = total_ref[at, :]
        normal = normal_ref[at, :].astype(wide_type)
        scaled = grad * gain_attn
        rstd = rstd_ref[at, 0:1]
        grad_sum = rstd * (scaled - mean_last(scaled) - normal * mean_last(scaled * normal))
        grad_low = grad_sum.astype(low_type)
        branch_ref[at, :] = grad_low
        sums[3:4, :] += jnp.sum(grad * normal, 0, keepdims=True)
        sums[4:5, :] += jnp.sum(grad, 0, keepdims=True)
        sums[5:6, :] += jnp.sum(grad_low.astype(wide_type), 0, keepdims=True)

    tiles(size, 512, one)
    branch = branch_ref[...]
    for offset in range(heads):
        context = ctx_ref[offset]
        weights = wo_ref[head ^ offset]
        grad_context = dot_nt(branch, weights).astype(low_type)
        dctx_ref[offset] = grad_context
        part = dot_tn(context, branch)

        @pl.when(step == 0)
        def _():
            acc[offset] = part

        @pl.when(step > 0)
        def _():
            acc[offset] += part

    @pl.when(step == pl.num_programs(0) - 1)
    def _():
        for offset in range(heads):
            for part in range(PARTS):
                held[part, offset] = acc[offset, part * rows : (part + 1) * rows, :].astype(low_type)
        for slot in range(PARTS // 2):
            near_ref[slot] = held[index_ref[slot]]
            far_ref[slot] = held[index_ref[slot + PARTS // 2]]
        block = gb_ref.shape[1] // PARTS
        for slot in range(PARTS):
            inner_sums[pl.ds(index_ref[slot], 1), :] = gb_ref[:, slot * block : (slot + 1) * block]
        lines = [jnp.zeros((1, 2 * block), wide_type), sums[0:6, :]]
        for pair in range(PARTS // 2):
            both = [inner_sums[2 * pair + half : 2 * pair + half + 1, :] for half in range(2)]
            lines.append(jnp.concatenate(both, 1))
        lines.append(jnp.zeros((5, 2 * block), wide_type))
        spare_ref[...] = jnp.zeros_like(spare_ref)
        spare_ref[0:16, :] = jnp.concatenate(lines, 0).astype(low_type)


def norm_back(
    index, total, normal, rstd, context, w_output, gain, sums, gb, deps
):
    tokens, width = total.shape
    heads, group = w_output.shape[:2]
    size = tokens
    tile = pl.BlockSpec((size, width), lambda i, *_: (i, 0))
    groups = pl.BlockSpec((heads, size, group), lambda i, *_: (0, i, 0))
    half = (PARTS // 2, heads, group // PARTS, width)
    return pl.pallas_call(
        norm_back_kernel,
        grid_spec=pltpu.PrefetchScalarGridSpec(
            num_scalar_prefetch=1,
            grid=(1,),
            in_specs=[
                tile,
                tile,
                pl.BlockSpec((size, 128), lambda i, *_: (i, 0)),
                groups,
                whole_spec(w_output.shape),
                whole_spec(gain.shape),
                whole_spec(sums.shape),
                whole_spec(gb.shape),
            ]
            + [anywhere] * len(deps),
            out_specs=[
                tile,
                groups,
                whole_spec(half),
                whole_spec(half),
                whole_spec((HD, width)),
            ],
            scratch_shapes=[
                pltpu.VMEM((8, width), wide_type),
                pltpu.VMEM((heads, group, width), wide_type),
                pltpu.VMEM((PARTS,) + half[1:], low_type),
                pltpu.VMEM((PARTS, gb.shape[1] // PARTS), wide_type),
            ],
        ),
        out_shape=[
            like((tokens, width)),
            like(context.shape),
            like(half),
            like(half),
            like((HD, width)),
        ],
        compiler_params=room,
        cost_estimate=estimate(
            4 * tokens * width * width, 2 * tokens * width * 8 + 6 * width * width
        ),
    )(index, far(total), far(normal), far(rstd), far(context), far(w_output), gain, far(sums), far(gb), *[far(dep) for dep in deps])


def input_kernel(branch_ref, grads_ref, shard_ref, weights_ref, *refs):
    total = branch_ref[...].astype(wide_type) + dot_nn(grads_ref[0], shard_ref[0])
    for group in range(weights_ref.shape[0]):
        total += dot_nn(grads_ref[group + 1], weights_ref[group])
    refs[-1][...] = total


def input_back(branch, grads, shard, weights, deps):
    tokens, width = branch.shape
    size = tokens // 2
    tile = pl.BlockSpec((size, width), lambda i: (i, 0))
    groups = pl.BlockSpec((grads.shape[0], size, 640), lambda i: (0, i, 0))
    return pl.pallas_call(
        input_kernel,
        grid=(2,),
        in_specs=[tile, groups, whole_spec(shard.shape), whole_spec(weights.shape)]
        + [anywhere] * len(deps),
        out_specs=tile,
        out_shape=far_like((tokens, width), wide_type),
        compiler_params=room,
        cost_estimate=estimate(2 * tokens * width * 640 * 4, 16 * tokens * width),
    )(branch, grads, shard, weights, *[far(dep) for dep in deps])


def finish_kernel(index_ref, *refs):
    owns, blocks = refs[0:2], refs[2:4]
    q_ref, k_ref, v_ref, wo_ref, bq_ref, bv_ref, gb_ref = refs[4:11]
    vectors = refs[11:17]
    held, small_rows = refs[-2:]
    rows = held.shape[1]
    heads, extra, width = blocks[0].shape[1:]
    head, row = index_ref[PARTS], index_ref[PARTS + 1]
    for slot in range(PARTS):
        part = index_ref[slot]
        half, place = divmod(slot, PARTS // 2)
        held[part] = owns[half][place]
        for offset in range(heads):
            at = pl.ds(pl.multiple_of(part * extra, 8), extra)
            wo_ref[head ^ offset, at, :] = blocks[half][place, offset].astype(wide_type)
    whole = held[...].reshape(PARTS * rows, width)
    for ref, first, second in ((q_ref, 0, 384), (k_ref, 128, 512), (v_ref, 256, 448)):
        ref[0:128, :] = whole[first : first + 128].astype(wide_type)
        ref[128:192, :] = whole[second : second + HD].astype(wide_type)
    small_rows[...] = whole[576:592].astype(wide_type)
    sums = small_rows[0:1, :]
    for ref, first, second in ((bq_ref, 0, 384), (bv_ref, 256, 448)):
        joined = jnp.concatenate([sums[:, first : first + 128], sums[:, second : second + HD]], 1)
        ref[...] = joined.reshape(ref.shape)
    for which, ref in enumerate(vectors):
        ref[...] = small_rows[1 + which : 2 + which, :].reshape(ref.shape)
    block = gb_ref.shape[0]
    per_row = width // block
    place = row * heads + head
    sums = small_rows[pl.ds(7 + place // per_row, 1), :]
    total = jnp.zeros((1, block), wide_type)
    for which in range(per_row):
        total = jnp.where(
            place % per_row == which, sums[:, which * block : (which + 1) * block], total
        )
    gb_ref[...] = total.reshape(gb_ref.shape)


def finish(index, owns, blocks, block):
    rows = 640 // PARTS
    heads, extra, width = blocks[0].shape[1:]
    group = PARTS * extra
    pieces = owns + blocks
    shapes = (
        [like((group, width), wide_type)] * 3
        + [like((heads, group, width), wide_type)]
        + [like((group,), wide_type)] * 2
        + [like((block,), wide_type)]
        + [like((width,), wide_type)] * 6
    )
    return pl.pallas_call(
        finish_kernel,
        grid_spec=pltpu.PrefetchScalarGridSpec(
            num_scalar_prefetch=1,
            grid=(1,),
            in_specs=[whole_spec(piece.shape) for piece in pieces],
            out_specs=[whole_spec(shape.shape) for shape in shapes],
            scratch_shapes=[
                pltpu.VMEM((PARTS, rows, width), low_type),
                pltpu.VMEM((16, width), wide_type),
            ],
        ),
        out_shape=shapes,
        compiler_params=room,
        cost_estimate=estimate(0, 16 * width * width),
    )(index, *pieces)


def local(
    grid,
    layer_in,
    segment_ids,
    w_query,
    w_key,
    w_value,
    b_query,
    b_value,
    w_output,
    b_output,
    gain_attn,
    shift_attn,
    w_inner,
    b_inner,
    w_outer,
    b_outer,
    gain_ffn,
    shift_ffn,
    cotangent,
):
    tokens, width = layer_in.shape
    length = segment_ids.shape[1]
    group = w_query.shape[1]
    hidden = w_inner.shape[1]
    heads = grid.heads
    row = lax.axis_index("rows")
    head = lax.axis_index("heads")

    head_index = head.astype(jnp.int32)[None]
    part = grid.part_of(row.astype(jnp.int32))[None]
    shard, piece = pack(part, w_query.T, w_key.T, w_value.T, b_query, b_value)
    got = [grid.across_heads(piece, offset) for offset in range(1, heads)]
    own = attend_own(head_index, layer_in, shard, segment_ids, heads)
    parts = jnp.concatenate([grid.part_of(grid.helper_parts()), head_index])

    row_slots = grid.row_slots()
    w_in, w_out, b_in = w_inner, w_outer, b_inner
    if not grid.native:
        w_in = jnp.take(w_in.reshape(width, grid.rows, -1), row_slots, axis=1).reshape(width, hidden)
        w_out = jnp.take(w_out.reshape(grid.rows, -1, width), row_slots, axis=0).reshape(hidden, width)
        b_in = jnp.take(b_in.reshape(grid.rows, -1), row_slots, axis=0).reshape(hidden)
    natural = jnp.arange(PARTS, dtype=jnp.int32)
    index = jnp.concatenate([row_slots if grid.native else natural, head_index])
    w_output_heads = w_output.reshape(heads, group, width)
    vectors = [b_output, gain_attn, shift_attn, b_outer, gain_ffn, shift_ffn]
    held = join(got, (own[1],))
    held = [held] + grid.across_chips([held] * 4)
    held = held + [grid.across_core(value) for value in held]

    queries, keys, values, context, w_rest = attend_rest(parts, layer_in, held, segment_ids, own)
    rstd, sums, gb_inner, normal, layer_out, total, outer_near, outer_far, inner_near, inner_far = ffn(
        index, layer_in, context, w_output_heads, cotangent, vectors, w_in, w_out, b_in
    )
    slot_shape = (grid.rows // 2, hidden // grid.rows, width)
    outer_got = grid.across_core(outer_far.reshape(slot_shape))
    inner_got = grid.across_core(inner_far.reshape(slot_shape))
    if not grid.native:
        gb_inner = jnp.take(gb_inner.reshape(grid.rows, -1), grid.row_places(), axis=0).reshape(1, hidden)
    folded = functools.partial(fold, grid, head_index)
    first, second = grid.steps - 2, grid.steps - 1

    branch, grad_context, wo_near, wo_far, spare = norm_back(
        index, total, normal, rstd, context, w_output_heads, gain_attn, sums, gb_inner, ()
    )
    wo_near, wo_far = grid.spread_parts(wo_near, wo_far)

    ((outer, outer_send), (inner, inner_send)), (wo_far,) = folded(
        [
            ([outer_near.reshape(slot_shape), outer_got], "core"),
            ([inner_near.reshape(slot_shape), inner_got], "core"),
        ],
        (),
        (wo_far,),
    )
    outer_got = grid.across_chip(outer_send, first)
    inner_got = grid.across_chip(inner_send, first)
    wo_got = grid.across_core(wo_far)
    grads, near, far_half = attend_back(
        index, layer_in, queries, keys, values, context, grad_context, spare, (inner_send,), length
    )
    near, far_half = grid.spread_parts(near, far_half)
    ((outer, outer_send), (inner, inner_send), wo), (far_half,) = folded(
        [
            ([outer, outer_got], "halves"),
            ([inner, inner_got], "halves"),
            ([wo_near, wo_got], "spread"),
        ],
        (),
        (far_half,),
    )
    outer_got = grid.across_chip(outer_send, second)
    wo_got = grid.across_chips(wo)
    got = grid.across_core(far_half)
    input_grad = input_back(branch, grads, shard, w_rest, (wo[3],))
    (outer, (near, send)), (inner_send,) = folded(
        [
            ([outer[0], outer_got[0], wo[0]] + wo_got, "zpack"),
            ([near, got], "core"),
        ],
        (input_grad,),
        (inner_send,),
    )
    outer_got = [grid.across_heads(outer[offset], offset) for offset in range(1, heads)]
    got = grid.across_chip(send, first)
    ((upper, wo, *outer_send), (near, send)), (inner_send,) = folded(
        [
            ([outer[0]] + outer_got + list(outer[heads + 1 :]), "zsplit"),
            ([near, got], "halves"),
        ],
        (),
        (inner_send,),
    )
    outer_got = [grid.across_heads(outer_send[offset - 1], offset) for offset in range(1, heads)]
    got = grid.across_chip(send, second)
    inner_got = grid.across_chip(inner_send, second)
    (groups, (out_w_outer, wo), inner), _ = folded(
        [
            ([near[0], got[0]], "slots"),
            ([upper, outer[heads], wo] + outer_got, "zlast"),
            ([inner[0], inner_got[0]], "heads"),
        ],
    )
    got = [grid.across_heads(groups[offset], offset) for offset in range(1, heads)]
    if grid.native:
        wo_got = grid.across_chips([wo] * 4)
    ((own,),), inner = folded([([groups[0]] + got, "sum")], (), inner)
    inner_got = [grid.across_heads(inner[offset], offset) for offset in range(1, heads)]
    if grid.native:
        own_got = grid.across_chips([own] * 4)
        ((out_w_inner,), (own,), (wo,)), _ = folded(
            [
                ([inner[0]] + inner_got, "wide"),
                ([own] + own_got, "stack"),
                ([wo] + wo_got, "stack"),
            ]
        )
        owns, blocks = [own, grid.across_core(own)], [wo, grid.across_core(wo)]
    else:
        ((out_w_inner,),), _ = folded([([inner[0]] + inner_got, "wide")])
        own = grid.gather_wide(own).reshape(PARTS, -1, width)
        wo = grid.coarse(grid.gather_wide(wo))
        owns, blocks = [own[: PARTS // 2], own[PARTS // 2 :]], [wo[: PARTS // 2], wo[PARTS // 2 :]]
    block = hidden // (grid.rows * heads)
    gw_query, gw_key, gw_value, gw_output, gb_query, gb_value, gb_inner, *vector = finish(
        jnp.concatenate([index, row.astype(jnp.int32)[None]]), owns, blocks, block
    )
    return (
        layer_out,
        input_grad,
        gw_query.T,
        gw_key.T,
        gw_value.T,
        gb_query,
        gb_value,
        gw_output.reshape(width, width),
        vector[5],
        vector[3],
        vector[4],
        out_w_inner.T,
        gb_inner,
        out_w_outer,
        vector[2],
        vector[0],
        vector[1],
    )


def solution(mesh):
    grid = Grid(mesh)
    return jax.shard_map(
        lambda *values: local(grid, *values),
        mesh=mesh,
        in_specs=(
            P(("rows", "heads"), None),
            P("rows", None),
            P(None, "heads"),
            P(None, "heads"),
            P(None, "heads"),
            P("heads"),
            P("heads"),
            P(),
            P(),
            P(),
            P(),
            P(),
            P(),
            P(),
            P(),
            P(),
            P(),
            P(("rows", "heads"), None),
        ),
        out_specs=(
            P(("rows", "heads"), None),
            P(("rows", "heads"), None),
            P(None, "heads"),
            P(None, "heads"),
            P(None, "heads"),
            P("heads"),
            P("heads"),
            P(),
            P(),
            P(),
            P(),
            P(None, ("rows", "heads")),
            P(("rows", "heads")),
            P(("rows", "heads"), None),
            P(),
            P(),
            P(),
        ),
        check_vma=False,
    )
```
